32 devices in a mesh: band: 8 (over y, x, core), grp: 4 (over z).
Axes of the slice: x: 2, y: 2, z: 4, core: 2. Of those that a mesh axis runs over, the one named last changes fastest.
Arguments:
- spectral: bfloat16 [640, 2, 4, 16, 640], P(('band', 'grp')), may hold values from -6 to 6
- legendre: bfloat16 [640, 640, 640], P(('band', 'grp')), may hold values from -4 to 4
- owner_table: int32 [640], replicated, may hold values from 0 to 639, as said below
Outputs:
- spectral_out: float32 [640, 2, 4, 16, 640], P(('band', 'grp'))
The draws below stay inside these ranges and needn't reach their ends.
Inputs may be any that keep to these rules, and one draw needn't show every extreme that they name: `owner_table`: A permutation of the zonal wavenumbers. Slot s of the whole array belongs to device s // 20 along band+grp. For each q below 10, slots 2q and 2q + 1 of every device hold wavenumbers whose sum is (4q + 2) * 32 - 1.
All inputs are finite; a program needn't handle non-finite values.
Results may differ from the reference program's by a relative error of at most 0.0067.
Values may be sent and summed in bfloat16 or wider, within the bound.
No kernel may reach another device: no remote copies, remote signals or barrier semaphores. Data moves between devices by JAX's collectives and lax.ppermute only.
A program may use at most 192 MiB of HBM per device.

```python
import math
import jax
import jax.numpy as jnp
from jax import lax

M = 640
N = 640
NLAT = 1280
NLON = 2560
FIELDS = 4
LEV = 16
MDEV = 20
NHALF = 640


def draw_owner_table(key, part):
    device_count = M // MDEV
    columns = []
    shuffled = None
    for row_number in range(MDEV):
        if row_number % 2 == 1:
            columns.append(row_number * device_count + device_count - 1 - shuffled)
        else:
            shuffled = jax.random.permutation(jax.random.fold_in(key, row_number + 17), device_count)
            columns.append(row_number * device_count + shuffled)
    return jnp.stack(columns, axis=1).reshape(M).astype(jnp.int32)


def level_of(own_key, shape, split, least, top_value):
    level, own = 1.0, jax.random.fold_in(own_key, 6)
    for position, blocks in split:
        heights = jnp.exp(jax.random.uniform(jax.random.fold_in(own, position), (blocks,), jnp.float32, least / len(split), top_value / len(split)))
        level = level * jnp.repeat(heights, shape[position] // blocks).reshape([-1 if axis == position else 1 for axis in range(len(shape))])
    return level


def gaussian(key, dims, spread, bound, split=(), held_as=jnp.bfloat16):
    loudness = level_of(key, dims, split, -0.22, 0.18) if split else 1.0
    drawn = jax.random.normal(key, dims, jnp.float32) * spread * loudness
    return jnp.minimum(jnp.maximum(drawn, -bound), bound).astype(held_as)


def setup_inputs(seed: int = 0) -> dict:
    keys = jax.random.split(jax.random.key(seed), 4)
    spectral = gaussian(keys[0], (M, 2, FIELDS, LEV, N), 1.0, 6.0, ((0, 32),))
    legendre = gaussian(keys[1], (M, N, NHALF), 1.0, 4.0, ((0, 32),))
    owner_table = draw_owner_table(jax.random.fold_in(keys[3], 71), 0)
    return {"spectral": spectral, "legendre": legendre, "owner_table": owner_table}


def parity_sign(wavenumber, length):
    degree_index = jnp.arange(length, dtype=jnp.int32)
    odd_part = (degree_index[None, :] - wavenumber[:, None]) % 2
    return (1 - 2 * odd_part).astype(jnp.float32)

def make_trig(wavenumber):
    lon_index = jnp.arange(NLON, dtype=jnp.int32)
    phases = wavenumber[:, None] * lon_index[None, :] % NLON
    angles = phases.astype(jnp.float32) * (2.0 * math.pi / NLON)
    return jnp.stack([jnp.cos(angles), -jnp.sin(angles)], axis=1).astype(jnp.bfloat16)

def reference(spectral, legendre, owner_table):
    highest = lax.Precision.HIGHEST
    wavenumber = owner_table.astype(jnp.int32)
    degree_index = jnp.arange(N, dtype=jnp.int32)
    keep_mask = (degree_index[None, :] >= wavenumber[:, None]).astype(jnp.float32)
    parity = parity_sign(wavenumber, N)
    row_total = 2 * FIELDS * LEV

    def inverse_one(packed):
        spec_slot, table_slot, keep_slot, sign_slot = packed
        flattened = spec_slot.astype(jnp.float32).reshape(row_total, N) * keep_slot[None, :]
        table_wide = table_slot.astype(jnp.float32)
        northern = jnp.dot(flattened, table_wide, precision=highest)
        mirrored = jnp.dot(flattened * sign_slot[None, :], table_wide, precision=highest)
        combined = jnp.concatenate([northern, jnp.flip(mirrored, axis=1)], axis=1)
        return (combined * (1.0 / math.sqrt(N))).astype(jnp.bfloat16).reshape(2, FIELDS, LEV, NLAT)
    fourier = lax.map(inverse_one, (spectral, legendre, keep_mask, parity))
    trig_wide = make_trig(wavenumber).astype(jnp.float32)

    def grid_level(level_fourier):
        grid_values = jnp.einsum('scfi,scl->fil', level_fourier.astype(jnp.float32), trig_wide, precision=highest)
        grid_values = grid_values * (1.0 / math.sqrt(M))
        product = (grid_values * jnp.roll(grid_values, -1, axis=0)).astype(jnp.bfloat16)
        product = lax.optimization_barrier(product).astype(jnp.float32)
        zonal_coeffs = jnp.einsum('fil,scl->scfi', product, trig_wide, precision=highest)
        return (zonal_coeffs * (2.0 / math.sqrt(NLON))).astype(jnp.bfloat16)
    zonal_coeffs = lax.map(grid_level, jnp.moveaxis(fourier, 3, 0))
    zonal_coeffs = jnp.moveaxis(zonal_coeffs, 0, 3)

    def direct_one(packed):
        zonal_slot, table_slot, keep_slot, sign_slot = packed
        values = zonal_slot.astype(jnp.float32).reshape(row_total, NLAT)
        northern = values[:, :NHALF]
        mirrored = jnp.flip(values[:, NHALF:], axis=1)
        plus_part = lax.optimization_barrier((northern + mirrored).astype(jnp.bfloat16)).astype(jnp.float32)
        minus_part = lax.optimization_barrier((northern - mirrored).astype(jnp.bfloat16)).astype(jnp.float32)
        table_wide = table_slot.astype(jnp.float32)
        out_plus = jnp.dot(plus_part, table_wide.T, precision=highest)
        out_minus = jnp.dot(minus_part, table_wide.T, precision=highest)
        chosen = jnp.where(sign_slot[None, :] > 0, out_plus, out_minus)
        chosen = chosen * keep_slot[None, :] * (1.0 / math.sqrt(NLAT))
        return chosen.reshape(2, FIELDS, LEV, N)
    return lax.map(direct_one, (zonal_coeffs, legendre, keep_mask, parity))
```

```python
import functools
import math

import jax
import jax.numpy as jnp
from jax import lax
from jax.experimental import pallas as pl
from jax.experimental.pallas import tpu as pltpu
from jax.sharding import PartitionSpec as P

LANES = 128
AXES = ("band", "grp")
VMEM_BYTES = 56 * 1024 * 1024


def synthesis_kernel(slots, levels, fields, scale, spec_ref, keep_ref, flip_ref, table_ref, out_ref, rows_ref):
    step = pl.program_id(0)
    block = spec_ref.shape[0]
    row_total = spec_ref.shape[1]
    stride = 2 * slots
    for j in range(block):
        kept = spec_ref[j] * keep_ref[j]
        both = jnp.concatenate([kept, spec_ref[j] * flip_ref[j]], axis=0)
        halves = jnp.dot(both, table_ref[j], preferred_element_type=jnp.float32) * scale
        first = 2 * (step * block + j)
        for hemi in range(2):
            for part in range(2):
                for field in range(fields):
                    at = hemi * row_total + (part * fields + field) * levels
                    target = hemi * levels * stride + first + part
                    rows_ref[field, pl.ds(target, levels, stride=stride), :] = halves[at : at + levels]

    @pl.when(step == pl.num_programs(0) - 1)
    def _():
        for field in range(fields):
            out_ref[:, pl.ds(field * LANES, LANES)] = rows_ref[field].astype(out_ref.dtype)


def synthesize(spec_rows, keep, flip, legendre, tile, fields, levels):
    slots, row_total, degrees = spec_rows.shape
    block = 4
    rows = 2 * levels * 2 * slots
    return pl.pallas_call(
        functools.partial(synthesis_kernel, slots, levels, fields, 1.0 / math.sqrt(degrees)),
        grid=(slots // block,),
        in_specs=[
            pl.BlockSpec((block, row_total, degrees), lambda i: (i, 0, 0)),
            pl.BlockSpec((block, 1, degrees), lambda i: (i, 0, 0)),
            pl.BlockSpec((block, 1, degrees), lambda i: (i, 0, 0)),
            pl.BlockSpec((block, degrees, LANES), lambda i: (i, 0, tile)),
        ],
        out_specs=pl.BlockSpec((rows, fields * LANES), lambda i: (0, 0)),
        out_shape=jax.ShapeDtypeStruct((rows, fields * LANES), jnp.bfloat16),
        scratch_shapes=[pltpu.VMEM((fields, rows, LANES), jnp.float32)],
        compiler_params=pltpu.CompilerParams(vmem_limit_bytes=VMEM_BYTES),
        cost_estimate=pl.CostEstimate(
            flops=4 * slots * row_total * degrees * LANES,
            bytes_accessed=2 * slots * degrees * (row_total + LANES) + 2 * rows * fields * LANES,
            transcendentals=0,
        ),
        name="synthesis",
    )(spec_rows, keep, flip, legendre)


def longitude_kernel(grid_scale, zonal_scale, rows_ref, by_lon_ref, by_wave_ref, out_ref, sum_ref):
    step = pl.program_id(0)
    values = jnp.dot(by_lon_ref[...], rows_ref[...], preferred_element_type=jnp.float32) * grid_scale
    following = jnp.concatenate([values[:, LANES:], values[:, :LANES]], axis=1)
    product = (values * following).astype(jnp.bfloat16)
    share = jnp.dot(by_wave_ref[...], product, preferred_element_type=jnp.float32)

    @pl.when(step == 0)
    def _():
        sum_ref[...] = share

    @pl.when(step > 0)
    def _():
        sum_ref[...] += share

    @pl.when(step == pl.num_programs(0) - 1)
    def _():
        out_ref[...] = (sum_ref[...] * zonal_scale).astype(out_ref.dtype)


def longitudes(rows, by_lon, by_wave):
    depth, width = rows.shape
    lon_count = by_lon.shape[0]
    lon_block = lon_count // 5
    return pl.pallas_call(
        functools.partial(longitude_kernel, 1.0 / math.sqrt(depth // 2), 2.0 / math.sqrt(lon_count)),
        grid=(lon_count // lon_block,),
        in_specs=[
            pl.BlockSpec((depth, width), lambda i: (0, 0)),
            pl.BlockSpec((lon_block, depth), lambda i: (i, 0)),
            pl.BlockSpec((depth, lon_block), lambda i: (0, i)),
        ],
        out_specs=pl.BlockSpec((depth, width), lambda i: (0, 0)),
        out_shape=jax.ShapeDtypeStruct((depth, width), jnp.bfloat16),
        scratch_shapes=[pltpu.VMEM((depth, width), jnp.float32)],
        compiler_params=pltpu.CompilerParams(vmem_limit_bytes=VMEM_BYTES),
        cost_estimate=pl.CostEstimate(
            flops=4 * depth * width * lon_count,
            bytes_accessed=4 * depth * (width + lon_count),
            transcendentals=0,
        ),
        name="longitudes",
    )(rows, by_lon, by_wave)


def fold_kernel(slots, levels, fields, rows_ref, out_ref, plus_ref, minus_ref):
    half = rows_ref.shape[0] // 2
    stride = 2 * slots
    for field in range(fields):
        lanes = pl.ds(field * LANES, LANES)
        north = rows_ref[:half, lanes].astype(jnp.float32)
        south = rows_ref[half:, lanes].astype(jnp.float32)
        plus_ref[field] = north + south
        minus_ref[field] = north - south
    for slot in range(slots):
        for which, folded_ref in enumerate((plus_ref, minus_ref)):
            for part in range(2):
                for field in range(fields):
                    at = ((which * 2 + part) * fields + field) * levels
                    out_ref[slot, at : at + levels, :] = folded_ref[
                        field, pl.ds(2 * slot + part, levels, stride=stride), :
                    ].astype(out_ref.dtype)


def fold(rows, slots, levels, fields):
    row_total = 2 * fields * levels
    shape = (slots, 2 * row_total, LANES)
    half = pltpu.VMEM((fields, rows.shape[0] // 2, LANES), jnp.float32)
    return pl.pallas_call(
        functools.partial(fold_kernel, slots, levels, fields),
        in_specs=[pl.BlockSpec(rows.shape, lambda: (0, 0))],
        out_specs=pl.BlockSpec(shape, lambda: (0, 0, 0)),
        out_shape=jax.ShapeDtypeStruct(shape, jnp.bfloat16),
        scratch_shapes=[half, half],
        compiler_params=pltpu.CompilerParams(vmem_limit_bytes=VMEM_BYTES),
        cost_estimate=pl.CostEstimate(flops=2 * rows.size, bytes_accessed=4 * rows.size, transcendentals=0),
        name="fold",
    )(rows)


def analysis_kernel(tiles, *refs):
    folded_refs = refs[:tiles]
    even_ref, odd_ref, table_ref, out_ref = refs[tiles:]
    row_total = out_ref.shape[1]
    for j in range(out_ref.shape[0]):
        folded = jnp.concatenate([ref[j] for ref in folded_refs], axis=1)
        sums = lax.dot_general(
            folded, table_ref[j], (((1,), (1,)), ((), ())), preferred_element_type=jnp.float32
        )
        out_ref[j] = sums[:row_total] * even_ref[j] + sums[row_total:] * odd_ref[j]


def analyze(folded, even, odd, legendre, row_total):
    slots, degrees, lat_count = legendre.shape
    block = 2
    tiles = len(folded)
    folded_spec = pl.BlockSpec((block, 2 * row_total, LANES), lambda i: (i, 0, 0))
    mask_spec = pl.BlockSpec((block, 1, degrees), lambda i: (i, 0, 0))
    return pl.pallas_call(
        functools.partial(analysis_kernel, tiles),
        grid=(slots // block,),
        in_specs=[folded_spec] * tiles
        + [mask_spec, mask_spec, pl.BlockSpec((block, degrees, lat_count), lambda i: (i, 0, 0))],
        out_specs=pl.BlockSpec((block, row_total, degrees), lambda i: (i, 0, 0)),
        out_shape=jax.ShapeDtypeStruct((slots, row_total, degrees), jnp.float32),
        compiler_params=pltpu.CompilerParams(vmem_limit_bytes=VMEM_BYTES),
        cost_estimate=pl.CostEstimate(
            flops=4 * slots * row_total * degrees * lat_count,
            bytes_accessed=2 * slots * (degrees * lat_count + 2 * row_total * (lat_count + degrees)),
            transcendentals=0,
        ),
        name="analysis",
    )(*folded, even, odd, legendre)


def trig_tables(owner_table, lon_count):
    waves = jnp.repeat(owner_table, 2)
    quarter = jnp.tile(jnp.array([0, lon_count // 4], jnp.int32), owner_table.shape[0])
    lon_index = jnp.arange(lon_count, dtype=jnp.int32)

    def table(wave, turn, lon):
        phase = (wave * lon + turn) % lon_count
        return jnp.cos(phase.astype(jnp.float32) * (2.0 * math.pi / lon_count)).astype(jnp.bfloat16)

    by_lon = table(waves[None, :], quarter[None, :], lon_index[:, None])
    by_wave = table(waves[:, None], quarter[:, None], lon_index[None, :])
    return by_lon, by_wave


def exchange(rows):
    return lax.all_to_all(rows, AXES, split_axis=0, concat_axis=0, tiled=True)


def by_hemisphere_and_level(spectral, legendre, owner_table):
    slots, _, fields, levels, degrees = spectral.shape
    half_lat = legendre.shape[2]
    lon_count = 4 * half_lat
    row_total = 2 * fields * levels
    tiles = half_lat // LANES
    wavenumber = lax.dynamic_slice_in_dim(owner_table, lax.axis_index(AXES) * slots, slots)
    distance = jnp.arange(degrees, dtype=jnp.int32)[None, :] - wavenumber[:, None]
    kept = distance >= 0
    is_odd = distance % 2 != 0
    keep = kept.astype(jnp.bfloat16)[:, None, :]
    flip = jnp.where(is_odd, -keep[:, 0], keep[:, 0])[:, None, :]
    scale = 1.0 / math.sqrt(2 * half_lat)
    even = jnp.where(kept & ~is_odd, scale, 0.0).astype(jnp.float32)[:, None, :]
    odd = jnp.where(kept & is_odd, scale, 0.0).astype(jnp.float32)[:, None, :]
    spec_rows = spectral.reshape(slots, row_total, degrees)
    sent = [synthesize(spec_rows, keep, flip, legendre, t, fields, levels) for t in range(tiles)]
    arrived = [exchange(rows) for rows in sent]
    by_lon, by_wave = trig_tables(owner_table, lon_count)
    zonal = [longitudes(rows, by_lon, by_wave) for rows in arrived]
    returned = [exchange(rows) for rows in zonal]
    folded = [fold(rows, slots, levels, fields) for rows in returned]
    out = analyze(folded, even, odd, legendre, row_total)
    return out.reshape(slots, 2, fields, levels, degrees)


def make_trig(wavenumber, lon_count):
    lon_index = jnp.arange(lon_count, dtype=jnp.int32)
    phases = wavenumber[:, None] * lon_index[None, :] % lon_count
    angles = phases.astype(jnp.float32) * (2.0 * math.pi / lon_count)
    return jnp.stack([jnp.cos(angles), -jnp.sin(angles)], axis=1).astype(jnp.bfloat16)


def by_level_and_latitude(spectral, legendre, owner_table):
    slot_count, _, fields, levels, degrees = spectral.shape
    half_lat = legendre.shape[2]
    lat_count = 2 * half_lat
    lon_count = 2 * lat_count
    wave_count = owner_table.shape[0]
    band_count = lax.axis_size("band")
    group_count = lax.axis_size("grp")
    device_count = band_count * group_count
    level_block = levels // band_count
    lat_block = lat_count // group_count
    row_total = 2 * fields * levels
    row_width = fields * level_block * lat_block
    slot_start = lax.axis_index(("band", "grp")) * slot_count
    wavenumber = lax.dynamic_slice_in_dim(owner_table, slot_start, slot_count)
    degree_index = jnp.arange(degrees, dtype=jnp.int32)
    keep_mask = (degree_index[None, :] >= wavenumber[:, None]).astype(jnp.bfloat16)
    odd_part = (degree_index[None, :] - wavenumber[:, None]) % 2
    flip_sign = (1 - 2 * odd_part).astype(jnp.bfloat16)
    spec_rows = spectral.reshape(slot_count, row_total, degrees) * keep_mask[:, None, :]
    both_rows = jnp.concatenate([spec_rows, spec_rows * flip_sign[:, None, :]], axis=1)
    halves = jnp.einsum("srn,snt->srt", both_rows, legendre, preferred_element_type=jnp.float32)
    northern = halves[:, :row_total]
    mirrored = halves[:, row_total:]
    fourier = jnp.concatenate([northern, jnp.flip(mirrored, axis=2)], axis=2)
    fourier = fourier.reshape(
        slot_count, 2, fields, band_count, level_block, group_count, lat_block
    )
    fourier = jnp.transpose(fourier, (0, 1, 2, 3, 5, 4, 6))
    fourier_low = (fourier * (1.0 / math.sqrt(degrees))).astype(jnp.bfloat16)
    packed = fourier_low.reshape(1, slot_count, 2, fields, device_count, level_block, lat_block)
    arrived = lax.all_to_all(packed, ("band", "grp"), split_axis=4, concat_axis=0, tiled=True)
    arrived = arrived.reshape(-1, 2, row_width)
    trig_rows = make_trig(owner_table, lon_count)
    grid_values = jnp.einsum("scw,scl->wl", arrived, trig_rows, preferred_element_type=jnp.float32)
    grid_values = (grid_values * (1.0 / math.sqrt(wave_count))).reshape(
        fields, level_block * lat_block, lon_count
    )
    product = (grid_values * jnp.roll(grid_values, -1, axis=0)).astype(jnp.bfloat16)
    zonal_coeffs = jnp.einsum(
        "wl,scl->scw",
        product.reshape(row_width, lon_count),
        trig_rows,
        preferred_element_type=jnp.float32,
    )
    zonal_coeffs = (zonal_coeffs * (2.0 / math.sqrt(lon_count))).astype(jnp.bfloat16)
    sendback = zonal_coeffs.reshape(device_count, slot_count, 2, fields, 1, level_block, lat_block)
    returned = lax.all_to_all(sendback, ("band", "grp"), split_axis=0, concat_axis=4, tiled=True)
    returned = returned.reshape(
        slot_count, 2, fields, band_count, group_count, level_block, lat_block
    )
    returned = jnp.transpose(returned, (0, 1, 2, 3, 5, 4, 6)).reshape(slot_count, row_total, lat_count)
    northern_part = returned[:, :, :half_lat].astype(jnp.float32)
    mirror_part = jnp.flip(returned[:, :, half_lat:], axis=2).astype(jnp.float32)
    plus_part = (northern_part + mirror_part).astype(jnp.bfloat16)
    minus_part = (northern_part - mirror_part).astype(jnp.bfloat16)
    stacked = jnp.concatenate([plus_part, minus_part], axis=1)
    projected = jnp.einsum("srt,snt->srn", stacked, legendre, preferred_element_type=jnp.float32)
    even_rows = flip_sign[:, None, :] > 0
    chosen = jnp.where(even_rows, projected[:, :row_total], projected[:, row_total:])
    chosen = chosen * keep_mask.astype(jnp.float32)[:, None, :] * (1.0 / math.sqrt(lat_count))
    return chosen.reshape(slot_count, 2, fields, levels, degrees)


def on_device(spectral, legendre, owner_table):
    slots, _, _, levels, _ = spectral.shape
    whole_hemispheres = lax.axis_size("band") * lax.axis_size("grp") == 2 * levels
    if whole_hemispheres and legendre.shape[2] % LANES == 0 and slots % 4 == 0 and levels % 8 == 0:
        return by_hemisphere_and_level(spectral, legendre, owner_table)
    return by_level_and_latitude(spectral, legendre, owner_table)


def solution(mesh):
    placed = (P(("band", "grp"), None, None, None, None), P(("band", "grp"), None, None), P())
    return jax.shard_map(
        on_device,
        mesh=mesh,
        in_specs=placed,
        out_specs=P(("band", "grp"), None, None, None, None),
        check_vma=False,
    )
```

```python
import functools
import math

import jax
import jax.numpy as jnp
from jax import lax
from jax.experimental import pallas as pl
from jax.experimental.pallas import tpu as pltpu
from jax.sharding import PartitionSpec as P

LANES = 128
AXES = ("band", "grp")
VMEM_BYTES = 56 * 1024 * 1024


def synthesis_kernel(slots, levels, fields, scale, plane_ref, spec_ref, keep_ref, flip_ref, table_ref, *refs):
    out_refs, rows_ref = refs[:-1], refs[-1]
    step = pl.program_id(0)
    block = spec_ref.shape[0]
    row_total = spec_ref.shape[1]
    stride = 2 * slots
    for j in range(block):
        kept = spec_ref[j] * keep_ref[j]
        both = jnp.concatenate([kept, spec_ref[j] * flip_ref[j]], axis=0)
        halves = jnp.dot(both, table_ref[j], preferred_element_type=jnp.float32) * scale
        first = 2 * (step * block + j)
        for hemi in range(2):
            for part in range(2):
                for field in range(fields):
                    at = hemi * row_total + (part * fields + field) * levels
                    target = hemi * levels * stride + first + part
                    rows_ref[field, pl.ds(target, levels, stride=stride), :] = halves[at : at + levels]

    @pl.when(step == pl.num_programs(0) - 1)
    def _():
        for apart, out_ref in enumerate(out_refs):
            size = out_ref.shape[0]
            rows = pl.ds(pl.multiple_of((plane_ref[0] ^ apart) * size, size), size)
            for field in range(fields):
                out_ref[:, pl.ds(field * LANES, LANES)] = rows_ref[field, rows, :].astype(out_ref.dtype)


def synthesize(plane, planes, spec_rows, keep, flip, legendre, tile, fields, levels):
    slots, row_total, degrees = spec_rows.shape
    block = 4
    rows = 2 * levels * 2 * slots
    shape = (rows // planes, fields * LANES)
    return pl.pallas_call(
        functools.partial(synthesis_kernel, slots, levels, fields, 1.0 / math.sqrt(degrees)),
        grid_spec=pltpu.PrefetchScalarGridSpec(
            num_scalar_prefetch=1,
            grid=(slots // block,),
            in_specs=[
                pl.BlockSpec((block, row_total, degrees), lambda i, _: (i, 0, 0)),
                pl.BlockSpec((block, 1, degrees), lambda i, _: (i, 0, 0)),
                pl.BlockSpec((block, 1, degrees), lambda i, _: (i, 0, 0)),
                pl.BlockSpec((block, degrees, LANES), lambda i, _: (i, 0, tile)),
            ],
            out_specs=[pl.BlockSpec(shape, lambda i, _: (0, 0))] * planes,
            scratch_shapes=[pltpu.VMEM((fields, rows, LANES), jnp.float32)],
        ),
        out_shape=[jax.ShapeDtypeStruct(shape, jnp.bfloat16)] * planes,
        compiler_params=pltpu.CompilerParams(vmem_limit_bytes=VMEM_BYTES),
        cost_estimate=pl.CostEstimate(
            flops=4 * slots * row_total * degrees * LANES,
            bytes_accessed=2 * slots * degrees * (row_total + LANES) + 2 * rows * fields * LANES,
            transcendentals=0,
        ),
        name="synthesis",
    )(plane, spec_rows, keep, flip, legendre)


def longitude_kernel(grid_scale, zonal_scale, rows_ref, by_lon_ref, by_wave_ref, out_ref, sum_ref):
    step = pl.program_id(0)
    values = jnp.dot(by_lon_ref[...], rows_ref[...], preferred_element_type=jnp.float32) * grid_scale
    following = jnp.concatenate([values[:, LANES:], values[:, :LANES]], axis=1)
    product = (values * following).astype(jnp.bfloat16)
    share = jnp.dot(by_wave_ref[...], product, preferred_element_type=jnp.float32)

    @pl.when(step == 0)
    def _():
        sum_ref[...] = share

    @pl.when(step > 0)
    def _():
        sum_ref[...] += share

    @pl.when(step == pl.num_programs(0) - 1)
    def _():
        out_ref[...] = (sum_ref[...] * zonal_scale).astype(out_ref.dtype)


def longitudes(rows, by_lon, by_wave):
    depth, width = rows.shape
    lon_count = by_lon.shape[0]
    lon_block = lon_count // 5
    return pl.pallas_call(
        functools.partial(longitude_kernel, 1.0 / math.sqrt(depth // 2), 2.0 / math.sqrt(lon_count)),
        grid=(lon_count // lon_block,),
        in_specs=[
            pl.BlockSpec((depth, width), lambda i: (0, 0)),
            pl.BlockSpec((lon_block, depth), lambda i: (i, 0)),
            pl.BlockSpec((depth, lon_block), lambda i: (0, i)),
        ],
        out_specs=pl.BlockSpec((depth, width), lambda i: (0, 0)),
        out_shape=jax.ShapeDtypeStruct((depth, width), jnp.bfloat16),
        scratch_shapes=[pltpu.VMEM((depth, width), jnp.float32)],
        compiler_params=pltpu.CompilerParams(vmem_limit_bytes=VMEM_BYTES),
        cost_estimate=pl.CostEstimate(
            flops=4 * depth * width * lon_count,
            bytes_accessed=4 * depth * (width + lon_count),
            transcendentals=0,
        ),
        name="longitudes",
    )(rows, by_lon, by_wave)


def fold_kernel(slots, levels, fields, plane_ref, *refs):
    rows_refs, out_ref, rows_ref = refs[:-2], refs[-2], refs[-1]
    stride = 2 * slots
    half = levels * stride
    for apart, arrived_ref in enumerate(rows_refs):
        size = arrived_ref.shape[0]
        rows = pl.ds(pl.multiple_of((plane_ref[0] ^ apart) * size, size), size)
        for field in range(fields):
            rows_ref[field, rows, :] = arrived_ref[:, pl.ds(field * LANES, LANES)].astype(jnp.float32)
    for slot in range(slots):
        for part in range(2):
            for field in range(fields):
                first = 2 * slot + part
                north = rows_ref[field, pl.ds(first, levels, stride=stride), :]
                south = rows_ref[field, pl.ds(half + first, levels, stride=stride), :]
                at = (part * fields + field) * levels
                out_ref[slot, at : at + levels, :] = (north + south).astype(out_ref.dtype)
                at += 2 * fields * levels
                out_ref[slot, at : at + levels, :] = (north - south).astype(out_ref.dtype)


def fold(plane, parts, slots, levels, fields):
    row_total = 2 * fields * levels
    shape = (slots, 2 * row_total, LANES)
    rows = 2 * levels * 2 * slots
    size = rows * fields * LANES
    return pl.pallas_call(
        functools.partial(fold_kernel, slots, levels, fields),
        in_specs=[pl.BlockSpec(memory_space=pltpu.SMEM)] + [pl.BlockSpec(x.shape, lambda: (0, 0)) for x in parts],
        out_specs=pl.BlockSpec(shape, lambda: (0, 0, 0)),
        out_shape=jax.ShapeDtypeStruct(shape, jnp.bfloat16),
        scratch_shapes=[pltpu.VMEM((fields, rows, LANES), jnp.float32)],
        compiler_params=pltpu.CompilerParams(vmem_limit_bytes=VMEM_BYTES),
        cost_estimate=pl.CostEstimate(flops=2 * size, bytes_accessed=4 * size, transcendentals=0),
        name="fold",
    )(plane, *parts)


def analysis_kernel(tiles, *refs):
    folded_refs = refs[:tiles]
    even_ref, odd_ref, table_ref, out_ref = refs[tiles:]
    row_total = out_ref.shape[1]
    for j in range(out_ref.shape[0]):
        folded = jnp.concatenate([ref[j] for ref in folded_refs], axis=1)
        sums = lax.dot_general(
            folded, table_ref[j], (((1,), (1,)), ((), ())), preferred_element_type=jnp.float32
        )
        out_ref[j] = sums[:row_total] * even_ref[j] + sums[row_total:] * odd_ref[j]


def analyze(folded, even, odd, legendre, row_total):
    slots, degrees, lat_count = legendre.shape
    block = 2
    tiles = len(folded)
    folded_spec = pl.BlockSpec((block, 2 * row_total, LANES), lambda i: (i, 0, 0))
    mask_spec = pl.BlockSpec((block, 1, degrees), lambda i: (i, 0, 0))
    return pl.pallas_call(
        functools.partial(analysis_kernel, tiles),
        grid=(slots // block,),
        in_specs=[folded_spec] * tiles
        + [mask_spec, mask_spec, pl.BlockSpec((block, degrees, lat_count), lambda i: (i, 0, 0))],
        out_specs=pl.BlockSpec((block, row_total, degrees), lambda i: (i, 0, 0)),
        out_shape=jax.ShapeDtypeStruct((slots, row_total, degrees), jnp.float32),
        compiler_params=pltpu.CompilerParams(vmem_limit_bytes=VMEM_BYTES),
        cost_estimate=pl.CostEstimate(
            flops=4 * slots * row_total * degrees * lat_count,
            bytes_accessed=2 * slots * (degrees * lat_count + 2 * row_total * (lat_count + degrees)),
            transcendentals=0,
        ),
        name="analysis",
    )(*folded, even, odd, legendre)


def trig_kernel(cos_base_ref, sin_base_ref, cos_turn_ref, sin_turn_ref, by_wave_ref, by_lon_ref):
    for j in range(cos_base_ref.shape[1]):
        cos_base, sin_base = cos_base_ref[:, j : j + 1], sin_base_ref[:, j : j + 1]
        angles = cos_base * cos_turn_ref[...] - sin_base * sin_turn_ref[...]
        by_wave_ref[:, pl.ds(j * LANES, LANES)] = angles.astype(by_wave_ref.dtype)
        by_lon_ref[pl.ds(j * LANES, LANES), :] = angles.T.astype(by_lon_ref.dtype)


def trig_tables(owner_table, lon_count):
    waves = jnp.repeat(owner_table, 2).astype(jnp.float32)[:, None]
    quarter = jnp.tile(jnp.array([0, lon_count // 4], jnp.float32), owner_table.shape[0])[:, None]
    unit = 2.0 * math.pi / lon_count

    def angles(lon, turn):
        phase = waves * lon + turn
        return (phase - lon_count * jnp.floor(phase * (1.0 / lon_count))) * unit

    base = angles(jnp.arange(0, lon_count, LANES, dtype=jnp.float32)[None, :], quarter)
    turn = angles(jnp.arange(LANES, dtype=jnp.float32)[None, :], 0.0)
    depth = waves.shape[0]
    blocks = lon_count // LANES
    rows = 256
    small = pl.BlockSpec((rows, blocks), lambda i: (i, 0))
    wide = pl.BlockSpec((rows, LANES), lambda i: (i, 0))
    return pl.pallas_call(
        trig_kernel,
        grid=(depth // rows,),
        in_specs=[small, small, wide, wide],
        out_specs=[
            pl.BlockSpec((rows, lon_count), lambda i: (i, 0)),
            pl.BlockSpec((lon_count, rows), lambda i: (0, i)),
        ],
        out_shape=[
            jax.ShapeDtypeStruct((depth, lon_count), jnp.bfloat16),
            jax.ShapeDtypeStruct((lon_count, depth), jnp.bfloat16),
        ],
        compiler_params=pltpu.CompilerParams(vmem_limit_bytes=VMEM_BYTES),
        cost_estimate=pl.CostEstimate(
            flops=8 * depth * lon_count, bytes_accessed=4 * depth * lon_count, transcendentals=0
        ),
        name="trig",
    )(jnp.cos(base), jnp.sin(base), jnp.cos(turn), jnp.sin(turn))


def across_planes(parts):
    planes = len(parts)
    return [parts[0]] + [
        lax.ppermute(parts[x], "grp", [(p, p ^ x) for p in range(planes)]) for x in range(1, planes)
    ]


def within_plane(rows, planes):
    bands = lax.axis_size("band")
    cut = rows.reshape(planes, bands, -1, rows.shape[1])
    return lax.all_to_all(cut, "band", split_axis=1, concat_axis=1, tiled=True).reshape(rows.shape)


def by_hemisphere_and_level(spectral, legendre, owner_table):
    slots, _, fields, levels, degrees = spectral.shape
    half_lat = legendre.shape[2]
    lon_count = 4 * half_lat
    row_total = 2 * fields * levels
    tiles = half_lat // LANES
    wavenumber = lax.dynamic_slice_in_dim(owner_table, lax.axis_index(AXES) * slots, slots)
    distance = jnp.arange(degrees, dtype=jnp.int32)[None, :] - wavenumber[:, None]
    kept = distance >= 0
    is_odd = distance % 2 != 0
    keep = kept.astype(jnp.bfloat16)[:, None, :]
    flip = jnp.where(is_odd, -keep[:, 0], keep[:, 0])[:, None, :]
    scale = 1.0 / math.sqrt(2 * half_lat)
    even = jnp.where(kept & ~is_odd, scale, 0.0).astype(jnp.float32)[:, None, :]
    odd = jnp.where(kept & is_odd, scale, 0.0).astype(jnp.float32)[:, None, :]
    spec_rows = spectral.reshape(slots, row_total, degrees)
    planes, bands = lax.axis_size("grp"), lax.axis_size("band")
    plane = lax.axis_index("grp")
    apart = jnp.arange(planes, dtype=jnp.int32) ^ plane
    owners = jnp.take(owner_table.reshape(bands, planes, slots), apart, axis=1)
    owners = jnp.swapaxes(owners, 0, 1).reshape(-1)
    plane = plane.reshape(1)
    sent = [synthesize(plane, planes, spec_rows, keep, flip, legendre, t, fields, levels) for t in range(tiles)]
    arrived = [within_plane(jnp.concatenate(across_planes(parts), axis=0), planes) for parts in sent]
    by_wave, by_lon = trig_tables(owners, lon_count)
    zonal = [longitudes(rows, by_lon, by_wave) for rows in arrived]
    returned = [across_planes(jnp.split(within_plane(rows, planes), planes, axis=0)) for rows in zonal]
    folded = [fold(plane, parts, slots, levels, fields) for parts in returned]
    out = analyze(folded, even, odd, legendre, row_total)
    return out.reshape(slots, 2, fields, levels, degrees)


def make_trig(wavenumber, lon_count):
    lon_index = jnp.arange(lon_count, dtype=jnp.int32)
    phases = wavenumber[:, None] * lon_index[None, :] % lon_count
    angles = phases.astype(jnp.float32) * (2.0 * math.pi / lon_count)
    return jnp.stack([jnp.cos(angles), -jnp.sin(angles)], axis=1).astype(jnp.bfloat16)


def by_level_and_latitude(spectral, legendre, owner_table):
    slot_count, _, fields, levels, degrees = spectral.shape
    half_lat = legendre.shape[2]
    lat_count = 2 * half_lat
    lon_count = 2 * lat_count
    wave_count = owner_table.shape[0]
    band_count = lax.axis_size("band")
    group_count = lax.axis_size("grp")
    device_count = band_count * group_count
    level_block = levels // band_count
    lat_block = lat_count // group_count
    row_total = 2 * fields * levels
    row_width = fields * level_block * lat_block
    slot_start = lax.axis_index(("band", "grp")) * slot_count
    wavenumber = lax.dynamic_slice_in_dim(owner_table, slot_start, slot_count)
    degree_index = jnp.arange(degrees, dtype=jnp.int32)
    keep_mask = (degree_index[None, :] >= wavenumber[:, None]).astype(jnp.bfloat16)
    odd_part = (degree_index[None, :] - wavenumber[:, None]) % 2
    flip_sign = (1 - 2 * odd_part).astype(jnp.bfloat16)
    spec_rows = spectral.reshape(slot_count, row_total, degrees) * keep_mask[:, None, :]
    both_rows = jnp.concatenate([spec_rows, spec_rows * flip_sign[:, None, :]], axis=1)
    halves = jnp.einsum("srn,snt->srt", both_rows, legendre, preferred_element_type=jnp.float32)
    northern = halves[:, :row_total]
    mirrored = halves[:, row_total:]
    fourier = jnp.concatenate([northern, jnp.flip(mirrored, axis=2)], axis=2)
    fourier = fourier.reshape(
        slot_count, 2, fields, band_count, level_block, group_count, lat_block
    )
    fourier = jnp.transpose(fourier, (0, 1, 2, 3, 5, 4, 6))
    fourier_low = (fourier * (1.0 / math.sqrt(degrees))).astype(jnp.bfloat16)
    packed = fourier_low.reshape(1, slot_count, 2, fields, device_count, level_block, lat_block)
    arrived = lax.all_to_all(packed, ("band", "grp"), split_axis=4, concat_axis=0, tiled=True)
    arrived = arrived.reshape(-1, 2, row_width)
    trig_rows = make_trig(owner_table, lon_count)
    grid_values = jnp.einsum("scw,scl->wl", arrived, trig_rows, preferred_element_type=jnp.float32)
    grid_values = (grid_values * (1.0 / math.sqrt(wave_count))).reshape(
        fields, level_block * lat_block, lon_count
    )
    product = (grid_values * jnp.roll(grid_values, -1, axis=0)).astype(jnp.bfloat16)
    zonal_coeffs = jnp.einsum(
        "wl,scl->scw",
        product.reshape(row_width, lon_count),
        trig_rows,
        preferred_element_type=jnp.float32,
    )
    zonal_coeffs = (zonal_coeffs * (2.0 / math.sqrt(lon_count))).astype(jnp.bfloat16)
    sendback = zonal_coeffs.reshape(device_count, slot_count, 2, fields, 1, level_block, lat_block)
    returned = lax.all_to_all(sendback, ("band", "grp"), split_axis=0, concat_axis=4, tiled=True)
    returned = returned.reshape(
        slot_count, 2, fields, band_count, group_count, level_block, lat_block
    )
    returned = jnp.transpose(returned, (0, 1, 2, 3, 5, 4, 6)).reshape(slot_count, row_total, lat_count)
    northern_part = returned[:, :, :half_lat].astype(jnp.float32)
    mirror_part = jnp.flip(returned[:, :, half_lat:], axis=2).astype(jnp.float32)
    plus_part = (northern_part + mirror_part).astype(jnp.bfloat16)
    minus_part = (northern_part - mirror_part).astype(jnp.bfloat16)
    stacked = jnp.concatenate([plus_part, minus_part], axis=1)
    projected = jnp.einsum("srt,snt->srn", stacked, legendre, preferred_element_type=jnp.float32)
    even_rows = flip_sign[:, None, :] > 0
    chosen = jnp.where(even_rows, projected[:, :row_total], projected[:, row_total:])
    chosen = chosen * keep_mask.astype(jnp.float32)[:, None, :] * (1.0 / math.sqrt(lat_count))
    return chosen.reshape(slot_count, 2, fields, levels, degrees)


def on_device(spectral, legendre, owner_table):
    slots, _, _, levels, _ = spectral.shape
    planes = lax.axis_size("grp")
    whole_hemispheres = lax.axis_size("band") * planes == 2 * levels and planes & (planes - 1) == 0
    if whole_hemispheres and legendre.shape[2] % LANES == 0 and slots % 4 == 0 and levels % 8 == 0:
        return by_hemisphere_and_level(spectral, legendre, owner_table)
    return by_level_and_latitude(spectral, legendre, owner_table)


def solution(mesh):
    placed = (P(("band", "grp"), None, None, None, None), P(("band", "grp"), None, None), P())
    return jax.shard_map(
        on_device,
        mesh=mesh,
        in_specs=placed,
        out_specs=P(("band", "grp"), None, None, None, None),
        check_vma=False,
    )
```

```python
import functools
import math

import jax
import jax.numpy as jnp
from jax import lax
from jax.experimental import pallas as pl
from jax.experimental.pallas import tpu as pltpu
from jax.sharding import PartitionSpec as P

LANES = 128
AXES = ("band", "grp")
VMEM_BYTES = 56 * 1024 * 1024


def synthesis_kernel(slots, levels, fields, least, scale, plane_ref, spec_ref, keep_ref, flip_ref, table_ref, *refs):
    out_refs, rows_ref = refs[:-1], refs[-1]
    tiles = rows_ref.shape[1]
    step = pl.program_id(0)
    block = spec_ref.shape[0]
    row_total = spec_ref.shape[1]
    stride = 2 * slots

    def run(group):
        start = least[group]
        for j in range(block):
            spec = spec_ref[j, :, start:]
            both = jnp.concatenate([spec * keep_ref[j, :, start:], spec * flip_ref[j, :, start:]], axis=0)
            halves = jnp.dot(both, table_ref[j, start:, :], preferred_element_type=jnp.float32) * scale
            first = 2 * (group * block + j)
            for hemi in range(2):
                for part in range(2):
                    for field in range(fields):
                        at = hemi * row_total + (part * fields + field) * levels
                        target = pl.ds(hemi * levels * stride + first + part, levels, stride=stride)
                        for tile in range(tiles):
                            lanes = slice(tile * LANES, (tile + 1) * LANES)
                            rows_ref[field, tile, target, :] = halves[at : at + levels, lanes]

    for group in range(slots // block):
        pl.when(step == group)(functools.partial(run, group))

    @pl.when(step == pl.num_programs(0) - 1)
    def _():
        for apart, out_ref in enumerate(out_refs):
            size = out_ref.shape[0]
            rows = pl.ds(pl.multiple_of((plane_ref[0] ^ apart) * size, size), size)
            for field in range(fields):
                for tile in range(tiles):
                    lanes = pl.ds((field * tiles + tile) * LANES, LANES)
                    out_ref[:, lanes] = rows_ref[field, tile, rows, :].astype(out_ref.dtype)


def synthesize(plane, planes, spec_rows, keep, flip, legendre, chunk, fields, levels, least):
    slots, row_total, degrees = spec_rows.shape
    block = slots // len(least)
    rows = 2 * levels * 2 * slots
    at, tiles = chunk
    shape = (rows // planes, fields * tiles * LANES)
    return pl.pallas_call(
        functools.partial(synthesis_kernel, slots, levels, fields, least, 1.0 / math.sqrt(degrees)),
        grid_spec=pltpu.PrefetchScalarGridSpec(
            num_scalar_prefetch=1,
            grid=(slots // block,),
            in_specs=[
                pl.BlockSpec((block, row_total, degrees), lambda i, _: (i, 0, 0)),
                pl.BlockSpec((block, 1, degrees), lambda i, _: (i, 0, 0)),
                pl.BlockSpec((block, 1, degrees), lambda i, _: (i, 0, 0)),
                pl.BlockSpec((block, degrees, tiles * LANES), lambda i, _: (i, 0, at // tiles)),
            ],
            out_specs=[pl.BlockSpec(shape, lambda i, _: (0, 0))] * planes,
            scratch_shapes=[pltpu.VMEM((fields, tiles, rows, LANES), jnp.float32)],
        ),
        out_shape=[jax.ShapeDtypeStruct(shape, jnp.bfloat16)] * planes,
        compiler_params=pltpu.CompilerParams(vmem_limit_bytes=VMEM_BYTES),
        cost_estimate=pl.CostEstimate(
            flops=4 * slots * row_total * degrees * tiles * LANES,
            bytes_accessed=2 * slots * degrees * (row_total + tiles * LANES) + 2 * rows * shape[1],
            transcendentals=0,
        ),
        name="synthesis",
    )(plane, spec_rows, keep, flip, legendre)


def longitude_kernel(fields, grid_scale, zonal_scale, rows_ref, by_lon_ref, by_wave_ref, out_ref, sum_ref):
    step = pl.program_id(0)
    values = jnp.dot(by_lon_ref[...], rows_ref[...], preferred_element_type=jnp.float32) * grid_scale
    one = values.shape[1] // fields
    following = jnp.concatenate([values[:, one:], values[:, :one]], axis=1)
    product = (values * following).astype(jnp.bfloat16)
    share = jnp.dot(by_wave_ref[...], product, preferred_element_type=jnp.float32)

    @pl.when(step == 0)
    def _():
        sum_ref[...] = share

    @pl.when(step > 0)
    def _():
        sum_ref[...] += share

    @pl.when(step == pl.num_programs(0) - 1)
    def _():
        out_ref[...] = (sum_ref[...] * zonal_scale).astype(out_ref.dtype)


def longitudes(rows, by_lon, by_wave, fields):
    depth, width = rows.shape
    lon_count = by_lon.shape[0]
    lon_block = lon_count // 5
    return pl.pallas_call(
        functools.partial(longitude_kernel, fields, 1.0 / math.sqrt(depth // 2), 2.0 / math.sqrt(lon_count)),
        grid=(lon_count // lon_block,),
        in_specs=[
            pl.BlockSpec((depth, width), lambda i: (0, 0)),
            pl.BlockSpec((lon_block, depth), lambda i: (i, 0)),
            pl.BlockSpec((depth, lon_block), lambda i: (0, i)),
        ],
        out_specs=pl.BlockSpec((depth, width), lambda i: (0, 0)),
        out_shape=jax.ShapeDtypeStruct((depth, width), jnp.bfloat16),
        scratch_shapes=[pltpu.VMEM((depth, width), jnp.float32)],
        compiler_params=pltpu.CompilerParams(vmem_limit_bytes=VMEM_BYTES),
        cost_estimate=pl.CostEstimate(
            flops=4 * depth * width * lon_count,
            bytes_accessed=4 * depth * (width + lon_count),
            transcendentals=0,
        ),
        name="longitudes",
    )(rows, by_lon, by_wave)


def fold_kernel(slots, levels, fields, plane_ref, *refs):
    rows_refs, out_ref, rows_ref = refs[:-2], refs[-2], refs[-1]
    tiles = rows_ref.shape[1]
    stride = 2 * slots
    half = levels * stride
    for apart, arrived_ref in enumerate(rows_refs):
        size = arrived_ref.shape[0]
        rows = pl.ds(pl.multiple_of((plane_ref[0] ^ apart) * size, size), size)
        for field in range(fields):
            for tile in range(tiles):
                lanes = pl.ds((field * tiles + tile) * LANES, LANES)
                rows_ref[field, tile, rows, :] = arrived_ref[:, lanes].astype(jnp.float32)
    for slot in range(slots):
        for part in range(2):
            for field in range(fields):
                for tile in range(tiles):
                    first = 2 * slot + part
                    north = rows_ref[field, tile, pl.ds(first, levels, stride=stride), :]
                    south = rows_ref[field, tile, pl.ds(half + first, levels, stride=stride), :]
                    lanes = pl.ds(tile * LANES, LANES)
                    at = (part * fields + field) * levels
                    out_ref[slot, at : at + levels, lanes] = (north + south).astype(out_ref.dtype)
                    at += 2 * fields * levels
                    out_ref[slot, at : at + levels, lanes] = (north - south).astype(out_ref.dtype)


def fold(plane, parts, slots, levels, fields):
    row_total = 2 * fields * levels
    rows = 2 * levels * 2 * slots
    tiles = parts[0].shape[1] // (fields * LANES)
    shape = (slots, 2 * row_total, tiles * LANES)
    size = rows * parts[0].shape[1]
    return pl.pallas_call(
        functools.partial(fold_kernel, slots, levels, fields),
        in_specs=[pl.BlockSpec(memory_space=pltpu.SMEM)] + [pl.BlockSpec(x.shape, lambda: (0, 0)) for x in parts],
        out_specs=pl.BlockSpec(shape, lambda: (0, 0, 0)),
        out_shape=jax.ShapeDtypeStruct(shape, jnp.bfloat16),
        scratch_shapes=[pltpu.VMEM((fields, tiles, rows, LANES), jnp.float32)],
        compiler_params=pltpu.CompilerParams(vmem_limit_bytes=VMEM_BYTES),
        cost_estimate=pl.CostEstimate(flops=2 * size, bytes_accessed=4 * size, transcendentals=0),
        name="fold",
    )(plane, *parts)


def analysis_kernel(chunks, least, *refs):
    folded_refs = refs[:chunks]
    even_ref, odd_ref, table_ref, out_ref = refs[chunks:]
    row_total, degrees = out_ref.shape[1:]
    step = pl.program_id(0)

    def run(group):
        start = least[group]
        for j in range(out_ref.shape[0]):
            folded = jnp.concatenate([ref[j] for ref in folded_refs], axis=1)
            sums = lax.dot_general(
                folded, table_ref[j, start:, :], (((1,), (1,)), ((), ())), preferred_element_type=jnp.float32
            )
            kept = sums[:row_total] * even_ref[j, :, start:] + sums[row_total:] * odd_ref[j, :, start:]
            out_ref[j, :, start:] = kept
            if start:
                out_ref[j, :, :start] = jnp.zeros((row_total, start), out_ref.dtype)

    for group in range(len(least)):
        pl.when(step == group)(functools.partial(run, group))


def analyze(folded, even, odd, legendre, row_total, least):
    slots, degrees, lat_count = legendre.shape
    block = slots // len(least)
    mask_spec = pl.BlockSpec((block, 1, degrees), lambda i: (i, 0, 0))
    return pl.pallas_call(
        functools.partial(analysis_kernel, len(folded), least),
        grid=(len(least),),
        in_specs=[pl.BlockSpec((block,) + x.shape[1:], lambda i: (i, 0, 0)) for x in folded]
        + [mask_spec, mask_spec, pl.BlockSpec((block, degrees, lat_count), lambda i: (i, 0, 0))],
        out_specs=pl.BlockSpec((block, row_total, degrees), lambda i: (i, 0, 0)),
        out_shape=jax.ShapeDtypeStruct((slots, row_total, degrees), jnp.float32),
        compiler_params=pltpu.CompilerParams(vmem_limit_bytes=VMEM_BYTES),
        cost_estimate=pl.CostEstimate(
            flops=4 * slots * row_total * degrees * lat_count,
            bytes_accessed=2 * slots * (degrees * lat_count + 2 * row_total * (lat_count + degrees)),
            transcendentals=0,
        ),
        name="analysis",
    )(*folded, even, odd, legendre)


def trig_kernel(cos_base_ref, sin_base_ref, cos_turn_ref, sin_turn_ref, cos_base_t, sin_base_t, cos_turn_t, sin_turn_t, by_wave_ref, by_lon_ref):
    for j in range(cos_base_ref.shape[1]):
        lanes = pl.ds(j * LANES, LANES)
        cos_base, sin_base = cos_base_ref[:, j : j + 1], sin_base_ref[:, j : j + 1]
        angles = cos_base * cos_turn_ref[...] - sin_base * sin_turn_ref[...]
        by_wave_ref[:, lanes] = angles.astype(by_wave_ref.dtype)
        cos_base, sin_base = cos_base_t[j : j + 1, :], sin_base_t[j : j + 1, :]
        angles = cos_base * cos_turn_t[...] - sin_base * sin_turn_t[...]
        by_lon_ref[lanes, :] = angles.astype(by_lon_ref.dtype)


def trig_tables(owner_table, lon_count):
    waves = jnp.repeat(owner_table, 2).astype(jnp.float32)[:, None]
    quarter = jnp.tile(jnp.array([0, lon_count // 4], jnp.float32), owner_table.shape[0])[:, None]
    unit = 2.0 * math.pi / lon_count

    def angles(lon, turn):
        phase = waves * lon + turn
        return (phase - lon_count * jnp.floor(phase * (1.0 / lon_count))) * unit

    base = angles(jnp.arange(0, lon_count, LANES, dtype=jnp.float32)[None, :], quarter)
    turn = angles(jnp.arange(LANES, dtype=jnp.float32)[None, :], 0.0)
    depth = waves.shape[0]
    blocks = lon_count // LANES
    rows = 256
    small = pl.BlockSpec((rows, blocks), lambda i: (i, 0))
    wide = pl.BlockSpec((rows, LANES), lambda i: (i, 0))
    small_t = pl.BlockSpec((blocks, rows), lambda i: (0, i))
    wide_t = pl.BlockSpec((LANES, rows), lambda i: (0, i))
    parts = (jnp.cos(base), jnp.sin(base), jnp.cos(turn), jnp.sin(turn))
    return pl.pallas_call(
        trig_kernel,
        grid=(depth // rows,),
        in_specs=[small, small, wide, wide, small_t, small_t, wide_t, wide_t],
        out_specs=[
            pl.BlockSpec((rows, lon_count), lambda i: (i, 0)),
            pl.BlockSpec((lon_count, rows), lambda i: (0, i)),
        ],
        out_shape=[
            jax.ShapeDtypeStruct((depth, lon_count), jnp.bfloat16),
            jax.ShapeDtypeStruct((lon_count, depth), jnp.bfloat16),
        ],
        compiler_params=pltpu.CompilerParams(vmem_limit_bytes=VMEM_BYTES),
        cost_estimate=pl.CostEstimate(
            flops=8 * depth * lon_count, bytes_accessed=4 * depth * lon_count, transcendentals=0
        ),
        name="trig",
    )(*parts, *[x.T for x in parts])


def across_planes(parts):
    planes = len(parts)
    return [parts[0]] + [
        lax.ppermute(parts[x], "grp", [(p, p ^ x) for p in range(planes)]) for x in range(1, planes)
    ]


def within_plane(rows):
    bands = lax.axis_size("band")
    cut = rows.reshape(bands, -1, rows.shape[-1])
    return lax.all_to_all(cut, "band", split_axis=0, concat_axis=0, tiled=True)


def after(value, *others):
    return lax.optimization_barrier((value, others))[0]


def by_hemisphere_and_level(spectral, legendre, owner_table):
    slots, _, fields, levels, degrees = spectral.shape
    half_lat = legendre.shape[2]
    lon_count = 4 * half_lat
    row_total = 2 * fields * levels
    tiles = half_lat // LANES
    wavenumber = lax.dynamic_slice_in_dim(owner_table, lax.axis_index(AXES) * slots, slots)
    distance = jnp.arange(degrees, dtype=jnp.int32)[None, :] - wavenumber[:, None]
    kept = distance >= 0
    is_odd = distance % 2 != 0
    keep = kept.astype(jnp.bfloat16)[:, None, :]
    flip = jnp.where(is_odd, -keep[:, 0], keep[:, 0])[:, None, :]
    scale = 1.0 / math.sqrt(2 * half_lat)
    even = jnp.where(kept & ~is_odd, scale, 0.0).astype(jnp.float32)[:, None, :]
    odd = jnp.where(kept & is_odd, scale, 0.0).astype(jnp.float32)[:, None, :]
    spec_rows = spectral.reshape(slots, row_total, degrees)
    planes, bands = lax.axis_size("grp"), lax.axis_size("band")
    plane = lax.axis_index("grp")
    apart = jnp.arange(planes, dtype=jnp.int32) ^ plane
    owners = jnp.take(owner_table.reshape(bands, planes, slots), apart, axis=1).reshape(-1)
    plane = plane.reshape(1)
    least = tuple(4 * g * bands * planes for g in range(slots // 4))
    chunks = [(tiles - 1, 1)] if tiles % 2 else []
    chunks += [(t, 2) for t in range(0, tiles - 1, 2)]

    def send(spec, chunk):
        return synthesize(plane, planes, spec, keep, flip, legendre, chunk, fields, levels, least)

    def gather(parts):
        width = parts[0].shape[-1]
        stacked = jnp.stack([x.reshape(bands, -1, width) for x in parts], axis=1)
        return within_plane(stacked).reshape(-1, width)

    def give_back(rows):
        width = rows.shape[-1]
        cut = within_plane(rows).reshape(bands, planes, -1, width)
        return across_planes([cut[:, x].reshape(-1, width) for x in range(planes)])

    def transform(rows):
        return longitudes(rows, by_lon, by_wave, fields)

    sent = send(spec_rows, chunks[0])
    by_wave, by_lon = trig_tables(owners, lon_count)
    following = send(after(spec_rows, by_wave), chunks[1])
    returned = []
    for position in range(len(chunks)):
        moved = across_planes(sent)
        if following is not None:
            moved = after(moved, *following)
        zonal = transform(gather(moved))
        sent = following
        following = None
        if position + 2 < len(chunks):
            following = send(after(spec_rows, zonal), chunks[position + 2])
        returned.append(give_back(zonal))
    folded = {chunk: fold(plane, parts, slots, levels, fields) for chunk, parts in zip(chunks, returned)}
    out = analyze([folded[chunk] for chunk in sorted(chunks)], even, odd, legendre, row_total, least)
    return out.reshape(slots, 2, fields, levels, degrees)


def make_trig(wavenumber, lon_count):
    lon_index = jnp.arange(lon_count, dtype=jnp.int32)
    phases = wavenumber[:, None] * lon_index[None, :] % lon_count
    angles = phases.astype(jnp.float32) * (2.0 * math.pi / lon_count)
    return jnp.stack([jnp.cos(angles), -jnp.sin(angles)], axis=1).astype(jnp.bfloat16)


def by_level_and_latitude(spectral, legendre, owner_table):
    slot_count, _, fields, levels, degrees = spectral.shape
    half_lat = legendre.shape[2]
    lat_count = 2 * half_lat
    lon_count = 2 * lat_count
    wave_count = owner_table.shape[0]
    band_count = lax.axis_size("band")
    group_count = lax.axis_size("grp")
    device_count = band_count * group_count
    level_block = levels // band_count
    lat_block = lat_count // group_count
    row_total = 2 * fields * levels
    row_width = fields * level_block * lat_block
    slot_start = lax.axis_index(("band", "grp")) * slot_count
    wavenumber = lax.dynamic_slice_in_dim(owner_table, slot_start, slot_count)
    degree_index = jnp.arange(degrees, dtype=jnp.int32)
    keep_mask = (degree_index[None, :] >= wavenumber[:, None]).astype(jnp.bfloat16)
    odd_part = (degree_index[None, :] - wavenumber[:, None]) % 2
    flip_sign = (1 - 2 * odd_part).astype(jnp.bfloat16)
    spec_rows = spectral.reshape(slot_count, row_total, degrees) * keep_mask[:, None, :]
    both_rows = jnp.concatenate([spec_rows, spec_rows * flip_sign[:, None, :]], axis=1)
    halves = jnp.einsum("srn,snt->srt", both_rows, legendre, preferred_element_type=jnp.float32)
    northern = halves[:, :row_total]
    mirrored = halves[:, row_total:]
    fourier = jnp.concatenate([northern, jnp.flip(mirrored, axis=2)], axis=2)
    fourier = fourier.reshape(
        slot_count, 2, fields, band_count, level_block, group_count, lat_block
    )
    fourier = jnp.transpose(fourier, (0, 1, 2, 3, 5, 4, 6))
    fourier_low = (fourier * (1.0 / math.sqrt(degrees))).astype(jnp.bfloat16)
    packed = fourier_low.reshape(1, slot_count, 2, fields, device_count, level_block, lat_block)
    arrived = lax.all_to_all(packed, ("band", "grp"), split_axis=4, concat_axis=0, tiled=True)
    arrived = arrived.reshape(-1, 2, row_width)
    trig_rows = make_trig(owner_table, lon_count)
    grid_values = jnp.einsum("scw,scl->wl", arrived, trig_rows, preferred_element_type=jnp.float32)
    grid_values = (grid_values * (1.0 / math.sqrt(wave_count))).reshape(
        fields, level_block * lat_block, lon_count
    )
    product = (grid_values * jnp.roll(grid_values, -1, axis=0)).astype(jnp.bfloat16)
    zonal_coeffs = jnp.einsum(
        "wl,scl->scw",
        product.reshape(row_width, lon_count),
        trig_rows,
        preferred_element_type=jnp.float32,
    )
    zonal_coeffs = (zonal_coeffs * (2.0 / math.sqrt(lon_count))).astype(jnp.bfloat16)
    sendback = zonal_coeffs.reshape(device_count, slot_count, 2, fields, 1, level_block, lat_block)
    returned = lax.all_to_all(sendback, ("band", "grp"), split_axis=0, concat_axis=4, tiled=True)
    returned = returned.reshape(
        slot_count, 2, fields, band_count, group_count, level_block, lat_block
    )
    returned = jnp.transpose(returned, (0, 1, 2, 3, 5, 4, 6)).reshape(slot_count, row_total, lat_count)
    northern_part = returned[:, :, :half_lat].astype(jnp.float32)
    mirror_part = jnp.flip(returned[:, :, half_lat:], axis=2).astype(jnp.float32)
    plus_part = (northern_part + mirror_part).astype(jnp.bfloat16)
    minus_part = (northern_part - mirror_part).astype(jnp.bfloat16)
    stacked = jnp.concatenate([plus_part, minus_part], axis=1)
    projected = jnp.einsum("srt,snt->srn", stacked, legendre, preferred_element_type=jnp.float32)
    even_rows = flip_sign[:, None, :] > 0
    chosen = jnp.where(even_rows, projected[:, :row_total], projected[:, row_total:])
    chosen = chosen * keep_mask.astype(jnp.float32)[:, None, :] * (1.0 / math.sqrt(lat_count))
    return chosen.reshape(slot_count, 2, fields, levels, degrees)


def on_device(spectral, legendre, owner_table):
    slots, _, _, levels, _ = spectral.shape
    planes = lax.axis_size("grp")
    whole_hemispheres = lax.axis_size("band") * planes == 2 * levels and planes & (planes - 1) == 0
    if whole_hemispheres and legendre.shape[2] % LANES == 0 and slots % 4 == 0 and levels % 8 == 0:
        return by_hemisphere_and_level(spectral, legendre, owner_table)
    return by_level_and_latitude(spectral, legendre, owner_table)


def solution(mesh):
    placed = (P(("band", "grp"), None, None, None, None), P(("band", "grp"), None, None), P())
    return jax.shard_map(
        on_device,
        mesh=mesh,
        in_specs=placed,
        out_specs=P(("band", "grp"), None, None, None, None),
        check_vma=False,
    )
```

```python
import functools
import math

import jax
import jax.numpy as jnp
from jax import lax
from jax.experimental import pallas as pl
from jax.experimental.pallas import tpu as pltpu
from jax.sharding import PartitionSpec as P

LANES = 128
AXES = ("band", "grp")
VMEM_BYTES = 56 * 1024 * 1024
BRIEF = pl.CostEstimate(flops=10**6, bytes_accessed=10**4, transcendentals=0)


def synthesis_kernel(slots, levels, fields, least, scale, plane_ref, spec_ref, keep_ref, flip_ref, table_ref, *refs):
    out_refs, rows_ref = refs[:-1], refs[-1]
    tiles = rows_ref.shape[1]
    step = pl.program_id(0)
    block = spec_ref.shape[0]
    row_total = spec_ref.shape[1]
    stride = 2 * slots

    def run(group):
        start = least[group]
        for j in range(block):
            spec = spec_ref[j, :, start:]
            both = jnp.concatenate([spec * keep_ref[j, :, start:], spec * flip_ref[j, :, start:]], axis=0)
            halves = jnp.dot(both, table_ref[j, start:, :], preferred_element_type=jnp.float32) * scale
            first = 2 * (group * block + j)
            for hemi in range(2):
                for part in range(2):
                    for field in range(fields):
                        at = hemi * row_total + (part * fields + field) * levels
                        target = pl.ds(hemi * levels * stride + first + part, levels, stride=stride)
                        for tile in range(tiles):
                            lanes = slice(tile * LANES, (tile + 1) * LANES)
                            rows_ref[field, tile, target, :] = halves[at : at + levels, lanes]

    for group in range(slots // block):
        pl.when(step == group)(functools.partial(run, group))

    @pl.when(step == pl.num_programs(0) - 1)
    def _():
        for apart, out_ref in enumerate(out_refs):
            size = out_ref.shape[0]
            rows = pl.ds(pl.multiple_of(lax.rem(plane_ref[0] + apart, len(out_refs)) * size, size), size)
            for field in range(fields):
                for tile in range(tiles):
                    lanes = pl.ds((field * tiles + tile) * LANES, LANES)
                    out_ref[:, lanes] = rows_ref[field, tile, rows, :].astype(out_ref.dtype)


def synthesize(plane, planes, spec_rows, keep, flip, legendre, chunk, fields, levels, least):
    slots, row_total, degrees = spec_rows.shape
    block = slots // len(least)
    rows = 2 * levels * 2 * slots
    at, tiles = chunk
    shape = (rows // planes, fields * tiles * LANES)
    return pl.pallas_call(
        functools.partial(synthesis_kernel, slots, levels, fields, least, 1.0 / math.sqrt(degrees)),
        grid_spec=pltpu.PrefetchScalarGridSpec(
            num_scalar_prefetch=1,
            grid=(slots // block,),
            in_specs=[
                pl.BlockSpec((block, row_total, degrees), lambda i, _: (i, 0, 0)),
                pl.BlockSpec((block, 1, degrees), lambda i, _: (i, 0, 0)),
                pl.BlockSpec((block, 1, degrees), lambda i, _: (i, 0, 0)),
                pl.BlockSpec((block, degrees, tiles * LANES), lambda i, _: (i, 0, at // tiles)),
            ],
            out_specs=[pl.BlockSpec(shape, lambda i, _: (0, 0))] * planes,
            scratch_shapes=[pltpu.VMEM((fields, tiles, rows, LANES), jnp.float32)],
        ),
        out_shape=[jax.ShapeDtypeStruct(shape, jnp.bfloat16)] * planes,
        compiler_params=pltpu.CompilerParams(vmem_limit_bytes=VMEM_BYTES),
        cost_estimate=BRIEF,
        name="synthesis",
    )(plane, spec_rows, keep, flip, legendre)


def longitude_kernel(fields, grid_scale, zonal_scale, rows_ref, by_lon_ref, by_wave_ref, out_ref, sum_ref):
    step = pl.program_id(0)
    values = jnp.dot(by_lon_ref[...], rows_ref[...], preferred_element_type=jnp.float32) * grid_scale
    one = values.shape[1] // fields
    following = jnp.concatenate([values[:, one:], values[:, :one]], axis=1)
    product = (values * following).astype(jnp.bfloat16)
    share = jnp.dot(by_wave_ref[...], product, preferred_element_type=jnp.float32)

    @pl.when(step == 0)
    def _():
        sum_ref[...] = share

    @pl.when(step > 0)
    def _():
        sum_ref[...] += share

    @pl.when(step == pl.num_programs(0) - 1)
    def _():
        out_ref[...] = (sum_ref[...] * zonal_scale).astype(out_ref.dtype)


def longitudes(rows, by_lon, by_wave, fields):
    depth, width = rows.shape
    lon_count = by_lon.shape[0]
    lon_block = lon_count // 5
    return pl.pallas_call(
        functools.partial(longitude_kernel, fields, 1.0 / math.sqrt(depth // 2), 2.0 / math.sqrt(lon_count)),
        grid=(lon_count // lon_block,),
        in_specs=[
            pl.BlockSpec((depth, width), lambda i: (0, 0)),
            pl.BlockSpec((lon_block, depth), lambda i: (i, 0)),
            pl.BlockSpec((depth, lon_block), lambda i: (0, i)),
        ],
        out_specs=pl.BlockSpec((depth, width), lambda i: (0, 0)),
        out_shape=jax.ShapeDtypeStruct((depth, width), jnp.bfloat16),
        scratch_shapes=[pltpu.VMEM((depth, width), jnp.float32)],
        compiler_params=pltpu.CompilerParams(vmem_limit_bytes=VMEM_BYTES),
        cost_estimate=BRIEF,
        name="longitudes",
    )(rows, by_lon, by_wave)


def fold_kernel(slots, levels, fields, plane_ref, *refs):
    rows_refs, out_ref, rows_ref = refs[:-2], refs[-2], refs[-1]
    tiles = rows_ref.shape[1]
    stride = 2 * slots
    half = levels * stride
    for apart, arrived_ref in enumerate(rows_refs):
        size = arrived_ref.shape[0]
        rows = pl.ds(pl.multiple_of(lax.rem(plane_ref[0] + apart, len(rows_refs)) * size, size), size)
        for field in range(fields):
            for tile in range(tiles):
                lanes = pl.ds((field * tiles + tile) * LANES, LANES)
                rows_ref[field, tile, rows, :] = arrived_ref[:, lanes].astype(jnp.float32)
    for slot in range(slots):
        for part in range(2):
            for field in range(fields):
                for tile in range(tiles):
                    first = 2 * slot + part
                    north = rows_ref[field, tile, pl.ds(first, levels, stride=stride), :]
                    south = rows_ref[field, tile, pl.ds(half + first, levels, stride=stride), :]
                    lanes = pl.ds(tile * LANES, LANES)
                    at = (part * fields + field) * levels
                    out_ref[slot, at : at + levels, lanes] = (north + south).astype(out_ref.dtype)
                    at += 2 * fields * levels
                    out_ref[slot, at : at + levels, lanes] = (north - south).astype(out_ref.dtype)


def fold(plane, parts, slots, levels, fields):
    row_total = 2 * fields * levels
    rows = 2 * levels * 2 * slots
    tiles = parts[0].shape[1] // (fields * LANES)
    shape = (slots, 2 * row_total, tiles * LANES)
    size = rows * parts[0].shape[1]
    return pl.pallas_call(
        functools.partial(fold_kernel, slots, levels, fields),
        in_specs=[pl.BlockSpec(memory_space=pltpu.SMEM)] + [pl.BlockSpec(x.shape, lambda: (0, 0)) for x in parts],
        out_specs=pl.BlockSpec(shape, lambda: (0, 0, 0)),
        out_shape=jax.ShapeDtypeStruct(shape, jnp.bfloat16),
        scratch_shapes=[pltpu.VMEM((fields, tiles, rows, LANES), jnp.float32)],
        compiler_params=pltpu.CompilerParams(vmem_limit_bytes=VMEM_BYTES),
        cost_estimate=BRIEF,
        name="fold",
    )(plane, *parts)


def analysis_kernel(chunks, least, *refs):
    folded_refs = refs[:chunks]
    even_ref, odd_ref, table_ref, out_ref = refs[chunks:]
    row_total, degrees = out_ref.shape[1:]
    step = pl.program_id(0)

    def run(group):
        start = least[group]
        for j in range(out_ref.shape[0]):
            folded = jnp.concatenate([ref[j] for ref in folded_refs], axis=1)
            sums = lax.dot_general(
                folded, table_ref[j, start:, :], (((1,), (1,)), ((), ())), preferred_element_type=jnp.float32
            )
            kept = sums[:row_total] * even_ref[j, :, start:] + sums[row_total:] * odd_ref[j, :, start:]
            out_ref[j, :, start:] = kept
            if start:
                out_ref[j, :, :start] = jnp.zeros((row_total, start), out_ref.dtype)

    for group in range(len(least)):
        pl.when(step == group)(functools.partial(run, group))


def analyze(folded, even, odd, legendre, row_total, least):
    slots, degrees, lat_count = legendre.shape
    block = slots // len(least)
    mask_spec = pl.BlockSpec((block, 1, degrees), lambda i: (i, 0, 0))
    return pl.pallas_call(
        functools.partial(analysis_kernel, len(folded), least),
        grid=(len(least),),
        in_specs=[pl.BlockSpec((block,) + x.shape[1:], lambda i: (i, 0, 0)) for x in folded]
        + [mask_spec, mask_spec, pl.BlockSpec((block, degrees, lat_count), lambda i: (i, 0, 0))],
        out_specs=pl.BlockSpec((block, row_total, degrees), lambda i: (i, 0, 0)),
        out_shape=jax.ShapeDtypeStruct((slots, row_total, degrees), jnp.float32),
        compiler_params=pltpu.CompilerParams(vmem_limit_bytes=VMEM_BYTES),
        cost_estimate=pl.CostEstimate(
            flops=4 * slots * row_total * degrees * lat_count,
            bytes_accessed=2 * slots * (degrees * lat_count + 2 * row_total * (lat_count + degrees)),
            transcendentals=0,
        ),
        name="analysis",
    )(*folded, even, odd, legendre)


def trig_kernel(cos_base_ref, sin_base_ref, cos_turn_ref, sin_turn_ref, cos_base_t, sin_base_t, cos_turn_t, sin_turn_t, by_wave_ref, by_lon_ref):
    for j in range(cos_base_ref.shape[1]):
        lanes = pl.ds(j * LANES, LANES)
        cos_base, sin_base = cos_base_ref[:, j : j + 1], sin_base_ref[:, j : j + 1]
        angles = cos_base * cos_turn_ref[...] - sin_base * sin_turn_ref[...]
        by_wave_ref[:, lanes] = angles.astype(by_wave_ref.dtype)
        cos_base, sin_base = cos_base_t[j : j + 1, :], sin_base_t[j : j + 1, :]
        angles = cos_base * cos_turn_t[...] - sin_base * sin_turn_t[...]
        by_lon_ref[lanes, :] = angles.astype(by_lon_ref.dtype)


def trig_tables(owner_table, lon_count):
    waves = jnp.repeat(owner_table, 2).astype(jnp.float32)[:, None]
    quarter = jnp.tile(jnp.array([0, lon_count // 4], jnp.float32), owner_table.shape[0])[:, None]
    unit = 2.0 * math.pi / lon_count

    def angles(lon, turn):
        phase = waves * lon + turn
        return (phase - lon_count * jnp.floor(phase * (1.0 / lon_count))) * unit

    base = angles(jnp.arange(0, lon_count, LANES, dtype=jnp.float32)[None, :], quarter)
    turn = angles(jnp.arange(LANES, dtype=jnp.float32)[None, :], 0.0)
    depth = waves.shape[0]
    blocks = lon_count // LANES
    rows = 256
    small = pl.BlockSpec((rows, blocks), lambda i: (i, 0))
    wide = pl.BlockSpec((rows, LANES), lambda i: (i, 0))
    small_t = pl.BlockSpec((blocks, rows), lambda i: (0, i))
    wide_t = pl.BlockSpec((LANES, rows), lambda i: (0, i))
    parts = (jnp.cos(base), jnp.sin(base), jnp.cos(turn), jnp.sin(turn))
    return pl.pallas_call(
        trig_kernel,
        grid=(depth // rows,),
        in_specs=[small, small, wide, wide, small_t, small_t, wide_t, wide_t],
        out_specs=[
            pl.BlockSpec((rows, lon_count), lambda i: (i, 0)),
            pl.BlockSpec((lon_count, rows), lambda i: (0, i)),
        ],
        out_shape=[
            jax.ShapeDtypeStruct((depth, lon_count), jnp.bfloat16),
            jax.ShapeDtypeStruct((lon_count, depth), jnp.bfloat16),
        ],
        compiler_params=pltpu.CompilerParams(vmem_limit_bytes=VMEM_BYTES),
        cost_estimate=BRIEF,
        name="trig",
    )(*parts, *[x.T for x in parts])


def across_planes(parts, way):
    planes = len(parts)
    return [parts[0]] + [
        lax.ppermute(parts[x], "grp", [(p, (p + way * x) % planes) for p in range(planes)]) for x in range(1, planes)
    ]


def within_plane(rows):
    bands = lax.axis_size("band")
    cut = rows.reshape(bands, -1, rows.shape[-1])
    return lax.all_to_all(cut, "band", split_axis=0, concat_axis=0, tiled=True)


def after(value, *others):
    return lax.optimization_barrier((value, others))[0]


def by_hemisphere_and_level(spectral, legendre, owner_table):
    slots, _, fields, levels, degrees = spectral.shape
    half_lat = legendre.shape[2]
    lon_count = 4 * half_lat
    row_total = 2 * fields * levels
    tiles = half_lat // LANES
    wavenumber = lax.dynamic_slice_in_dim(owner_table, lax.axis_index(AXES) * slots, slots)
    distance = jnp.arange(degrees, dtype=jnp.int32)[None, :] - wavenumber[:, None]
    kept = distance >= 0
    is_odd = distance % 2 != 0
    keep = kept.astype(jnp.bfloat16)[:, None, :]
    flip = jnp.where(is_odd, -keep[:, 0], keep[:, 0])[:, None, :]
    scale = 1.0 / math.sqrt(2 * half_lat)
    even = jnp.where(kept & ~is_odd, scale, 0.0).astype(jnp.float32)[:, None, :]
    odd = jnp.where(kept & is_odd, scale, 0.0).astype(jnp.float32)[:, None, :]
    spec_rows = spectral.reshape(slots, row_total, degrees)
    planes, bands = lax.axis_size("grp"), lax.axis_size("band")
    plane = lax.axis_index("grp")
    sources = (plane + planes - jnp.arange(planes, dtype=jnp.int32)) % planes
    owners = jnp.take(owner_table.reshape(bands, planes, slots), sources, axis=1).reshape(-1)
    plane = plane.reshape(1)
    least = tuple(4 * g * bands * planes for g in range(slots // 4))

    def send(spec, tile):
        return synthesize(plane, planes, spec, keep, flip, legendre, (tile, 1), fields, levels, least)

    def stack(parts):
        width = parts[0].shape[-1]
        return jnp.stack([x.reshape(bands, -1, width) for x in parts], axis=1)

    def give_back(cut, *others):
        width = cut.shape[-1]
        cut = cut.reshape(bands, planes, -1, width)
        parts = [cut[:, x].reshape(-1, width) for x in range(planes)]
        return across_planes(after(parts, *others), -1)

    sent, moved, arrived, zonal, cuts, folded = [], [], [], [], [], []
    for t in range(tiles + 2):
        if t < tiles:
            spec = spec_rows
            if t == 1:
                by_wave, by_lon = trig_tables(owners, lon_count)
                spec = after(spec_rows, by_wave)
            elif t >= 2:
                spec = after(spec_rows, *moved[t - 2])
            sent.append(send(spec, t))
            moved.append(across_planes(sent[t], 1))
        if t >= 1 and t - 1 < tiles:
            ready = after(moved[t - 1], *sent[t]) if t < tiles else moved[t - 1]
            if t >= 3:
                ready = after(ready, cuts[t - 3])
            arrived.append(within_plane(stack(ready)))
        if t >= 2:
            rows = arrived[t - 2]
            values = longitudes(rows.reshape(-1, rows.shape[-1]), by_lon, by_wave, fields)
            if t - 1 < tiles:
                values = after(values, arrived[t - 1])
            cuts.append(within_plane(values))
    for t in range(tiles):
        parts = give_back(cuts[t], *([folded[t - 2]] if t >= 2 else []))
        folded.append(fold(plane, parts, slots, levels, fields))
    out = analyze(folded, even, odd, legendre, row_total, least)
    return out.reshape(slots, 2, fields, levels, degrees)


def make_trig(wavenumber, lon_count):
    lon_index = jnp.arange(lon_count, dtype=jnp.int32)
    phases = wavenumber[:, None] * lon_index[None, :] % lon_count
    angles = phases.astype(jnp.float32) * (2.0 * math.pi / lon_count)
    return jnp.stack([jnp.cos(angles), -jnp.sin(angles)], axis=1).astype(jnp.bfloat16)


def by_level_and_latitude(spectral, legendre, owner_table):
    slot_count, _, fields, levels, degrees = spectral.shape
    half_lat = legendre.shape[2]
    lat_count = 2 * half_lat
    lon_count = 2 * lat_count
    wave_count = owner_table.shape[0]
    band_count = lax.axis_size("band")
    group_count = lax.axis_size("grp")
    device_count = band_count * group_count
    level_block = levels // band_count
    lat_block = lat_count // group_count
    row_total = 2 * fields * levels
    row_width = fields * level_block * lat_block
    slot_start = lax.axis_index(("band", "grp")) * slot_count
    wavenumber = lax.dynamic_slice_in_dim(owner_table, slot_start, slot_count)
    degree_index = jnp.arange(degrees, dtype=jnp.int32)
    keep_mask = (degree_index[None, :] >= wavenumber[:, None]).astype(jnp.bfloat16)
    odd_part = (degree_index[None, :] - wavenumber[:, None]) % 2
    flip_sign = (1 - 2 * odd_part).astype(jnp.bfloat16)
    spec_rows = spectral.reshape(slot_count, row_total, degrees) * keep_mask[:, None, :]
    both_rows = jnp.concatenate([spec_rows, spec_rows * flip_sign[:, None, :]], axis=1)
    halves = jnp.einsum("srn,snt->srt", both_rows, legendre, preferred_element_type=jnp.float32)
    northern = halves[:, :row_total]
    mirrored = halves[:, row_total:]
    fourier = jnp.concatenate([northern, jnp.flip(mirrored, axis=2)], axis=2)
    fourier = fourier.reshape(
        slot_count, 2, fields, band_count, level_block, group_count, lat_block
    )
    fourier = jnp.transpose(fourier, (0, 1, 2, 3, 5, 4, 6))
    fourier_low = (fourier * (1.0 / math.sqrt(degrees))).astype(jnp.bfloat16)
    packed = fourier_low.reshape(1, slot_count, 2, fields, device_count, level_block, lat_block)
    arrived = lax.all_to_all(packed, ("band", "grp"), split_axis=4, concat_axis=0, tiled=True)
    arrived = arrived.reshape(-1, 2, row_width)
    trig_rows = make_trig(owner_table, lon_count)
    grid_values = jnp.einsum("scw,scl->wl", arrived, trig_rows, preferred_element_type=jnp.float32)
    grid_values = (grid_values * (1.0 / math.sqrt(wave_count))).reshape(
        fields, level_block * lat_block, lon_count
    )
    product = (grid_values * jnp.roll(grid_values, -1, axis=0)).astype(jnp.bfloat16)
    zonal_coeffs = jnp.einsum(
        "wl,scl->scw",
        product.reshape(row_width, lon_count),
        trig_rows,
        preferred_element_type=jnp.float32,
    )
    zonal_coeffs = (zonal_coeffs * (2.0 / math.sqrt(lon_count))).astype(jnp.bfloat16)
    sendback = zonal_coeffs.reshape(device_count, slot_count, 2, fields, 1, level_block, lat_block)
    returned = lax.all_to_all(sendback, ("band", "grp"), split_axis=0, concat_axis=4, tiled=True)
    returned = returned.reshape(
        slot_count, 2, fields, band_count, group_count, level_block, lat_block
    )
    returned = jnp.transpose(returned, (0, 1, 2, 3, 5, 4, 6)).reshape(slot_count, row_total, lat_count)
    northern_part = returned[:, :, :half_lat].astype(jnp.float32)
    mirror_part = jnp.flip(returned[:, :, half_lat:], axis=2).astype(jnp.float32)
    plus_part = (northern_part + mirror_part).astype(jnp.bfloat16)
    minus_part = (northern_part - mirror_part).astype(jnp.bfloat16)
    stacked = jnp.concatenate([plus_part, minus_part], axis=1)
    projected = jnp.einsum("srt,snt->srn", stacked, legendre, preferred_element_type=jnp.float32)
    even_rows = flip_sign[:, None, :] > 0
    chosen = jnp.where(even_rows, projected[:, :row_total], projected[:, row_total:])
    chosen = chosen * keep_mask.astype(jnp.float32)[:, None, :] * (1.0 / math.sqrt(lat_count))
    return chosen.reshape(slot_count, 2, fields, levels, degrees)


def on_device(spectral, legendre, owner_table):
    slots, _, _, levels, _ = spectral.shape
    planes = lax.axis_size("grp")
    whole_hemispheres = lax.axis_size("band") * planes == 2 * levels and planes & (planes - 1) == 0
    if whole_hemispheres and legendre.shape[2] % LANES == 0 and slots % 4 == 0 and levels % 8 == 0:
        return by_hemisphere_and_level(spectral, legendre, owner_table)
    return by_level_and_latitude(spectral, legendre, owner_table)


def solution(mesh):
    placed = (P(("band", "grp"), None, None, None, None), P(("band", "grp"), None, None), P())
    return jax.shard_map(
        on_device,
        mesh=mesh,
        in_specs=placed,
        out_specs=P(("band", "grp"), None, None, None, None),
        check_vma=False,
    )
```

```python
import functools
import math

import jax
import jax.numpy as jnp
from jax import lax
from jax.experimental import pallas as pl
from jax.experimental.pallas import tpu as pltpu
from jax.sharding import PartitionSpec as P

LANES = 128
AXES = ("band", "grp")
VMEM_BYTES = 56 * 1024 * 1024
BRIEF = pl.CostEstimate(flops=10**6, bytes_accessed=10**4, transcendentals=0)


def synthesis_kernel(slots, levels, fields, least, scale, plane_ref, spec_ref, keep_ref, flip_ref, table_ref, *refs):
    out_refs, rows_ref = refs[:-1], refs[-1]
    tiles = rows_ref.shape[1]
    step = pl.program_id(0)
    block = spec_ref.shape[0]
    row_total = spec_ref.shape[1]
    stride = 2 * slots

    def run(group):
        start = least[group]
        for j in range(block):
            spec = spec_ref[j, :, start:]
            both = jnp.concatenate([spec * keep_ref[j, :, start:], spec * flip_ref[j, :, start:]], axis=0)
            halves = jnp.dot(both, table_ref[j, start:, :], preferred_element_type=jnp.float32) * scale
            first = 2 * (group * block + j)
            for hemi in range(2):
                for part in range(2):
                    for field in range(fields):
                        at = hemi * row_total + (part * fields + field) * levels
                        target = pl.ds(hemi * levels * stride + first + part, levels, stride=stride)
                        for tile in range(tiles):
                            lanes = slice(tile * LANES, (tile + 1) * LANES)
                            rows_ref[field, tile, target, :] = halves[at : at + levels, lanes]

    for group in range(slots // block):
        pl.when(step == group)(functools.partial(run, group))

    @pl.when(step == pl.num_programs(0) - 1)
    def _():
        for apart, out_ref in enumerate(out_refs):
            size = out_ref.shape[0]
            rows = pl.ds(pl.multiple_of(lax.rem(plane_ref[0] + apart, len(out_refs)) * size, size), size)
            for field in range(fields):
                for tile in range(tiles):
                    lanes = pl.ds((field * tiles + tile) * LANES, LANES)
                    out_ref[:, lanes] = rows_ref[field, tile, rows, :].astype(out_ref.dtype)


def synthesize(plane, planes, spec_rows, keep, flip, legendre, chunk, fields, levels, least):
    slots, row_total, degrees = spec_rows.shape
    block = slots // len(least)
    rows = 2 * levels * 2 * slots
    at, tiles = chunk
    shape = (rows // planes, fields * tiles * LANES)
    return pl.pallas_call(
        functools.partial(synthesis_kernel, slots, levels, fields, least, 1.0 / math.sqrt(degrees)),
        grid_spec=pltpu.PrefetchScalarGridSpec(
            num_scalar_prefetch=1,
            grid=(slots // block,),
            in_specs=[
                pl.BlockSpec((block, row_total, degrees), lambda i, _: (i, 0, 0)),
                pl.BlockSpec((block, 1, degrees), lambda i, _: (i, 0, 0)),
                pl.BlockSpec((block, 1, degrees), lambda i, _: (i, 0, 0)),
                pl.BlockSpec((block, degrees, tiles * LANES), lambda i, _: (i, 0, at // tiles)),
            ],
            out_specs=[pl.BlockSpec(shape, lambda i, _: (0, 0))] * planes,
            scratch_shapes=[pltpu.VMEM((fields, tiles, rows, LANES), jnp.float32)],
        ),
        out_shape=[jax.ShapeDtypeStruct(shape, jnp.bfloat16)] * planes,
        compiler_params=pltpu.CompilerParams(vmem_limit_bytes=VMEM_BYTES),
        cost_estimate=BRIEF,
        name="synthesis",
    )(plane, spec_rows, keep, flip, legendre)


def longitude_kernel(fields, grid_scale, zonal_scale, rows_ref, by_lon_ref, by_wave_ref, out_ref, sum_ref):
    step = pl.program_id(0)
    values = jnp.dot(by_lon_ref[...], rows_ref[...], preferred_element_type=jnp.float32) * grid_scale
    one = values.shape[1] // fields
    following = jnp.concatenate([values[:, one:], values[:, :one]], axis=1)
    product = (values * following).astype(jnp.bfloat16)
    share = jnp.dot(by_wave_ref[...], product, preferred_element_type=jnp.float32)

    @pl.when(step == 0)
    def _():
        sum_ref[...] = share

    @pl.when(step > 0)
    def _():
        sum_ref[...] += share

    @pl.when(step == pl.num_programs(0) - 1)
    def _():
        out_ref[...] = (sum_ref[...] * zonal_scale).astype(out_ref.dtype)


def longitudes(rows, by_lon, by_wave, fields):
    depth, width = rows.shape
    lon_count = by_lon.shape[0]
    lon_block = lon_count // 5
    return pl.pallas_call(
        functools.partial(longitude_kernel, fields, 1.0 / math.sqrt(depth // 2), 2.0 / math.sqrt(lon_count)),
        grid=(lon_count // lon_block,),
        in_specs=[
            pl.BlockSpec((depth, width), lambda i: (0, 0)),
            pl.BlockSpec((lon_block, depth), lambda i: (i, 0)),
            pl.BlockSpec((depth, lon_block), lambda i: (0, i)),
        ],
        out_specs=pl.BlockSpec((depth, width), lambda i: (0, 0)),
        out_shape=jax.ShapeDtypeStruct((depth, width), jnp.bfloat16),
        scratch_shapes=[pltpu.VMEM((depth, width), jnp.float32)],
        compiler_params=pltpu.CompilerParams(vmem_limit_bytes=VMEM_BYTES),
        cost_estimate=BRIEF,
        name="longitudes",
    )(rows, by_lon, by_wave)


def fold_kernel(slots, levels, fields, plane_ref, *refs):
    rows_refs, out_ref, rows_ref = refs[:-2], refs[-2], refs[-1]
    tiles = rows_ref.shape[1]
    stride = 2 * slots
    half = levels * stride
    for apart, arrived_ref in enumerate(rows_refs):
        size = arrived_ref.shape[0]
        rows = pl.ds(pl.multiple_of(lax.rem(plane_ref[0] + apart, len(rows_refs)) * size, size), size)
        for field in range(fields):
            for tile in range(tiles):
                lanes = pl.ds((field * tiles + tile) * LANES, LANES)
                rows_ref[field, tile, rows, :] = arrived_ref[:, lanes].astype(jnp.float32)
    for slot in range(slots):
        for part in range(2):
            for field in range(fields):
                for tile in range(tiles):
                    first = 2 * slot + part
                    north = rows_ref[field, tile, pl.ds(first, levels, stride=stride), :]
                    south = rows_ref[field, tile, pl.ds(half + first, levels, stride=stride), :]
                    lanes = pl.ds(tile * LANES, LANES)
                    at = (part * fields + field) * levels
                    out_ref[slot, at : at + levels, lanes] = (north + south).astype(out_ref.dtype)
                    at += 2 * fields * levels
                    out_ref[slot, at : at + levels, lanes] = (north - south).astype(out_ref.dtype)


def fold(plane, parts, slots, levels, fields):
    row_total = 2 * fields * levels
    rows = 2 * levels * 2 * slots
    tiles = parts[0].shape[1] // (fields * LANES)
    shape = (slots, 2 * row_total, tiles * LANES)
    size = rows * parts[0].shape[1]
    return pl.pallas_call(
        functools.partial(fold_kernel, slots, levels, fields),
        in_specs=[pl.BlockSpec(memory_space=pltpu.SMEM)] + [pl.BlockSpec(x.shape, lambda: (0, 0)) for x in parts],
        out_specs=pl.BlockSpec(shape, lambda: (0, 0, 0)),
        out_shape=jax.ShapeDtypeStruct(shape, jnp.bfloat16),
        scratch_shapes=[pltpu.VMEM((fields, tiles, rows, LANES), jnp.float32)],
        compiler_params=pltpu.CompilerParams(vmem_limit_bytes=VMEM_BYTES),
        cost_estimate=BRIEF,
        name="fold",
    )(plane, *parts)


def analysis_kernel(chunks, least, *refs):
    folded_refs = refs[:chunks]
    even_ref, odd_ref, table_ref, out_ref = refs[chunks:]
    row_total, degrees = out_ref.shape[1:]
    step = pl.program_id(0)

    def run(group):
        start = least[group]
        for j in range(out_ref.shape[0]):
            folded = jnp.concatenate([ref[j] for ref in folded_refs], axis=1)
            sums = lax.dot_general(
                folded, table_ref[j, start:, :], (((1,), (1,)), ((), ())), preferred_element_type=jnp.float32
            )
            kept = sums[:row_total] * even_ref[j, :, start:] + sums[row_total:] * odd_ref[j, :, start:]
            out_ref[j, :, start:] = kept
            if start:
                out_ref[j, :, :start] = jnp.zeros((row_total, start), out_ref.dtype)

    for group in range(len(least)):
        pl.when(step == group)(functools.partial(run, group))


def analyze(folded, even, odd, legendre, row_total, least):
    slots, degrees, lat_count = legendre.shape
    block = slots // len(least)
    mask_spec = pl.BlockSpec((block, 1, degrees), lambda i: (i, 0, 0))
    return pl.pallas_call(
        functools.partial(analysis_kernel, len(folded), least),
        grid=(len(least),),
        in_specs=[pl.BlockSpec((block,) + x.shape[1:], lambda i: (i, 0, 0)) for x in folded]
        + [mask_spec, mask_spec, pl.BlockSpec((block, degrees, lat_count), lambda i: (i, 0, 0))],
        out_specs=pl.BlockSpec((block, row_total, degrees), lambda i: (i, 0, 0)),
        out_shape=jax.ShapeDtypeStruct((slots, row_total, degrees), jnp.float32),
        compiler_params=pltpu.CompilerParams(vmem_limit_bytes=VMEM_BYTES),
        cost_estimate=pl.CostEstimate(
            flops=4 * slots * row_total * degrees * lat_count,
            bytes_accessed=2 * slots * (degrees * lat_count + 2 * row_total * (lat_count + degrees)),
            transcendentals=0,
        ),
        name="analysis",
    )(*folded, even, odd, legendre)


def trig_kernel(cos_base_ref, sin_base_ref, cos_turn_ref, sin_turn_ref, cos_base_t, sin_base_t, cos_turn_t, sin_turn_t, by_wave_ref, by_lon_ref):
    for j in range(cos_base_ref.shape[1]):
        lanes = pl.ds(j * LANES, LANES)
        cos_base, sin_base = cos_base_ref[:, j : j + 1], sin_base_ref[:, j : j + 1]
        angles = cos_base * cos_turn_ref[...] - sin_base * sin_turn_ref[...]
        by_wave_ref[:, lanes] = angles.astype(by_wave_ref.dtype)
        cos_base, sin_base = cos_base_t[j : j + 1, :], sin_base_t[j : j + 1, :]
        angles = cos_base * cos_turn_t[...] - sin_base * sin_turn_t[...]
        by_lon_ref[lanes, :] = angles.astype(by_lon_ref.dtype)


def trig_tables(owner_table, lon_count):
    waves = jnp.repeat(owner_table, 2).astype(jnp.float32)[:, None]
    quarter = jnp.tile(jnp.array([0, lon_count // 4], jnp.float32), owner_table.shape[0])[:, None]
    unit = 2.0 * math.pi / lon_count

    def angles(lon, turn):
        phase = waves * lon + turn
        return (phase - lon_count * jnp.floor(phase * (1.0 / lon_count))) * unit

    base = angles(jnp.arange(0, lon_count, LANES, dtype=jnp.float32)[None, :], quarter)
    turn = angles(jnp.arange(LANES, dtype=jnp.float32)[None, :], 0.0)
    depth = waves.shape[0]
    blocks = lon_count // LANES
    rows = 256
    small = pl.BlockSpec((rows, blocks), lambda i: (i, 0))
    wide = pl.BlockSpec((rows, LANES), lambda i: (i, 0))
    small_t = pl.BlockSpec((blocks, rows), lambda i: (0, i))
    wide_t = pl.BlockSpec((LANES, rows), lambda i: (0, i))
    parts = (jnp.cos(base), jnp.sin(base), jnp.cos(turn), jnp.sin(turn))
    return pl.pallas_call(
        trig_kernel,
        grid=(depth // rows,),
        in_specs=[small, small, wide, wide, small_t, small_t, wide_t, wide_t],
        out_specs=[
            pl.BlockSpec((rows, lon_count), lambda i: (i, 0)),
            pl.BlockSpec((lon_count, rows), lambda i: (0, i)),
        ],
        out_shape=[
            jax.ShapeDtypeStruct((depth, lon_count), jnp.bfloat16),
            jax.ShapeDtypeStruct((lon_count, depth), jnp.bfloat16),
        ],
        compiler_params=pltpu.CompilerParams(vmem_limit_bytes=VMEM_BYTES),
        cost_estimate=BRIEF,
        name="trig",
    )(*parts, *[x.T for x in parts])


def exchange(rows):
    return lax.all_to_all(rows, AXES, split_axis=0, concat_axis=0, tiled=True)


def after(value, *others):
    return lax.optimization_barrier((value, others))[0]


def by_hemisphere_and_level(spectral, legendre, owner_table):
    slots, _, fields, levels, degrees = spectral.shape
    half_lat = legendre.shape[2]
    lon_count = 4 * half_lat
    row_total = 2 * fields * levels
    tiles = half_lat // LANES
    wavenumber = lax.dynamic_slice_in_dim(owner_table, lax.axis_index(AXES) * slots, slots)
    distance = jnp.arange(degrees, dtype=jnp.int32)[None, :] - wavenumber[:, None]
    kept = distance >= 0
    is_odd = distance % 2 != 0
    keep = kept.astype(jnp.bfloat16)[:, None, :]
    flip = jnp.where(is_odd, -keep[:, 0], keep[:, 0])[:, None, :]
    scale = 1.0 / math.sqrt(2 * half_lat)
    even = jnp.where(kept & ~is_odd, scale, 0.0).astype(jnp.float32)[:, None, :]
    odd = jnp.where(kept & is_odd, scale, 0.0).astype(jnp.float32)[:, None, :]
    spec_rows = spectral.reshape(slots, row_total, degrees)
    least = tuple(8 * g * levels for g in range(slots // 4))
    plane = jnp.zeros((1,), jnp.int32)

    def send(spec, tile):
        return exchange(synthesize(plane, 1, spec, keep, flip, legendre, (tile, 1), fields, levels, least)[0])

    arrived = [send(spec_rows, 0)]
    by_wave, by_lon = trig_tables(owner_table, lon_count)
    later = after(spec_rows, by_wave)
    arrived += [send(later, tile) for tile in range(1, tiles)]
    zonal = [longitudes(rows, by_lon, by_wave, fields) for rows in arrived]
    returned = [exchange(rows) for rows in zonal]
    folded = [fold(plane, [rows], slots, levels, fields) for rows in returned]
    out = analyze(folded, even, odd, legendre, row_total, least)
    return out.reshape(slots, 2, fields, levels, degrees)


def make_trig(wavenumber, lon_count):
    lon_index = jnp.arange(lon_count, dtype=jnp.int32)
    phases = wavenumber[:, None] * lon_index[None, :] % lon_count
    angles = phases.astype(jnp.float32) * (2.0 * math.pi / lon_count)
    return jnp.stack([jnp.cos(angles), -jnp.sin(angles)], axis=1).astype(jnp.bfloat16)


def by_level_and_latitude(spectral, legendre, owner_table):
    slot_count, _, fields, levels, degrees = spectral.shape
    half_lat = legendre.shape[2]
    lat_count = 2 * half_lat
    lon_count = 2 * lat_count
    wave_count = owner_table.shape[0]
    band_count = lax.axis_size("band")
    group_count = lax.axis_size("grp")
    device_count = band_count * group_count
    level_block = levels // band_count
    lat_block = lat_count // group_count
    row_total = 2 * fields * levels
    row_width = fields * level_block * lat_block
    slot_start = lax.axis_index(("band", "grp")) * slot_count
    wavenumber = lax.dynamic_slice_in_dim(owner_table, slot_start, slot_count)
    degree_index = jnp.arange(degrees, dtype=jnp.int32)
    keep_mask = (degree_index[None, :] >= wavenumber[:, None]).astype(jnp.bfloat16)
    odd_part = (degree_index[None, :] - wavenumber[:, None]) % 2
    flip_sign = (1 - 2 * odd_part).astype(jnp.bfloat16)
    spec_rows = spectral.reshape(slot_count, row_total, degrees) * keep_mask[:, None, :]
    both_rows = jnp.concatenate([spec_rows, spec_rows * flip_sign[:, None, :]], axis=1)
    halves = jnp.einsum("srn,snt->srt", both_rows, legendre, preferred_element_type=jnp.float32)
    northern = halves[:, :row_total]
    mirrored = halves[:, row_total:]
    fourier = jnp.concatenate([northern, jnp.flip(mirrored, axis=2)], axis=2)
    fourier = fourier.reshape(
        slot_count, 2, fields, band_count, level_block, group_count, lat_block
    )
    fourier = jnp.transpose(fourier, (0, 1, 2, 3, 5, 4, 6))
    fourier_low = (fourier * (1.0 / math.sqrt(degrees))).astype(jnp.bfloat16)
    packed = fourier_low.reshape(1, slot_count, 2, fields, device_count, level_block, lat_block)
    arrived = lax.all_to_all(packed, ("band", "grp"), split_axis=4, concat_axis=0, tiled=True)
    arrived = arrived.reshape(-1, 2, row_width)
    trig_rows = make_trig(owner_table, lon_count)
    grid_values = jnp.einsum("scw,scl->wl", arrived, trig_rows, preferred_element_type=jnp.float32)
    grid_values = (grid_values * (1.0 / math.sqrt(wave_count))).reshape(
        fields, level_block * lat_block, lon_count
    )
    product = (grid_values * jnp.roll(grid_values, -1, axis=0)).astype(jnp.bfloat16)
    zonal_coeffs = jnp.einsum(
        "wl,scl->scw",
        product.reshape(row_width, lon_count),
        trig_rows,
        preferred_element_type=jnp.float32,
    )
    zonal_coeffs = (zonal_coeffs * (2.0 / math.sqrt(lon_count))).astype(jnp.bfloat16)
    sendback = zonal_coeffs.reshape(device_count, slot_count, 2, fields, 1, level_block, lat_block)
    returned = lax.all_to_all(sendback, ("band", "grp"), split_axis=0, concat_axis=4, tiled=True)
    returned = returned.reshape(
        slot_count, 2, fields, band_count, group_count, level_block, lat_block
    )
    returned = jnp.transpose(returned, (0, 1, 2, 3, 5, 4, 6)).reshape(slot_count, row_total, lat_count)
    northern_part = returned[:, :, :half_lat].astype(jnp.float32)
    mirror_part = jnp.flip(returned[:, :, half_lat:], axis=2).astype(jnp.float32)
    plus_part = (northern_part + mirror_part).astype(jnp.bfloat16)
    minus_part = (northern_part - mirror_part).astype(jnp.bfloat16)
    stacked = jnp.concatenate([plus_part, minus_part], axis=1)
    projected = jnp.einsum("srt,snt->srn", stacked, legendre, preferred_element_type=jnp.float32)
    even_rows = flip_sign[:, None, :] > 0
    chosen = jnp.where(even_rows, projected[:, :row_total], projected[:, row_total:])
    chosen = chosen * keep_mask.astype(jnp.float32)[:, None, :] * (1.0 / math.sqrt(lat_count))
    return chosen.reshape(slot_count, 2, fields, levels, degrees)


def on_device(spectral, legendre, owner_table):
    slots, _, _, levels, _ = spectral.shape
    whole_hemispheres = lax.axis_size("band") * lax.axis_size("grp") == 2 * levels
    if whole_hemispheres and legendre.shape[2] % LANES == 0 and slots % 4 == 0 and levels % 16 == 0:
        return by_hemisphere_and_level(spectral, legendre, owner_table)
    return by_level_and_latitude(spectral, legendre, owner_table)


def solution(mesh):
    placed = (P(("band", "grp"), None, None, None, None), P(("band", "grp"), None, None), P())
    return jax.shard_map(
        on_device,
        mesh=mesh,
        in_specs=placed,
        out_specs=P(("band", "grp"), None, None, None, None),
        check_vma=False,
    )
```

```python
import functools
import math

import jax
import jax.numpy as jnp
from jax import lax
from jax.experimental import pallas as pl
from jax.experimental.pallas import tpu as pltpu
from jax.sharding import PartitionSpec as P

LANES = 128
AXES = ("band", "grp")
VMEM_BYTES = 56 * 1024 * 1024


def synthesis_kernel(slots, levels, fields, least, scale, plane_ref, spec_ref, keep_ref, flip_ref, table_ref, *refs):
    out_refs, rows_ref = refs[:-1], refs[-1]
    tiles = rows_ref.shape[1]
    step = pl.program_id(0)
    block = spec_ref.shape[0]
    row_total = spec_ref.shape[1]
    stride = 2 * slots

    def run(group):
        start = least[group]
        for j in range(block):
            spec = spec_ref[j, :, start:]
            both = jnp.concatenate([spec * keep_ref[j, :, start:], spec * flip_ref[j, :, start:]], axis=0)
            halves = jnp.dot(both, table_ref[j, start:, :], preferred_element_type=jnp.float32) * scale
            first = 2 * (group * block + j)
            for hemi in range(2):
                for part in range(2):
                    for field in range(fields):
                        at = hemi * row_total + (part * fields + field) * levels
                        target = pl.ds(hemi * levels * stride + first + part, levels, stride=stride)
                        for tile in range(tiles):
                            lanes = slice(tile * LANES, (tile + 1) * LANES)
                            rows_ref[field, tile, target, :] = halves[at : at + levels, lanes]

    for group in range(slots // block):
        pl.when(step == group)(functools.partial(run, group))

    @pl.when(step == pl.num_programs(0) - 1)
    def _():
        for apart, out_ref in enumerate(out_refs):
            size = out_ref.shape[0]
            rows = pl.ds(pl.multiple_of(lax.rem(plane_ref[0] + apart, len(out_refs)) * size, size), size)
            for field in range(fields):
                for tile in range(tiles):
                    lanes = pl.ds((field * tiles + tile) * LANES, LANES)
                    out_ref[:, lanes] = rows_ref[field, tile, rows, :].astype(out_ref.dtype)


def synthesize(plane, planes, spec_rows, keep, flip, legendre, chunk, fields, levels, least):
    slots, row_total, degrees = spec_rows.shape
    block = slots // len(least)
    rows = 2 * levels * 2 * slots
    at, tiles = chunk
    shape = (rows // planes, fields * tiles * LANES)
    return pl.pallas_call(
        functools.partial(synthesis_kernel, slots, levels, fields, least, 1.0 / math.sqrt(degrees)),
        grid_spec=pltpu.PrefetchScalarGridSpec(
            num_scalar_prefetch=1,
            grid=(slots // block,),
            in_specs=[
                pl.BlockSpec((block, row_total, degrees), lambda i, _: (i, 0, 0)),
                pl.BlockSpec((block, 1, degrees), lambda i, _: (i, 0, 0)),
                pl.BlockSpec((block, 1, degrees), lambda i, _: (i, 0, 0)),
                pl.BlockSpec((block, degrees, tiles * LANES), lambda i, _: (i, 0, at // tiles)),
            ],
            out_specs=[pl.BlockSpec(shape, lambda i, _: (0, 0))] * planes,
            scratch_shapes=[pltpu.VMEM((fields, tiles, rows, LANES), jnp.float32)],
        ),
        out_shape=[jax.ShapeDtypeStruct(shape, jnp.bfloat16)] * planes,
        compiler_params=pltpu.CompilerParams(vmem_limit_bytes=VMEM_BYTES),
        cost_estimate=pl.CostEstimate(
            flops=4 * slots * row_total * degrees * tiles * LANES,
            bytes_accessed=2 * slots * degrees * (row_total + tiles * LANES) + 2 * rows * shape[1],
            transcendentals=0,
        ),
        name="synthesis",
    )(plane, spec_rows, keep, flip, legendre)


def longitude_kernel(fields, grid_scale, zonal_scale, rows_ref, by_lon_ref, by_wave_ref, out_ref, sum_ref):
    step = pl.program_id(0)
    values = jnp.dot(by_lon_ref[...], rows_ref[...], preferred_element_type=jnp.float32) * grid_scale
    one = values.shape[1] // fields
    following = jnp.concatenate([values[:, one:], values[:, :one]], axis=1)
    product = (values * following).astype(jnp.bfloat16)
    share = jnp.dot(by_wave_ref[...], product, preferred_element_type=jnp.float32)

    @pl.when(step == 0)
    def _():
        sum_ref[...] = share

    @pl.when(step > 0)
    def _():
        sum_ref[...] += share

    @pl.when(step == pl.num_programs(0) - 1)
    def _():
        out_ref[...] = (sum_ref[...] * zonal_scale).astype(out_ref.dtype)


def longitudes(rows, by_lon, by_wave, fields):
    depth, width = rows.shape
    lon_count = by_lon.shape[0]
    lon_block = lon_count // 5
    return pl.pallas_call(
        functools.partial(longitude_kernel, fields, 1.0 / math.sqrt(depth // 2), 2.0 / math.sqrt(lon_count)),
        grid=(lon_count // lon_block,),
        in_specs=[
            pl.BlockSpec((depth, width), lambda i: (0, 0)),
            pl.BlockSpec((lon_block, depth), lambda i: (i, 0)),
            pl.BlockSpec((depth, lon_block), lambda i: (0, i)),
        ],
        out_specs=pl.BlockSpec((depth, width), lambda i: (0, 0)),
        out_shape=jax.ShapeDtypeStruct((depth, width), jnp.bfloat16),
        scratch_shapes=[pltpu.VMEM((depth, width), jnp.float32)],
        compiler_params=pltpu.CompilerParams(vmem_limit_bytes=VMEM_BYTES),
        cost_estimate=pl.CostEstimate(
            flops=4 * depth * width * lon_count,
            bytes_accessed=4 * depth * (width + lon_count),
            transcendentals=0,
        ),
        name="longitudes",
    )(rows, by_lon, by_wave)


def fold_kernel(slots, levels, fields, plane_ref, *refs):
    rows_refs, out_ref, rows_ref = refs[:-2], refs[-2], refs[-1]
    tiles = rows_ref.shape[1]
    stride = 2 * slots
    half = levels * stride
    for apart, arrived_ref in enumerate(rows_refs):
        size = arrived_ref.shape[0]
        rows = pl.ds(pl.multiple_of(lax.rem(plane_ref[0] + apart, len(rows_refs)) * size, size), size)
        for field in range(fields):
            for tile in range(tiles):
                lanes = pl.ds((field * tiles + tile) * LANES, LANES)
                rows_ref[field, tile, rows, :] = arrived_ref[:, lanes].astype(jnp.float32)
    for slot in range(slots):
        for part in range(2):
            for field in range(fields):
                for tile in range(tiles):
                    first = 2 * slot + part
                    north = rows_ref[field, tile, pl.ds(first, levels, stride=stride), :]
                    south = rows_ref[field, tile, pl.ds(half + first, levels, stride=stride), :]
                    lanes = pl.ds(tile * LANES, LANES)
                    at = (part * fields + field) * levels
                    out_ref[slot, at : at + levels, lanes] = (north + south).astype(out_ref.dtype)
                    at += 2 * fields * levels
                    out_ref[slot, at : at + levels, lanes] = (north - south).astype(out_ref.dtype)


def fold(plane, parts, slots, levels, fields):
    row_total = 2 * fields * levels
    rows = 2 * levels * 2 * slots
    tiles = parts[0].shape[1] // (fields * LANES)
    shape = (slots, 2 * row_total, tiles * LANES)
    size = rows * parts[0].shape[1]
    return pl.pallas_call(
        functools.partial(fold_kernel, slots, levels, fields),
        in_specs=[pl.BlockSpec(memory_space=pltpu.SMEM)] + [pl.BlockSpec(x.shape, lambda: (0, 0)) for x in parts],
        out_specs=pl.BlockSpec(shape, lambda: (0, 0, 0)),
        out_shape=jax.ShapeDtypeStruct(shape, jnp.bfloat16),
        scratch_shapes=[pltpu.VMEM((fields, tiles, rows, LANES), jnp.float32)],
        compiler_params=pltpu.CompilerParams(vmem_limit_bytes=VMEM_BYTES),
        cost_estimate=pl.CostEstimate(flops=2 * size, bytes_accessed=4 * size, transcendentals=0),
        name="fold",
    )(plane, *parts)


def analysis_kernel(chunks, least, adds, *refs):
    folded_refs = refs[:chunks]
    even_ref, odd_ref, table_ref = refs[chunks : chunks + 3]
    base_ref, out_ref = refs[-2], refs[-1]
    row_total, degrees = out_ref.shape[1:]
    step = pl.program_id(0)

    def run(group):
        start = least[group]
        for j in range(out_ref.shape[0]):
            folded = jnp.concatenate([ref[j] for ref in folded_refs], axis=1)
            sums = lax.dot_general(
                folded, table_ref[j, start:, :], (((1,), (1,)), ((), ())), preferred_element_type=jnp.float32
            )
            kept = sums[:row_total] * even_ref[j, :, start:] + sums[row_total:] * odd_ref[j, :, start:]
            if adds:
                kept = kept + base_ref[j, :, start:]
            out_ref[j, :, start:] = kept
            if start:
                out_ref[j, :, :start] = jnp.zeros((row_total, start), out_ref.dtype)

    for group in range(len(least)):
        pl.when(step == group)(functools.partial(run, group))


def analyze(folded, even, odd, legendre, row_total, least, first_tile, base=None):
    slots, degrees, _ = legendre.shape
    block = slots // len(least)
    lat_count = len(folded) * LANES
    table_block = first_tile // len(folded)
    mask_spec = pl.BlockSpec((block, 1, degrees), lambda i: (i, 0, 0))
    sums_spec = pl.BlockSpec((block, row_total, degrees), lambda i: (i, 0, 0))
    return pl.pallas_call(
        functools.partial(analysis_kernel, len(folded), least, base is not None),
        grid=(len(least),),
        in_specs=[pl.BlockSpec((block,) + x.shape[1:], lambda i: (i, 0, 0)) for x in folded]
        + [mask_spec, mask_spec, pl.BlockSpec((block, degrees, lat_count), lambda i: (i, 0, table_block))]
        + ([sums_spec] if base is not None else []),
        out_specs=sums_spec,
        out_shape=jax.ShapeDtypeStruct((slots, row_total, degrees), jnp.float32),
        compiler_params=pltpu.CompilerParams(vmem_limit_bytes=VMEM_BYTES),
        cost_estimate=pl.CostEstimate(
            flops=4 * slots * row_total * degrees * lat_count,
            bytes_accessed=2 * slots * (degrees * lat_count + 2 * row_total * (lat_count + degrees)),
            transcendentals=0,
        ),
        name="analysis",
    )(*folded, even, odd, legendre, *([base] if base is not None else []))


def trig_kernel(cos_base_ref, sin_base_ref, cos_turn_ref, sin_turn_ref, cos_base_t, sin_base_t, cos_turn_t, sin_turn_t, by_wave_ref, by_lon_ref):
    for j in range(cos_base_ref.shape[1]):
        lanes = pl.ds(j * LANES, LANES)
        cos_base, sin_base = cos_base_ref[:, j : j + 1], sin_base_ref[:, j : j + 1]
        angles = cos_base * cos_turn_ref[...] - sin_base * sin_turn_ref[...]
        by_wave_ref[:, lanes] = angles.astype(by_wave_ref.dtype)
        cos_base, sin_base = cos_base_t[j : j + 1, :], sin_base_t[j : j + 1, :]
        angles = cos_base * cos_turn_t[...] - sin_base * sin_turn_t[...]
        by_lon_ref[lanes, :] = angles.astype(by_lon_ref.dtype)


def trig_tables(owner_table, lon_count):
    waves = jnp.repeat(owner_table, 2).astype(jnp.float32)[:, None]
    quarter = jnp.tile(jnp.array([0, lon_count // 4], jnp.float32), owner_table.shape[0])[:, None]
    unit = 2.0 * math.pi / lon_count

    def angles(lon, turn):
        phase = waves * lon + turn
        return (phase - lon_count * jnp.floor(phase * (1.0 / lon_count))) * unit

    base = angles(jnp.arange(0, lon_count, LANES, dtype=jnp.float32)[None, :], quarter)
    turn = angles(jnp.arange(LANES, dtype=jnp.float32)[None, :], 0.0)
    depth = waves.shape[0]
    blocks = lon_count // LANES
    rows = 256
    small = pl.BlockSpec((rows, blocks), lambda i: (i, 0))
    wide = pl.BlockSpec((rows, LANES), lambda i: (i, 0))
    small_t = pl.BlockSpec((blocks, rows), lambda i: (0, i))
    wide_t = pl.BlockSpec((LANES, rows), lambda i: (0, i))
    parts = (jnp.cos(base), jnp.sin(base), jnp.cos(turn), jnp.sin(turn))
    return pl.pallas_call(
        trig_kernel,
        grid=(depth // rows,),
        in_specs=[small, small, wide, wide, small_t, small_t, wide_t, wide_t],
        out_specs=[
            pl.BlockSpec((rows, lon_count), lambda i: (i, 0)),
            pl.BlockSpec((lon_count, rows), lambda i: (0, i)),
        ],
        out_shape=[
            jax.ShapeDtypeStruct((depth, lon_count), jnp.bfloat16),
            jax.ShapeDtypeStruct((lon_count, depth), jnp.bfloat16),
        ],
        compiler_params=pltpu.CompilerParams(vmem_limit_bytes=VMEM_BYTES),
        cost_estimate=pl.CostEstimate(
            flops=8 * depth * lon_count, bytes_accessed=4 * depth * lon_count, transcendentals=0
        ),
        name="trig",
    )(*parts, *[x.T for x in parts])


def exchange(rows):
    return lax.all_to_all(rows, AXES, split_axis=0, concat_axis=0, tiled=True)


def after(value, *others):
    return lax.optimization_barrier((value, others))[0]


def by_hemisphere_and_level(spectral, legendre, owner_table):
    slots, _, fields, levels, degrees = spectral.shape
    half_lat = legendre.shape[2]
    lon_count = 4 * half_lat
    row_total = 2 * fields * levels
    tiles = half_lat // LANES
    wavenumber = lax.dynamic_slice_in_dim(owner_table, lax.axis_index(AXES) * slots, slots)
    distance = jnp.arange(degrees, dtype=jnp.int32)[None, :] - wavenumber[:, None]
    kept = distance >= 0
    is_odd = distance % 2 != 0
    keep = kept.astype(jnp.bfloat16)[:, None, :]
    flip = jnp.where(is_odd, -keep[:, 0], keep[:, 0])[:, None, :]
    scale = 1.0 / math.sqrt(2 * half_lat)
    even = jnp.where(kept & ~is_odd, scale, 0.0).astype(jnp.float32)[:, None, :]
    odd = jnp.where(kept & is_odd, scale, 0.0).astype(jnp.float32)[:, None, :]
    spec_rows = spectral.reshape(slots, row_total, degrees)
    least = tuple(8 * g * levels for g in range(slots // 4))
    plane = jnp.zeros((1,), jnp.int32)

    def send(spec, tile):
        return synthesize(plane, 1, spec, keep, flip, legendre, (tile, 1), fields, levels, least)[0]

    sent = [send(spec_rows, 0)]
    by_wave, by_lon = trig_tables(after(owner_table, sent[0]), lon_count)
    later = after(spec_rows, by_wave)
    sent += [send(later, tile) for tile in range(1, tiles)]
    arrived = [exchange(rows) for rows in sent]
    zonal = [longitudes(rows, by_lon, by_wave, fields) for rows in arrived]
    returned = [exchange(rows) for rows in zonal]
    folded = [fold(plane, [rows], slots, levels, fields) for rows in returned]
    base = analyze(folded[:-1], even, odd, legendre, row_total, least, 0)
    out = analyze(folded[-1:], even, odd, legendre, row_total, least, tiles - 1, base)
    return out.reshape(slots, 2, fields, levels, degrees)


def make_trig(wavenumber, lon_count):
    lon_index = jnp.arange(lon_count, dtype=jnp.int32)
    phases = wavenumber[:, None] * lon_index[None, :] % lon_count
    angles = phases.astype(jnp.float32) * (2.0 * math.pi / lon_count)
    return jnp.stack([jnp.cos(angles), -jnp.sin(angles)], axis=1).astype(jnp.bfloat16)


def by_level_and_latitude(spectral, legendre, owner_table):
    slot_count, _, fields, levels, degrees = spectral.shape
    half_lat = legendre.shape[2]
    lat_count = 2 * half_lat
    lon_count = 2 * lat_count
    wave_count = owner_table.shape[0]
    band_count = lax.axis_size("band")
    group_count = lax.axis_size("grp")
    device_count = band_count * group_count
    level_block = levels // band_count
    lat_block = lat_count // group_count
    row_total = 2 * fields * levels
    row_width = fields * level_block * lat_block
    slot_start = lax.axis_index(("band", "grp")) * slot_count
    wavenumber = lax.dynamic_slice_in_dim(owner_table, slot_start, slot_count)
    degree_index = jnp.arange(degrees, dtype=jnp.int32)
    keep_mask = (degree_index[None, :] >= wavenumber[:, None]).astype(jnp.bfloat16)
    odd_part = (degree_index[None, :] - wavenumber[:, None]) % 2
    flip_sign = (1 - 2 * odd_part).astype(jnp.bfloat16)
    spec_rows = spectral.reshape(slot_count, row_total, degrees) * keep_mask[:, None, :]
    both_rows = jnp.concatenate([spec_rows, spec_rows * flip_sign[:, None, :]], axis=1)
    halves = jnp.einsum("srn,snt->srt", both_rows, legendre, preferred_element_type=jnp.float32)
    northern = halves[:, :row_total]
    mirrored = halves[:, row_total:]
    fourier = jnp.concatenate([northern, jnp.flip(mirrored, axis=2)], axis=2)
    fourier = fourier.reshape(
        slot_count, 2, fields, band_count, level_block, group_count, lat_block
    )
    fourier = jnp.transpose(fourier, (0, 1, 2, 3, 5, 4, 6))
    fourier_low = (fourier * (1.0 / math.sqrt(degrees))).astype(jnp.bfloat16)
    packed = fourier_low.reshape(1, slot_count, 2, fields, device_count, level_block, lat_block)
    arrived = lax.all_to_all(packed, ("band", "grp"), split_axis=4, concat_axis=0, tiled=True)
    arrived = arrived.reshape(-1, 2, row_width)
    trig_rows = make_trig(owner_table, lon_count)
    grid_values = jnp.einsum("scw,scl->wl", arrived, trig_rows, preferred_element_type=jnp.float32)
    grid_values = (grid_values * (1.0 / math.sqrt(wave_count))).reshape(
        fields, level_block * lat_block, lon_count
    )
    product = (grid_values * jnp.roll(grid_values, -1, axis=0)).astype(jnp.bfloat16)
    zonal_coeffs = jnp.einsum(
        "wl,scl->scw",
        product.reshape(row_width, lon_count),
        trig_rows,
        preferred_element_type=jnp.float32,
    )
    zonal_coeffs = (zonal_coeffs * (2.0 / math.sqrt(lon_count))).astype(jnp.bfloat16)
    sendback = zonal_coeffs.reshape(device_count, slot_count, 2, fields, 1, level_block, lat_block)
    returned = lax.all_to_all(sendback, ("band", "grp"), split_axis=0, concat_axis=4, tiled=True)
    returned = returned.reshape(
        slot_count, 2, fields, band_count, group_count, level_block, lat_block
    )
    returned = jnp.transpose(returned, (0, 1, 2, 3, 5, 4, 6)).reshape(slot_count, row_total, lat_count)
    northern_part = returned[:, :, :half_lat].astype(jnp.float32)
    mirror_part = jnp.flip(returned[:, :, half_lat:], axis=2).astype(jnp.float32)
    plus_part = (northern_part + mirror_part).astype(jnp.bfloat16)
    minus_part = (northern_part - mirror_part).astype(jnp.bfloat16)
    stacked = jnp.concatenate([plus_part, minus_part], axis=1)
    projected = jnp.einsum("srt,snt->srn", stacked, legendre, preferred_element_type=jnp.float32)
    even_rows = flip_sign[:, None, :] > 0
    chosen = jnp.where(even_rows, projected[:, :row_total], projected[:, row_total:])
    chosen = chosen * keep_mask.astype(jnp.float32)[:, None, :] * (1.0 / math.sqrt(lat_count))
    return chosen.reshape(slot_count, 2, fields, levels, degrees)


def on_device(spectral, legendre, owner_table):
    slots, _, _, levels, _ = spectral.shape
    whole_hemispheres = lax.axis_size("band") * lax.axis_size("grp") == 2 * levels
    if whole_hemispheres and legendre.shape[2] % LANES == 0 and slots % 4 == 0 and levels % 16 == 0:
        return by_hemisphere_and_level(spectral, legendre, owner_table)
    return by_level_and_latitude(spectral, legendre, owner_table)


def solution(mesh):
    placed = (P(("band", "grp"), None, None, None, None), P(("band", "grp"), None, None), P())
    return jax.shard_map(
        on_device,
        mesh=mesh,
        in_specs=placed,
        out_specs=P(("band", "grp"), None, None, None, None),
        check_vma=False,
    )
```

```python
import functools
import math

import jax
import jax.numpy as jnp
from jax import lax
from jax.experimental import pallas as pl
from jax.experimental.pallas import tpu as pltpu
from jax.sharding import PartitionSpec as P

LANES = 128
AXES = ("band", "grp")
VMEM_BYTES = 24 * 1024 * 1024
WIDE_VMEM_BYTES = 40 * 1024 * 1024


def synthesis_kernel(slots, levels, fields, least, scale, first_ref, owner_ref, spec_ref, table_ref, out_ref, rows_ref):
    tiles = rows_ref.shape[1]
    step = pl.program_id(0)
    block = spec_ref.shape[0]
    row_total = spec_ref.shape[1]
    stride = 2 * slots

    def run(group):
        start = least[group]
        for j in range(block):
            spec = spec_ref[j, :, start:]
            wave = owner_ref[first_ref[0] + group * block + j]
            distance = lax.broadcasted_iota(jnp.int32, (1, spec.shape[1]), 1) + (start - wave)
            keep = jnp.where(distance >= 0, 1.0, 0.0)
            flip = jnp.where(distance % 2 == 0, keep, -keep)
            both = jnp.concatenate([spec * keep.astype(spec.dtype), spec * flip.astype(spec.dtype)], axis=0)
            halves = jnp.dot(both, table_ref[j, start:, :], preferred_element_type=jnp.float32) * scale
            first = 2 * (group * block + j)
            for hemi in range(2):
                for part in range(2):
                    for field in range(fields):
                        at = hemi * row_total + (part * fields + field) * levels
                        target = pl.ds(hemi * levels * stride + first + part, levels, stride=stride)
                        for tile in range(tiles):
                            lanes = slice(tile * LANES, (tile + 1) * LANES)
                            rows_ref[field, tile, target, :] = halves[at : at + levels, lanes]

    for group in range(slots // block):
        pl.when(step == group)(functools.partial(run, group))

    @pl.when(step == pl.num_programs(0) - 1)
    def _():
        for field in range(fields):
            for tile in range(tiles):
                lanes = pl.ds((field * tiles + tile) * LANES, LANES)
                out_ref[:, lanes] = rows_ref[field, tile].astype(out_ref.dtype)


def synthesize(first, owner_table, spec_rows, legendre, chunk, fields, levels, least):
    slots, row_total, degrees = spec_rows.shape
    block = slots // len(least)
    rows = 2 * levels * 2 * slots
    at, tiles = chunk
    shape = (rows, fields * tiles * LANES)
    return pl.pallas_call(
        functools.partial(synthesis_kernel, slots, levels, fields, least, 1.0 / math.sqrt(degrees)),
        grid_spec=pltpu.PrefetchScalarGridSpec(
            num_scalar_prefetch=2,
            grid=(slots // block,),
            in_specs=[
                pl.BlockSpec((block, row_total, degrees), lambda i, *_: (i, 0, 0)),
                pl.BlockSpec((block, degrees, tiles * LANES), lambda i, *_: (i, 0, at // tiles)),
            ],
            out_specs=pl.BlockSpec(shape, lambda i, *_: (0, 0)),
            scratch_shapes=[pltpu.VMEM((fields, tiles, rows, LANES), jnp.float32)],
        ),
        out_shape=jax.ShapeDtypeStruct(shape, jnp.bfloat16),
        compiler_params=pltpu.CompilerParams(vmem_limit_bytes=VMEM_BYTES),
        cost_estimate=pl.CostEstimate(
            flops=4 * slots * row_total * degrees * tiles * LANES,
            bytes_accessed=2 * slots * degrees * (row_total + tiles * LANES) + 2 * rows * shape[1],
            transcendentals=0,
        ),
        name="synthesis",
    )(first, owner_table, spec_rows, legendre)


def longitude_kernel(fields, grid_scale, zonal_scale, rows_ref, by_lon_ref, by_wave_ref, out_ref, sum_ref):
    step = pl.program_id(0)
    values = jnp.dot(by_lon_ref[...], rows_ref[...], preferred_element_type=jnp.float32) * grid_scale
    one = values.shape[1] // fields
    following = jnp.concatenate([values[:, one:], values[:, :one]], axis=1)
    product = (values * following).astype(jnp.bfloat16)
    share = jnp.dot(by_wave_ref[...], product, preferred_element_type=jnp.float32)

    @pl.when(step == 0)
    def _():
        sum_ref[...] = share

    @pl.when(step > 0)
    def _():
        sum_ref[...] += share

    @pl.when(step == pl.num_programs(0) - 1)
    def _():
        out_ref[...] = (sum_ref[...] * zonal_scale).astype(out_ref.dtype)


def longitudes(rows, by_lon, by_wave, fields):
    depth, width = rows.shape
    lon_count = by_lon.shape[0]
    lon_block = lon_count // 5
    return pl.pallas_call(
        functools.partial(longitude_kernel, fields, 1.0 / math.sqrt(depth // 2), 2.0 / math.sqrt(lon_count)),
        grid=(lon_count // lon_block,),
        in_specs=[
            pl.BlockSpec((depth, width), lambda i: (0, 0)),
            pl.BlockSpec((lon_block, depth), lambda i: (i, 0)),
            pl.BlockSpec((depth, lon_block), lambda i: (0, i)),
        ],
        out_specs=pl.BlockSpec((depth, width), lambda i: (0, 0)),
        out_shape=jax.ShapeDtypeStruct((depth, width), jnp.bfloat16),
        scratch_shapes=[pltpu.VMEM((depth, width), jnp.float32)],
        compiler_params=pltpu.CompilerParams(vmem_limit_bytes=WIDE_VMEM_BYTES),
        cost_estimate=pl.CostEstimate(
            flops=4 * depth * width * lon_count,
            bytes_accessed=4 * depth * (width + lon_count),
            transcendentals=0,
        ),
        name="longitudes",
    )(rows, by_lon, by_wave)


def fold_kernel(slots, levels, fields, arrived_ref, out_ref, rows_ref):
    tiles = rows_ref.shape[1]
    stride = 2 * slots
    half = levels * stride
    for field in range(fields):
        for tile in range(tiles):
            lanes = pl.ds((field * tiles + tile) * LANES, LANES)
            rows_ref[field, tile] = arrived_ref[:, lanes].astype(jnp.float32)
    for slot in range(slots):
        for part in range(2):
            for field in range(fields):
                for tile in range(tiles):
                    first = 2 * slot + part
                    north = rows_ref[field, tile, pl.ds(first, levels, stride=stride), :]
                    south = rows_ref[field, tile, pl.ds(half + first, levels, stride=stride), :]
                    lanes = pl.ds(tile * LANES, LANES)
                    at = (part * fields + field) * levels
                    out_ref[slot, at : at + levels, lanes] = (north + south).astype(out_ref.dtype)
                    at += 2 * fields * levels
                    out_ref[slot, at : at + levels, lanes] = (north - south).astype(out_ref.dtype)


def fold(arrived, slots, levels, fields):
    row_total = 2 * fields * levels
    rows, width = arrived.shape
    tiles = width // (fields * LANES)
    shape = (slots, 2 * row_total, tiles * LANES)
    return pl.pallas_call(
        functools.partial(fold_kernel, slots, levels, fields),
        in_specs=[pl.BlockSpec((rows, width), lambda: (0, 0))],
        out_specs=pl.BlockSpec(shape, lambda: (0, 0, 0)),
        out_shape=jax.ShapeDtypeStruct(shape, jnp.bfloat16),
        scratch_shapes=[pltpu.VMEM((fields, tiles, rows, LANES), jnp.float32)],
        compiler_params=pltpu.CompilerParams(vmem_limit_bytes=VMEM_BYTES),
        cost_estimate=pl.CostEstimate(flops=2 * rows * width, bytes_accessed=4 * rows * width, transcendentals=0),
        name="fold",
    )(arrived)


def analysis_kernel(chunks, least, adds, *refs):
    folded_refs = refs[:chunks]
    even_ref, odd_ref, table_ref = refs[chunks : chunks + 3]
    base_ref, out_ref = refs[-2], refs[-1]
    row_total, degrees = out_ref.shape[1:]
    step = pl.program_id(0)

    def run(group):
        start = least[group]
        for j in range(out_ref.shape[0]):
            folded = jnp.concatenate([ref[j] for ref in folded_refs], axis=1)
            sums = lax.dot_general(
                folded, table_ref[j, start:, :], (((1,), (1,)), ((), ())), preferred_element_type=jnp.float32
            )
            kept = sums[:row_total] * even_ref[j, :, start:] + sums[row_total:] * odd_ref[j, :, start:]
            if adds:
                kept = kept + base_ref[j, :, start:]
            out_ref[j, :, start:] = kept
            if start:
                out_ref[j, :, :start] = jnp.zeros((row_total, start), out_ref.dtype)

    for group in range(len(least)):
        pl.when(step == group)(functools.partial(run, group))


def analyze(folded, even, odd, legendre, row_total, least, first_tile, base=None):
    slots, degrees, _ = legendre.shape
    block = slots // len(least)
    lat_count = sum(x.shape[2] for x in folded)
    table_block = first_tile * LANES // lat_count
    mask_spec = pl.BlockSpec((block, 1, degrees), lambda i: (i, 0, 0))
    sums_spec = pl.BlockSpec((block, row_total, degrees), lambda i: (i, 0, 0))
    return pl.pallas_call(
        functools.partial(analysis_kernel, len(folded), least, base is not None),
        grid=(len(least),),
        in_specs=[pl.BlockSpec((block,) + x.shape[1:], lambda i: (i, 0, 0)) for x in folded]
        + [mask_spec, mask_spec, pl.BlockSpec((block, degrees, lat_count), lambda i: (i, 0, table_block))]
        + ([sums_spec] if base is not None else []),
        out_specs=sums_spec,
        out_shape=jax.ShapeDtypeStruct((slots, row_total, degrees), jnp.float32),
        compiler_params=pltpu.CompilerParams(vmem_limit_bytes=VMEM_BYTES),
        cost_estimate=pl.CostEstimate(
            flops=4 * slots * row_total * degrees * lat_count,
            bytes_accessed=2 * slots * (degrees * lat_count + 2 * row_total * (lat_count + degrees)),
            transcendentals=0,
        ),
        name="analysis",
    )(*folded, even, odd, legendre, *([base] if base is not None else []))


def after(value, *others):
    return lax.optimization_barrier((value, others))[0]


def trig_kernel(cos_base_ref, sin_base_ref, cos_turn_ref, sin_turn_ref, cos_base_t, sin_base_t, cos_turn_t, sin_turn_t, by_wave_ref, by_lon_ref):
    for j in range(cos_base_ref.shape[1]):
        lanes = pl.ds(j * LANES, LANES)
        cos_base, sin_base = cos_base_ref[:, j : j + 1], sin_base_ref[:, j : j + 1]
        angles = cos_base * cos_turn_ref[...] - sin_base * sin_turn_ref[...]
        by_wave_ref[:, lanes] = angles.astype(by_wave_ref.dtype)
        cos_base, sin_base = cos_base_t[j : j + 1, :], sin_base_t[j : j + 1, :]
        angles = cos_base * cos_turn_t[...] - sin_base * sin_turn_t[...]
        by_lon_ref[lanes, :] = angles.astype(by_lon_ref.dtype)


def trig_tables(owner_table, lon_count, *others):
    waves = jnp.repeat(owner_table, 2).astype(jnp.float32)[:, None]
    quarter = jnp.tile(jnp.array([0, lon_count // 4], jnp.float32), owner_table.shape[0])[:, None]
    unit = 2.0 * math.pi / lon_count

    def angles(lon, turn):
        phase = waves * lon + turn
        return (phase - lon_count * jnp.floor(phase * (1.0 / lon_count))) * unit

    base = angles(jnp.arange(0, lon_count, LANES, dtype=jnp.float32)[None, :], quarter)
    turn = angles(jnp.arange(LANES, dtype=jnp.float32)[None, :], 0.0)
    depth = waves.shape[0]
    blocks = lon_count // LANES
    rows = 256
    small = pl.BlockSpec((rows, blocks), lambda i: (i, 0))
    wide = pl.BlockSpec((rows, LANES), lambda i: (i, 0))
    small_t = pl.BlockSpec((blocks, rows), lambda i: (0, i))
    wide_t = pl.BlockSpec((LANES, rows), lambda i: (0, i))
    parts = (jnp.cos(base), jnp.sin(base), jnp.cos(turn), jnp.sin(turn))
    parts = after(parts, *others)
    return pl.pallas_call(
        trig_kernel,
        grid=(depth // rows,),
        in_specs=[small, small, wide, wide, small_t, small_t, wide_t, wide_t],
        out_specs=[
            pl.BlockSpec((rows, lon_count), lambda i: (i, 0)),
            pl.BlockSpec((lon_count, rows), lambda i: (0, i)),
        ],
        out_shape=[
            jax.ShapeDtypeStruct((depth, lon_count), jnp.bfloat16),
            jax.ShapeDtypeStruct((lon_count, depth), jnp.bfloat16),
        ],
        compiler_params=pltpu.CompilerParams(vmem_limit_bytes=VMEM_BYTES),
        cost_estimate=pl.CostEstimate(
            flops=8 * depth * lon_count, bytes_accessed=4 * depth * lon_count, transcendentals=0
        ),
        name="trig",
    )(*parts, *[x.T for x in parts])


def exchange(rows):
    return lax.all_to_all(rows, AXES, split_axis=0, concat_axis=0, tiled=True)


def by_hemisphere_and_level(spectral, legendre, owner_table):
    slots, _, fields, levels, degrees = spectral.shape
    half_lat = legendre.shape[2]
    lon_count = 4 * half_lat
    row_total = 2 * fields * levels
    tiles = half_lat // LANES
    first = lax.axis_index(AXES).astype(jnp.int32) * slots
    spec_rows = spectral.reshape(slots, row_total, degrees)
    least = tuple(8 * g * levels for g in range(slots // 4))
    chunks = [(t, 2) for t in range(0, tiles - 1, 2)] + ([(tiles - 1, 1)] if tiles % 2 else [])
    count = len(chunks)

    def send(spec, chunk):
        return synthesize(first.reshape(1), owner_table, spec, legendre, chunk, fields, levels, least)

    sent, arrived = {}, {}
    spec = spec_rows
    for position, chunk in enumerate(chunks[-1:] + chunks[:-1]):
        sent[chunk] = send(spec, chunk)
        arrived[chunk] = exchange(sent[chunk])
        if position == 0:
            spec = after(spec, sent[chunk])
            turning = after(owner_table, sent[chunk])
            landed = arrived[chunk]
        elif position == 1:
            by_wave, by_lon = trig_tables(turning, lon_count, sent[chunk], landed)
            spec = after(spec, by_wave)
    returned = [exchange(longitudes(arrived[chunk], by_lon, by_wave, fields)) for chunk in chunks]
    folded = [fold(rows, slots, levels, fields) for rows in returned[:-1]]
    wavenumber = lax.dynamic_slice_in_dim(after(owner_table, by_wave), first, slots)
    distance = jnp.arange(degrees, dtype=jnp.int32)[None, :] - wavenumber[:, None]
    scale = 1.0 / math.sqrt(2 * half_lat)
    even = jnp.where((distance >= 0) & (distance % 2 == 0), scale, 0.0).astype(jnp.float32)[:, None, :]
    odd = jnp.where((distance >= 0) & (distance % 2 != 0), scale, 0.0).astype(jnp.float32)[:, None, :]
    base = analyze(folded, even, odd, legendre, row_total, least, 0)
    last = fold(after(returned[-1], base), slots, levels, fields)
    out = analyze([last], even, odd, legendre, row_total, least, chunks[-1][0], base)
    return out.reshape(slots, 2, fields, levels, degrees)


def make_trig(wavenumber, lon_count):
    lon_index = jnp.arange(lon_count, dtype=jnp.int32)
    phases = wavenumber[:, None] * lon_index[None, :] % lon_count
    angles = phases.astype(jnp.float32) * (2.0 * math.pi / lon_count)
    return jnp.stack([jnp.cos(angles), -jnp.sin(angles)], axis=1).astype(jnp.bfloat16)


def by_level_and_latitude(spectral, legendre, owner_table):
    slot_count, _, fields, levels, degrees = spectral.shape
    half_lat = legendre.shape[2]
    lat_count = 2 * half_lat
    lon_count = 2 * lat_count
    wave_count = owner_table.shape[0]
    band_count = lax.axis_size("band")
    group_count = lax.axis_size("grp")
    device_count = band_count * group_count
    level_block = levels // band_count
    lat_block = lat_count // group_count
    row_total = 2 * fields * levels
    row_width = fields * level_block * lat_block
    slot_start = lax.axis_index(("band", "grp")) * slot_count
    wavenumber = lax.dynamic_slice_in_dim(owner_table, slot_start, slot_count)
    degree_index = jnp.arange(degrees, dtype=jnp.int32)
    keep_mask = (degree_index[None, :] >= wavenumber[:, None]).astype(jnp.bfloat16)
    odd_part = (degree_index[None, :] - wavenumber[:, None]) % 2
    flip_sign = (1 - 2 * odd_part).astype(jnp.bfloat16)
    spec_rows = spectral.reshape(slot_count, row_total, degrees) * keep_mask[:, None, :]
    both_rows = jnp.concatenate([spec_rows, spec_rows * flip_sign[:, None, :]], axis=1)
    halves = jnp.einsum("srn,snt->srt", both_rows, legendre, preferred_element_type=jnp.float32)
    northern = halves[:, :row_total]
    mirrored = halves[:, row_total:]
    fourier = jnp.concatenate([northern, jnp.flip(mirrored, axis=2)], axis=2)
    fourier = fourier.reshape(
        slot_count, 2, fields, band_count, level_block, group_count, lat_block
    )
    fourier = jnp.transpose(fourier, (0, 1, 2, 3, 5, 4, 6))
    fourier_low = (fourier * (1.0 / math.sqrt(degrees))).astype(jnp.bfloat16)
    packed = fourier_low.reshape(1, slot_count, 2, fields, device_count, level_block, lat_block)
    arrived = lax.all_to_all(packed, ("band", "grp"), split_axis=4, concat_axis=0, tiled=True)
    arrived = arrived.reshape(-1, 2, row_width)
    trig_rows = make_trig(owner_table, lon_count)
    grid_values = jnp.einsum("scw,scl->wl", arrived, trig_rows, preferred_element_type=jnp.float32)
    grid_values = (grid_values * (1.0 / math.sqrt(wave_count))).reshape(
        fields, level_block * lat_block, lon_count
    )
    product = (grid_values * jnp.roll(grid_values, -1, axis=0)).astype(jnp.bfloat16)
    zonal_coeffs = jnp.einsum(
        "wl,scl->scw",
        product.reshape(row_width, lon_count),
        trig_rows,
        preferred_element_type=jnp.float32,
    )
    zonal_coeffs = (zonal_coeffs * (2.0 / math.sqrt(lon_count))).astype(jnp.bfloat16)
    sendback = zonal_coeffs.reshape(device_count, slot_count, 2, fields, 1, level_block, lat_block)
    returned = lax.all_to_all(sendback, ("band", "grp"), split_axis=0, concat_axis=4, tiled=True)
    returned = returned.reshape(
        slot_count, 2, fields, band_count, group_count, level_block, lat_block
    )
    returned = jnp.transpose(returned, (0, 1, 2, 3, 5, 4, 6)).reshape(slot_count, row_total, lat_count)
    northern_part = returned[:, :, :half_lat].astype(jnp.float32)
    mirror_part = jnp.flip(returned[:, :, half_lat:], axis=2).astype(jnp.float32)
    plus_part = (northern_part + mirror_part).astype(jnp.bfloat16)
    minus_part = (northern_part - mirror_part).astype(jnp.bfloat16)
    stacked = jnp.concatenate([plus_part, minus_part], axis=1)
    projected = jnp.einsum("srt,snt->srn", stacked, legendre, preferred_element_type=jnp.float32)
    even_rows = flip_sign[:, None, :] > 0
    chosen = jnp.where(even_rows, projected[:, :row_total], projected[:, row_total:])
    chosen = chosen * keep_mask.astype(jnp.float32)[:, None, :] * (1.0 / math.sqrt(lat_count))
    return chosen.reshape(slot_count, 2, fields, levels, degrees)


def on_device(spectral, legendre, owner_table):
    slots, _, _, levels, _ = spectral.shape
    whole_hemispheres = lax.axis_size("band") * lax.axis_size("grp") == 2 * levels
    if whole_hemispheres and legendre.shape[2] % (2 * LANES) == LANES and slots % 4 == 0 and levels % 16 == 0:
        return by_hemisphere_and_level(spectral, legendre, owner_table)
    return by_level_and_latitude(spectral, legendre, owner_table)


def solution(mesh):
    placed = (P(("band", "grp"), None, None, None, None), P(("band", "grp"), None, None), P())
    return jax.shard_map(
        on_device,
        mesh=mesh,
        in_specs=placed,
        out_specs=P(("band", "grp"), None, None, None, None),
        check_vma=False,
    )
```

```python
import functools
import math

import jax
import jax.numpy as jnp
from jax import lax
from jax.experimental import pallas as pl
from jax.experimental.pallas import tpu as pltpu
from jax.sharding import PartitionSpec as P

LANES = 128
AXES = ("band", "grp")
VMEM_BYTES = 62 * 1024 * 1024


def synthesis_kernel(slots, levels, fields, least, scale, first_ref, owner_ref, spec_ref, *refs):
    table_refs, out_ref, rows_ref = refs[:-2], refs[-2], refs[-1]
    tiles = rows_ref.shape[1]
    step = pl.program_id(0)
    block = spec_ref.shape[0]
    row_total = spec_ref.shape[1]
    stride = 2 * slots

    def run(group):
        start = least[group]
        for j in range(block):
            spec = spec_ref[j, :, start:]
            wave = owner_ref[first_ref[0] + group * block + j]
            distance = lax.broadcasted_iota(jnp.int32, (1, spec.shape[1]), 1) + (start - wave)
            keep = jnp.where(distance >= 0, 1.0, 0.0)
            flip = jnp.where(distance % 2 == 0, keep, -keep)
            both = jnp.concatenate([spec * keep.astype(spec.dtype), spec * flip.astype(spec.dtype)], axis=0)
            table = jnp.concatenate([ref[j, start:, :] for ref in table_refs], axis=1)
            halves = jnp.dot(both, table, preferred_element_type=jnp.float32) * scale
            first = 2 * (group * block + j)
            for hemi in range(2):
                for part in range(2):
                    for field in range(fields):
                        at = hemi * row_total + (part * fields + field) * levels
                        target = pl.ds(hemi * levels * stride + first + part, levels, stride=stride)
                        for tile in range(tiles):
                            lanes = slice(tile * LANES, (tile + 1) * LANES)
                            rows_ref[field, tile, target, :] = halves[at : at + levels, lanes]

    for group in range(slots // block):
        pl.when(step == group)(functools.partial(run, group))

    @pl.when(step == pl.num_programs(0) - 1)
    def _():
        for field in range(fields):
            for tile in range(tiles):
                lanes = pl.ds((field * tiles + tile) * LANES, LANES)
                out_ref[:, lanes] = rows_ref[field, tile].astype(out_ref.dtype)


def synthesize(first, owner_table, spec_rows, legendre, chunk, fields, levels, least):
    slots, row_total, degrees = spec_rows.shape
    block = slots // len(least)
    rows = 2 * levels * 2 * slots
    at, tiles = chunk
    shape = (rows, fields * tiles * LANES)
    return pl.pallas_call(
        functools.partial(synthesis_kernel, slots, levels, fields, least, 1.0 / math.sqrt(degrees)),
        grid_spec=pltpu.PrefetchScalarGridSpec(
            num_scalar_prefetch=2,
            grid=(slots // block,),
            in_specs=[
                pl.BlockSpec((block, row_total, degrees), lambda i, *_: (i, 0, 0)),
            ]
            + [pl.BlockSpec((block, degrees, LANES), lambda i, *_, t=at + t: (i, 0, t)) for t in range(tiles)],
            out_specs=pl.BlockSpec(shape, lambda i, *_: (0, 0)),
            scratch_shapes=[pltpu.VMEM((fields, tiles, rows, LANES), jnp.float32)],
        ),
        out_shape=jax.ShapeDtypeStruct(shape, jnp.bfloat16),
        compiler_params=pltpu.CompilerParams(vmem_limit_bytes=VMEM_BYTES),
        cost_estimate=pl.CostEstimate(
            flops=4 * slots * row_total * degrees * tiles * LANES,
            bytes_accessed=2 * slots * degrees * (row_total + tiles * LANES) + 2 * rows * shape[1],
            transcendentals=0,
        ),
        name="synthesis",
    )(first, owner_table, spec_rows, *[legendre] * tiles)


def longitude_kernel(fields, grid_scale, zonal_scale, rows_ref, by_lon_ref, by_wave_ref, out_ref, sum_ref):
    step = pl.program_id(0)
    values = jnp.dot(by_lon_ref[...], rows_ref[...], preferred_element_type=jnp.float32) * grid_scale
    one = values.shape[1] // fields
    following = jnp.concatenate([values[:, one:], values[:, :one]], axis=1)
    product = (values * following).astype(jnp.bfloat16)
    share = jnp.dot(by_wave_ref[...], product, preferred_element_type=jnp.float32)

    @pl.when(step == 0)
    def _():
        sum_ref[...] = share

    @pl.when(step > 0)
    def _():
        sum_ref[...] += share

    @pl.when(step == pl.num_programs(0) - 1)
    def _():
        out_ref[...] = (sum_ref[...] * zonal_scale).astype(out_ref.dtype)


def longitudes(rows, by_lon, by_wave, fields):
    depth, width = rows.shape
    lon_count = by_lon.shape[0]
    lon_block = lon_count // 5
    return pl.pallas_call(
        functools.partial(longitude_kernel, fields, 1.0 / math.sqrt(depth // 2), 2.0 / math.sqrt(lon_count)),
        grid=(lon_count // lon_block,),
        in_specs=[
            pl.BlockSpec((depth, width), lambda i: (0, 0)),
            pl.BlockSpec((lon_block, depth), lambda i: (i, 0)),
            pl.BlockSpec((depth, lon_block), lambda i: (0, i)),
        ],
        out_specs=pl.BlockSpec((depth, width), lambda i: (0, 0)),
        out_shape=jax.ShapeDtypeStruct((depth, width), jnp.bfloat16),
        scratch_shapes=[pltpu.VMEM((depth, width), jnp.float32)],
        compiler_params=pltpu.CompilerParams(vmem_limit_bytes=VMEM_BYTES),
        cost_estimate=pl.CostEstimate(
            flops=4 * depth * width * lon_count,
            bytes_accessed=4 * depth * (width + lon_count),
            transcendentals=0,
        ),
        name="longitudes",
    )(rows, by_lon, by_wave)


def fold_kernel(slots, levels, fields, arrived_ref, out_ref, rows_ref):
    tiles = rows_ref.shape[1]
    stride = 2 * slots
    half = levels * stride
    for field in range(fields):
        for tile in range(tiles):
            lanes = pl.ds((field * tiles + tile) * LANES, LANES)
            rows_ref[field, tile] = arrived_ref[:, lanes].astype(jnp.float32)
    for slot in range(slots):
        for part in range(2):
            for field in range(fields):
                for tile in range(tiles):
                    first = 2 * slot + part
                    north = rows_ref[field, tile, pl.ds(first, levels, stride=stride), :]
                    south = rows_ref[field, tile, pl.ds(half + first, levels, stride=stride), :]
                    lanes = pl.ds(tile * LANES, LANES)
                    at = (part * fields + field) * levels
                    out_ref[slot, at : at + levels, lanes] = (north + south).astype(out_ref.dtype)
                    at += 2 * fields * levels
                    out_ref[slot, at : at + levels, lanes] = (north - south).astype(out_ref.dtype)


def fold(arrived, slots, levels, fields):
    row_total = 2 * fields * levels
    rows, width = arrived.shape
    tiles = width // (fields * LANES)
    shape = (slots, 2 * row_total, tiles * LANES)
    return pl.pallas_call(
        functools.partial(fold_kernel, slots, levels, fields),
        in_specs=[pl.BlockSpec((rows, width), lambda: (0, 0))],
        out_specs=pl.BlockSpec(shape, lambda: (0, 0, 0)),
        out_shape=jax.ShapeDtypeStruct(shape, jnp.bfloat16),
        scratch_shapes=[pltpu.VMEM((fields, tiles, rows, LANES), jnp.float32)],
        compiler_params=pltpu.CompilerParams(vmem_limit_bytes=VMEM_BYTES),
        cost_estimate=pl.CostEstimate(flops=2 * rows * width, bytes_accessed=4 * rows * width, transcendentals=0),
        name="fold",
    )(arrived)


def analysis_kernel(chunks, least, adds, *refs):
    folded_refs = refs[:chunks]
    even_ref, odd_ref = refs[chunks : chunks + 2]
    out_ref = refs[-1]
    table_refs = refs[chunks + 2 : -2 if adds else -1]
    row_total, degrees = out_ref.shape[1:]
    step = pl.program_id(0)

    def run(group):
        start = least[group]
        for j in range(out_ref.shape[0]):
            folded = jnp.concatenate([ref[j] for ref in folded_refs], axis=1)
            table = jnp.concatenate([ref[j, start:, :] for ref in table_refs], axis=1)
            sums = lax.dot_general(folded, table, (((1,), (1,)), ((), ())), preferred_element_type=jnp.float32)
            kept = sums[:row_total] * even_ref[j, :, start:] + sums[row_total:] * odd_ref[j, :, start:]
            if adds:
                kept = kept + refs[-2][j, :, start:]
            out_ref[j, :, start:] = kept
            if start:
                out_ref[j, :, :start] = jnp.zeros((row_total, start), out_ref.dtype)

    for group in range(len(least)):
        pl.when(step == group)(functools.partial(run, group))


def analyze(folded, even, odd, legendre, row_total, least, first_tile, base=None):
    slots, degrees, _ = legendre.shape
    block = slots // len(least)
    lat_count = sum(x.shape[2] for x in folded)
    tiles = lat_count // LANES
    mask_spec = pl.BlockSpec((block, 1, degrees), lambda i: (i, 0, 0))
    sums_spec = pl.BlockSpec((block, row_total, degrees), lambda i: (i, 0, 0))
    return pl.pallas_call(
        functools.partial(analysis_kernel, len(folded), least, base is not None),
        grid=(len(least),),
        in_specs=[pl.BlockSpec((block,) + x.shape[1:], lambda i: (i, 0, 0)) for x in folded]
        + [mask_spec, mask_spec]
        + [pl.BlockSpec((block, degrees, LANES), lambda i, t=first_tile + t: (i, 0, t)) for t in range(tiles)]
        + ([sums_spec] if base is not None else []),
        out_specs=sums_spec,
        out_shape=jax.ShapeDtypeStruct((slots, row_total, degrees), jnp.float32),
        compiler_params=pltpu.CompilerParams(vmem_limit_bytes=VMEM_BYTES),
        cost_estimate=pl.CostEstimate(
            flops=4 * slots * row_total * degrees * lat_count,
            bytes_accessed=2 * slots * (degrees * lat_count + 2 * row_total * (lat_count + degrees)),
            transcendentals=0,
        ),
        name="analysis",
    )(*folded, even, odd, *[legendre] * tiles, *([base] if base is not None else []))


def after(value, *others):
    return lax.optimization_barrier((value, others))[0]


def trig_kernel(cos_base_ref, sin_base_ref, cos_turn_ref, sin_turn_ref, cos_base_t, sin_base_t, cos_turn_t, sin_turn_t, by_wave_ref, by_lon_ref):
    for j in range(cos_base_ref.shape[1]):
        lanes = pl.ds(j * LANES, LANES)
        cos_base, sin_base = cos_base_ref[:, j : j + 1], sin_base_ref[:, j : j + 1]
        angles = cos_base * cos_turn_ref[...] - sin_base * sin_turn_ref[...]
        by_wave_ref[:, lanes] = angles.astype(by_wave_ref.dtype)
        cos_base, sin_base = cos_base_t[j : j + 1, :], sin_base_t[j : j + 1, :]
        angles = cos_base * cos_turn_t[...] - sin_base * sin_turn_t[...]
        by_lon_ref[lanes, :] = angles.astype(by_lon_ref.dtype)


def trig_tables(owner_table, lon_count, *others):
    waves = jnp.repeat(owner_table, 2).astype(jnp.float32)[:, None]
    quarter = jnp.tile(jnp.array([0, lon_count // 4], jnp.float32), owner_table.shape[0])[:, None]
    unit = 2.0 * math.pi / lon_count

    def angles(lon, turn):
        phase = waves * lon + turn
        return (phase - lon_count * jnp.floor(phase * (1.0 / lon_count))) * unit

    base = angles(jnp.arange(0, lon_count, LANES, dtype=jnp.float32)[None, :], quarter)
    turn = angles(jnp.arange(LANES, dtype=jnp.float32)[None, :], 0.0)
    depth = waves.shape[0]
    blocks = lon_count // LANES
    rows = 256
    small = pl.BlockSpec((rows, blocks), lambda i: (i, 0))
    wide = pl.BlockSpec((rows, LANES), lambda i: (i, 0))
    small_t = pl.BlockSpec((blocks, rows), lambda i: (0, i))
    wide_t = pl.BlockSpec((LANES, rows), lambda i: (0, i))
    parts = (jnp.cos(base), jnp.sin(base), jnp.cos(turn), jnp.sin(turn))
    parts = after(parts, *others)
    return pl.pallas_call(
        trig_kernel,
        grid=(depth // rows,),
        in_specs=[small, small, wide, wide, small_t, small_t, wide_t, wide_t],
        out_specs=[
            pl.BlockSpec((rows, lon_count), lambda i: (i, 0)),
            pl.BlockSpec((lon_count, rows), lambda i: (0, i)),
        ],
        out_shape=[
            jax.ShapeDtypeStruct((depth, lon_count), jnp.bfloat16),
            jax.ShapeDtypeStruct((lon_count, depth), jnp.bfloat16),
        ],
        compiler_params=pltpu.CompilerParams(vmem_limit_bytes=VMEM_BYTES),
        cost_estimate=pl.CostEstimate(
            flops=8 * depth * lon_count, bytes_accessed=4 * depth * lon_count, transcendentals=0
        ),
        name="trig",
    )(*parts, *[x.T for x in parts])


def exchange(rows):
    return lax.all_to_all(rows, AXES, split_axis=0, concat_axis=0, tiled=True)


def by_hemisphere_and_level(spectral, legendre, owner_table):
    slots, _, fields, levels, degrees = spectral.shape
    half_lat = legendre.shape[2]
    lon_count = 4 * half_lat
    row_total = 2 * fields * levels
    tiles = half_lat // LANES
    first = lax.axis_index(AXES).astype(jnp.int32) * slots
    spec_rows = spectral.reshape(slots, row_total, degrees)
    least = tuple(8 * g * levels for g in range(slots // 4))
    cut = tiles // 2
    chunks = [(cut, tiles - cut), (0, cut)]

    def send(spec, chunk):
        return synthesize(first.reshape(1), owner_table, spec, legendre, chunk, fields, levels, least)

    large = send(spec_rows, chunks[0])
    small = send(after(spec_rows, large), chunks[1])
    arrived = [exchange(large)]
    arrived.append(exchange(after(small, *arrived)))
    by_wave, by_lon = trig_tables(after(owner_table, large), lon_count, small)
    zonal = [longitudes(rows, by_lon, by_wave, fields) for rows in arrived]
    returned = [exchange(zonal[0])]
    returned.append(exchange(after(zonal[1], *returned)))
    wavenumber = lax.dynamic_slice_in_dim(after(owner_table, by_wave), first, slots)
    distance = jnp.arange(degrees, dtype=jnp.int32)[None, :] - wavenumber[:, None]
    scale = 1.0 / math.sqrt(2 * half_lat)
    even = jnp.where((distance >= 0) & (distance % 2 == 0), scale, 0.0).astype(jnp.float32)[:, None, :]
    odd = jnp.where((distance >= 0) & (distance % 2 != 0), scale, 0.0).astype(jnp.float32)[:, None, :]
    out = analyze([fold(returned[0], slots, levels, fields)], even, odd, legendre, row_total, least, cut)
    last = fold(after(returned[1], out), slots, levels, fields)
    out = analyze([last], even, odd, legendre, row_total, least, 0, out)
    return out.reshape(slots, 2, fields, levels, degrees)


def make_trig(wavenumber, lon_count):
    lon_index = jnp.arange(lon_count, dtype=jnp.int32)
    phases = wavenumber[:, None] * lon_index[None, :] % lon_count
    angles = phases.astype(jnp.float32) * (2.0 * math.pi / lon_count)
    return jnp.stack([jnp.cos(angles), -jnp.sin(angles)], axis=1).astype(jnp.bfloat16)


def by_level_and_latitude(spectral, legendre, owner_table):
    slot_count, _, fields, levels, degrees = spectral.shape
    half_lat = legendre.shape[2]
    lat_count = 2 * half_lat
    lon_count = 2 * lat_count
    wave_count = owner_table.shape[0]
    band_count = lax.axis_size("band")
    group_count = lax.axis_size("grp")
    device_count = band_count * group_count
    level_block = levels // band_count
    lat_block = lat_count // group_count
    row_total = 2 * fields * levels
    row_width = fields * level_block * lat_block
    slot_start = lax.axis_index(("band", "grp")) * slot_count
    wavenumber = lax.dynamic_slice_in_dim(owner_table, slot_start, slot_count)
    degree_index = jnp.arange(degrees, dtype=jnp.int32)
    keep_mask = (degree_index[None, :] >= wavenumber[:, None]).astype(jnp.bfloat16)
    odd_part = (degree_index[None, :] - wavenumber[:, None]) % 2
    flip_sign = (1 - 2 * odd_part).astype(jnp.bfloat16)
    spec_rows = spectral.reshape(slot_count, row_total, degrees) * keep_mask[:, None, :]
    both_rows = jnp.concatenate([spec_rows, spec_rows * flip_sign[:, None, :]], axis=1)
    halves = jnp.einsum("srn,snt->srt", both_rows, legendre, preferred_element_type=jnp.float32)
    northern = halves[:, :row_total]
    mirrored = halves[:, row_total:]
    fourier = jnp.concatenate([northern, jnp.flip(mirrored, axis=2)], axis=2)
    fourier = fourier.reshape(
        slot_count, 2, fields, band_count, level_block, group_count, lat_block
    )
    fourier = jnp.transpose(fourier, (0, 1, 2, 3, 5, 4, 6))
    fourier_low = (fourier * (1.0 / math.sqrt(degrees))).astype(jnp.bfloat16)
    packed = fourier_low.reshape(1, slot_count, 2, fields, device_count, level_block, lat_block)
    arrived = lax.all_to_all(packed, ("band", "grp"), split_axis=4, concat_axis=0, tiled=True)
    arrived = arrived.reshape(-1, 2, row_width)
    trig_rows = make_trig(owner_table, lon_count)
    grid_values = jnp.einsum("scw,scl->wl", arrived, trig_rows, preferred_element_type=jnp.float32)
    grid_values = (grid_values * (1.0 / math.sqrt(wave_count))).reshape(
        fields, level_block * lat_block, lon_count
    )
    product = (grid_values * jnp.roll(grid_values, -1, axis=0)).astype(jnp.bfloat16)
    zonal_coeffs = jnp.einsum(
        "wl,scl->scw",
        product.reshape(row_width, lon_count),
        trig_rows,
        preferred_element_type=jnp.float32,
    )
    zonal_coeffs = (zonal_coeffs * (2.0 / math.sqrt(lon_count))).astype(jnp.bfloat16)
    sendback = zonal_coeffs.reshape(device_count, slot_count, 2, fields, 1, level_block, lat_block)
    returned = lax.all_to_all(sendback, ("band", "grp"), split_axis=0, concat_axis=4, tiled=True)
    returned = returned.reshape(
        slot_count, 2, fields, band_count, group_count, level_block, lat_block
    )
    returned = jnp.transpose(returned, (0, 1, 2, 3, 5, 4, 6)).reshape(slot_count, row_total, lat_count)
    northern_part = returned[:, :, :half_lat].astype(jnp.float32)
    mirror_part = jnp.flip(returned[:, :, half_lat:], axis=2).astype(jnp.float32)
    plus_part = (northern_part + mirror_part).astype(jnp.bfloat16)
    minus_part = (northern_part - mirror_part).astype(jnp.bfloat16)
    stacked = jnp.concatenate([plus_part, minus_part], axis=1)
    projected = jnp.einsum("srt,snt->srn", stacked, legendre, preferred_element_type=jnp.float32)
    even_rows = flip_sign[:, None, :] > 0
    chosen = jnp.where(even_rows, projected[:, :row_total], projected[:, row_total:])
    chosen = chosen * keep_mask.astype(jnp.float32)[:, None, :] * (1.0 / math.sqrt(lat_count))
    return chosen.reshape(slot_count, 2, fields, levels, degrees)


def on_device(spectral, legendre, owner_table):
    slots, _, _, levels, _ = spectral.shape
    whole_hemispheres = lax.axis_size("band") * lax.axis_size("grp") == 2 * levels
    if whole_hemispheres and legendre.shape[2] % LANES == 0 and legendre.shape[2] > LANES and slots % 4 == 0 and levels % 16 == 0:
        return by_hemisphere_and_level(spectral, legendre, owner_table)
    return by_level_and_latitude(spectral, legendre, owner_table)


def solution(mesh):
    placed = (P(("band", "grp"), None, None, None, None), P(("band", "grp"), None, None), P())
    return jax.shard_map(
        on_device,
        mesh=mesh,
        in_specs=placed,
        out_specs=P(("band", "grp"), None, None, None, None),
        check_vma=False,
    )
```

```python
import functools
import math

import jax
import jax.numpy as jnp
from jax import lax
from jax.experimental import pallas as pl
from jax.experimental.pallas import tpu as pltpu
from jax.sharding import PartitionSpec as P

LANES = 128
AXES = ("band", "grp")
VMEM_BYTES = 62 * 1024 * 1024


def synthesis_kernel(
    slots, levels, fields, least, chunk, scale, first_ref, owner_ref, spec_ref, table_ref, out_ref, rows_ref, sems, *held
):
    at, tiles = chunk
    groups = len(least)
    block = slots // groups
    row_total, degrees = spec_ref.shape[1:]
    stride = 2 * slots
    copies = []
    for group, start in enumerate(least):
        mine = pl.ds(group * block, block)
        left = pl.ds(start, degrees - start)
        lanes = pl.ds(at * LANES, tiles * LANES)
        copies.append(
            (
                pltpu.make_async_copy(spec_ref.at[mine, :, left], held[2 * group], sems.at[2 * group]),
                pltpu.make_async_copy(table_ref.at[mine, left, lanes], held[2 * group + 1], sems.at[2 * group + 1]),
            )
        )
    order = range(groups - 1, -1, -1)
    for group in order:
        for copy in copies[group]:
            copy.start()
    for group in order:
        for copy in copies[group]:
            copy.wait()
        for j in range(block):
            spec = held[2 * group][j]
            wave = owner_ref[first_ref[0] + group * block + j]
            distance = lax.broadcasted_iota(jnp.int32, (1, spec.shape[1]), 1) + (least[group] - wave)
            keep = jnp.where(distance >= 0, 1.0, 0.0)
            flip = jnp.where(distance % 2 == 0, keep, -keep)
            both = jnp.concatenate([spec * keep.astype(spec.dtype), spec * flip.astype(spec.dtype)], axis=0)
            halves = jnp.dot(both, held[2 * group + 1][j], preferred_element_type=jnp.float32) * scale
            first = 2 * (group * block + j)
            for hemi in range(2):
                for part in range(2):
                    for field in range(fields):
                        row = hemi * row_total + (part * fields + field) * levels
                        target = pl.ds(hemi * levels * stride + first + part, levels, stride=stride)
                        for tile in range(tiles):
                            lanes = slice(tile * LANES, (tile + 1) * LANES)
                            rows_ref[field, tile, target, :] = halves[row : row + levels, lanes]
    for field in range(fields):
        for tile in range(tiles):
            lanes = pl.ds((field * tiles + tile) * LANES, LANES)
            out_ref[:, lanes] = rows_ref[field, tile].astype(out_ref.dtype)


def synthesize(first, owner_table, spec_rows, legendre, chunk, fields, levels, least):
    slots, row_total, degrees = spec_rows.shape
    block = slots // len(least)
    rows = 2 * levels * 2 * slots
    tiles = chunk[1]
    shape = (rows, fields * tiles * LANES)
    held = []
    for start in least:
        held.append(pltpu.VMEM((block, row_total, degrees - start), jnp.bfloat16))
        held.append(pltpu.VMEM((block, degrees - start, tiles * LANES), jnp.bfloat16))
    return pl.pallas_call(
        functools.partial(synthesis_kernel, slots, levels, fields, least, chunk, 1.0 / math.sqrt(degrees)),
        in_specs=[pl.BlockSpec(memory_space=pltpu.SMEM)] * 2 + [pl.BlockSpec(memory_space=pl.ANY)] * 2,
        out_specs=pl.BlockSpec(shape, lambda: (0, 0)),
        out_shape=jax.ShapeDtypeStruct(shape, jnp.bfloat16),
        scratch_shapes=[
            pltpu.VMEM((fields, tiles, rows, LANES), jnp.float32),
            pltpu.SemaphoreType.DMA((2 * len(least),)),
            *held,
        ],
        compiler_params=pltpu.CompilerParams(vmem_limit_bytes=VMEM_BYTES),
        cost_estimate=pl.CostEstimate(
            flops=4 * slots * row_total * degrees * tiles * LANES,
            bytes_accessed=2 * slots * degrees * (row_total + tiles * LANES) + 2 * rows * shape[1],
            transcendentals=0,
        ),
        name="synthesis",
    )(first, owner_table, spec_rows, legendre)


def longitude_kernel(fields, grid_scale, zonal_scale, rows_ref, by_lon_ref, by_wave_ref, out_ref, sum_ref):
    step = pl.program_id(0)
    values = jnp.dot(by_lon_ref[...], rows_ref[...], preferred_element_type=jnp.float32) * grid_scale
    one = values.shape[1] // fields
    following = jnp.concatenate([values[:, one:], values[:, :one]], axis=1)
    product = (values * following).astype(jnp.bfloat16)
    share = jnp.dot(by_wave_ref[...], product, preferred_element_type=jnp.float32)

    @pl.when(step == 0)
    def _():
        sum_ref[...] = share

    @pl.when(step > 0)
    def _():
        sum_ref[...] += share

    @pl.when(step == pl.num_programs(0) - 1)
    def _():
        out_ref[...] = (sum_ref[...] * zonal_scale).astype(out_ref.dtype)


def longitudes(rows, by_lon, by_wave, fields):
    depth, width = rows.shape
    lon_count = by_lon.shape[0]
    lon_block = lon_count // 5
    return pl.pallas_call(
        functools.partial(longitude_kernel, fields, 1.0 / math.sqrt(depth // 2), 2.0 / math.sqrt(lon_count)),
        grid=(lon_count // lon_block,),
        in_specs=[
            pl.BlockSpec((depth, width), lambda i: (0, 0)),
            pl.BlockSpec((lon_block, depth), lambda i: (i, 0)),
            pl.BlockSpec((depth, lon_block), lambda i: (0, i)),
        ],
        out_specs=pl.BlockSpec((depth, width), lambda i: (0, 0)),
        out_shape=jax.ShapeDtypeStruct((depth, width), jnp.bfloat16),
        scratch_shapes=[pltpu.VMEM((depth, width), jnp.float32)],
        compiler_params=pltpu.CompilerParams(vmem_limit_bytes=VMEM_BYTES),
        cost_estimate=pl.CostEstimate(
            flops=4 * depth * width * lon_count,
            bytes_accessed=4 * depth * (width + lon_count),
            transcendentals=0,
        ),
        name="longitudes",
    )(rows, by_lon, by_wave)


def fold_kernel(slots, levels, fields, arrived_ref, out_ref, rows_ref):
    tiles = rows_ref.shape[1]
    stride = 2 * slots
    half = levels * stride
    for field in range(fields):
        for tile in range(tiles):
            lanes = pl.ds((field * tiles + tile) * LANES, LANES)
            rows_ref[field, tile] = arrived_ref[:, lanes].astype(jnp.float32)
    for slot in range(slots):
        for part in range(2):
            for field in range(fields):
                for tile in range(tiles):
                    first = 2 * slot + part
                    north = rows_ref[field, tile, pl.ds(first, levels, stride=stride), :]
                    south = rows_ref[field, tile, pl.ds(half + first, levels, stride=stride), :]
                    lanes = pl.ds(tile * LANES, LANES)
                    at = (part * fields + field) * levels
                    out_ref[slot, at : at + levels, lanes] = (north + south).astype(out_ref.dtype)
                    at += 2 * fields * levels
                    out_ref[slot, at : at + levels, lanes] = (north - south).astype(out_ref.dtype)


def fold(arrived, slots, levels, fields):
    row_total = 2 * fields * levels
    rows, width = arrived.shape
    tiles = width // (fields * LANES)
    shape = (slots, 2 * row_total, tiles * LANES)
    return pl.pallas_call(
        functools.partial(fold_kernel, slots, levels, fields),
        in_specs=[pl.BlockSpec((rows, width), lambda: (0, 0))],
        out_specs=pl.BlockSpec(shape, lambda: (0, 0, 0)),
        out_shape=jax.ShapeDtypeStruct(shape, jnp.bfloat16),
        scratch_shapes=[pltpu.VMEM((fields, tiles, rows, LANES), jnp.float32)],
        compiler_params=pltpu.CompilerParams(vmem_limit_bytes=VMEM_BYTES),
        cost_estimate=pl.CostEstimate(flops=2 * rows * width, bytes_accessed=4 * rows * width, transcendentals=0),
        name="fold",
    )(arrived)


def analysis_kernel(least, folded_ref, even_ref, odd_ref, *refs):
    table_refs, out_ref = refs[:-1], refs[-1]
    row_total, degrees = out_ref.shape[1:]
    step = pl.program_id(0)

    def run(group):
        start = least[group]
        for j in range(out_ref.shape[0]):
            table = jnp.concatenate([ref[j, start:, :] for ref in table_refs], axis=1)
            sums = lax.dot_general(
                folded_ref[j], table, (((1,), (1,)), ((), ())), preferred_element_type=jnp.float32
            )
            kept = sums[:row_total] * even_ref[j, :, start:] + sums[row_total:] * odd_ref[j, :, start:]
            out_ref[j, :, start:] = kept
            if start:
                out_ref[j, :, :start] = jnp.zeros((row_total, start), out_ref.dtype)

    for group in range(len(least)):
        pl.when(step == group)(functools.partial(run, group))


def analyze(folded, even, odd, legendre, row_total, least, chunk):
    slots, degrees, _ = legendre.shape
    block = slots // len(least)
    at, tiles = chunk
    mask_spec = pl.BlockSpec((block, 1, degrees), lambda i: (i, 0, 0))
    return pl.pallas_call(
        functools.partial(analysis_kernel, least),
        grid=(len(least),),
        in_specs=[pl.BlockSpec((block,) + folded.shape[1:], lambda i: (i, 0, 0)), mask_spec, mask_spec]
        + [pl.BlockSpec((block, degrees, LANES), lambda i, t=at + t: (i, 0, t)) for t in range(tiles)],
        out_specs=pl.BlockSpec((block, row_total, degrees), lambda i: (i, 0, 0)),
        out_shape=jax.ShapeDtypeStruct((slots, row_total, degrees), jnp.float32),
        compiler_params=pltpu.CompilerParams(vmem_limit_bytes=VMEM_BYTES),
        cost_estimate=pl.CostEstimate(
            flops=4 * slots * row_total * degrees * tiles * LANES,
            bytes_accessed=2 * slots * (degrees * tiles * LANES + 2 * row_total * (tiles * LANES + degrees)),
            transcendentals=0,
        ),
        name="analysis",
    )(folded, even, odd, *[legendre] * tiles)


def closing_kernel(
    levels, fields, least, chunk, arrived_ref, table_ref, base_ref, even_ref, odd_ref, out_ref, *refs
):
    got_ref, north_ref, south_ref, sems = refs[:4]
    held = refs[4:]
    at, tiles = chunk
    groups = len(least)
    slots, row_total, degrees = base_ref.shape
    block = slots // groups
    stride = 2 * slots
    half = levels * stride
    arriving = [
        pltpu.make_async_copy(
            arrived_ref.at[:, pl.ds(field * tiles * LANES, tiles * LANES)], got_ref.at[field], sems.at[3 * groups + field]
        )
        for field in range(fields)
    ]
    tables, sums, results = [], [], []
    for group, start in enumerate(least):
        mine = pl.ds(group * block, block)
        left = pl.ds(start, degrees - start)
        lanes = pl.ds(at * LANES, tiles * LANES)
        held_table, held_sums = held[2 * group], held[2 * group + 1]
        tables.append(pltpu.make_async_copy(table_ref.at[mine, left, lanes], held_table, sems.at[3 * group]))
        sums.append(pltpu.make_async_copy(base_ref.at[mine, :, left], held_sums, sems.at[3 * group + 1]))
        results.append(pltpu.make_async_copy(held_sums, out_ref.at[mine, :, left], sems.at[3 * group + 2]))
    for copy in arriving:
        copy.start()
    for group in range(groups):
        tables[group].start()
        sums[group].start()
    for field in range(fields):
        arriving[field].wait()
        for tile in range(tiles):
            lanes = pl.ds(tile * LANES, LANES)
            north = got_ref[field, :half, lanes].astype(jnp.float32)
            south = got_ref[field, half:, lanes].astype(jnp.float32)
            north_ref[field, tile] = north + south
            south_ref[field, tile] = north - south
    for group, start in enumerate(least):
        tables[group].wait()
        sums[group].wait()
        held_table, held_sums = held[2 * group], held[2 * group + 1]
        for j in range(block):
            slot = group * block + j
            folded = jnp.concatenate(
                [
                    jnp.concatenate(
                        [
                            ref[field, tile, pl.ds(2 * slot + part, levels, stride=stride), :].astype(jnp.bfloat16)
                            for ref in (north_ref, south_ref)
                            for part in range(2)
                            for field in range(fields)
                        ],
                        axis=0,
                    )
                    for tile in range(tiles)
                ],
                axis=1,
            )
            more = lax.dot_general(
                folded, held_table[j], (((1,), (1,)), ((), ())), preferred_element_type=jnp.float32
            )
            even, odd = even_ref[slot, :, start:], odd_ref[slot, :, start:]
            held_sums[j] = held_sums[j] + more[:row_total] * even + more[row_total:] * odd
        results[group].start()
    for copy in results:
        copy.wait()


def close(arrived, base, even, odd, legendre, fields, levels, least, chunk):
    slots, row_total, degrees = base.shape
    block = slots // len(least)
    rows, width = arrived.shape
    tiles = chunk[1]
    half = pltpu.VMEM((fields, tiles, rows // 2, LANES), jnp.float32)
    held = []
    for start in least:
        held.append(pltpu.VMEM((block, degrees - start, tiles * LANES), jnp.bfloat16))
        held.append(pltpu.VMEM((block, row_total, degrees - start), jnp.float32))
    anywhere = pl.BlockSpec(memory_space=pl.ANY)
    return pl.pallas_call(
        functools.partial(closing_kernel, levels, fields, least, chunk),
        in_specs=[anywhere, anywhere, anywhere] + [pl.BlockSpec(even.shape, lambda: (0, 0, 0))] * 2,
        out_specs=anywhere,
        out_shape=jax.ShapeDtypeStruct(base.shape, jnp.float32),
        input_output_aliases={2: 0},
        scratch_shapes=[
            pltpu.VMEM((fields, rows, tiles * LANES), jnp.bfloat16),
            half,
            half,
            pltpu.SemaphoreType.DMA((3 * len(least) + fields,)),
            *held,
        ],
        compiler_params=pltpu.CompilerParams(vmem_limit_bytes=VMEM_BYTES),
        cost_estimate=pl.CostEstimate(
            flops=4 * slots * row_total * degrees * tiles * LANES,
            bytes_accessed=8 * slots * row_total * degrees + 2 * rows * width,
            transcendentals=0,
        ),
        name="closing",
    )(arrived, legendre, base, even, odd)


def after(value, *others):
    return lax.optimization_barrier((value, others))[0]


def trig_kernel(cos_base_ref, sin_base_ref, cos_turn_ref, sin_turn_ref, cos_base_t, sin_base_t, cos_turn_t, sin_turn_t, by_wave_ref, by_lon_ref):
    for j in range(cos_base_ref.shape[1]):
        lanes = pl.ds(j * LANES, LANES)
        cos_base, sin_base = cos_base_ref[:, j : j + 1], sin_base_ref[:, j : j + 1]
        angles = cos_base * cos_turn_ref[...] - sin_base * sin_turn_ref[...]
        by_wave_ref[:, lanes] = angles.astype(by_wave_ref.dtype)
        cos_base, sin_base = cos_base_t[j : j + 1, :], sin_base_t[j : j + 1, :]
        angles = cos_base * cos_turn_t[...] - sin_base * sin_turn_t[...]
        by_lon_ref[lanes, :] = angles.astype(by_lon_ref.dtype)


def trig_tables(owner_table, lon_count, *others):
    waves = jnp.repeat(owner_table, 2).astype(jnp.float32)[:, None]
    quarter = jnp.tile(jnp.array([0, lon_count // 4], jnp.float32), owner_table.shape[0])[:, None]
    unit = 2.0 * math.pi / lon_count

    def angles(lon, turn):
        phase = waves * lon + turn
        return (phase - lon_count * jnp.floor(phase * (1.0 / lon_count))) * unit

    base = angles(jnp.arange(0, lon_count, LANES, dtype=jnp.float32)[None, :], quarter)
    turn = angles(jnp.arange(LANES, dtype=jnp.float32)[None, :], 0.0)
    depth = waves.shape[0]
    blocks = lon_count // LANES
    rows = 256
    small = pl.BlockSpec((rows, blocks), lambda i: (i, 0))
    wide = pl.BlockSpec((rows, LANES), lambda i: (i, 0))
    small_t = pl.BlockSpec((blocks, rows), lambda i: (0, i))
    wide_t = pl.BlockSpec((LANES, rows), lambda i: (0, i))
    parts = (jnp.cos(base), jnp.sin(base), jnp.cos(turn), jnp.sin(turn))
    parts = after(parts, *others)
    return pl.pallas_call(
        trig_kernel,
        grid=(depth // rows,),
        in_specs=[small, small, wide, wide, small_t, small_t, wide_t, wide_t],
        out_specs=[
            pl.BlockSpec((rows, lon_count), lambda i: (i, 0)),
            pl.BlockSpec((lon_count, rows), lambda i: (0, i)),
        ],
        out_shape=[
            jax.ShapeDtypeStruct((depth, lon_count), jnp.bfloat16),
            jax.ShapeDtypeStruct((lon_count, depth), jnp.bfloat16),
        ],
        compiler_params=pltpu.CompilerParams(vmem_limit_bytes=VMEM_BYTES),
        cost_estimate=pl.CostEstimate(
            flops=8 * depth * lon_count, bytes_accessed=4 * depth * lon_count, transcendentals=0
        ),
        name="trig",
    )(*parts, *[x.T for x in parts])


def exchange(rows):
    return lax.all_to_all(rows, AXES, split_axis=0, concat_axis=0, tiled=True)


def by_hemisphere_and_level(spectral, legendre, owner_table):
    slots, _, fields, levels, degrees = spectral.shape
    half_lat = legendre.shape[2]
    lon_count = 4 * half_lat
    row_total = 2 * fields * levels
    tiles = half_lat // LANES
    first = lax.axis_index(AXES).astype(jnp.int32) * slots
    spec_rows = spectral.reshape(slots, row_total, degrees)
    least = tuple(8 * g * levels for g in range(slots // 4))
    cut = tiles - tiles // 2
    chunks = [(0, cut), (cut, tiles - cut)]

    def send(spec, chunk):
        return synthesize(first.reshape(1), owner_table, spec, legendre, chunk, fields, levels, least)

    large = send(spec_rows, chunks[0])
    small = send(after(spec_rows, large), chunks[1])
    arrived = [exchange(large)]
    arrived.append(exchange(after(small, *arrived)))
    by_wave, by_lon = trig_tables(after(owner_table, large), lon_count, small)
    zonal = [longitudes(rows, by_lon, by_wave, fields) for rows in arrived]
    returned = [exchange(zonal[0])]
    returned.append(exchange(after(zonal[1], *returned)))
    wavenumber = lax.dynamic_slice_in_dim(after(owner_table, by_wave), first, slots)
    distance = jnp.arange(degrees, dtype=jnp.int32)[None, :] - wavenumber[:, None]
    scale = 1.0 / math.sqrt(2 * half_lat)
    even = jnp.where((distance >= 0) & (distance % 2 == 0), scale, 0.0).astype(jnp.float32)[:, None, :]
    odd = jnp.where((distance >= 0) & (distance % 2 != 0), scale, 0.0).astype(jnp.float32)[:, None, :]
    base = analyze(fold(returned[0], slots, levels, fields), even, odd, legendre, row_total, least, chunks[0])
    last = after(returned[1], base)
    out = close(last, base, even, odd, legendre, fields, levels, least, chunks[1])
    return out.reshape(slots, 2, fields, levels, degrees)


def make_trig(wavenumber, lon_count):
    lon_index = jnp.arange(lon_count, dtype=jnp.int32)
    phases = wavenumber[:, None] * lon_index[None, :] % lon_count
    angles = phases.astype(jnp.float32) * (2.0 * math.pi / lon_count)
    return jnp.stack([jnp.cos(angles), -jnp.sin(angles)], axis=1).astype(jnp.bfloat16)


def by_level_and_latitude(spectral, legendre, owner_table):
    slot_count, _, fields, levels, degrees = spectral.shape
    half_lat = legendre.shape[2]
    lat_count = 2 * half_lat
    lon_count = 2 * lat_count
    wave_count = owner_table.shape[0]
    band_count = lax.axis_size("band")
    group_count = lax.axis_size("grp")
    device_count = band_count * group_count
    level_block = levels // band_count
    lat_block = lat_count // group_count
    row_total = 2 * fields * levels
    row_width = fields * level_block * lat_block
    slot_start = lax.axis_index(("band", "grp")) * slot_count
    wavenumber = lax.dynamic_slice_in_dim(owner_table, slot_start, slot_count)
    degree_index = jnp.arange(degrees, dtype=jnp.int32)
    keep_mask = (degree_index[None, :] >= wavenumber[:, None]).astype(jnp.bfloat16)
    odd_part = (degree_index[None, :] - wavenumber[:, None]) % 2
    flip_sign = (1 - 2 * odd_part).astype(jnp.bfloat16)
    spec_rows = spectral.reshape(slot_count, row_total, degrees) * keep_mask[:, None, :]
    both_rows = jnp.concatenate([spec_rows, spec_rows * flip_sign[:, None, :]], axis=1)
    halves = jnp.einsum("srn,snt->srt", both_rows, legendre, preferred_element_type=jnp.float32)
    northern = halves[:, :row_total]
    mirrored = halves[:, row_total:]
    fourier = jnp.concatenate([northern, jnp.flip(mirrored, axis=2)], axis=2)
    fourier = fourier.reshape(
        slot_count, 2, fields, band_count, level_block, group_count, lat_block
    )
    fourier = jnp.transpose(fourier, (0, 1, 2, 3, 5, 4, 6))
    fourier_low = (fourier * (1.0 / math.sqrt(degrees))).astype(jnp.bfloat16)
    packed = fourier_low.reshape(1, slot_count, 2, fields, device_count, level_block, lat_block)
    arrived = lax.all_to_all(packed, ("band", "grp"), split_axis=4, concat_axis=0, tiled=True)
    arrived = arrived.reshape(-1, 2, row_width)
    trig_rows = make_trig(owner_table, lon_count)
    grid_values = jnp.einsum("scw,scl->wl", arrived, trig_rows, preferred_element_type=jnp.float32)
    grid_values = (grid_values * (1.0 / math.sqrt(wave_count))).reshape(
        fields, level_block * lat_block, lon_count
    )
    product = (grid_values * jnp.roll(grid_values, -1, axis=0)).astype(jnp.bfloat16)
    zonal_coeffs = jnp.einsum(
        "wl,scl->scw",
        product.reshape(row_width, lon_count),
        trig_rows,
        preferred_element_type=jnp.float32,
    )
    zonal_coeffs = (zonal_coeffs * (2.0 / math.sqrt(lon_count))).astype(jnp.bfloat16)
    sendback = zonal_coeffs.reshape(device_count, slot_count, 2, fields, 1, level_block, lat_block)
    returned = lax.all_to_all(sendback, ("band", "grp"), split_axis=0, concat_axis=4, tiled=True)
    returned = returned.reshape(
        slot_count, 2, fields, band_count, group_count, level_block, lat_block
    )
    returned = jnp.transpose(returned, (0, 1, 2, 3, 5, 4, 6)).reshape(slot_count, row_total, lat_count)
    northern_part = returned[:, :, :half_lat].astype(jnp.float32)
    mirror_part = jnp.flip(returned[:, :, half_lat:], axis=2).astype(jnp.float32)
    plus_part = (northern_part + mirror_part).astype(jnp.bfloat16)
    minus_part = (northern_part - mirror_part).astype(jnp.bfloat16)
    stacked = jnp.concatenate([plus_part, minus_part], axis=1)
    projected = jnp.einsum("srt,snt->srn", stacked, legendre, preferred_element_type=jnp.float32)
    even_rows = flip_sign[:, None, :] > 0
    chosen = jnp.where(even_rows, projected[:, :row_total], projected[:, row_total:])
    chosen = chosen * keep_mask.astype(jnp.float32)[:, None, :] * (1.0 / math.sqrt(lat_count))
    return chosen.reshape(slot_count, 2, fields, levels, degrees)


def on_device(spectral, legendre, owner_table):
    slots, _, _, levels, _ = spectral.shape
    whole_hemispheres = lax.axis_size("band") * lax.axis_size("grp") == 2 * levels
    if whole_hemispheres and legendre.shape[2] % LANES == 0 and legendre.shape[2] > LANES and slots % 4 == 0 and levels % 16 == 0:
        return by_hemisphere_and_level(spectral, legendre, owner_table)
    return by_level_and_latitude(spectral, legendre, owner_table)


def solution(mesh):
    placed = (P(("band", "grp"), None, None, None, None), P(("band", "grp"), None, None), P())
    return jax.shard_map(
        on_device,
        mesh=mesh,
        in_specs=placed,
        out_specs=P(("band", "grp"), None, None, None, None),
        check_vma=False,
    )
```

```python
import functools
import math

import jax
import jax.numpy as jnp
from jax import lax
from jax.experimental import pallas as pl
from jax.experimental.pallas import tpu as pltpu
from jax.sharding import PartitionSpec as P

LANES = 128
AXES = ("band", "grp")
VMEM_BYTES = 62 * 1024 * 1024


def synthesis_kernel(
    slots, levels, fields, least, chunk, scale, first_ref, owner_ref, spec_ref, table_ref, out_ref, rows_ref, sems, *held
):
    at, tiles = chunk
    groups = len(least)
    block = 4
    row_total, degrees = spec_ref.shape[1:]
    stride = 2 * slots
    copies = []
    for group, start in enumerate(least):
        mine = pl.ds(group * block, block)
        left = pl.ds(start, degrees - start)
        lanes = pl.ds(at * LANES, tiles * LANES)
        copies.append(
            (
                pltpu.make_async_copy(spec_ref.at[mine, :, left], held[2 * group], sems.at[2 * group]),
                pltpu.make_async_copy(table_ref.at[mine, left, lanes], held[2 * group + 1], sems.at[2 * group + 1]),
            )
        )
    order = range(groups - 1, -1, -1)
    for group in order:
        for copy in copies[group]:
            copy.start()
    for group in order:
        for copy in copies[group]:
            copy.wait()
        for j in range(block):
            spec = held[2 * group][j]
            wave = owner_ref[first_ref[0] + group * block + j]
            distance = lax.broadcasted_iota(jnp.int32, (1, spec.shape[1]), 1) + (least[group] - wave)
            keep = jnp.where(distance >= 0, 1.0, 0.0)
            flip = jnp.where(distance % 2 == 0, keep, -keep)
            both = jnp.concatenate([spec * keep.astype(spec.dtype), spec * flip.astype(spec.dtype)], axis=0)
            halves = jnp.dot(both, held[2 * group + 1][j], preferred_element_type=jnp.float32) * scale
            first = 2 * (group * block + j)
            for hemi in range(2):
                for part in range(2):
                    for field in range(fields):
                        row = hemi * row_total + (part * fields + field) * levels
                        target = pl.ds(hemi * levels * stride + first + part, levels, stride=stride)
                        for tile in range(tiles):
                            lanes = slice(tile * LANES, (tile + 1) * LANES)
                            rows_ref[field, tile, target, :] = halves[row : row + levels, lanes]
    for field in range(fields):
        for tile in range(tiles):
            lanes = pl.ds((field * tiles + tile) * LANES, LANES)
            out_ref[:, lanes] = rows_ref[field, tile].astype(out_ref.dtype)


def synthesize(first, owner_table, spec_rows, legendre, chunk, fields, levels, least):
    _, row_total, degrees = spec_rows.shape
    block = 4
    slots = block * len(least)
    rows = 2 * levels * 2 * slots
    tiles = chunk[1]
    shape = (rows, fields * tiles * LANES)
    held = []
    for start in least:
        held.append(pltpu.VMEM((block, row_total, degrees - start), jnp.bfloat16))
        held.append(pltpu.VMEM((block, degrees - start, tiles * LANES), jnp.bfloat16))
    return pl.pallas_call(
        functools.partial(synthesis_kernel, slots, levels, fields, least, chunk, 1.0 / math.sqrt(degrees)),
        in_specs=[pl.BlockSpec(memory_space=pltpu.SMEM)] * 2 + [pl.BlockSpec(memory_space=pl.ANY)] * 2,
        out_specs=pl.BlockSpec(shape, lambda: (0, 0)),
        out_shape=jax.ShapeDtypeStruct(shape, jnp.bfloat16),
        scratch_shapes=[
            pltpu.VMEM((fields, tiles, rows, LANES), jnp.float32),
            pltpu.SemaphoreType.DMA((2 * len(least),)),
            *held,
        ],
        compiler_params=pltpu.CompilerParams(vmem_limit_bytes=VMEM_BYTES),
        cost_estimate=pl.CostEstimate(
            flops=4 * slots * row_total * degrees * tiles * LANES,
            bytes_accessed=2 * slots * degrees * (row_total + tiles * LANES) + 2 * rows * shape[1],
            transcendentals=0,
        ),
        name="synthesis",
    )(first, owner_table, spec_rows, legendre)


def longitude_kernel(
    fields, grid_scale, zonal_scale, rows_ref, far_ref, by_lon_ref, by_wave_ref, out_ref, far_out_ref, sum_ref
):
    step = pl.program_id(0)
    near = rows_ref.shape[0]
    values = jnp.dot(by_lon_ref[:, :near], rows_ref[...], preferred_element_type=jnp.float32)
    values = values + jnp.dot(by_lon_ref[:, near:], far_ref[...], preferred_element_type=jnp.float32)
    values = values * grid_scale
    one = values.shape[1] // fields
    following = jnp.concatenate([values[:, one:], values[:, :one]], axis=1)
    product = (values * following).astype(jnp.bfloat16)
    share = jnp.dot(by_wave_ref[...], product, preferred_element_type=jnp.float32)

    @pl.when(step == 0)
    def _():
        sum_ref[...] = share

    @pl.when(step > 0)
    def _():
        sum_ref[...] += share

    @pl.when(step == pl.num_programs(0) - 1)
    def _():
        out_ref[...] = (sum_ref[:near, :] * zonal_scale).astype(out_ref.dtype)
        far_out_ref[...] = (sum_ref[near:, :] * zonal_scale).astype(far_out_ref.dtype)


def longitudes(rows, far, by_lon, by_wave, fields):
    depth, width = rows.shape[0] + far.shape[0], rows.shape[1]
    lon_count = by_lon.shape[0]
    lon_block = lon_count // 5
    near_spec = pl.BlockSpec(rows.shape, lambda i: (0, 0))
    far_spec = pl.BlockSpec(far.shape, lambda i: (0, 0))
    return pl.pallas_call(
        functools.partial(longitude_kernel, fields, 1.0 / math.sqrt(depth // 2), 2.0 / math.sqrt(lon_count)),
        grid=(lon_count // lon_block,),
        in_specs=[
            near_spec,
            far_spec,
            pl.BlockSpec((lon_block, depth), lambda i: (i, 0)),
            pl.BlockSpec((depth, lon_block), lambda i: (0, i)),
        ],
        out_specs=[near_spec, far_spec],
        out_shape=[jax.ShapeDtypeStruct(x.shape, jnp.bfloat16) for x in (rows, far)],
        scratch_shapes=[pltpu.VMEM((depth, width), jnp.float32)],
        compiler_params=pltpu.CompilerParams(vmem_limit_bytes=VMEM_BYTES),
        cost_estimate=pl.CostEstimate(
            flops=4 * depth * width * lon_count,
            bytes_accessed=4 * depth * (width + lon_count),
            transcendentals=0,
        ),
        name="longitudes",
    )(rows, far, by_lon, by_wave)


def far_synthesis_kernel(fields, chunks, scale, hemi_ref, waves_ref, spec_ref, table_ref, *refs):
    out_refs, rows_ref = refs[:-1], refs[-1]
    step = pl.program_id(0)
    owners = spec_ref.shape[0]
    degrees = spec_ref.shape[-1]
    degree = lax.broadcasted_iota(jnp.int32, (1, degrees), 1)
    half = degrees // 2
    rows = 2 * fields

    def signed(owner, slot):
        spec = spec_ref[owner, min(slot, 2)]
        wave = waves_ref[4 * (step * owners + owner) + slot]
        if slot < 2:
            distance, inside = degree - wave, degree >= 0
        else:
            shift = half if slot == 2 else 0
            distance = degree + shift - wave
            inside = degree < half if slot == 2 else degree >= half
        keep = jnp.where(inside & (distance >= 0), 1.0, 0.0)
        turned = jnp.where(distance % 2 == 0, keep, -keep)
        return spec * jnp.where(hemi_ref[0] == 0, keep, turned).astype(spec.dtype)

    for owner in range(owners):
        for pick in ((0,), (1,), (2, 3)):
            block = min(pick[0], 2)
            both = jnp.concatenate([signed(owner, slot) for slot in pick], axis=0)
            table = table_ref[owner, pl.ds(block * degrees, degrees), :]
            sums = jnp.dot(both, table, preferred_element_type=jnp.float32) * scale
            for at, slot in enumerate(pick):
                target = pl.ds(2 * (4 * owner + slot), 2)
                for field in range(fields):
                    rows_ref[field, target, :] = sums[at * rows + 2 * field : at * rows + 2 * field + 2]
    for (first, tiles), out_ref in zip(chunks, out_refs):
        width = tiles * LANES
        for field in range(fields):
            taken = rows_ref[field, :, pl.ds(first * LANES, width)]
            out_ref[:, pl.ds(field * width, width)] = taken.astype(out_ref.dtype)


def far_synthesize(hemi, waves, spec, table, fields, chunks, scale):
    devices, _, rows, degrees = spec.shape
    lat_count = table.shape[-1]
    block = 4
    height = 8 * block
    shapes = [(8 * devices, fields * tiles * LANES) for _, tiles in chunks]
    return pl.pallas_call(
        functools.partial(far_synthesis_kernel, fields, chunks, scale),
        grid=(devices // block,),
        in_specs=[pl.BlockSpec(memory_space=pltpu.SMEM)] * 2
        + [
            pl.BlockSpec((block, 3, rows, degrees), lambda i: (i, 0, 0, 0)),
            pl.BlockSpec((block, 3 * degrees, lat_count), lambda i: (i, 0, 0)),
        ],
        out_specs=[pl.BlockSpec((height, shape[1]), lambda i: (i, 0)) for shape in shapes],
        out_shape=[jax.ShapeDtypeStruct(shape, jnp.bfloat16) for shape in shapes],
        scratch_shapes=[pltpu.VMEM((fields, height, lat_count), jnp.float32)],
        compiler_params=pltpu.CompilerParams(vmem_limit_bytes=VMEM_BYTES),
        cost_estimate=pl.CostEstimate(
            flops=8 * devices * rows * degrees * lat_count,
            bytes_accessed=6 * devices * degrees * lat_count + 16 * devices * fields * lat_count,
            transcendentals=0,
        ),
        name="far_synthesis",
    )(hemi, waves, spec, table)


def far_analysis_kernel(fields, chunks, table_ref, *refs):
    zonal_refs, out_ref, rows_ref = refs[:-2], refs[-2], refs[-1]
    owners = table_ref.shape[0]
    degrees = out_ref.shape[-1]
    rows = 2 * fields
    for (first, tiles), zonal_ref in zip(chunks, zonal_refs):
        width = tiles * LANES
        for field in range(fields):
            lanes = pl.ds(first * LANES, width)
            rows_ref[field, :, lanes] = zonal_ref[:, pl.ds(field * width, width)].astype(jnp.float32)
    lower = lax.broadcasted_iota(jnp.int32, (1, degrees), 1) < degrees // 2
    for owner in range(owners):
        for pick in ((0,), (1,), (2, 3)):
            block = min(pick[0], 2)
            zonal = jnp.concatenate(
                [
                    rows_ref[field, pl.ds(2 * (4 * owner + slot), 2), :]
                    for slot in pick
                    for field in range(fields)
                ],
                axis=0,
            ).astype(jnp.bfloat16)
            table = table_ref[owner, pl.ds(block * degrees, degrees), :]
            sums = lax.dot_general(zonal, table, (((1,), (1,)), ((), ())), preferred_element_type=jnp.float32)
            if len(pick) == 2:
                sums = jnp.where(lower, sums[:rows], sums[rows:])
            out_ref[owner, pl.ds(block * rows, rows), :] = sums


def far_analyze(zonal, table, fields, chunks):
    devices, depth, lat_count = table.shape
    degrees = depth // 3
    block = 4
    height = 8 * block
    rows = 2 * fields
    return pl.pallas_call(
        functools.partial(far_analysis_kernel, fields, chunks),
        grid=(devices // block,),
        in_specs=[pl.BlockSpec((block, depth, lat_count), lambda i: (i, 0, 0))]
        + [pl.BlockSpec((height, x.shape[1]), lambda i: (i, 0)) for x in zonal],
        out_specs=pl.BlockSpec((block, 3 * rows, degrees), lambda i: (i, 0, 0)),
        out_shape=jax.ShapeDtypeStruct((devices, 3 * rows, degrees), jnp.float32),
        scratch_shapes=[pltpu.VMEM((fields, height, lat_count), jnp.float32)],
        compiler_params=pltpu.CompilerParams(vmem_limit_bytes=VMEM_BYTES),
        cost_estimate=pl.CostEstimate(
            flops=8 * devices * rows * degrees * lat_count,
            bytes_accessed=2 * devices * depth * lat_count + 16 * devices * fields * lat_count,
            transcendentals=0,
        ),
        name="far_analysis",
    )(table, *zonal)


def fold_kernel(slots, levels, fields, arrived_ref, out_ref, rows_ref):
    tiles = rows_ref.shape[1]
    stride = 2 * slots
    half = levels * stride
    for field in range(fields):
        for tile in range(tiles):
            lanes = pl.ds((field * tiles + tile) * LANES, LANES)
            rows_ref[field, tile] = arrived_ref[:, lanes].astype(jnp.float32)
    for slot in range(slots):
        for part in range(2):
            for field in range(fields):
                for tile in range(tiles):
                    first = 2 * slot + part
                    north = rows_ref[field, tile, pl.ds(first, levels, stride=stride), :]
                    south = rows_ref[field, tile, pl.ds(half + first, levels, stride=stride), :]
                    lanes = pl.ds(tile * LANES, LANES)
                    at = (part * fields + field) * levels
                    out_ref[slot, at : at + levels, lanes] = (north + south).astype(out_ref.dtype)
                    at += 2 * fields * levels
                    out_ref[slot, at : at + levels, lanes] = (north - south).astype(out_ref.dtype)


def fold(arrived, slots, levels, fields):
    row_total = 2 * fields * levels
    rows, width = arrived.shape
    tiles = width // (fields * LANES)
    shape = (slots, 2 * row_total, tiles * LANES)
    return pl.pallas_call(
        functools.partial(fold_kernel, slots, levels, fields),
        in_specs=[pl.BlockSpec((rows, width), lambda: (0, 0))],
        out_specs=pl.BlockSpec(shape, lambda: (0, 0, 0)),
        out_shape=jax.ShapeDtypeStruct(shape, jnp.bfloat16),
        scratch_shapes=[pltpu.VMEM((fields, tiles, rows, LANES), jnp.float32)],
        compiler_params=pltpu.CompilerParams(vmem_limit_bytes=VMEM_BYTES),
        cost_estimate=pl.CostEstimate(flops=2 * rows * width, bytes_accessed=4 * rows * width, transcendentals=0),
        name="fold",
    )(arrived)


def analysis_kernel(least, folded_ref, far_ref, even_ref, odd_ref, *refs):
    table_refs, out_ref = refs[:-1], refs[-1]
    row_total, degrees = out_ref.shape[1:]
    step = pl.program_id(0)

    def run(group):
        start = least[group]
        for j in range(out_ref.shape[0]):
            table = jnp.concatenate([ref[j, start:, :] for ref in table_refs], axis=1)
            sums = lax.dot_general(
                folded_ref[j], table, (((1,), (1,)), ((), ())), preferred_element_type=jnp.float32
            )
            kept = sums[:row_total] * even_ref[j, :, start:] + sums[row_total:] * odd_ref[j, :, start:]
            out_ref[j, :, start:] = kept
            if start:
                out_ref[j, :, :start] = jnp.zeros((row_total, start), out_ref.dtype)

    for group in range(len(least)):
        pl.when(step == group)(functools.partial(run, group))

    @pl.when(step == len(least))
    def _():
        width = far_ref.shape[2]
        out_ref[:, :, : degrees - width] = jnp.zeros((out_ref.shape[0], row_total, degrees - width), out_ref.dtype)
        out_ref[:, :, degrees - width :] = far_ref[...]


def analyze(folded, far, even, odd, legendre, row_total, least, chunk):
    slots, degrees, _ = legendre.shape
    block = 4
    near = len(least) - 1
    at, tiles = chunk
    mask_spec = pl.BlockSpec((block, 1, degrees), lambda i: (i, 0, 0))
    return pl.pallas_call(
        functools.partial(analysis_kernel, least),
        grid=(len(least) + 1,),
        in_specs=[
            pl.BlockSpec((block,) + folded.shape[1:], lambda i: (jnp.minimum(i, near), 0, 0)),
            pl.BlockSpec(far.shape, lambda i: (0, 0, 0)),
            mask_spec,
            mask_spec,
        ]
        + [
            pl.BlockSpec((block, degrees, LANES), lambda i, t=at + t: (jnp.minimum(i, near), 0, t))
            for t in range(tiles)
        ],
        out_specs=pl.BlockSpec((block, row_total, degrees), lambda i: (i, 0, 0)),
        out_shape=jax.ShapeDtypeStruct((slots, row_total, degrees), jnp.float32),
        compiler_params=pltpu.CompilerParams(vmem_limit_bytes=VMEM_BYTES),
        cost_estimate=pl.CostEstimate(
            flops=4 * slots * row_total * degrees * tiles * LANES,
            bytes_accessed=2 * slots * (degrees * tiles * LANES + 2 * row_total * (tiles * LANES + degrees)),
            transcendentals=0,
        ),
        name="analysis",
    )(folded, far, even, odd, *[legendre] * tiles)


def closing_kernel(
    levels, fields, least, chunk, arrived_ref, table_ref, base_ref, even_ref, odd_ref, out_ref, *refs
):
    got_ref, north_ref, south_ref, sems = refs[:4]
    held = refs[4:]
    at, tiles = chunk
    groups = len(least)
    _, row_total, degrees = base_ref.shape
    block = 4
    slots = block * groups
    stride = 2 * slots
    half = levels * stride
    arriving = [
        pltpu.make_async_copy(
            arrived_ref.at[:, pl.ds(field * tiles * LANES, tiles * LANES)], got_ref.at[field], sems.at[3 * groups + field]
        )
        for field in range(fields)
    ]
    tables, sums, results = [], [], []
    for group, start in enumerate(least):
        mine = pl.ds(group * block, block)
        left = pl.ds(start, degrees - start)
        lanes = pl.ds(at * LANES, tiles * LANES)
        held_table, held_sums = held[2 * group], held[2 * group + 1]
        tables.append(pltpu.make_async_copy(table_ref.at[mine, left, lanes], held_table, sems.at[3 * group]))
        sums.append(pltpu.make_async_copy(base_ref.at[mine, :, left], held_sums, sems.at[3 * group + 1]))
        results.append(pltpu.make_async_copy(held_sums, out_ref.at[mine, :, left], sems.at[3 * group + 2]))
    for copy in arriving:
        copy.start()
    for group in range(groups):
        tables[group].start()
        sums[group].start()
    for field in range(fields):
        arriving[field].wait()
        for tile in range(tiles):
            lanes = pl.ds(tile * LANES, LANES)
            north = got_ref[field, :half, lanes].astype(jnp.float32)
            south = got_ref[field, half:, lanes].astype(jnp.float32)
            north_ref[field, tile] = north + south
            south_ref[field, tile] = north - south
    for group, start in enumerate(least):
        tables[group].wait()
        sums[group].wait()
        held_table, held_sums = held[2 * group], held[2 * group + 1]
        for j in range(block):
            slot = group * block + j
            folded = jnp.concatenate(
                [
                    jnp.concatenate(
                        [
                            ref[field, tile, pl.ds(2 * slot + part, levels, stride=stride), :].astype(jnp.bfloat16)
                            for ref in (north_ref, south_ref)
                            for part in range(2)
                            for field in range(fields)
                        ],
                        axis=0,
                    )
                    for tile in range(tiles)
                ],
                axis=1,
            )
            more = lax.dot_general(
                folded, held_table[j], (((1,), (1,)), ((), ())), preferred_element_type=jnp.float32
            )
            even, odd = even_ref[slot, :, start:], odd_ref[slot, :, start:]
            held_sums[j] = held_sums[j] + more[:row_total] * even + more[row_total:] * odd
        results[group].start()
    for copy in results:
        copy.wait()


def close(arrived, base, even, odd, legendre, fields, levels, least, chunk):
    slots, row_total, degrees = base.shape
    block = 4
    rows, width = arrived.shape
    tiles = chunk[1]
    half = pltpu.VMEM((fields, tiles, rows // 2, LANES), jnp.float32)
    held = []
    for start in least:
        held.append(pltpu.VMEM((block, degrees - start, tiles * LANES), jnp.bfloat16))
        held.append(pltpu.VMEM((block, row_total, degrees - start), jnp.float32))
    anywhere = pl.BlockSpec(memory_space=pl.ANY)
    return pl.pallas_call(
        functools.partial(closing_kernel, levels, fields, least, chunk),
        in_specs=[anywhere, anywhere, anywhere] + [pl.BlockSpec(even.shape, lambda: (0, 0, 0))] * 2,
        out_specs=anywhere,
        out_shape=jax.ShapeDtypeStruct(base.shape, jnp.float32),
        input_output_aliases={2: 0},
        scratch_shapes=[
            pltpu.VMEM((fields, rows, tiles * LANES), jnp.bfloat16),
            half,
            half,
            pltpu.SemaphoreType.DMA((3 * len(least) + fields,)),
            *held,
        ],
        compiler_params=pltpu.CompilerParams(vmem_limit_bytes=VMEM_BYTES),
        cost_estimate=pl.CostEstimate(
            flops=4 * slots * row_total * degrees * tiles * LANES,
            bytes_accessed=8 * slots * row_total * degrees + 2 * rows * width,
            transcendentals=0,
        ),
        name="closing",
    )(arrived, legendre, base, even, odd)


def after(value, *others):
    return lax.optimization_barrier((value, others))[0]


def trig_kernel(cos_base_ref, sin_base_ref, cos_turn_ref, sin_turn_ref, cos_base_t, sin_base_t, cos_turn_t, sin_turn_t, by_wave_ref, by_lon_ref):
    for j in range(cos_base_ref.shape[1]):
        lanes = pl.ds(j * LANES, LANES)
        cos_base, sin_base = cos_base_ref[:, j : j + 1], sin_base_ref[:, j : j + 1]
        angles = cos_base * cos_turn_ref[...] - sin_base * sin_turn_ref[...]
        by_wave_ref[:, lanes] = angles.astype(by_wave_ref.dtype)
        cos_base, sin_base = cos_base_t[j : j + 1, :], sin_base_t[j : j + 1, :]
        angles = cos_base * cos_turn_t[...] - sin_base * sin_turn_t[...]
        by_lon_ref[lanes, :] = angles.astype(by_lon_ref.dtype)


def trig_tables(owner_table, lon_count, *others):
    waves = jnp.repeat(owner_table, 2).astype(jnp.float32)[:, None]
    quarter = jnp.tile(jnp.array([0, lon_count // 4], jnp.float32), owner_table.shape[0])[:, None]
    unit = 2.0 * math.pi / lon_count

    def angles(lon, turn):
        phase = waves * lon + turn
        return (phase - lon_count * jnp.floor(phase * (1.0 / lon_count))) * unit

    base = angles(jnp.arange(0, lon_count, LANES, dtype=jnp.float32)[None, :], quarter)
    turn = angles(jnp.arange(LANES, dtype=jnp.float32)[None, :], 0.0)
    depth = waves.shape[0]
    blocks = lon_count // LANES
    rows = 256
    small = pl.BlockSpec((rows, blocks), lambda i: (i, 0))
    wide = pl.BlockSpec((rows, LANES), lambda i: (i, 0))
    small_t = pl.BlockSpec((blocks, rows), lambda i: (0, i))
    wide_t = pl.BlockSpec((LANES, rows), lambda i: (0, i))
    parts = (jnp.cos(base), jnp.sin(base), jnp.cos(turn), jnp.sin(turn))
    parts = after(parts, *others)
    return pl.pallas_call(
        trig_kernel,
        grid=(depth // rows,),
        in_specs=[small, small, wide, wide, small_t, small_t, wide_t, wide_t],
        out_specs=[
            pl.BlockSpec((rows, lon_count), lambda i: (i, 0)),
            pl.BlockSpec((lon_count, rows), lambda i: (0, i)),
        ],
        out_shape=[
            jax.ShapeDtypeStruct((depth, lon_count), jnp.bfloat16),
            jax.ShapeDtypeStruct((lon_count, depth), jnp.bfloat16),
        ],
        compiler_params=pltpu.CompilerParams(vmem_limit_bytes=VMEM_BYTES),
        cost_estimate=pl.CostEstimate(
            flops=8 * depth * lon_count, bytes_accessed=4 * depth * lon_count, transcendentals=0
        ),
        name="trig",
    )(*parts, *[x.T for x in parts])


def exchange(rows):
    return lax.all_to_all(rows, AXES, split_axis=0, concat_axis=0, tiled=True)


def by_hemisphere_and_level(spectral, legendre, owner_table):
    slots, _, fields, levels, degrees = spectral.shape
    half_lat = legendre.shape[2]
    lon_count = 4 * half_lat
    row_total = 2 * fields * levels
    tiles = half_lat // LANES
    first = lax.axis_index(AXES).astype(jnp.int32) * slots
    spec_rows = spectral.reshape(slots, row_total, degrees)
    devices = 2 * levels
    least = tuple(4 * g * devices for g in range(slots // 4 - 1))
    near = slots - 4
    far_least, last_least = near * devices, (near + 2) * devices
    cut = tiles - tiles // 2
    chunks = [(0, cut), (cut, tiles - cut)]
    by_device = owner_table.reshape(devices, slots)
    waves = jnp.concatenate([by_device[:, :near].reshape(-1), by_device[:, near:].reshape(-1)])

    far_table = jnp.concatenate(
        [
            legendre[near : near + 2, far_least:].reshape(-1, half_lat),
            legendre[near + 2 :, last_least:].reshape(-1, half_lat),
        ]
    )
    far_spec = spec_rows[near:, :, far_least:]
    packed = jnp.concatenate([far_spec[2, :, last_least - far_least :], far_spec[3, :, last_least - far_least :]], axis=1)
    far_spec = jnp.concatenate([far_spec[:2].reshape(2 * row_total, -1), packed])
    all_spec = lax.all_gather(far_spec, AXES, axis=0, tiled=True)
    all_table = lax.all_gather(far_table, AXES, axis=0, tiled=True).reshape(devices, -1, half_lat)
    own = lax.axis_index(AXES).astype(jnp.int32)
    all_spec = all_spec.reshape(devices, 3, 2, fields, levels, degrees - far_least)
    own_spec = lax.dynamic_index_in_dim(all_spec, own % levels, axis=4, keepdims=False)
    own_spec = jnp.swapaxes(own_spec, 2, 3).reshape(devices, 3, 2 * fields, degrees - far_least)
    far_waves = by_device[:, near:].reshape(-1) - far_least
    far_rows = far_synthesize(
        (own // levels).reshape(1), far_waves, own_spec, all_table, fields, chunks, 1.0 / math.sqrt(degrees)
    )

    def send(spec, chunk):
        return synthesize(first.reshape(1), owner_table, spec, legendre, chunk, fields, levels, least)

    large = send(spec_rows, chunks[0])
    small = send(after(spec_rows, large), chunks[1])
    arrived = [exchange(large)]
    by_wave, by_lon = trig_tables(after(waves, large), lon_count, small)
    arrived.append(exchange(after(small, by_wave, *arrived)))
    zonal = [longitudes(rows, far, by_lon, by_wave, fields) for rows, far in zip(arrived, far_rows)]
    returned = [exchange(zonal[0][0])]
    far_sums = far_analyze([far for _, far in zonal], all_table, fields, chunks)
    far_sums = far_sums.reshape(devices * 6 * fields, -1).astype(jnp.bfloat16)
    far_back = exchange(after(far_sums, *returned))
    returned.append(exchange(after(zonal[1][0], far_back)))
    wavenumber = lax.dynamic_slice_in_dim(after(owner_table, by_wave), first, slots)
    distance = jnp.arange(degrees, dtype=jnp.int32)[None, :] - wavenumber[:, None]
    scale = 1.0 / math.sqrt(2 * half_lat)
    even = jnp.where((distance >= 0) & (distance % 2 == 0), scale, 0.0).astype(jnp.float32)[:, None, :]
    odd = jnp.where((distance >= 0) & (distance % 2 != 0), scale, 0.0).astype(jnp.float32)[:, None, :]
    far_even, far_odd = even[near:, :, far_least:], odd[near:, :, far_least:]
    parts = far_back.astype(jnp.float32).reshape(2, levels, 3, fields, 2, -1)
    parts = jnp.transpose(parts, (0, 2, 4, 3, 1, 5)).reshape(2, 3, row_total, -1)
    width = last_least - far_least
    empty = jnp.zeros((2, 1, row_total, width), jnp.float32)
    parts = jnp.concatenate(
        [
            parts[:, :2],
            jnp.concatenate([empty, parts[:, 2:, :, :width]], axis=3),
            jnp.concatenate([empty, parts[:, 2:, :, width:]], axis=3),
        ],
        axis=1,
    )
    far_out = (parts[0] + parts[1]) * far_even + (parts[0] - parts[1]) * far_odd
    folded = fold(returned[0], near, levels, fields)
    base = analyze(folded, far_out, even, odd, legendre, row_total, least, chunks[0])
    last = after(returned[1], base)
    out = close(last, base, even, odd, legendre, fields, levels, least, chunks[1])
    return out.reshape(slots, 2, fields, levels, degrees)


def make_trig(wavenumber, lon_count):
    lon_index = jnp.arange(lon_count, dtype=jnp.int32)
    phases = wavenumber[:, None] * lon_index[None, :] % lon_count
    angles = phases.astype(jnp.float32) * (2.0 * math.pi / lon_count)
    return jnp.stack([jnp.cos(angles), -jnp.sin(angles)], axis=1).astype(jnp.bfloat16)


def by_level_and_latitude(spectral, legendre, owner_table):
    slot_count, _, fields, levels, degrees = spectral.shape
    half_lat = legendre.shape[2]
    lat_count = 2 * half_lat
    lon_count = 2 * lat_count
    wave_count = owner_table.shape[0]
    band_count = lax.axis_size("band")
    group_count = lax.axis_size("grp")
    device_count = band_count * group_count
    level_block = levels // band_count
    lat_block = lat_count // group_count
    row_total = 2 * fields * levels
    row_width = fields * level_block * lat_block
    slot_start = lax.axis_index(("band", "grp")) * slot_count
    wavenumber = lax.dynamic_slice_in_dim(owner_table, slot_start, slot_count)
    degree_index = jnp.arange(degrees, dtype=jnp.int32)
    keep_mask = (degree_index[None, :] >= wavenumber[:, None]).astype(jnp.bfloat16)
    odd_part = (degree_index[None, :] - wavenumber[:, None]) % 2
    flip_sign = (1 - 2 * odd_part).astype(jnp.bfloat16)
    spec_rows = spectral.reshape(slot_count, row_total, degrees) * keep_mask[:, None, :]
    both_rows = jnp.concatenate([spec_rows, spec_rows * flip_sign[:, None, :]], axis=1)
    halves = jnp.einsum("srn,snt->srt", both_rows, legendre, preferred_element_type=jnp.float32)
    northern = halves[:, :row_total]
    mirrored = halves[:, row_total:]
    fourier = jnp.concatenate([northern, jnp.flip(mirrored, axis=2)], axis=2)
    fourier = fourier.reshape(
        slot_count, 2, fields, band_count, level_block, group_count, lat_block
    )
    fourier = jnp.transpose(fourier, (0, 1, 2, 3, 5, 4, 6))
    fourier_low = (fourier * (1.0 / math.sqrt(degrees))).astype(jnp.bfloat16)
    packed = fourier_low.reshape(1, slot_count, 2, fields, device_count, level_block, lat_block)
    arrived = lax.all_to_all(packed, ("band", "grp"), split_axis=4, concat_axis=0, tiled=True)
    arrived = arrived.reshape(-1, 2, row_width)
    trig_rows = make_trig(owner_table, lon_count)
    grid_values = jnp.einsum("scw,scl->wl", arrived, trig_rows, preferred_element_type=jnp.float32)
    grid_values = (grid_values * (1.0 / math.sqrt(wave_count))).reshape(
        fields, level_block * lat_block, lon_count
    )
    product = (grid_values * jnp.roll(grid_values, -1, axis=0)).astype(jnp.bfloat16)
    zonal_coeffs = jnp.einsum(
        "wl,scl->scw",
        product.reshape(row_width, lon_count),
        trig_rows,
        preferred_element_type=jnp.float32,
    )
    zonal_coeffs = (zonal_coeffs * (2.0 / math.sqrt(lon_count))).astype(jnp.bfloat16)
    sendback = zonal_coeffs.reshape(device_count, slot_count, 2, fields, 1, level_block, lat_block)
    returned = lax.all_to_all(sendback, ("band", "grp"), split_axis=0, concat_axis=4, tiled=True)
    returned = returned.reshape(
        slot_count, 2, fields, band_count, group_count, level_block, lat_block
    )
    returned = jnp.transpose(returned, (0, 1, 2, 3, 5, 4, 6)).reshape(slot_count, row_total, lat_count)
    northern_part = returned[:, :, :half_lat].astype(jnp.float32)
    mirror_part = jnp.flip(returned[:, :, half_lat:], axis=2).astype(jnp.float32)
    plus_part = (northern_part + mirror_part).astype(jnp.bfloat16)
    minus_part = (northern_part - mirror_part).astype(jnp.bfloat16)
    stacked = jnp.concatenate([plus_part, minus_part], axis=1)
    projected = jnp.einsum("srt,snt->srn", stacked, legendre, preferred_element_type=jnp.float32)
    even_rows = flip_sign[:, None, :] > 0
    chosen = jnp.where(even_rows, projected[:, :row_total], projected[:, row_total:])
    chosen = chosen * keep_mask.astype(jnp.float32)[:, None, :] * (1.0 / math.sqrt(lat_count))
    return chosen.reshape(slot_count, 2, fields, levels, degrees)


def on_device(spectral, legendre, owner_table):
    slots, _, _, levels, _ = spectral.shape
    whole_hemispheres = lax.axis_size("band") * lax.axis_size("grp") == 2 * levels
    few_left = legendre.shape[1] - (slots - 4) * 2 * levels == LANES
    if whole_hemispheres and few_left and legendre.shape[2] % LANES == 0 and legendre.shape[2] > LANES and slots % 4 == 0 and levels % 16 == 0:
        return by_hemisphere_and_level(spectral, legendre, owner_table)
    return by_level_and_latitude(spectral, legendre, owner_table)


def solution(mesh):
    placed = (P(("band", "grp"), None, None, None, None), P(("band", "grp"), None, None), P())
    return jax.shard_map(
        on_device,
        mesh=mesh,
        in_specs=placed,
        out_specs=P(("band", "grp"), None, None, None, None),
        check_vma=False,
    )
```

```python
import functools
import math

import jax
import jax.numpy as jnp
from jax import lax
from jax.experimental import pallas as pl
from jax.experimental.pallas import tpu as pltpu
from jax.sharding import PartitionSpec as P

LANES = 128
AXES = ("band", "grp")
VMEM_BYTES = 62 * 1024 * 1024


def synthesis_kernel(
    slots, levels, fields, least, chunk, scale, first_ref, owner_ref, spec_ref, table_ref, out_ref, rows_ref, sems, *held
):
    at, tiles = chunk
    groups = len(least)
    block = slots // groups
    row_total, degrees = spec_ref.shape[1:]
    stride = 2 * slots
    copies = []
    for group, start in enumerate(least):
        mine = pl.ds(group * block, block)
        left = pl.ds(start, degrees - start)
        lanes = pl.ds(at * LANES, tiles * LANES)
        copies.append(
            (
                pltpu.make_async_copy(spec_ref.at[mine, :, left], held[2 * group], sems.at[2 * group]),
                pltpu.make_async_copy(table_ref.at[mine, left, lanes], held[2 * group + 1], sems.at[2 * group + 1]),
            )
        )
    order = range(groups - 1, -1, -1)
    for group in order:
        for copy in copies[group]:
            copy.start()
    for group in order:
        for copy in copies[group]:
            copy.wait()
        for j in range(block):
            spec = held[2 * group][j]
            wave = owner_ref[first_ref[0] + group * block + j]
            distance = lax.broadcasted_iota(jnp.int32, (1, spec.shape[1]), 1) + (least[group] - wave)
            keep = jnp.where(distance >= 0, 1.0, 0.0)
            flip = jnp.where(distance % 2 == 0, keep, -keep)
            both = jnp.concatenate([spec * keep.astype(spec.dtype), spec * flip.astype(spec.dtype)], axis=0)
            halves = jnp.dot(both, held[2 * group + 1][j], preferred_element_type=jnp.float32) * scale
            first = 2 * (group * block + j)
            for hemi in range(2):
                for part in range(2):
                    for field in range(fields):
                        row = hemi * row_total + (part * fields + field) * levels
                        target = pl.ds(hemi * levels * stride + first + part, levels, stride=stride)
                        for tile in range(tiles):
                            lanes = slice(tile * LANES, (tile + 1) * LANES)
                            rows_ref[field, tile, target, :] = halves[row : row + levels, lanes]
    for field in range(fields):
        for tile in range(tiles):
            lanes = pl.ds((field * tiles + tile) * LANES, LANES)
            out_ref[:, lanes] = rows_ref[field, tile].astype(out_ref.dtype)


def synthesize(first, owner_table, spec_rows, legendre, chunk, fields, levels, least):
    slots, row_total, degrees = spec_rows.shape
    block = slots // len(least)
    rows = 2 * levels * 2 * slots
    tiles = chunk[1]
    shape = (rows, fields * tiles * LANES)
    held = []
    for start in least:
        held.append(pltpu.VMEM((block, row_total, degrees - start), jnp.bfloat16))
        held.append(pltpu.VMEM((block, degrees - start, tiles * LANES), jnp.bfloat16))
    return pl.pallas_call(
        functools.partial(synthesis_kernel, slots, levels, fields, least, chunk, 1.0 / math.sqrt(degrees)),
        in_specs=[pl.BlockSpec(memory_space=pltpu.SMEM)] * 2 + [pl.BlockSpec(memory_space=pl.ANY)] * 2,
        out_specs=pl.BlockSpec(shape, lambda: (0, 0)),
        out_shape=jax.ShapeDtypeStruct(shape, jnp.bfloat16),
        scratch_shapes=[
            pltpu.VMEM((fields, tiles, rows, LANES), jnp.float32),
            pltpu.SemaphoreType.DMA((2 * len(least),)),
            *held,
        ],
        compiler_params=pltpu.CompilerParams(vmem_limit_bytes=VMEM_BYTES),
        cost_estimate=pl.CostEstimate(
            flops=4 * slots * row_total * degrees * tiles * LANES,
            bytes_accessed=2 * slots * degrees * (row_total + tiles * LANES) + 2 * rows * shape[1],
            transcendentals=0,
        ),
        name="synthesis",
    )(first, owner_table, spec_rows, legendre)


def longitude_kernel(fields, grid_scale, zonal_scale, rows_ref, by_lon_ref, by_wave_ref, out_ref, sum_ref):
    step = pl.program_id(0)
    values = jnp.dot(by_lon_ref[...], rows_ref[...], preferred_element_type=jnp.float32) * grid_scale
    one = values.shape[1] // fields
    following = jnp.concatenate([values[:, one:], values[:, :one]], axis=1)
    product = (values * following).astype(jnp.bfloat16)
    share = jnp.dot(by_wave_ref[...], product, preferred_element_type=jnp.float32)

    @pl.when(step == 0)
    def _():
        sum_ref[...] = share

    @pl.when(step > 0)
    def _():
        sum_ref[...] += share

    @pl.when(step == pl.num_programs(0) - 1)
    def _():
        out_ref[...] = (sum_ref[...] * zonal_scale).astype(out_ref.dtype)


def longitudes(rows, by_lon, by_wave, fields):
    depth, width = rows.shape
    lon_count = by_lon.shape[0]
    lon_block = lon_count // 5
    return pl.pallas_call(
        functools.partial(longitude_kernel, fields, 1.0 / math.sqrt(depth // 2), 2.0 / math.sqrt(lon_count)),
        grid=(lon_count // lon_block,),
        in_specs=[
            pl.BlockSpec((depth, width), lambda i: (0, 0)),
            pl.BlockSpec((lon_block, depth), lambda i: (i, 0)),
            pl.BlockSpec((depth, lon_block), lambda i: (0, i)),
        ],
        out_specs=pl.BlockSpec((depth, width), lambda i: (0, 0)),
        out_shape=jax.ShapeDtypeStruct((depth, width), jnp.bfloat16),
        scratch_shapes=[pltpu.VMEM((depth, width), jnp.float32)],
        compiler_params=pltpu.CompilerParams(vmem_limit_bytes=VMEM_BYTES),
        cost_estimate=pl.CostEstimate(
            flops=4 * depth * width * lon_count,
            bytes_accessed=4 * depth * (width + lon_count),
            transcendentals=0,
        ),
        name="longitudes",
    )(rows, by_lon, by_wave)


def fold_kernel(slots, levels, fields, arrived_ref, out_ref, rows_ref):
    tiles = rows_ref.shape[1]
    stride = 2 * slots
    half = levels * stride
    for field in range(fields):
        for tile in range(tiles):
            lanes = pl.ds((field * tiles + tile) * LANES, LANES)
            rows_ref[field, tile] = arrived_ref[:, lanes].astype(jnp.float32)
    for slot in range(slots):
        for part in range(2):
            for field in range(fields):
                for tile in range(tiles):
                    first = 2 * slot + part
                    north = rows_ref[field, tile, pl.ds(first, levels, stride=stride), :]
                    south = rows_ref[field, tile, pl.ds(half + first, levels, stride=stride), :]
                    lanes = pl.ds(tile * LANES, LANES)
                    at = (part * fields + field) * levels
                    out_ref[slot, at : at + levels, lanes] = (north + south).astype(out_ref.dtype)
                    at += 2 * fields * levels
                    out_ref[slot, at : at + levels, lanes] = (north - south).astype(out_ref.dtype)


def fold(arrived, slots, levels, fields):
    row_total = 2 * fields * levels
    rows, width = arrived.shape
    tiles = width // (fields * LANES)
    shape = (slots, 2 * row_total, tiles * LANES)
    return pl.pallas_call(
        functools.partial(fold_kernel, slots, levels, fields),
        in_specs=[pl.BlockSpec((rows, width), lambda: (0, 0))],
        out_specs=pl.BlockSpec(shape, lambda: (0, 0, 0)),
        out_shape=jax.ShapeDtypeStruct(shape, jnp.bfloat16),
        scratch_shapes=[pltpu.VMEM((fields, tiles, rows, LANES), jnp.float32)],
        compiler_params=pltpu.CompilerParams(vmem_limit_bytes=VMEM_BYTES),
        cost_estimate=pl.CostEstimate(flops=2 * rows * width, bytes_accessed=4 * rows * width, transcendentals=0),
        name="fold",
    )(arrived)


def analysis_kernel(least, folded_ref, even_ref, odd_ref, *refs):
    table_refs, out_ref = refs[:-1], refs[-1]
    row_total, degrees = out_ref.shape[1:]
    step = pl.program_id(0)

    def run(group):
        start = least[group]
        for j in range(out_ref.shape[0]):
            table = jnp.concatenate([ref[j, start:, :] for ref in table_refs], axis=1)
            sums = lax.dot_general(
                folded_ref[j], table, (((1,), (1,)), ((), ())), preferred_element_type=jnp.float32
            )
            kept = sums[:row_total] * even_ref[j, :, start:] + sums[row_total:] * odd_ref[j, :, start:]
            out_ref[j, :, start:] = kept
            if start:
                out_ref[j, :, :start] = jnp.zeros((row_total, start), out_ref.dtype)

    for group in range(len(least)):
        pl.when(step == group)(functools.partial(run, group))


def analyze(folded, even, odd, legendre, row_total, least, chunk):
    slots, degrees, _ = legendre.shape
    block = slots // len(least)
    at, tiles = chunk
    mask_spec = pl.BlockSpec((block, 1, degrees), lambda i: (i, 0, 0))
    return pl.pallas_call(
        functools.partial(analysis_kernel, least),
        grid=(len(least),),
        in_specs=[pl.BlockSpec((block,) + folded.shape[1:], lambda i: (i, 0, 0)), mask_spec, mask_spec]
        + [pl.BlockSpec((block, degrees, LANES), lambda i, t=at + t: (i, 0, t)) for t in range(tiles)],
        out_specs=pl.BlockSpec((block, row_total, degrees), lambda i: (i, 0, 0)),
        out_shape=jax.ShapeDtypeStruct((slots, row_total, degrees), jnp.float32),
        compiler_params=pltpu.CompilerParams(vmem_limit_bytes=VMEM_BYTES),
        cost_estimate=pl.CostEstimate(
            flops=4 * slots * row_total * degrees * tiles * LANES,
            bytes_accessed=2 * slots * (degrees * tiles * LANES + 2 * row_total * (tiles * LANES + degrees)),
            transcendentals=0,
        ),
        name="analysis",
    )(folded, even, odd, *[legendre] * tiles)


def closing_kernel(
    levels, fields, least, chunk, arrived_ref, table_ref, base_ref, even_ref, odd_ref, out_ref, *refs
):
    got_ref, north_ref, south_ref, sems = refs[:4]
    held = refs[4:]
    at, tiles = chunk
    groups = len(least)
    slots, row_total, degrees = base_ref.shape
    block = slots // groups
    stride = 2 * slots
    half = levels * stride
    arriving = [
        pltpu.make_async_copy(
            arrived_ref.at[:, pl.ds(field * tiles * LANES, tiles * LANES)], got_ref.at[field], sems.at[3 * groups + field]
        )
        for field in range(fields)
    ]
    tables, sums, results = [], [], []
    for group, start in enumerate(least):
        mine = pl.ds(group * block, block)
        left = pl.ds(start, degrees - start)
        lanes = pl.ds(at * LANES, tiles * LANES)
        held_table, held_sums = held[2 * group], held[2 * group + 1]
        tables.append(pltpu.make_async_copy(table_ref.at[mine, left, lanes], held_table, sems.at[3 * group]))
        sums.append(pltpu.make_async_copy(base_ref.at[mine, :, left], held_sums, sems.at[3 * group + 1]))
        results.append(pltpu.make_async_copy(held_sums, out_ref.at[mine, :, left], sems.at[3 * group + 2]))
    for copy in arriving:
        copy.start()
    for group in range(groups):
        tables[group].start()
        sums[group].start()
    for field in range(fields):
        arriving[field].wait()
        for tile in range(tiles):
            lanes = pl.ds(tile * LANES, LANES)
            north = got_ref[field, :half, lanes].astype(jnp.float32)
            south = got_ref[field, half:, lanes].astype(jnp.float32)
            north_ref[field, tile] = north + south
            south_ref[field, tile] = north - south
    for group, start in enumerate(least):
        tables[group].wait()
        sums[group].wait()
        held_table, held_sums = held[2 * group], held[2 * group + 1]
        for j in range(block):
            slot = group * block + j
            folded = jnp.concatenate(
                [
                    jnp.concatenate(
                        [
                            ref[field, tile, pl.ds(2 * slot + part, levels, stride=stride), :].astype(jnp.bfloat16)
                            for ref in (north_ref, south_ref)
                            for part in range(2)
                            for field in range(fields)
                        ],
                        axis=0,
                    )
                    for tile in range(tiles)
                ],
                axis=1,
            )
            more = lax.dot_general(
                folded, held_table[j], (((1,), (1,)), ((), ())), preferred_element_type=jnp.float32
            )
            even, odd = even_ref[slot, :, start:], odd_ref[slot, :, start:]
            held_sums[j] = held_sums[j] + more[:row_total] * even + more[row_total:] * odd
        results[group].start()
    for copy in results:
        copy.wait()


def close(arrived, base, even, odd, legendre, fields, levels, least, chunk):
    slots, row_total, degrees = base.shape
    block = slots // len(least)
    rows, width = arrived.shape
    tiles = chunk[1]
    half = pltpu.VMEM((fields, tiles, rows // 2, LANES), jnp.float32)
    held = []
    for start in least:
        held.append(pltpu.VMEM((block, degrees - start, tiles * LANES), jnp.bfloat16))
        held.append(pltpu.VMEM((block, row_total, degrees - start), jnp.float32))
    anywhere = pl.BlockSpec(memory_space=pl.ANY)
    return pl.pallas_call(
        functools.partial(closing_kernel, levels, fields, least, chunk),
        in_specs=[anywhere, anywhere, anywhere] + [pl.BlockSpec(even.shape, lambda: (0, 0, 0))] * 2,
        out_specs=anywhere,
        out_shape=jax.ShapeDtypeStruct(base.shape, jnp.float32),
        input_output_aliases={2: 0},
        scratch_shapes=[
            pltpu.VMEM((fields, rows, tiles * LANES), jnp.bfloat16),
            half,
            half,
            pltpu.SemaphoreType.DMA((3 * len(least) + fields,)),
            *held,
        ],
        compiler_params=pltpu.CompilerParams(vmem_limit_bytes=VMEM_BYTES),
        cost_estimate=pl.CostEstimate(
            flops=4 * slots * row_total * degrees * tiles * LANES,
            bytes_accessed=8 * slots * row_total * degrees + 2 * rows * width,
            transcendentals=0,
        ),
        name="closing",
    )(arrived, legendre, base, even, odd)


def after(value, *others):
    return lax.optimization_barrier((value, others))[0]


def trig_kernel(cos_base_ref, sin_base_ref, cos_turn_ref, sin_turn_ref, cos_base_t, sin_base_t, cos_turn_t, sin_turn_t, by_wave_ref, by_lon_ref):
    for j in range(cos_base_ref.shape[1]):
        lanes = pl.ds(j * LANES, LANES)
        cos_base, sin_base = cos_base_ref[:, j : j + 1], sin_base_ref[:, j : j + 1]
        angles = cos_base * cos_turn_ref[...] - sin_base * sin_turn_ref[...]
        by_wave_ref[:, lanes] = angles.astype(by_wave_ref.dtype)
        cos_base, sin_base = cos_base_t[j : j + 1, :], sin_base_t[j : j + 1, :]
        angles = cos_base * cos_turn_t[...] - sin_base * sin_turn_t[...]
        by_lon_ref[lanes, :] = angles.astype(by_lon_ref.dtype)


def trig_tables(owner_table, lon_count, *others):
    waves = jnp.repeat(owner_table, 2).astype(jnp.float32)[:, None]
    quarter = jnp.tile(jnp.array([0, lon_count // 4], jnp.float32), owner_table.shape[0])[:, None]
    unit = 2.0 * math.pi / lon_count

    def angles(lon, turn):
        phase = waves * lon + turn
        return (phase - lon_count * jnp.floor(phase * (1.0 / lon_count))) * unit

    base = angles(jnp.arange(0, lon_count, LANES, dtype=jnp.float32)[None, :], quarter)
    turn = angles(jnp.arange(LANES, dtype=jnp.float32)[None, :], 0.0)
    depth = waves.shape[0]
    blocks = lon_count // LANES
    rows = 256
    small = pl.BlockSpec((rows, blocks), lambda i: (i, 0))
    wide = pl.BlockSpec((rows, LANES), lambda i: (i, 0))
    small_t = pl.BlockSpec((blocks, rows), lambda i: (0, i))
    wide_t = pl.BlockSpec((LANES, rows), lambda i: (0, i))
    parts = (jnp.cos(base), jnp.sin(base), jnp.cos(turn), jnp.sin(turn))
    parts = after(parts, *others)
    return pl.pallas_call(
        trig_kernel,
        grid=(depth // rows,),
        in_specs=[small, small, wide, wide, small_t, small_t, wide_t, wide_t],
        out_specs=[
            pl.BlockSpec((rows, lon_count), lambda i: (i, 0)),
            pl.BlockSpec((lon_count, rows), lambda i: (0, i)),
        ],
        out_shape=[
            jax.ShapeDtypeStruct((depth, lon_count), jnp.bfloat16),
            jax.ShapeDtypeStruct((lon_count, depth), jnp.bfloat16),
        ],
        compiler_params=pltpu.CompilerParams(vmem_limit_bytes=VMEM_BYTES),
        cost_estimate=pl.CostEstimate(
            flops=8 * depth * lon_count, bytes_accessed=4 * depth * lon_count, transcendentals=0
        ),
        name="trig",
    )(*parts, *[x.T for x in parts])


def exchange(rows):
    return lax.all_to_all(rows, AXES[::-1], split_axis=0, concat_axis=0, tiled=True)


def by_hemisphere_and_level(spectral, legendre, owner_table):
    slots, _, fields, levels, degrees = spectral.shape
    half_lat = legendre.shape[2]
    lon_count = 4 * half_lat
    row_total = 2 * fields * levels
    tiles = half_lat // LANES
    first = lax.axis_index(AXES).astype(jnp.int32) * slots
    spec_rows = spectral.reshape(slots, row_total, degrees)
    least = tuple(8 * g * levels for g in range(slots // 4))
    cut = tiles - tiles // 2
    chunks = [(0, cut), (cut, tiles - cut)]

    def send(spec, chunk):
        return synthesize(first.reshape(1), owner_table, spec, legendre, chunk, fields, levels, least)

    large = send(spec_rows, chunks[0])
    small = send(after(spec_rows, large), chunks[1])
    arrived = [exchange(large)]
    arrived.append(exchange(after(small, *arrived)))
    bands, planes = lax.axis_size("band"), lax.axis_size("grp")
    arriving = jnp.swapaxes(owner_table.reshape(bands, planes, slots), 0, 1).reshape(-1)
    by_wave, by_lon = trig_tables(after(arriving, large), lon_count, small)
    zonal = [longitudes(rows, by_lon, by_wave, fields) for rows in arrived]
    returned = [exchange(zonal[0])]
    returned.append(exchange(after(zonal[1], *returned)))
    wavenumber = lax.dynamic_slice_in_dim(after(owner_table, by_wave), first, slots)
    distance = jnp.arange(degrees, dtype=jnp.int32)[None, :] - wavenumber[:, None]
    scale = 1.0 / math.sqrt(2 * half_lat)
    even = jnp.where((distance >= 0) & (distance % 2 == 0), scale, 0.0).astype(jnp.float32)[:, None, :]
    odd = jnp.where((distance >= 0) & (distance % 2 != 0), scale, 0.0).astype(jnp.float32)[:, None, :]
    base = analyze(fold(returned[0], slots, levels, fields), even, odd, legendre, row_total, least, chunks[0])
    last = after(returned[1], base)
    out = close(last, base, even, odd, legendre, fields, levels, least, chunks[1])
    return out.reshape(slots, 2, fields, levels, degrees)


def make_trig(wavenumber, lon_count):
    lon_index = jnp.arange(lon_count, dtype=jnp.int32)
    phases = wavenumber[:, None] * lon_index[None, :] % lon_count
    angles = phases.astype(jnp.float32) * (2.0 * math.pi / lon_count)
    return jnp.stack([jnp.cos(angles), -jnp.sin(angles)], axis=1).astype(jnp.bfloat16)


def by_level_and_latitude(spectral, legendre, owner_table):
    slot_count, _, fields, levels, degrees = spectral.shape
    half_lat = legendre.shape[2]
    lat_count = 2 * half_lat
    lon_count = 2 * lat_count
    wave_count = owner_table.shape[0]
    band_count = lax.axis_size("band")
    group_count = lax.axis_size("grp")
    device_count = band_count * group_count
    level_block = levels // band_count
    lat_block = lat_count // group_count
    row_total = 2 * fields * levels
    row_width = fields * level_block * lat_block
    slot_start = lax.axis_index(("band", "grp")) * slot_count
    wavenumber = lax.dynamic_slice_in_dim(owner_table, slot_start, slot_count)
    degree_index = jnp.arange(degrees, dtype=jnp.int32)
    keep_mask = (degree_index[None, :] >= wavenumber[:, None]).astype(jnp.bfloat16)
    odd_part = (degree_index[None, :] - wavenumber[:, None]) % 2
    flip_sign = (1 - 2 * odd_part).astype(jnp.bfloat16)
    spec_rows = spectral.reshape(slot_count, row_total, degrees) * keep_mask[:, None, :]
    both_rows = jnp.concatenate([spec_rows, spec_rows * flip_sign[:, None, :]], axis=1)
    halves = jnp.einsum("srn,snt->srt", both_rows, legendre, preferred_element_type=jnp.float32)
    northern = halves[:, :row_total]
    mirrored = halves[:, row_total:]
    fourier = jnp.concatenate([northern, jnp.flip(mirrored, axis=2)], axis=2)
    fourier = fourier.reshape(
        slot_count, 2, fields, band_count, level_block, group_count, lat_block
    )
    fourier = jnp.transpose(fourier, (0, 1, 2, 3, 5, 4, 6))
    fourier_low = (fourier * (1.0 / math.sqrt(degrees))).astype(jnp.bfloat16)
    packed = fourier_low.reshape(1, slot_count, 2, fields, device_count, level_block, lat_block)
    arrived = lax.all_to_all(packed, ("band", "grp"), split_axis=4, concat_axis=0, tiled=True)
    arrived = arrived.reshape(-1, 2, row_width)
    trig_rows = make_trig(owner_table, lon_count)
    grid_values = jnp.einsum("scw,scl->wl", arrived, trig_rows, preferred_element_type=jnp.float32)
    grid_values = (grid_values * (1.0 / math.sqrt(wave_count))).reshape(
        fields, level_block * lat_block, lon_count
    )
    product = (grid_values * jnp.roll(grid_values, -1, axis=0)).astype(jnp.bfloat16)
    zonal_coeffs = jnp.einsum(
        "wl,scl->scw",
        product.reshape(row_width, lon_count),
        trig_rows,
        preferred_element_type=jnp.float32,
    )
    zonal_coeffs = (zonal_coeffs * (2.0 / math.sqrt(lon_count))).astype(jnp.bfloat16)
    sendback = zonal_coeffs.reshape(device_count, slot_count, 2, fields, 1, level_block, lat_block)
    returned = lax.all_to_all(sendback, ("band", "grp"), split_axis=0, concat_axis=4, tiled=True)
    returned = returned.reshape(
        slot_count, 2, fields, band_count, group_count, level_block, lat_block
    )
    returned = jnp.transpose(returned, (0, 1, 2, 3, 5, 4, 6)).reshape(slot_count, row_total, lat_count)
    northern_part = returned[:, :, :half_lat].astype(jnp.float32)
    mirror_part = jnp.flip(returned[:, :, half_lat:], axis=2).astype(jnp.float32)
    plus_part = (northern_part + mirror_part).astype(jnp.bfloat16)
    minus_part = (northern_part - mirror_part).astype(jnp.bfloat16)
    stacked = jnp.concatenate([plus_part, minus_part], axis=1)
    projected = jnp.einsum("srt,snt->srn", stacked, legendre, preferred_element_type=jnp.float32)
    even_rows = flip_sign[:, None, :] > 0
    chosen = jnp.where(even_rows, projected[:, :row_total], projected[:, row_total:])
    chosen = chosen * keep_mask.astype(jnp.float32)[:, None, :] * (1.0 / math.sqrt(lat_count))
    return chosen.reshape(slot_count, 2, fields, levels, degrees)


def on_device(spectral, legendre, owner_table):
    slots, _, _, levels, _ = spectral.shape
    whole_hemispheres = lax.axis_size("band") * lax.axis_size("grp") == 2 * levels
    if whole_hemispheres and legendre.shape[2] % LANES == 0 and legendre.shape[2] > LANES and slots % 4 == 0 and levels % 16 == 0:
        return by_hemisphere_and_level(spectral, legendre, owner_table)
    return by_level_and_latitude(spectral, legendre, owner_table)


def solution(mesh):
    placed = (P(("band", "grp"), None, None, None, None), P(("band", "grp"), None, None), P())
    return jax.shard_map(
        on_device,
        mesh=mesh,
        in_specs=placed,
        out_specs=P(("band", "grp"), None, None, None, None),
        check_vma=False,
    )
```

```python
import functools
import math

import jax
import jax.numpy as jnp
from jax import lax
from jax.experimental import pallas as pl
from jax.experimental.pallas import tpu as pltpu
from jax.sharding import PartitionSpec as P

LANES = 128
AXES = ("band", "grp")
VMEM_BYTES = 62 * 1024 * 1024


def synthesis_kernel(
    slots, levels, fields, least, chunk, scale, first_ref, owner_ref, spec_ref, table_ref, out_ref, rows_ref, sems, *held
):
    at, tiles = chunk
    groups = len(least)
    block = 4
    row_total, degrees = spec_ref.shape[1:]
    stride = 2 * slots
    copies = []
    for group, start in enumerate(least):
        mine = pl.ds(group * block, block)
        left = pl.ds(start, degrees - start)
        lanes = pl.ds(at * LANES, tiles * LANES)
        copies.append(
            (
                pltpu.make_async_copy(spec_ref.at[mine, :, left], held[2 * group], sems.at[2 * group]),
                pltpu.make_async_copy(table_ref.at[mine, left, lanes], held[2 * group + 1], sems.at[2 * group + 1]),
            )
        )
    order = range(groups - 1, -1, -1)
    for group in order:
        for copy in copies[group]:
            copy.start()
    for group in order:
        for copy in copies[group]:
            copy.wait()
        for j in range(block):
            spec = held[2 * group][j]
            wave = owner_ref[first_ref[0] + group * block + j]
            distance = lax.broadcasted_iota(jnp.int32, (1, spec.shape[1]), 1) + (least[group] - wave)
            keep = jnp.where(distance >= 0, 1.0, 0.0)
            flip = jnp.where(distance % 2 == 0, keep, -keep)
            both = jnp.concatenate([spec * keep.astype(spec.dtype), spec * flip.astype(spec.dtype)], axis=0)
            halves = jnp.dot(both, held[2 * group + 1][j], preferred_element_type=jnp.float32) * scale
            first = 2 * (group * block + j)
            for hemi in range(2):
                for part in range(2):
                    for field in range(fields):
                        row = hemi * row_total + (part * fields + field) * levels
                        target = pl.ds(hemi * levels * stride + first + part, levels, stride=stride)
                        for tile in range(tiles):
                            lanes = slice(tile * LANES, (tile + 1) * LANES)
                            rows_ref[field, tile, target, :] = halves[row : row + levels, lanes]
    for field in range(fields):
        for tile in range(tiles):
            lanes = pl.ds((field * tiles + tile) * LANES, LANES)
            out_ref[:, lanes] = rows_ref[field, tile].astype(out_ref.dtype)


def synthesize(first, owner_table, spec_rows, legendre, chunk, fields, levels, least):
    _, row_total, degrees = spec_rows.shape
    block = 4
    slots = block * len(least)
    rows = 2 * levels * 2 * slots
    tiles = chunk[1]
    shape = (rows, fields * tiles * LANES)
    held = []
    for start in least:
        held.append(pltpu.VMEM((block, row_total, degrees - start), jnp.bfloat16))
        held.append(pltpu.VMEM((block, degrees - start, tiles * LANES), jnp.bfloat16))
    return pl.pallas_call(
        functools.partial(synthesis_kernel, slots, levels, fields, least, chunk, 1.0 / math.sqrt(degrees)),
        in_specs=[pl.BlockSpec(memory_space=pltpu.SMEM)] * 2 + [pl.BlockSpec(memory_space=pl.ANY)] * 2,
        out_specs=pl.BlockSpec(shape, lambda: (0, 0)),
        out_shape=jax.ShapeDtypeStruct(shape, jnp.bfloat16),
        scratch_shapes=[
            pltpu.VMEM((fields, tiles, rows, LANES), jnp.float32),
            pltpu.SemaphoreType.DMA((2 * len(least),)),
            *held,
        ],
        compiler_params=pltpu.CompilerParams(vmem_limit_bytes=VMEM_BYTES),
        cost_estimate=pl.CostEstimate(
            flops=4 * slots * row_total * degrees * tiles * LANES,
            bytes_accessed=2 * slots * degrees * (row_total + tiles * LANES) + 2 * rows * shape[1],
            transcendentals=0,
        ),
        name="synthesis",
    )(first, owner_table, spec_rows, legendre)


def longitude_kernel(
    fields, chunk, grid_scale, zonal_scale, rows_ref, far_ref, by_lon_ref, by_wave_ref, out_ref, far_out_ref, sum_ref
):
    step = pl.program_id(0)
    near = rows_ref.shape[0]
    values = jnp.dot(by_lon_ref[:, :near], rows_ref[...], preferred_element_type=jnp.float32)
    one = values.shape[1] // fields
    each = far_ref.shape[1] // fields
    starts = [field * each + chunk[0] * LANES for field in range(fields)]
    far = jnp.concatenate([far_ref[:, start : start + one] for start in starts], axis=1)
    values = values + jnp.dot(by_lon_ref[:, near:], far, preferred_element_type=jnp.float32)
    values = values * grid_scale
    following = jnp.concatenate([values[:, one:], values[:, :one]], axis=1)
    product = (values * following).astype(jnp.bfloat16)
    share = jnp.dot(by_wave_ref[...], product, preferred_element_type=jnp.float32)

    @pl.when(step == 0)
    def _():
        sum_ref[...] = share

    @pl.when(step > 0)
    def _():
        sum_ref[...] += share

    @pl.when(step == pl.num_programs(0) - 1)
    def _():
        out_ref[...] = (sum_ref[:near, :] * zonal_scale).astype(out_ref.dtype)
        far_out_ref[...] = (sum_ref[near:, :] * zonal_scale).astype(far_out_ref.dtype)


def longitudes(rows, far, by_lon, by_wave, fields, chunk):
    depth, width = rows.shape[0] + far.shape[0], rows.shape[1]
    lon_count = by_lon.shape[0]
    lon_block = lon_count // 5
    near_spec = pl.BlockSpec(rows.shape, lambda i: (0, 0))
    far_out = jax.ShapeDtypeStruct((far.shape[0], width), jnp.bfloat16)
    return pl.pallas_call(
        functools.partial(longitude_kernel, fields, chunk, 1.0 / math.sqrt(depth // 2), 2.0 / math.sqrt(lon_count)),
        grid=(lon_count // lon_block,),
        in_specs=[
            near_spec,
            pl.BlockSpec(far.shape, lambda i: (0, 0)),
            pl.BlockSpec((lon_block, depth), lambda i: (i, 0)),
            pl.BlockSpec((depth, lon_block), lambda i: (0, i)),
        ],
        out_specs=[near_spec, pl.BlockSpec(far_out.shape, lambda i: (0, 0))],
        out_shape=[jax.ShapeDtypeStruct(rows.shape, jnp.bfloat16), far_out],
        scratch_shapes=[pltpu.VMEM((depth, width), jnp.float32)],
        compiler_params=pltpu.CompilerParams(vmem_limit_bytes=VMEM_BYTES),
        cost_estimate=pl.CostEstimate(
            flops=4 * depth * width * lon_count,
            bytes_accessed=4 * depth * (width + lon_count),
            transcendentals=0,
        ),
        name="longitudes",
    )(rows, far, by_lon, by_wave)


def far_synthesis_kernel(levels, fields, scale, place_ref, waves_ref, own_ref, partner_ref, *refs):
    out_refs, rows_ref = refs[:-1], refs[-1]
    tiles = rows_ref.shape[1]
    half_lat = tiles * LANES
    stride = rows_ref.shape[2] // levels
    degree = lax.broadcasted_iota(jnp.int32, (1, LANES), 1)
    for slot in range(8):
        pack_ref, local = (own_ref, slot) if slot < 4 else (partner_ref, slot - 4)
        rows = pl.ds(min(local, 2) * LANES, LANES)
        distance = degree - waves_ref[slot] + (LANES // 2 if local == 2 else 0)
        keep = jnp.where(distance >= 0, 1.0, 0.0)
        if local >= 2:
            keep = jnp.where((degree < LANES // 2) if local == 2 else (degree >= LANES // 2), keep, 0.0)
        turned = jnp.where(distance % 2 == 0, keep, -keep)
        sign = jnp.where(place_ref[0] == 0, keep, turned)
        spec = pack_ref[rows, half_lat:]
        table = pack_ref[rows, :half_lat]
        sums = jnp.dot(spec * sign.astype(spec.dtype), table, preferred_element_type=jnp.float32) * scale
        for part in range(2):
            for field in range(fields):
                row = (part * fields + field) * levels
                for tile in range(tiles):
                    target = pl.ds(2 * slot + part, levels, stride=stride)
                    rows_ref[field, tile, target, :] = sums[row : row + levels, tile * LANES : (tile + 1) * LANES]
    for apart, out_ref in enumerate(out_refs):
        rows = pl.ds(pl.multiple_of((place_ref[1] ^ apart) * stride, stride), stride)
        for field in range(fields):
            for tile in range(tiles):
                lanes = pl.ds((field * tiles + tile) * LANES, LANES)
                out_ref[:, lanes] = rows_ref[field, tile, rows, :].astype(out_ref.dtype)


def far_synthesize(place, waves, own, partner, levels, fields, scale):
    tiles = own.shape[1] // LANES - 1
    shape = (16, fields * tiles * LANES)
    whole = pl.BlockSpec(own.shape, lambda: (0, 0))
    return pl.pallas_call(
        functools.partial(far_synthesis_kernel, levels, fields, scale),
        in_specs=[pl.BlockSpec(memory_space=pltpu.SMEM)] * 2 + [whole, whole],
        out_specs=[pl.BlockSpec(shape, lambda: (0, 0))] * levels,
        out_shape=[jax.ShapeDtypeStruct(shape, jnp.bfloat16)] * levels,
        scratch_shapes=[pltpu.VMEM((fields, tiles, 16 * levels, LANES), jnp.float32)],
        compiler_params=pltpu.CompilerParams(vmem_limit_bytes=VMEM_BYTES),
        cost_estimate=pl.CostEstimate(
            flops=16 * 2 * fields * levels * LANES * tiles * LANES, bytes_accessed=4 * own.size, transcendentals=0
        ),
        name="far_synthesis",
    )(place, waves, own, partner)


def far_analysis_kernel(levels, fields, chunks, place_ref, own_ref, partner_ref, *refs):
    zonal_refs, own_out_ref, partner_out_ref, rows_ref = refs[:levels], refs[-3], refs[-2], refs[-1]
    tiles = rows_ref.shape[1]
    stride = rows_ref.shape[2] // levels
    for apart, zonal_ref in enumerate(zonal_refs):
        rows = pl.ds(pl.multiple_of((place_ref[1] ^ apart) * stride, stride), stride)
        offset = 0
        for at, count in chunks:
            for field in range(fields):
                for tile in range(at, at + count):
                    rows_ref[field, tile, rows, :] = zonal_ref[:, pl.ds(offset, LANES)].astype(jnp.float32)
                    offset += LANES
    lower = lax.broadcasted_iota(jnp.int32, (1, LANES), 1) < LANES // 2
    for pack_ref, out_ref, base in ((own_ref, own_out_ref, 0), (partner_ref, partner_out_ref, 4)):
        sums = []
        for local in range(4):
            rows = pl.ds(min(local, 2) * LANES, LANES)
            zonal = jnp.concatenate(
                [
                    jnp.concatenate(
                        [
                            rows_ref[field, tile, pl.ds(2 * (base + local) + part, levels, stride=stride), :]
                            for part in range(2)
                            for field in range(fields)
                        ],
                        axis=0,
                    ).astype(jnp.bfloat16)
                    for tile in range(tiles)
                ],
                axis=1,
            )
            table = pack_ref[rows, : tiles * LANES]
            sums.append(
                lax.dot_general(zonal, table, (((1,), (1,)), ((), ())), preferred_element_type=jnp.float32)
            )
        sums[2] = jnp.where(lower, sums[2], sums[3])
        size = sums[0].shape[0]
        for block in range(3):
            out_ref[pl.ds(block * size, size), :] = sums[block].astype(out_ref.dtype)


def far_analyze(place, own, partner, zonal, levels, fields, chunks):
    tiles = own.shape[1] // LANES - 1
    shape = (3 * 2 * fields * levels, LANES)
    whole = pl.BlockSpec(own.shape, lambda: (0, 0))
    out_spec = pl.BlockSpec(shape, lambda: (0, 0))
    return pl.pallas_call(
        functools.partial(far_analysis_kernel, levels, fields, chunks),
        in_specs=[pl.BlockSpec(memory_space=pltpu.SMEM), whole, whole]
        + [pl.BlockSpec(x.shape, lambda: (0, 0)) for x in zonal],
        out_specs=[out_spec, out_spec],
        out_shape=[jax.ShapeDtypeStruct(shape, jnp.float32), jax.ShapeDtypeStruct(shape, jnp.bfloat16)],
        scratch_shapes=[pltpu.VMEM((fields, tiles, 16 * levels, LANES), jnp.float32)],
        compiler_params=pltpu.CompilerParams(vmem_limit_bytes=VMEM_BYTES),
        cost_estimate=pl.CostEstimate(
            flops=16 * 2 * fields * levels * LANES * tiles * LANES, bytes_accessed=4 * own.size, transcendentals=0
        ),
        name="far_analysis",
    )(place, own, partner, *zonal)


def fold_kernel(slots, levels, fields, arrived_ref, out_ref, rows_ref):
    tiles = rows_ref.shape[1]
    stride = 2 * slots
    half = levels * stride
    for field in range(fields):
        for tile in range(tiles):
            lanes = pl.ds((field * tiles + tile) * LANES, LANES)
            rows_ref[field, tile] = arrived_ref[:, lanes].astype(jnp.float32)
    for slot in range(slots):
        for part in range(2):
            for field in range(fields):
                for tile in range(tiles):
                    first = 2 * slot + part
                    north = rows_ref[field, tile, pl.ds(first, levels, stride=stride), :]
                    south = rows_ref[field, tile, pl.ds(half + first, levels, stride=stride), :]
                    lanes = pl.ds(tile * LANES, LANES)
                    at = (part * fields + field) * levels
                    out_ref[slot, at : at + levels, lanes] = (north + south).astype(out_ref.dtype)
                    at += 2 * fields * levels
                    out_ref[slot, at : at + levels, lanes] = (north - south).astype(out_ref.dtype)


def fold(arrived, slots, levels, fields):
    row_total = 2 * fields * levels
    rows, width = arrived.shape
    tiles = width // (fields * LANES)
    shape = (slots, 2 * row_total, tiles * LANES)
    return pl.pallas_call(
        functools.partial(fold_kernel, slots, levels, fields),
        in_specs=[pl.BlockSpec((rows, width), lambda: (0, 0))],
        out_specs=pl.BlockSpec(shape, lambda: (0, 0, 0)),
        out_shape=jax.ShapeDtypeStruct(shape, jnp.bfloat16),
        scratch_shapes=[pltpu.VMEM((fields, tiles, rows, LANES), jnp.float32)],
        compiler_params=pltpu.CompilerParams(vmem_limit_bytes=VMEM_BYTES),
        cost_estimate=pl.CostEstimate(flops=2 * rows * width, bytes_accessed=4 * rows * width, transcendentals=0),
        name="fold",
    )(arrived)


def analysis_kernel(least, folded_ref, far_ref, even_ref, odd_ref, *refs):
    table_refs, out_ref = refs[:-1], refs[-1]
    row_total, degrees = out_ref.shape[1:]
    step = pl.program_id(0)

    def run(group):
        start = least[group]
        for j in range(out_ref.shape[0]):
            table = jnp.concatenate([ref[j, start:, :] for ref in table_refs], axis=1)
            sums = lax.dot_general(
                folded_ref[j], table, (((1,), (1,)), ((), ())), preferred_element_type=jnp.float32
            )
            kept = sums[:row_total] * even_ref[j, :, start:] + sums[row_total:] * odd_ref[j, :, start:]
            out_ref[j, :, start:] = kept
            if start:
                out_ref[j, :, :start] = jnp.zeros((row_total, start), out_ref.dtype)

    for group in range(len(least)):
        pl.when(step == group)(functools.partial(run, group))

    @pl.when(step == len(least))
    def _():
        width = far_ref.shape[2]
        out_ref[:, :, : degrees - width] = jnp.zeros((out_ref.shape[0], row_total, degrees - width), out_ref.dtype)
        out_ref[:, :, degrees - width :] = far_ref[...]


def analyze(folded, far, even, odd, legendre, row_total, least, chunk):
    slots, degrees, _ = legendre.shape
    block = 4
    near = len(least) - 1
    at, tiles = chunk
    mask_spec = pl.BlockSpec((block, 1, degrees), lambda i: (i, 0, 0))
    return pl.pallas_call(
        functools.partial(analysis_kernel, least),
        grid=(len(least) + 1,),
        in_specs=[
            pl.BlockSpec((block,) + folded.shape[1:], lambda i: (jnp.minimum(i, near), 0, 0)),
            pl.BlockSpec(far.shape, lambda i: (0, 0, 0)),
            mask_spec,
            mask_spec,
        ]
        + [
            pl.BlockSpec((block, degrees, LANES), lambda i, t=at + t: (jnp.minimum(i, near), 0, t))
            for t in range(tiles)
        ],
        out_specs=pl.BlockSpec((block, row_total, degrees), lambda i: (i, 0, 0)),
        out_shape=jax.ShapeDtypeStruct((slots, row_total, degrees), jnp.float32),
        compiler_params=pltpu.CompilerParams(vmem_limit_bytes=VMEM_BYTES),
        cost_estimate=pl.CostEstimate(
            flops=4 * slots * row_total * degrees * tiles * LANES,
            bytes_accessed=2 * slots * (degrees * tiles * LANES + 2 * row_total * (tiles * LANES + degrees)),
            transcendentals=0,
        ),
        name="analysis",
    )(folded, far, even, odd, *[legendre] * tiles)


def closing_kernel(
    levels, fields, least, chunk, arrived_ref, table_ref, base_ref, even_ref, odd_ref, out_ref, *refs
):
    got_ref, north_ref, south_ref, sems = refs[:4]
    held = refs[4:]
    at, tiles = chunk
    groups = len(least)
    _, row_total, degrees = base_ref.shape
    block = 4
    slots = block * groups
    stride = 2 * slots
    half = levels * stride
    arriving = [
        pltpu.make_async_copy(
            arrived_ref.at[:, pl.ds(field * tiles * LANES, tiles * LANES)], got_ref.at[field], sems.at[3 * groups + field]
        )
        for field in range(fields)
    ]
    tables, sums, results = [], [], []
    for group, start in enumerate(least):
        mine = pl.ds(group * block, block)
        left = pl.ds(start, degrees - start)
        lanes = pl.ds(at * LANES, tiles * LANES)
        held_table, held_sums = held[2 * group], held[2 * group + 1]
        tables.append(pltpu.make_async_copy(table_ref.at[mine, left, lanes], held_table, sems.at[3 * group]))
        sums.append(pltpu.make_async_copy(base_ref.at[mine, :, left], held_sums, sems.at[3 * group + 1]))
        results.append(pltpu.make_async_copy(held_sums, out_ref.at[mine, :, left], sems.at[3 * group + 2]))
    for copy in arriving:
        copy.start()
    for group in range(groups):
        tables[group].start()
        sums[group].start()
    for field in range(fields):
        arriving[field].wait()
        for tile in range(tiles):
            lanes = pl.ds(tile * LANES, LANES)
            north = got_ref[field, :half, lanes].astype(jnp.float32)
            south = got_ref[field, half:, lanes].astype(jnp.float32)
            north_ref[field, tile] = north + south
            south_ref[field, tile] = north - south
    for group, start in enumerate(least):
        tables[group].wait()
        sums[group].wait()
        held_table, held_sums = held[2 * group], held[2 * group + 1]
        for j in range(block):
            slot = group * block + j
            folded = jnp.concatenate(
                [
                    jnp.concatenate(
                        [
                            ref[field, tile, pl.ds(2 * slot + part, levels, stride=stride), :].astype(jnp.bfloat16)
                            for ref in (north_ref, south_ref)
                            for part in range(2)
                            for field in range(fields)
                        ],
                        axis=0,
                    )
                    for tile in range(tiles)
                ],
                axis=1,
            )
            more = lax.dot_general(
                folded, held_table[j], (((1,), (1,)), ((), ())), preferred_element_type=jnp.float32
            )
            even, odd = even_ref[slot, :, start:], odd_ref[slot, :, start:]
            held_sums[j] = held_sums[j] + more[:row_total] * even + more[row_total:] * odd
        results[group].start()
    for copy in results:
        copy.wait()


def close(arrived, base, even, odd, legendre, fields, levels, least, chunk):
    slots, row_total, degrees = base.shape
    block = 4
    rows, width = arrived.shape
    tiles = chunk[1]
    half = pltpu.VMEM((fields, tiles, rows // 2, LANES), jnp.float32)
    held = []
    for start in least:
        held.append(pltpu.VMEM((block, degrees - start, tiles * LANES), jnp.bfloat16))
        held.append(pltpu.VMEM((block, row_total, degrees - start), jnp.float32))
    anywhere = pl.BlockSpec(memory_space=pl.ANY)
    return pl.pallas_call(
        functools.partial(closing_kernel, levels, fields, least, chunk),
        in_specs=[anywhere, anywhere, anywhere] + [pl.BlockSpec(even.shape, lambda: (0, 0, 0))] * 2,
        out_specs=anywhere,
        out_shape=jax.ShapeDtypeStruct(base.shape, jnp.float32),
        input_output_aliases={2: 0},
        scratch_shapes=[
            pltpu.VMEM((fields, rows, tiles * LANES), jnp.bfloat16),
            half,
            half,
            pltpu.SemaphoreType.DMA((3 * len(least) + fields,)),
            *held,
        ],
        compiler_params=pltpu.CompilerParams(vmem_limit_bytes=VMEM_BYTES),
        cost_estimate=pl.CostEstimate(
            flops=4 * slots * row_total * degrees * tiles * LANES,
            bytes_accessed=8 * slots * row_total * degrees + 2 * rows * width,
            transcendentals=0,
        ),
        name="closing",
    )(arrived, legendre, base, even, odd)


def across_halves(value):
    planes = lax.axis_size("grp")
    return lax.ppermute(value, "grp", [(p, (p + planes // 2) % planes) for p in range(planes)])


def within_half(parts):
    bands, planes = lax.axis_size("band"), lax.axis_size("grp")
    half = planes // 2
    moved = [parts[0]]
    for x in range(1, len(parts)):
        pairs = []
        for band in range(bands):
            for plane in range(planes):
                level = (plane % half * bands + band) ^ x
                target = level % bands * planes + plane // half * half + level // bands
                pairs.append((band * planes + plane, target))
        moved.append(lax.ppermute(parts[x], AXES, pairs))
    return moved


def after(value, *others):
    return lax.optimization_barrier((value, others))[0]


def trig_kernel(cos_base_ref, sin_base_ref, cos_turn_ref, sin_turn_ref, cos_base_t, sin_base_t, cos_turn_t, sin_turn_t, by_wave_ref, by_lon_ref):
    for j in range(cos_base_ref.shape[1]):
        lanes = pl.ds(j * LANES, LANES)
        cos_base, sin_base = cos_base_ref[:, j : j + 1], sin_base_ref[:, j : j + 1]
        angles = cos_base * cos_turn_ref[...] - sin_base * sin_turn_ref[...]
        by_wave_ref[:, lanes] = angles.astype(by_wave_ref.dtype)
        cos_base, sin_base = cos_base_t[j : j + 1, :], sin_base_t[j : j + 1, :]
        angles = cos_base * cos_turn_t[...] - sin_base * sin_turn_t[...]
        by_lon_ref[lanes, :] = angles.astype(by_lon_ref.dtype)


def trig_tables(owner_table, lon_count, *others):
    waves = jnp.repeat(owner_table, 2).astype(jnp.float32)[:, None]
    quarter = jnp.tile(jnp.array([0, lon_count // 4], jnp.float32), owner_table.shape[0])[:, None]
    unit = 2.0 * math.pi / lon_count

    def angles(lon, turn):
        phase = waves * lon + turn
        return (phase - lon_count * jnp.floor(phase * (1.0 / lon_count))) * unit

    base = angles(jnp.arange(0, lon_count, LANES, dtype=jnp.float32)[None, :], quarter)
    turn = angles(jnp.arange(LANES, dtype=jnp.float32)[None, :], 0.0)
    depth = waves.shape[0]
    blocks = lon_count // LANES
    rows = 256
    small = pl.BlockSpec((rows, blocks), lambda i: (i, 0))
    wide = pl.BlockSpec((rows, LANES), lambda i: (i, 0))
    small_t = pl.BlockSpec((blocks, rows), lambda i: (0, i))
    wide_t = pl.BlockSpec((LANES, rows), lambda i: (0, i))
    parts = (jnp.cos(base), jnp.sin(base), jnp.cos(turn), jnp.sin(turn))
    parts = after(parts, *others)
    return pl.pallas_call(
        trig_kernel,
        grid=(depth // rows,),
        in_specs=[small, small, wide, wide, small_t, small_t, wide_t, wide_t],
        out_specs=[
            pl.BlockSpec((rows, lon_count), lambda i: (i, 0)),
            pl.BlockSpec((lon_count, rows), lambda i: (0, i)),
        ],
        out_shape=[
            jax.ShapeDtypeStruct((depth, lon_count), jnp.bfloat16),
            jax.ShapeDtypeStruct((lon_count, depth), jnp.bfloat16),
        ],
        compiler_params=pltpu.CompilerParams(vmem_limit_bytes=VMEM_BYTES),
        cost_estimate=pl.CostEstimate(
            flops=8 * depth * lon_count, bytes_accessed=4 * depth * lon_count, transcendentals=0
        ),
        name="trig",
    )(*parts, *[x.T for x in parts])


def exchange(rows):
    return lax.all_to_all(rows, AXES[::-1], split_axis=0, concat_axis=0, tiled=True)


def by_hemisphere_and_level(spectral, legendre, owner_table):
    slots, _, fields, levels, degrees = spectral.shape
    half_lat = legendre.shape[2]
    lon_count = 4 * half_lat
    row_total = 2 * fields * levels
    tiles = half_lat // LANES
    first = lax.axis_index(AXES).astype(jnp.int32) * slots
    spec_rows = spectral.reshape(slots, row_total, degrees)
    devices = 2 * levels
    least = tuple(4 * g * devices for g in range(slots // 4 - 1))
    near = slots - 4
    far_least, last_least = near * devices, (near + 2) * devices
    cut = tiles - tiles // 2
    chunks = [(0, cut), (cut, tiles - cut)]

    def send(spec, chunk):
        return synthesize(first.reshape(1), owner_table, spec, legendre, chunk, fields, levels, least)

    large = send(spec_rows, chunks[0])
    arrived = [exchange(large)]

    late_spec, late_table = after((spec_rows, legendre), large)
    table = jnp.concatenate(
        [
            late_table[near : near + 2, far_least:].reshape(-1, half_lat),
            late_table[near + 2 :, last_least:].reshape(-1, half_lat),
        ]
    )
    spec = late_spec[near:, :, far_least:]
    width = last_least - far_least
    packed = jnp.concatenate([spec[2, :, width:], spec[3, :, width:]], axis=1)
    spec = jnp.concatenate([spec[:2].reshape(2 * row_total, -1), packed])
    own_pack = jnp.concatenate([table, spec], axis=1)
    partner_pack = across_halves(own_pack)

    bands, planes = lax.axis_size("band"), lax.axis_size("grp")
    by_device = jnp.swapaxes(owner_table.reshape(bands, planes, slots), 0, 1).reshape(2, levels, slots)
    plane = lax.axis_index("grp").astype(jnp.int32)
    hemi = plane // (planes // 2)
    level = plane % (planes // 2) * bands + lax.axis_index("band").astype(jnp.int32)
    place = jnp.stack([hemi, level])
    far = by_device[:, :, near:]
    both_halves = jnp.concatenate([far[0], far[1]], axis=1)
    swapped = jnp.concatenate([far[1], far[0]], axis=1)
    far_waves = jnp.where(hemi == 0, both_halves, swapped)
    far_waves = jnp.take(far_waves, jnp.arange(levels, dtype=jnp.int32) ^ level, axis=0)
    waves = jnp.concatenate([by_device[:, :, :near].reshape(-1), far_waves.reshape(-1)])

    small = send(after(spec_rows, large), chunks[1])
    by_wave, by_lon = trig_tables(after(waves, large), lon_count, small)
    far_rows = far_synthesize(
        place, far_waves[0] - far_least, own_pack, partner_pack, levels, fields, 1.0 / math.sqrt(degrees)
    )
    arrived.append(exchange(after(small, by_wave, *far_rows, *arrived)))
    far_rows = jnp.concatenate(within_half(far_rows))
    zonal = [
        longitudes(rows, far_rows, by_lon, by_wave, fields, chunk) for rows, chunk in zip(arrived, chunks)
    ]
    returned = [exchange(zonal[0][0])]
    far_zonal = jnp.concatenate([zonal[0][1], zonal[1][1]], axis=1)
    far_zonal = within_half([far_zonal[16 * x : 16 * x + 16] for x in range(levels)])
    own_sums, partner_sums = far_analyze(place, own_pack, partner_pack, far_zonal, levels, fields, chunks)
    returned.append(exchange(after(zonal[1][0], partner_sums, *returned)))
    other_sums = across_halves(partner_sums).astype(jnp.float32)
    north = jnp.where(hemi == 0, own_sums, other_sums)
    south = jnp.where(hemi == 0, other_sums, own_sums)
    wavenumber = lax.dynamic_slice_in_dim(after(owner_table, by_wave), first, slots)
    distance = jnp.arange(degrees, dtype=jnp.int32)[None, :] - wavenumber[:, None]
    scale = 1.0 / math.sqrt(2 * half_lat)
    even = jnp.where((distance >= 0) & (distance % 2 == 0), scale, 0.0).astype(jnp.float32)[:, None, :]
    odd = jnp.where((distance >= 0) & (distance % 2 != 0), scale, 0.0).astype(jnp.float32)[:, None, :]

    def unpack(sums):
        sums = sums.reshape(3, row_total, -1)
        empty = jnp.zeros((row_total, width), jnp.float32)
        third = jnp.concatenate([empty, sums[2, :, :width]], axis=1)
        fourth = jnp.concatenate([empty, sums[2, :, width:]], axis=1)
        return jnp.concatenate([sums[:2], third[None], fourth[None]])

    far_even, far_odd = even[near:, :, far_least:], odd[near:, :, far_least:]
    far_out = unpack(north + south) * far_even + unpack(north - south) * far_odd
    folded = fold(returned[0], near, levels, fields)
    base = analyze(folded, far_out, even, odd, legendre, row_total, least, chunks[0])
    last = after(returned[1], base)
    out = close(last, base, even, odd, legendre, fields, levels, least, chunks[1])
    return out.reshape(slots, 2, fields, levels, degrees)


def make_trig(wavenumber, lon_count):
    lon_index = jnp.arange(lon_count, dtype=jnp.int32)
    phases = wavenumber[:, None] * lon_index[None, :] % lon_count
    angles = phases.astype(jnp.float32) * (2.0 * math.pi / lon_count)
    return jnp.stack([jnp.cos(angles), -jnp.sin(angles)], axis=1).astype(jnp.bfloat16)


def by_level_and_latitude(spectral, legendre, owner_table):
    slot_count, _, fields, levels, degrees = spectral.shape
    half_lat = legendre.shape[2]
    lat_count = 2 * half_lat
    lon_count = 2 * lat_count
    wave_count = owner_table.shape[0]
    band_count = lax.axis_size("band")
    group_count = lax.axis_size("grp")
    device_count = band_count * group_count
    level_block = levels // band_count
    lat_block = lat_count // group_count
    row_total = 2 * fields * levels
    row_width = fields * level_block * lat_block
    slot_start = lax.axis_index(("band", "grp")) * slot_count
    wavenumber = lax.dynamic_slice_in_dim(owner_table, slot_start, slot_count)
    degree_index = jnp.arange(degrees, dtype=jnp.int32)
    keep_mask = (degree_index[None, :] >= wavenumber[:, None]).astype(jnp.bfloat16)
    odd_part = (degree_index[None, :] - wavenumber[:, None]) % 2
    flip_sign = (1 - 2 * odd_part).astype(jnp.bfloat16)
    spec_rows = spectral.reshape(slot_count, row_total, degrees) * keep_mask[:, None, :]
    both_rows = jnp.concatenate([spec_rows, spec_rows * flip_sign[:, None, :]], axis=1)
    halves = jnp.einsum("srn,snt->srt", both_rows, legendre, preferred_element_type=jnp.float32)
    northern = halves[:, :row_total]
    mirrored = halves[:, row_total:]
    fourier = jnp.concatenate([northern, jnp.flip(mirrored, axis=2)], axis=2)
    fourier = fourier.reshape(
        slot_count, 2, fields, band_count, level_block, group_count, lat_block
    )
    fourier = jnp.transpose(fourier, (0, 1, 2, 3, 5, 4, 6))
    fourier_low = (fourier * (1.0 / math.sqrt(degrees))).astype(jnp.bfloat16)
    packed = fourier_low.reshape(1, slot_count, 2, fields, device_count, level_block, lat_block)
    arrived = lax.all_to_all(packed, ("band", "grp"), split_axis=4, concat_axis=0, tiled=True)
    arrived = arrived.reshape(-1, 2, row_width)
    trig_rows = make_trig(owner_table, lon_count)
    grid_values = jnp.einsum("scw,scl->wl", arrived, trig_rows, preferred_element_type=jnp.float32)
    grid_values = (grid_values * (1.0 / math.sqrt(wave_count))).reshape(
        fields, level_block * lat_block, lon_count
    )
    product = (grid_values * jnp.roll(grid_values, -1, axis=0)).astype(jnp.bfloat16)
    zonal_coeffs = jnp.einsum(
        "wl,scl->scw",
        product.reshape(row_width, lon_count),
        trig_rows,
        preferred_element_type=jnp.float32,
    )
    zonal_coeffs = (zonal_coeffs * (2.0 / math.sqrt(lon_count))).astype(jnp.bfloat16)
    sendback = zonal_coeffs.reshape(device_count, slot_count, 2, fields, 1, level_block, lat_block)
    returned = lax.all_to_all(sendback, ("band", "grp"), split_axis=0, concat_axis=4, tiled=True)
    returned = returned.reshape(
        slot_count, 2, fields, band_count, group_count, level_block, lat_block
    )
    returned = jnp.transpose(returned, (0, 1, 2, 3, 5, 4, 6)).reshape(slot_count, row_total, lat_count)
    northern_part = returned[:, :, :half_lat].astype(jnp.float32)
    mirror_part = jnp.flip(returned[:, :, half_lat:], axis=2).astype(jnp.float32)
    plus_part = (northern_part + mirror_part).astype(jnp.bfloat16)
    minus_part = (northern_part - mirror_part).astype(jnp.bfloat16)
    stacked = jnp.concatenate([plus_part, minus_part], axis=1)
    projected = jnp.einsum("srt,snt->srn", stacked, legendre, preferred_element_type=jnp.float32)
    even_rows = flip_sign[:, None, :] > 0
    chosen = jnp.where(even_rows, projected[:, :row_total], projected[:, row_total:])
    chosen = chosen * keep_mask.astype(jnp.float32)[:, None, :] * (1.0 / math.sqrt(lat_count))
    return chosen.reshape(slot_count, 2, fields, levels, degrees)


def on_device(spectral, legendre, owner_table):
    slots, _, _, levels, _ = spectral.shape
    whole_hemispheres = lax.axis_size("band") * lax.axis_size("grp") == 2 * levels
    halves = lax.axis_size("grp") % 2 == 0 and levels & (levels - 1) == 0
    few_left = legendre.shape[1] - (slots - 4) * 2 * levels == LANES
    if whole_hemispheres and halves and few_left and legendre.shape[2] % LANES == 0 and legendre.shape[2] > LANES and slots % 4 == 0 and levels % 16 == 0:
        return by_hemisphere_and_level(spectral, legendre, owner_table)
    return by_level_and_latitude(spectral, legendre, owner_table)


def solution(mesh):
    placed = (P(("band", "grp"), None, None, None, None), P(("band", "grp"), None, None), P())
    return jax.shard_map(
        on_device,
        mesh=mesh,
        in_specs=placed,
        out_specs=P(("band", "grp"), None, None, None, None),
        check_vma=False,
    )
```

```python
import functools
import math

import jax
import jax.numpy as jnp
from jax import lax
from jax.experimental import pallas as pl
from jax.experimental.pallas import tpu as pltpu
from jax.sharding import PartitionSpec as P

LANES = 128
AXES = ("band", "grp")
VMEM_BYTES = 62 * 1024 * 1024


def padded(slots):
    return 2 * slots + 8


def synthesis_kernel(
    slots, levels, fields, least, chunk, scale, first_ref, owner_ref, spec_ref, table_ref, out_ref, rows_ref, sems, *held
):
    at, tiles = chunk
    groups = len(least)
    block = 4
    row_total, degrees = spec_ref.shape[1:]
    stride = padded(slots)
    copies = []
    for group, start in enumerate(least):
        mine = pl.ds(group * block, block)
        left = pl.ds(start, degrees - start)
        lanes = pl.ds(at * LANES, tiles * LANES)
        copies.append(
            (
                pltpu.make_async_copy(spec_ref.at[mine, :, left], held[2 * group], sems.at[2 * group]),
                pltpu.make_async_copy(table_ref.at[mine, left, lanes], held[2 * group + 1], sems.at[2 * group + 1]),
            )
        )
    order = range(groups - 1, -1, -1)
    for group in order:
        for copy in copies[group]:
            copy.start()
    for group in order:
        for copy in copies[group]:
            copy.wait()
        for j in range(block):
            spec = held[2 * group][j]
            wave = owner_ref[first_ref[0] + group * block + j]
            distance = lax.broadcasted_iota(jnp.int32, (1, spec.shape[1]), 1) + (least[group] - wave)
            keep = jnp.where(distance >= 0, 1.0, 0.0)
            flip = jnp.where(distance % 2 == 0, keep, -keep)
            both = jnp.concatenate([spec * keep.astype(spec.dtype), spec * flip.astype(spec.dtype)], axis=0)
            halves = jnp.dot(both, held[2 * group + 1][j], preferred_element_type=jnp.float32) * scale
            first = 2 * (group * block + j)
            for hemi in range(2):
                for part in range(2):
                    for field in range(fields):
                        row = hemi * row_total + (part * fields + field) * levels
                        target = pl.ds(hemi * levels * stride + first + part, levels, stride=stride)
                        for tile in range(tiles):
                            lanes = slice(tile * LANES, (tile + 1) * LANES)
                            rows_ref[field, tile, target, :] = halves[row : row + levels, lanes]
    for field in range(fields):
        for tile in range(tiles):
            lanes = pl.ds((field * tiles + tile) * LANES, LANES)
            rows = rows_ref[field, tile].reshape(2 * levels, stride, LANES)[:, : 2 * slots]
            out_ref[:, lanes] = rows.reshape(out_ref.shape[0], LANES).astype(out_ref.dtype)


def synthesize(first, owner_table, spec_rows, legendre, chunk, fields, levels, least):
    _, row_total, degrees = spec_rows.shape
    block = 4
    slots = block * len(least)
    rows = 2 * levels * 2 * slots
    tiles = chunk[1]
    shape = (rows, fields * tiles * LANES)
    held = []
    for start in least:
        held.append(pltpu.VMEM((block, row_total, degrees - start), jnp.bfloat16))
        held.append(pltpu.VMEM((block, degrees - start, tiles * LANES), jnp.bfloat16))
    return pl.pallas_call(
        functools.partial(synthesis_kernel, slots, levels, fields, least, chunk, 1.0 / math.sqrt(degrees)),
        in_specs=[pl.BlockSpec(memory_space=pltpu.SMEM)] * 2 + [pl.BlockSpec(memory_space=pl.ANY)] * 2,
        out_specs=pl.BlockSpec(shape, lambda: (0, 0)),
        out_shape=jax.ShapeDtypeStruct(shape, jnp.bfloat16),
        scratch_shapes=[
            pltpu.VMEM((fields, tiles, 2 * levels * padded(slots), LANES), jnp.float32),
            pltpu.SemaphoreType.DMA((2 * len(least),)),
            *held,
        ],
        compiler_params=pltpu.CompilerParams(vmem_limit_bytes=VMEM_BYTES),
        cost_estimate=pl.CostEstimate(
            flops=4 * slots * row_total * degrees * tiles * LANES,
            bytes_accessed=2 * slots * degrees * (row_total + tiles * LANES) + 2 * rows * shape[1],
            transcendentals=0,
        ),
        name="synthesis",
    )(first, owner_table, spec_rows, legendre)


def longitude_kernel(
    fields, chunk, grid_scale, zonal_scale, rows_ref, far_ref, by_lon_ref, by_wave_ref, out_ref, far_out_ref, sum_ref
):
    step = pl.program_id(0)
    near = rows_ref.shape[0]
    values = jnp.dot(by_lon_ref[:, :near], rows_ref[...], preferred_element_type=jnp.float32)
    one = values.shape[1] // fields
    each = far_ref.shape[1] // fields
    starts = [field * each + chunk[0] * LANES for field in range(fields)]
    far = jnp.concatenate([far_ref[:, start : start + one] for start in starts], axis=1)
    values = values + jnp.dot(by_lon_ref[:, near:], far, preferred_element_type=jnp.float32)
    values = values * grid_scale
    following = jnp.concatenate([values[:, one:], values[:, :one]], axis=1)
    product = (values * following).astype(jnp.bfloat16)
    share = jnp.dot(by_wave_ref[...], product, preferred_element_type=jnp.float32)

    @pl.when(step == 0)
    def _():
        sum_ref[...] = share

    @pl.when(step > 0)
    def _():
        sum_ref[...] += share

    @pl.when(step == pl.num_programs(0) - 1)
    def _():
        out_ref[...] = (sum_ref[:near, :] * zonal_scale).astype(out_ref.dtype)
        far_out_ref[...] = (sum_ref[near:, :] * zonal_scale).astype(far_out_ref.dtype)


def longitudes(rows, far, by_lon, by_wave, fields, chunk):
    depth, width = rows.shape[0] + far.shape[0], rows.shape[1]
    lon_count = by_lon.shape[0]
    lon_block = lon_count // 5
    near_spec = pl.BlockSpec(rows.shape, lambda i: (0, 0))
    far_out = jax.ShapeDtypeStruct((far.shape[0], width), jnp.bfloat16)
    return pl.pallas_call(
        functools.partial(longitude_kernel, fields, chunk, 1.0 / math.sqrt(depth // 2), 2.0 / math.sqrt(lon_count)),
        grid=(lon_count // lon_block,),
        in_specs=[
            near_spec,
            pl.BlockSpec(far.shape, lambda i: (0, 0)),
            pl.BlockSpec((lon_block, depth), lambda i: (i, 0)),
            pl.BlockSpec((depth, lon_block), lambda i: (0, i)),
        ],
        out_specs=[near_spec, pl.BlockSpec(far_out.shape, lambda i: (0, 0))],
        out_shape=[jax.ShapeDtypeStruct(rows.shape, jnp.bfloat16), far_out],
        scratch_shapes=[pltpu.VMEM((depth, width), jnp.float32)],
        compiler_params=pltpu.CompilerParams(vmem_limit_bytes=VMEM_BYTES),
        cost_estimate=pl.CostEstimate(
            flops=4 * depth * width * lon_count,
            bytes_accessed=4 * depth * (width + lon_count),
            transcendentals=0,
        ),
        name="longitudes",
    )(rows, far, by_lon, by_wave)


def pack_kernel(near, spec_ref, table_ref, out_ref, tail_ref, sems):
    degrees, half_lat = table_ref.shape[1:]
    half = LANES // 2
    copies = []

    def fetch(source, target):
        copies.append(pltpu.make_async_copy(source, target, sems.at[len(copies)]))
        copies[-1].start()

    lanes, sides = pl.ds(0, half_lat), pl.ds(half_lat, LANES)
    for slot in range(2):
        rows = pl.ds(slot * LANES, LANES)
        fetch(table_ref.at[near + slot, pl.ds(degrees - LANES, LANES), :], out_ref.at[rows, lanes])
        fetch(spec_ref.at[near + slot, :, pl.ds(degrees - LANES, LANES)], out_ref.at[rows, sides])
    for slot in range(2):
        rows = pl.ds(2 * LANES + slot * half, half)
        fetch(table_ref.at[near + 2 + slot, pl.ds(degrees - half, half), :], out_ref.at[rows, lanes])
        fetch(spec_ref.at[near + 2 + slot, :, pl.ds(degrees - LANES, LANES)], tail_ref.at[slot])
    for copy in copies:
        copy.wait()
    third = pltpu.roll(tail_ref[0].astype(jnp.float32), half, 1)
    lower = lax.broadcasted_iota(jnp.int32, third.shape, 1) < half
    both = jnp.where(lower, third, tail_ref[1].astype(jnp.float32))
    out_ref[pl.ds(2 * LANES, LANES), sides] = both.astype(out_ref.dtype)


def pack(spec_rows, legendre, near):
    shape = (3 * LANES, legendre.shape[2] + LANES)
    return pl.pallas_call(
        functools.partial(pack_kernel, near),
        in_specs=[pl.BlockSpec(memory_space=pl.ANY)] * 2,
        out_specs=pl.BlockSpec(shape, lambda: (0, 0)),
        out_shape=jax.ShapeDtypeStruct(shape, jnp.bfloat16),
        scratch_shapes=[
            pltpu.VMEM((2, spec_rows.shape[1], LANES), jnp.bfloat16),
            pltpu.SemaphoreType.DMA((8,)),
        ],
        compiler_params=pltpu.CompilerParams(vmem_limit_bytes=VMEM_BYTES),
        cost_estimate=pl.CostEstimate(flops=0, bytes_accessed=4 * shape[0] * shape[1], transcendentals=0),
        name="pack",
    )(spec_rows, legendre)


def far_synthesis_kernel(levels, fields, scale, place_ref, waves_ref, own_ref, partner_ref, *refs):
    out_refs, rows_ref = refs[:-1], refs[-1]
    tiles = rows_ref.shape[1]
    half_lat = tiles * LANES
    stride = rows_ref.shape[2] // levels
    degree = lax.broadcasted_iota(jnp.int32, (1, LANES), 1)
    for slot in range(8):
        pack_ref, local = (own_ref, slot) if slot < 4 else (partner_ref, slot - 4)
        rows = pl.ds(min(local, 2) * LANES, LANES)
        distance = degree - waves_ref[slot] + (LANES // 2 if local == 2 else 0)
        keep = jnp.where(distance >= 0, 1.0, 0.0)
        if local >= 2:
            keep = jnp.where((degree < LANES // 2) if local == 2 else (degree >= LANES // 2), keep, 0.0)
        turned = jnp.where(distance % 2 == 0, keep, -keep)
        sign = jnp.where(place_ref[0] == 0, keep, turned)
        spec = pack_ref[rows, half_lat:]
        table = pack_ref[rows, :half_lat]
        sums = jnp.dot(spec * sign.astype(spec.dtype), table, preferred_element_type=jnp.float32) * scale
        for part in range(2):
            for field in range(fields):
                row = (part * fields + field) * levels
                for tile in range(tiles):
                    target = pl.ds(2 * slot + part, levels, stride=stride)
                    rows_ref[field, tile, target, :] = sums[row : row + levels, tile * LANES : (tile + 1) * LANES]
    for apart, out_ref in enumerate(out_refs):
        rows = pl.ds(pl.multiple_of((place_ref[1] ^ apart) * stride, stride), stride)
        for field in range(fields):
            for tile in range(tiles):
                lanes = pl.ds((field * tiles + tile) * LANES, LANES)
                out_ref[:, lanes] = rows_ref[field, tile, rows, :].astype(out_ref.dtype)


def far_synthesize(place, waves, own, partner, levels, fields, scale):
    tiles = own.shape[1] // LANES - 1
    shape = (16, fields * tiles * LANES)
    whole = pl.BlockSpec(own.shape, lambda: (0, 0))
    return pl.pallas_call(
        functools.partial(far_synthesis_kernel, levels, fields, scale),
        in_specs=[pl.BlockSpec(memory_space=pltpu.SMEM)] * 2 + [whole, whole],
        out_specs=[pl.BlockSpec(shape, lambda: (0, 0))] * levels,
        out_shape=[jax.ShapeDtypeStruct(shape, jnp.bfloat16)] * levels,
        scratch_shapes=[pltpu.VMEM((fields, tiles, 16 * levels, LANES), jnp.float32)],
        compiler_params=pltpu.CompilerParams(vmem_limit_bytes=VMEM_BYTES),
        cost_estimate=pl.CostEstimate(
            flops=16 * 2 * fields * levels * LANES * tiles * LANES, bytes_accessed=4 * own.size, transcendentals=0
        ),
        name="far_synthesis",
    )(place, waves, own, partner)


def far_analysis_kernel(levels, fields, chunks, place_ref, own_ref, partner_ref, *refs):
    zonal_refs, own_out_ref, partner_out_ref, rows_ref = refs[:levels], refs[-3], refs[-2], refs[-1]
    tiles = rows_ref.shape[1]
    stride = rows_ref.shape[2] // levels
    for apart, zonal_ref in enumerate(zonal_refs):
        rows = pl.ds(pl.multiple_of((place_ref[1] ^ apart) * stride, stride), stride)
        offset = 0
        for at, count in chunks:
            for field in range(fields):
                for tile in range(at, at + count):
                    rows_ref[field, tile, rows, :] = zonal_ref[:, pl.ds(offset, LANES)].astype(jnp.float32)
                    offset += LANES
    lower = lax.broadcasted_iota(jnp.int32, (1, LANES), 1) < LANES // 2
    for pack_ref, out_ref, base in ((own_ref, own_out_ref, 0), (partner_ref, partner_out_ref, 4)):
        sums = []
        for local in range(4):
            rows = pl.ds(min(local, 2) * LANES, LANES)
            zonal = jnp.concatenate(
                [
                    jnp.concatenate(
                        [
                            rows_ref[field, tile, pl.ds(2 * (base + local) + part, levels, stride=stride), :]
                            for part in range(2)
                            for field in range(fields)
                        ],
                        axis=0,
                    ).astype(jnp.bfloat16)
                    for tile in range(tiles)
                ],
                axis=1,
            )
            table = pack_ref[rows, : tiles * LANES]
            sums.append(
                lax.dot_general(zonal, table, (((1,), (1,)), ((), ())), preferred_element_type=jnp.float32)
            )
        sums[2] = jnp.where(lower, sums[2], sums[3])
        size = sums[0].shape[0]
        for block in range(3):
            out_ref[pl.ds(block * size, size), :] = sums[block].astype(out_ref.dtype)


def far_analyze(place, own, partner, zonal, levels, fields, chunks):
    tiles = own.shape[1] // LANES - 1
    shape = (3 * 2 * fields * levels, LANES)
    whole = pl.BlockSpec(own.shape, lambda: (0, 0))
    out_spec = pl.BlockSpec(shape, lambda: (0, 0))
    return pl.pallas_call(
        functools.partial(far_analysis_kernel, levels, fields, chunks),
        in_specs=[pl.BlockSpec(memory_space=pltpu.SMEM), whole, whole]
        + [pl.BlockSpec(x.shape, lambda: (0, 0)) for x in zonal],
        out_specs=[out_spec, out_spec],
        out_shape=[jax.ShapeDtypeStruct(shape, jnp.float32), jax.ShapeDtypeStruct(shape, jnp.bfloat16)],
        scratch_shapes=[pltpu.VMEM((fields, tiles, 16 * levels, LANES), jnp.float32)],
        compiler_params=pltpu.CompilerParams(vmem_limit_bytes=VMEM_BYTES),
        cost_estimate=pl.CostEstimate(
            flops=16 * 2 * fields * levels * LANES * tiles * LANES, bytes_accessed=4 * own.size, transcendentals=0
        ),
        name="far_analysis",
    )(place, own, partner, *zonal)


def fold_kernel(slots, levels, fields, arrived_ref, out_ref, rows_ref):
    tiles = rows_ref.shape[1]
    stride = padded(slots)
    half = levels * stride
    for field in range(fields):
        for tile in range(tiles):
            lanes = pl.ds((field * tiles + tile) * LANES, LANES)
            rows = arrived_ref[:, lanes].astype(jnp.float32)
            for source in range(2 * levels):
                mine = rows[2 * slots * source : 2 * slots * (source + 1)]
                rows_ref[field, tile, pl.ds(stride * source, 2 * slots), :] = mine
    for slot in range(slots):
        for part in range(2):
            for field in range(fields):
                for tile in range(tiles):
                    first = 2 * slot + part
                    north = rows_ref[field, tile, pl.ds(first, levels, stride=stride), :]
                    south = rows_ref[field, tile, pl.ds(half + first, levels, stride=stride), :]
                    lanes = pl.ds(tile * LANES, LANES)
                    at = (part * fields + field) * levels
                    out_ref[slot, at : at + levels, lanes] = (north + south).astype(out_ref.dtype)
                    at += 2 * fields * levels
                    out_ref[slot, at : at + levels, lanes] = (north - south).astype(out_ref.dtype)


def fold(arrived, slots, levels, fields):
    row_total = 2 * fields * levels
    rows, width = arrived.shape
    tiles = width // (fields * LANES)
    shape = (slots, 2 * row_total, tiles * LANES)
    return pl.pallas_call(
        functools.partial(fold_kernel, slots, levels, fields),
        in_specs=[pl.BlockSpec((rows, width), lambda: (0, 0))],
        out_specs=pl.BlockSpec(shape, lambda: (0, 0, 0)),
        out_shape=jax.ShapeDtypeStruct(shape, jnp.bfloat16),
        scratch_shapes=[pltpu.VMEM((fields, tiles, 2 * levels * padded(slots), LANES), jnp.float32)],
        compiler_params=pltpu.CompilerParams(vmem_limit_bytes=VMEM_BYTES),
        cost_estimate=pl.CostEstimate(flops=2 * rows * width, bytes_accessed=4 * rows * width, transcendentals=0),
        name="fold",
    )(arrived)


def analysis_kernel(least, folded_ref, even_ref, odd_ref, *refs):
    table_refs, out_ref = refs[:-1], refs[-1]
    row_total, degrees = out_ref.shape[1:]
    step = pl.program_id(0)

    def run(group):
        start = least[group]
        for j in range(out_ref.shape[0]):
            table = jnp.concatenate([ref[j, start:, :] for ref in table_refs], axis=1)
            sums = lax.dot_general(
                folded_ref[j], table, (((1,), (1,)), ((), ())), preferred_element_type=jnp.float32
            )
            kept = sums[:row_total] * even_ref[j, :, start:] + sums[row_total:] * odd_ref[j, :, start:]
            out_ref[j, :, start:] = kept
            if start:
                out_ref[j, :, :start] = jnp.zeros((row_total, start), out_ref.dtype)

    for group in range(len(least)):
        pl.when(step == group)(functools.partial(run, group))

    @pl.when(step == len(least))
    def _():
        out_ref[...] = jnp.zeros(out_ref.shape, out_ref.dtype)


def analyze(folded, even, odd, legendre, row_total, least, chunk):
    slots, degrees, _ = legendre.shape
    block = 4
    near = len(least) - 1
    at, tiles = chunk
    mask_spec = pl.BlockSpec((block, 1, degrees), lambda i: (i, 0, 0))
    return pl.pallas_call(
        functools.partial(analysis_kernel, least),
        grid=(len(least) + 1,),
        in_specs=[
            pl.BlockSpec((block,) + folded.shape[1:], lambda i: (jnp.minimum(i, near), 0, 0)),
            mask_spec,
            mask_spec,
        ]
        + [
            pl.BlockSpec((block, degrees, LANES), lambda i, t=at + t: (jnp.minimum(i, near), 0, t))
            for t in range(tiles)
        ],
        out_specs=pl.BlockSpec((block, row_total, degrees), lambda i: (i, 0, 0)),
        out_shape=jax.ShapeDtypeStruct((slots, row_total, degrees), jnp.float32),
        compiler_params=pltpu.CompilerParams(vmem_limit_bytes=VMEM_BYTES),
        cost_estimate=pl.CostEstimate(
            flops=4 * slots * row_total * degrees * tiles * LANES,
            bytes_accessed=2 * slots * (degrees * tiles * LANES + 2 * row_total * (tiles * LANES + degrees)),
            transcendentals=0,
        ),
        name="analysis",
    )(folded, even, odd, *[legendre] * tiles)


def closing_kernel(
    levels, fields, least, chunk, hemi_ref, arrived_ref, table_ref, base_ref, even_ref, odd_ref, own_ref, other_ref, out_ref, *refs
):
    got_ref, north_ref, south_ref, far_ref, sems = refs[:5]
    held = refs[5:]
    at, tiles = chunk
    groups = len(least)
    _, row_total, degrees = base_ref.shape
    block = 4
    slots = block * groups
    each = 2 * slots
    stride = padded(slots)
    half = levels * each
    arriving = [
        pltpu.make_async_copy(
            arrived_ref.at[:, pl.ds(field * tiles * LANES, tiles * LANES)], got_ref.at[field], sems.at[3 * groups + field]
        )
        for field in range(fields)
    ]
    tables, sums, results = [], [], []
    for group, start in enumerate(least):
        mine = pl.ds(group * block, block)
        left = pl.ds(start, degrees - start)
        lanes = pl.ds(at * LANES, tiles * LANES)
        held_table, held_sums = held[2 * group], held[2 * group + 1]
        tables.append(pltpu.make_async_copy(table_ref.at[mine, left, lanes], held_table, sems.at[3 * group]))
        sums.append(pltpu.make_async_copy(base_ref.at[mine, :, left], held_sums, sems.at[3 * group + 1]))
        results.append(pltpu.make_async_copy(held_sums, out_ref.at[mine, :, left], sems.at[3 * group + 2]))
    for copy in arriving:
        copy.start()
    for group in range(groups):
        tables[group].start()
        sums[group].start()
    for local in range(4):
        rows = pl.ds(min(local, 2) * row_total, row_total)
        own, other = own_ref[rows, :], other_ref[rows, :].astype(jnp.float32)
        both, change = own + other, jnp.where(hemi_ref[0] == 0, own - other, other - own)
        if local == 2:
            both, change = pltpu.roll(both, LANES // 2, 1), pltpu.roll(change, LANES // 2, 1)
        even = even_ref[slots + local, :, degrees - LANES :]
        odd = odd_ref[slots + local, :, degrees - LANES :]
        far_ref[local] = both * even + change * odd
    finished = pltpu.make_async_copy(
        far_ref, out_ref.at[pl.ds(slots, 4), :, pl.ds(degrees - LANES, LANES)], sems.at[3 * groups + fields]
    )
    finished.start()
    for field in range(fields):
        arriving[field].wait()
        for tile in range(tiles):
            lanes = pl.ds(tile * LANES, LANES)
            north = got_ref[field, :half, lanes].astype(jnp.float32)
            south = got_ref[field, half:, lanes].astype(jnp.float32)
            plus, minus = north + south, north - south
            for level in range(levels):
                rows = pl.ds(stride * level, each)
                north_ref[field, tile, rows, :] = plus[each * level : each * (level + 1)]
                south_ref[field, tile, rows, :] = minus[each * level : each * (level + 1)]
    for group, start in enumerate(least):
        tables[group].wait()
        sums[group].wait()
        held_table, held_sums = held[2 * group], held[2 * group + 1]
        for j in range(block):
            slot = group * block + j
            folded = jnp.concatenate(
                [
                    jnp.concatenate(
                        [
                            ref[field, tile, pl.ds(2 * slot + part, levels, stride=stride), :].astype(jnp.bfloat16)
                            for ref in (north_ref, south_ref)
                            for part in range(2)
                            for field in range(fields)
                        ],
                        axis=0,
                    )
                    for tile in range(tiles)
                ],
                axis=1,
            )
            more = lax.dot_general(
                folded, held_table[j], (((1,), (1,)), ((), ())), preferred_element_type=jnp.float32
            )
            even, odd = even_ref[slot, :, start:], odd_ref[slot, :, start:]
            held_sums[j] = held_sums[j] + more[:row_total] * even + more[row_total:] * odd
        results[group].start()
    for copy in results:
        copy.wait()
    finished.wait()


def close(hemi, own, other, arrived, base, even, odd, legendre, fields, levels, least, chunk):
    slots, row_total, degrees = base.shape
    block = 4
    rows, width = arrived.shape
    tiles = chunk[1]
    half = pltpu.VMEM((fields, tiles, levels * padded(block * len(least)), LANES), jnp.float32)
    held = []
    for start in least:
        held.append(pltpu.VMEM((block, degrees - start, tiles * LANES), jnp.bfloat16))
        held.append(pltpu.VMEM((block, row_total, degrees - start), jnp.float32))
    anywhere = pl.BlockSpec(memory_space=pl.ANY)
    return pl.pallas_call(
        functools.partial(closing_kernel, levels, fields, least, chunk),
        in_specs=[pl.BlockSpec(memory_space=pltpu.SMEM), anywhere, anywhere, anywhere]
        + [pl.BlockSpec(even.shape, lambda: (0, 0, 0))] * 2
        + [pl.BlockSpec(own.shape, lambda: (0, 0))] * 2,
        out_specs=anywhere,
        out_shape=jax.ShapeDtypeStruct(base.shape, jnp.float32),
        input_output_aliases={3: 0},
        scratch_shapes=[
            pltpu.VMEM((fields, rows, tiles * LANES), jnp.bfloat16),
            half,
            half,
            pltpu.VMEM((4, row_total, LANES), jnp.float32),
            pltpu.SemaphoreType.DMA((3 * len(least) + fields + 1,)),
            *held,
        ],
        compiler_params=pltpu.CompilerParams(vmem_limit_bytes=VMEM_BYTES),
        cost_estimate=pl.CostEstimate(
            flops=4 * slots * row_total * degrees * tiles * LANES,
            bytes_accessed=8 * slots * row_total * degrees + 2 * rows * width,
            transcendentals=0,
        ),
        name="closing",
    )(hemi, arrived, legendre, base, even, odd, own, other)


def across_halves(value):
    planes = lax.axis_size("grp")
    return lax.ppermute(value, "grp", [(p, (p + planes // 2) % planes) for p in range(planes)])


def within_half(parts):
    bands, planes = lax.axis_size("band"), lax.axis_size("grp")
    half = planes // 2
    moved = [parts[0]]
    for x in range(1, len(parts)):
        pairs = []
        for band in range(bands):
            for plane in range(planes):
                level = (plane % half * bands + band) ^ x
                target = level % bands * planes + plane // half * half + level // bands
                pairs.append((band * planes + plane, target))
        moved.append(lax.ppermute(parts[x], AXES, pairs))
    return moved


def after(value, *others):
    return lax.optimization_barrier((value, others))[0]


def trig_kernel(cos_base_ref, sin_base_ref, cos_turn_ref, sin_turn_ref, cos_base_t, sin_base_t, cos_turn_t, sin_turn_t, by_wave_ref, by_lon_ref):
    for j in range(cos_base_ref.shape[1]):
        lanes = pl.ds(j * LANES, LANES)
        cos_base, sin_base = cos_base_ref[:, j : j + 1], sin_base_ref[:, j : j + 1]
        angles = cos_base * cos_turn_ref[...] - sin_base * sin_turn_ref[...]
        by_wave_ref[:, lanes] = angles.astype(by_wave_ref.dtype)
        cos_base, sin_base = cos_base_t[j : j + 1, :], sin_base_t[j : j + 1, :]
        angles = cos_base * cos_turn_t[...] - sin_base * sin_turn_t[...]
        by_lon_ref[lanes, :] = angles.astype(by_lon_ref.dtype)


def trig_tables(owner_table, lon_count, *others):
    waves = jnp.repeat(owner_table, 2).astype(jnp.float32)[:, None]
    quarter = jnp.tile(jnp.array([0, lon_count // 4], jnp.float32), owner_table.shape[0])[:, None]
    unit = 2.0 * math.pi / lon_count

    def angles(lon, turn):
        phase = waves * lon + turn
        return (phase - lon_count * jnp.floor(phase * (1.0 / lon_count))) * unit

    base = angles(jnp.arange(0, lon_count, LANES, dtype=jnp.float32)[None, :], quarter)
    turn = angles(jnp.arange(LANES, dtype=jnp.float32)[None, :], 0.0)
    depth = waves.shape[0]
    blocks = lon_count // LANES
    rows = 256
    small = pl.BlockSpec((rows, blocks), lambda i: (i, 0))
    wide = pl.BlockSpec((rows, LANES), lambda i: (i, 0))
    small_t = pl.BlockSpec((blocks, rows), lambda i: (0, i))
    wide_t = pl.BlockSpec((LANES, rows), lambda i: (0, i))
    parts = (jnp.cos(base), jnp.sin(base), jnp.cos(turn), jnp.sin(turn))
    parts = after(parts, *others)
    return pl.pallas_call(
        trig_kernel,
        grid=(depth // rows,),
        in_specs=[small, small, wide, wide, small_t, small_t, wide_t, wide_t],
        out_specs=[
            pl.BlockSpec((rows, lon_count), lambda i: (i, 0)),
            pl.BlockSpec((lon_count, rows), lambda i: (0, i)),
        ],
        out_shape=[
            jax.ShapeDtypeStruct((depth, lon_count), jnp.bfloat16),
            jax.ShapeDtypeStruct((lon_count, depth), jnp.bfloat16),
        ],
        compiler_params=pltpu.CompilerParams(vmem_limit_bytes=VMEM_BYTES),
        cost_estimate=pl.CostEstimate(
            flops=8 * depth * lon_count, bytes_accessed=4 * depth * lon_count, transcendentals=0
        ),
        name="trig",
    )(*parts, *[x.T for x in parts])


def exchange(rows):
    return lax.all_to_all(rows, AXES[::-1], split_axis=0, concat_axis=0, tiled=True)


def by_hemisphere_and_level(spectral, legendre, owner_table):
    slots, _, fields, levels, degrees = spectral.shape
    half_lat = legendre.shape[2]
    lon_count = 4 * half_lat
    row_total = 2 * fields * levels
    tiles = half_lat // LANES
    first = lax.axis_index(AXES).astype(jnp.int32) * slots
    spec_rows = spectral.reshape(slots, row_total, degrees)
    devices = 2 * levels
    least = tuple(4 * g * devices for g in range(slots // 4 - 1))
    near = slots - 4
    far_least = near * devices
    cut = tiles - tiles // 2
    chunks = [(0, cut), (cut, tiles - cut)]

    def send(spec, chunk):
        return synthesize(first.reshape(1), owner_table, spec, legendre, chunk, fields, levels, least)

    own_pack = pack(spec_rows, legendre, near)
    partner_pack = across_halves(own_pack)
    large = send(after(spec_rows, own_pack), chunks[0])

    bands, planes = lax.axis_size("band"), lax.axis_size("grp")
    by_device = jnp.swapaxes(owner_table.reshape(bands, planes, slots), 0, 1).reshape(2, levels, slots)
    plane = lax.axis_index("grp").astype(jnp.int32)
    hemi = plane // (planes // 2)
    level = plane % (planes // 2) * bands + lax.axis_index("band").astype(jnp.int32)
    place = jnp.stack([hemi, level])
    far = by_device[:, :, near:]
    both_halves = jnp.concatenate([far[0], far[1]], axis=1)
    swapped = jnp.concatenate([far[1], far[0]], axis=1)
    far_waves = jnp.where(hemi == 0, both_halves, swapped)
    far_waves = jnp.take(far_waves, jnp.arange(levels, dtype=jnp.int32) ^ level, axis=0)
    waves = jnp.concatenate([by_device[:, :, :near].reshape(-1), far_waves.reshape(-1)])

    small = send(after(spec_rows, large), chunks[1])
    by_wave, by_lon = trig_tables(after(waves, large), lon_count, small)
    arrived = [exchange(after(large, small, partner_pack))]
    far_rows = far_synthesize(
        place, far_waves[0] - far_least, own_pack, partner_pack, levels, fields, 1.0 / math.sqrt(degrees)
    )
    far_rows = jnp.concatenate(within_half(far_rows))
    arrived.append(exchange(after(small, far_rows, *arrived)))
    zonal = [
        longitudes(rows, far_rows, by_lon, by_wave, fields, chunk) for rows, chunk in zip(arrived, chunks)
    ]
    returned = [exchange(zonal[0][0])]
    far_zonal = jnp.concatenate([zonal[0][1], zonal[1][1]], axis=1)
    far_zonal = within_half([far_zonal[16 * x : 16 * x + 16] for x in range(levels)])
    own_sums, partner_sums = far_analyze(place, own_pack, partner_pack, far_zonal, levels, fields, chunks)
    returned.append(exchange(after(zonal[1][0], partner_sums, *returned)))
    other_sums = across_halves(partner_sums)
    wavenumber = lax.dynamic_slice_in_dim(after(owner_table, by_wave), first, slots)
    distance = jnp.arange(degrees, dtype=jnp.int32)[None, :] - wavenumber[:, None]
    scale = 1.0 / math.sqrt(2 * half_lat)
    even = jnp.where((distance >= 0) & (distance % 2 == 0), scale, 0.0).astype(jnp.float32)[:, None, :]
    odd = jnp.where((distance >= 0) & (distance % 2 != 0), scale, 0.0).astype(jnp.float32)[:, None, :]

    folded = fold(returned[0], near, levels, fields)
    base = analyze(folded, even, odd, legendre, row_total, least, chunks[0])
    last = after(returned[1], base)
    out = close(hemi.reshape(1), own_sums, other_sums, last, base, even, odd, legendre, fields, levels, least, chunks[1])
    return out.reshape(slots, 2, fields, levels, degrees)


def make_trig(wavenumber, lon_count):
    lon_index = jnp.arange(lon_count, dtype=jnp.int32)
    phases = wavenumber[:, None] * lon_index[None, :] % lon_count
    angles = phases.astype(jnp.float32) * (2.0 * math.pi / lon_count)
    return jnp.stack([jnp.cos(angles), -jnp.sin(angles)], axis=1).astype(jnp.bfloat16)


def by_level_and_latitude(spectral, legendre, owner_table):
    slot_count, _, fields, levels, degrees = spectral.shape
    half_lat = legendre.shape[2]
    lat_count = 2 * half_lat
    lon_count = 2 * lat_count
    wave_count = owner_table.shape[0]
    band_count = lax.axis_size("band")
    group_count = lax.axis_size("grp")
    device_count = band_count * group_count
    level_block = levels // band_count
    lat_block = lat_count // group_count
    row_total = 2 * fields * levels
    row_width = fields * level_block * lat_block
    slot_start = lax.axis_index(("band", "grp")) * slot_count
    wavenumber = lax.dynamic_slice_in_dim(owner_table, slot_start, slot_count)
    degree_index = jnp.arange(degrees, dtype=jnp.int32)
    keep_mask = (degree_index[None, :] >= wavenumber[:, None]).astype(jnp.bfloat16)
    odd_part = (degree_index[None, :] - wavenumber[:, None]) % 2
    flip_sign = (1 - 2 * odd_part).astype(jnp.bfloat16)
    spec_rows = spectral.reshape(slot_count, row_total, degrees) * keep_mask[:, None, :]
    both_rows = jnp.concatenate([spec_rows, spec_rows * flip_sign[:, None, :]], axis=1)
    halves = jnp.einsum("srn,snt->srt", both_rows, legendre, preferred_element_type=jnp.float32)
    northern = halves[:, :row_total]
    mirrored = halves[:, row_total:]
    fourier = jnp.concatenate([northern, jnp.flip(mirrored, axis=2)], axis=2)
    fourier = fourier.reshape(
        slot_count, 2, fields, band_count, level_block, group_count, lat_block
    )
    fourier = jnp.transpose(fourier, (0, 1, 2, 3, 5, 4, 6))
    fourier_low = (fourier * (1.0 / math.sqrt(degrees))).astype(jnp.bfloat16)
    packed = fourier_low.reshape(1, slot_count, 2, fields, device_count, level_block, lat_block)
    arrived = lax.all_to_all(packed, ("band", "grp"), split_axis=4, concat_axis=0, tiled=True)
    arrived = arrived.reshape(-1, 2, row_width)
    trig_rows = make_trig(owner_table, lon_count)
    grid_values = jnp.einsum("scw,scl->wl", arrived, trig_rows, preferred_element_type=jnp.float32)
    grid_values = (grid_values * (1.0 / math.sqrt(wave_count))).reshape(
        fields, level_block * lat_block, lon_count
    )
    product = (grid_values * jnp.roll(grid_values, -1, axis=0)).astype(jnp.bfloat16)
    zonal_coeffs = jnp.einsum(
        "wl,scl->scw",
        product.reshape(row_width, lon_count),
        trig_rows,
        preferred_element_type=jnp.float32,
    )
    zonal_coeffs = (zonal_coeffs * (2.0 / math.sqrt(lon_count))).astype(jnp.bfloat16)
    sendback = zonal_coeffs.reshape(device_count, slot_count, 2, fields, 1, level_block, lat_block)
    returned = lax.all_to_all(sendback, ("band", "grp"), split_axis=0, concat_axis=4, tiled=True)
    returned = returned.reshape(
        slot_count, 2, fields, band_count, group_count, level_block, lat_block
    )
    returned = jnp.transpose(returned, (0, 1, 2, 3, 5, 4, 6)).reshape(slot_count, row_total, lat_count)
    northern_part = returned[:, :, :half_lat].astype(jnp.float32)
    mirror_part = jnp.flip(returned[:, :, half_lat:], axis=2).astype(jnp.float32)
    plus_part = (northern_part + mirror_part).astype(jnp.bfloat16)
    minus_part = (northern_part - mirror_part).astype(jnp.bfloat16)
    stacked = jnp.concatenate([plus_part, minus_part], axis=1)
    projected = jnp.einsum("srt,snt->srn", stacked, legendre, preferred_element_type=jnp.float32)
    even_rows = flip_sign[:, None, :] > 0
    chosen = jnp.where(even_rows, projected[:, :row_total], projected[:, row_total:])
    chosen = chosen * keep_mask.astype(jnp.float32)[:, None, :] * (1.0 / math.sqrt(lat_count))
    return chosen.reshape(slot_count, 2, fields, levels, degrees)


def on_device(spectral, legendre, owner_table):
    slots, _, _, levels, _ = spectral.shape
    whole_hemispheres = lax.axis_size("band") * lax.axis_size("grp") == 2 * levels
    halves = lax.axis_size("grp") % 2 == 0 and levels & (levels - 1) == 0
    few_left = legendre.shape[1] - (slots - 4) * 2 * levels == LANES
    if whole_hemispheres and halves and few_left and legendre.shape[2] % LANES == 0 and legendre.shape[2] > LANES and slots % 4 == 0 and levels % 16 == 0:
        return by_hemisphere_and_level(spectral, legendre, owner_table)
    return by_level_and_latitude(spectral, legendre, owner_table)


def solution(mesh):
    placed = (P(("band", "grp"), None, None, None, None), P(("band", "grp"), None, None), P())
    return jax.shard_map(
        on_device,
        mesh=mesh,
        in_specs=placed,
        out_specs=P(("band", "grp"), None, None, None, None),
        check_vma=False,
    )
```

```python
import functools
import math

import jax
import jax.numpy as jnp
from jax import lax
from jax.experimental import pallas as pl
from jax.experimental.pallas import tpu as pltpu
from jax.sharding import PartitionSpec as P

LANES = 128
AXES = ("band", "grp")
VMEM_BYTES = 62 * 1024 * 1024


def padded(slots):
    return 2 * slots + 8


def synthesis_kernel(
    slots, levels, fields, least, chunk, scale, first_ref, owner_ref, spec_ref, table_ref, out_ref, rows_ref, sems, *held
):
    at, tiles = chunk
    groups = len(least)
    block = 4
    row_total, degrees = spec_ref.shape[1:]
    stride = padded(slots)
    copies = []
    for group, start in enumerate(least):
        mine = pl.ds(group * block, block)
        left = pl.ds(start, degrees - start)
        lanes = pl.ds(at * LANES, tiles * LANES)
        copies.append(
            (
                pltpu.make_async_copy(spec_ref.at[mine, :, left], held[2 * group], sems.at[2 * group]),
                pltpu.make_async_copy(table_ref.at[mine, left, lanes], held[2 * group + 1], sems.at[2 * group + 1]),
            )
        )
    order = range(groups - 1, -1, -1)
    for group in order:
        for copy in copies[group]:
            copy.start()
    for group in order:
        for copy in copies[group]:
            copy.wait()
        for j in range(block):
            spec = held[2 * group][j]
            wave = owner_ref[first_ref[0] + group * block + j]
            distance = lax.broadcasted_iota(jnp.int32, (1, spec.shape[1]), 1) + (least[group] - wave)
            keep = jnp.where(distance >= 0, 1.0, 0.0)
            flip = jnp.where(distance % 2 == 0, keep, -keep)
            both = jnp.concatenate([spec * keep.astype(spec.dtype), spec * flip.astype(spec.dtype)], axis=0)
            halves = jnp.dot(both, held[2 * group + 1][j], preferred_element_type=jnp.float32) * scale
            first = 2 * (group * block + j)
            for hemi in range(2):
                for part in range(2):
                    for field in range(fields):
                        row = hemi * row_total + (part * fields + field) * levels
                        target = pl.ds(hemi * levels * stride + first + part, levels, stride=stride)
                        for tile in range(tiles):
                            lanes = slice(tile * LANES, (tile + 1) * LANES)
                            rows_ref[field, tile, target, :] = halves[row : row + levels, lanes]
    for field in range(fields):
        for tile in range(tiles):
            lanes = pl.ds((field * tiles + tile) * LANES, LANES)
            rows = rows_ref[field, tile].reshape(2 * levels, stride, LANES)[:, : 2 * slots]
            out_ref[:, lanes] = rows.reshape(out_ref.shape[0], LANES).astype(out_ref.dtype)


def synthesize(first, owner_table, spec_rows, legendre, chunk, fields, levels, least):
    _, row_total, degrees = spec_rows.shape
    block = 4
    slots = block * len(least)
    rows = 2 * levels * 2 * slots
    tiles = chunk[1]
    shape = (rows, fields * tiles * LANES)
    held = []
    for start in least:
        held.append(pltpu.VMEM((block, row_total, degrees - start), jnp.bfloat16))
        held.append(pltpu.VMEM((block, degrees - start, tiles * LANES), jnp.bfloat16))
    return pl.pallas_call(
        functools.partial(synthesis_kernel, slots, levels, fields, least, chunk, 1.0 / math.sqrt(degrees)),
        in_specs=[pl.BlockSpec(memory_space=pltpu.SMEM)] * 2 + [pl.BlockSpec(memory_space=pl.ANY)] * 2,
        out_specs=pl.BlockSpec(shape, lambda: (0, 0)),
        out_shape=jax.ShapeDtypeStruct(shape, jnp.bfloat16),
        scratch_shapes=[
            pltpu.VMEM((fields, tiles, 2 * levels * padded(slots), LANES), jnp.float32),
            pltpu.SemaphoreType.DMA((2 * len(least),)),
            *held,
        ],
        compiler_params=pltpu.CompilerParams(vmem_limit_bytes=VMEM_BYTES),
        cost_estimate=pl.CostEstimate(
            flops=4 * slots * row_total * degrees * tiles * LANES,
            bytes_accessed=2 * slots * degrees * (row_total + tiles * LANES) + 2 * rows * shape[1],
            transcendentals=0,
        ),
        name="synthesis",
    )(first, owner_table, spec_rows, legendre)


def longitude_kernel(
    fields, chunk, grid_scale, zonal_scale, rows_ref, far_ref, by_lon_ref, by_wave_ref, out_ref, far_out_ref, sum_ref
):
    step = pl.program_id(0)
    near = rows_ref.shape[0]
    values = jnp.dot(by_lon_ref[:, :near], rows_ref[...], preferred_element_type=jnp.float32)
    one = values.shape[1] // fields
    each = far_ref.shape[1] // fields
    starts = [field * each + chunk[0] * LANES for field in range(fields)]
    far = jnp.concatenate([far_ref[:, start : start + one] for start in starts], axis=1)
    values = values + jnp.dot(by_lon_ref[:, near:], far, preferred_element_type=jnp.float32)
    values = values * grid_scale
    following = jnp.concatenate([values[:, one:], values[:, :one]], axis=1)
    product = (values * following).astype(jnp.bfloat16)
    share = jnp.dot(by_wave_ref[...], product, preferred_element_type=jnp.float32)

    @pl.when(step == 0)
    def _():
        sum_ref[...] = share

    @pl.when(step > 0)
    def _():
        sum_ref[...] += share

    @pl.when(step == pl.num_programs(0) - 1)
    def _():
        out_ref[...] = (sum_ref[:near, :] * zonal_scale).astype(out_ref.dtype)
        far_out_ref[...] = (sum_ref[near:, :] * zonal_scale).astype(far_out_ref.dtype)


def longitudes(rows, far, by_lon, by_wave, fields, chunk):
    depth, width = rows.shape[0] + far.shape[0], rows.shape[1]
    lon_count = by_lon.shape[0]
    lon_block = lon_count // 5
    near_spec = pl.BlockSpec(rows.shape, lambda i: (0, 0))
    far_out = jax.ShapeDtypeStruct((far.shape[0], width), jnp.bfloat16)
    return pl.pallas_call(
        functools.partial(longitude_kernel, fields, chunk, 1.0 / math.sqrt(depth // 2), 2.0 / math.sqrt(lon_count)),
        grid=(lon_count // lon_block,),
        in_specs=[
            near_spec,
            pl.BlockSpec(far.shape, lambda i: (0, 0)),
            pl.BlockSpec((lon_block, depth), lambda i: (i, 0)),
            pl.BlockSpec((depth, lon_block), lambda i: (0, i)),
        ],
        out_specs=[near_spec, pl.BlockSpec(far_out.shape, lambda i: (0, 0))],
        out_shape=[jax.ShapeDtypeStruct(rows.shape, jnp.bfloat16), far_out],
        scratch_shapes=[pltpu.VMEM((depth, width), jnp.float32)],
        compiler_params=pltpu.CompilerParams(vmem_limit_bytes=VMEM_BYTES),
        cost_estimate=pl.CostEstimate(
            flops=4 * depth * width * lon_count,
            bytes_accessed=4 * depth * (width + lon_count),
            transcendentals=0,
        ),
        name="longitudes",
    )(rows, far, by_lon, by_wave)


def pack_kernel(near, spec_ref, table_ref, out_ref, tail_ref, sems):
    degrees, half_lat = table_ref.shape[1:]
    half = LANES // 2
    copies = []

    def fetch(source, target):
        copies.append(pltpu.make_async_copy(source, target, sems.at[len(copies)]))
        copies[-1].start()

    lanes, sides = pl.ds(0, half_lat), pl.ds(half_lat, LANES)
    for slot in range(2):
        rows = pl.ds(slot * LANES, LANES)
        fetch(table_ref.at[near + slot, pl.ds(degrees - LANES, LANES), :], out_ref.at[rows, lanes])
        fetch(spec_ref.at[near + slot, :, pl.ds(degrees - LANES, LANES)], out_ref.at[rows, sides])
    for slot in range(2):
        rows = pl.ds(2 * LANES + slot * half, half)
        fetch(table_ref.at[near + 2 + slot, pl.ds(degrees - half, half), :], out_ref.at[rows, lanes])
        fetch(spec_ref.at[near + 2 + slot, :, pl.ds(degrees - LANES, LANES)], tail_ref.at[slot])
    for copy in copies:
        copy.wait()
    third = pltpu.roll(tail_ref[0].astype(jnp.float32), half, 1)
    lower = lax.broadcasted_iota(jnp.int32, third.shape, 1) < half
    both = jnp.where(lower, third, tail_ref[1].astype(jnp.float32))
    out_ref[pl.ds(2 * LANES, LANES), sides] = both.astype(out_ref.dtype)


def pack(spec_rows, legendre, near):
    shape = (3 * LANES, legendre.shape[2] + LANES)
    return pl.pallas_call(
        functools.partial(pack_kernel, near),
        in_specs=[pl.BlockSpec(memory_space=pl.ANY)] * 2,
        out_specs=pl.BlockSpec(shape, lambda: (0, 0)),
        out_shape=jax.ShapeDtypeStruct(shape, jnp.bfloat16),
        scratch_shapes=[
            pltpu.VMEM((2, spec_rows.shape[1], LANES), jnp.bfloat16),
            pltpu.SemaphoreType.DMA((8,)),
        ],
        compiler_params=pltpu.CompilerParams(vmem_limit_bytes=VMEM_BYTES),
        cost_estimate=pl.CostEstimate(flops=0, bytes_accessed=4 * shape[0] * shape[1], transcendentals=0),
        name="pack",
    )(spec_rows, legendre)


def far_synthesis_kernel(levels, fields, scale, place_ref, waves_ref, own_ref, partner_ref, *refs):
    out_refs, rows_ref = refs[:-1], refs[-1]
    tiles = rows_ref.shape[1]
    half_lat = tiles * LANES
    stride = rows_ref.shape[2] // levels
    degree = lax.broadcasted_iota(jnp.int32, (1, LANES), 1)
    for slot in range(8):
        pack_ref, local = (own_ref, slot) if slot < 4 else (partner_ref, slot - 4)
        rows = pl.ds(min(local, 2) * LANES, LANES)
        distance = degree - waves_ref[slot] + (LANES // 2 if local == 2 else 0)
        keep = jnp.where(distance >= 0, 1.0, 0.0)
        if local >= 2:
            keep = jnp.where((degree < LANES // 2) if local == 2 else (degree >= LANES // 2), keep, 0.0)
        turned = jnp.where(distance % 2 == 0, keep, -keep)
        sign = jnp.where(place_ref[0] == 0, keep, turned)
        spec = pack_ref[rows, half_lat:]
        table = pack_ref[rows, :half_lat]
        sums = jnp.dot(spec * sign.astype(spec.dtype), table, preferred_element_type=jnp.float32) * scale
        for part in range(2):
            for field in range(fields):
                row = (part * fields + field) * levels
                for tile in range(tiles):
                    target = pl.ds(2 * slot + part, levels, stride=stride)
                    rows_ref[field, tile, target, :] = sums[row : row + levels, tile * LANES : (tile + 1) * LANES]
    for apart, out_ref in enumerate(out_refs):
        rows = pl.ds(pl.multiple_of((place_ref[1] ^ apart) * stride, stride), stride)
        for field in range(fields):
            for tile in range(tiles):
                lanes = pl.ds((field * tiles + tile) * LANES, LANES)
                out_ref[:, lanes] = rows_ref[field, tile, rows, :].astype(out_ref.dtype)


def far_synthesize(place, waves, own, partner, levels, fields, scale):
    tiles = own.shape[1] // LANES - 1
    shape = (16, fields * tiles * LANES)
    whole = pl.BlockSpec(own.shape, lambda: (0, 0))
    return pl.pallas_call(
        functools.partial(far_synthesis_kernel, levels, fields, scale),
        in_specs=[pl.BlockSpec(memory_space=pltpu.SMEM)] * 2 + [whole, whole],
        out_specs=[pl.BlockSpec(shape, lambda: (0, 0))] * levels,
        out_shape=[jax.ShapeDtypeStruct(shape, jnp.bfloat16)] * levels,
        scratch_shapes=[pltpu.VMEM((fields, tiles, 16 * levels, LANES), jnp.float32)],
        compiler_params=pltpu.CompilerParams(vmem_limit_bytes=VMEM_BYTES),
        cost_estimate=pl.CostEstimate(
            flops=16 * 2 * fields * levels * LANES * tiles * LANES, bytes_accessed=4 * own.size, transcendentals=0
        ),
        name="far_synthesis",
    )(place, waves, own, partner)


def far_analysis_kernel(levels, fields, chunks, place_ref, own_ref, partner_ref, *refs):
    zonal_refs, own_out_ref, partner_out_ref, rows_ref = refs[:levels], refs[-3], refs[-2], refs[-1]
    tiles = rows_ref.shape[1]
    stride = rows_ref.shape[2] // levels
    for apart, zonal_ref in enumerate(zonal_refs):
        rows = pl.ds(pl.multiple_of((place_ref[1] ^ apart) * stride, stride), stride)
        offset = 0
        for at, count in chunks:
            for field in range(fields):
                for tile in range(at, at + count):
                    rows_ref[field, tile, rows, :] = zonal_ref[:, pl.ds(offset, LANES)].astype(jnp.float32)
                    offset += LANES
    lower = lax.broadcasted_iota(jnp.int32, (1, LANES), 1) < LANES // 2
    for pack_ref, out_ref, base in ((own_ref, own_out_ref, 0), (partner_ref, partner_out_ref, 4)):
        sums = []
        for local in range(4):
            rows = pl.ds(min(local, 2) * LANES, LANES)
            zonal = jnp.concatenate(
                [
                    jnp.concatenate(
                        [
                            rows_ref[field, tile, pl.ds(2 * (base + local) + part, levels, stride=stride), :]
                            for part in range(2)
                            for field in range(fields)
                        ],
                        axis=0,
                    ).astype(jnp.bfloat16)
                    for tile in range(tiles)
                ],
                axis=1,
            )
            table = pack_ref[rows, : tiles * LANES]
            sums.append(
                lax.dot_general(zonal, table, (((1,), (1,)), ((), ())), preferred_element_type=jnp.float32)
            )
        sums[2] = jnp.where(lower, sums[2], sums[3])
        size = sums[0].shape[0]
        for block in range(3):
            out_ref[pl.ds(block * size, size), :] = sums[block].astype(out_ref.dtype)


def far_analyze(place, own, partner, zonal, levels, fields, chunks):
    tiles = own.shape[1] // LANES - 1
    shape = (3 * 2 * fields * levels, LANES)
    whole = pl.BlockSpec(own.shape, lambda: (0, 0))
    out_spec = pl.BlockSpec(shape, lambda: (0, 0))
    return pl.pallas_call(
        functools.partial(far_analysis_kernel, levels, fields, chunks),
        in_specs=[pl.BlockSpec(memory_space=pltpu.SMEM), whole, whole]
        + [pl.BlockSpec(x.shape, lambda: (0, 0)) for x in zonal],
        out_specs=[out_spec, out_spec],
        out_shape=[jax.ShapeDtypeStruct(shape, jnp.float32), jax.ShapeDtypeStruct(shape, jnp.bfloat16)],
        scratch_shapes=[pltpu.VMEM((fields, tiles, 16 * levels, LANES), jnp.float32)],
        compiler_params=pltpu.CompilerParams(vmem_limit_bytes=VMEM_BYTES),
        cost_estimate=pl.CostEstimate(
            flops=16 * 2 * fields * levels * LANES * tiles * LANES, bytes_accessed=4 * own.size, transcendentals=0
        ),
        name="far_analysis",
    )(place, own, partner, *zonal)


def fold_kernel(slots, levels, fields, arrived_ref, out_ref, rows_ref):
    tiles = rows_ref.shape[1]
    stride = padded(slots)
    half = levels * stride
    for field in range(fields):
        for tile in range(tiles):
            lanes = pl.ds((field * tiles + tile) * LANES, LANES)
            rows = arrived_ref[:, lanes].astype(jnp.float32)
            for source in range(2 * levels):
                mine = rows[2 * slots * source : 2 * slots * (source + 1)]
                rows_ref[field, tile, pl.ds(stride * source, 2 * slots), :] = mine
    for slot in range(slots):
        for part in range(2):
            for field in range(fields):
                for tile in range(tiles):
                    first = 2 * slot + part
                    north = rows_ref[field, tile, pl.ds(first, levels, stride=stride), :]
                    south = rows_ref[field, tile, pl.ds(half + first, levels, stride=stride), :]
                    lanes = pl.ds(tile * LANES, LANES)
                    at = (part * fields + field) * levels
                    out_ref[slot, at : at + levels, lanes] = (north + south).astype(out_ref.dtype)
                    at += 2 * fields * levels
                    out_ref[slot, at : at + levels, lanes] = (north - south).astype(out_ref.dtype)


def fold(arrived, slots, levels, fields):
    row_total = 2 * fields * levels
    rows, width = arrived.shape
    tiles = width // (fields * LANES)
    shape = (slots, 2 * row_total, tiles * LANES)
    return pl.pallas_call(
        functools.partial(fold_kernel, slots, levels, fields),
        in_specs=[pl.BlockSpec((rows, width), lambda: (0, 0))],
        out_specs=pl.BlockSpec(shape, lambda: (0, 0, 0)),
        out_shape=jax.ShapeDtypeStruct(shape, jnp.bfloat16),
        scratch_shapes=[pltpu.VMEM((fields, tiles, 2 * levels * padded(slots), LANES), jnp.float32)],
        compiler_params=pltpu.CompilerParams(vmem_limit_bytes=VMEM_BYTES),
        cost_estimate=pl.CostEstimate(flops=2 * rows * width, bytes_accessed=4 * rows * width, transcendentals=0),
        name="fold",
    )(arrived)


def analysis_kernel(least, folded_ref, even_ref, odd_ref, *refs):
    table_refs, out_ref = refs[:-1], refs[-1]
    row_total, degrees = out_ref.shape[1:]
    step = pl.program_id(0)

    def run(group):
        start = least[group]
        for j in range(out_ref.shape[0]):
            table = jnp.concatenate([ref[j, start:, :] for ref in table_refs], axis=1)
            sums = lax.dot_general(
                folded_ref[j], table, (((1,), (1,)), ((), ())), preferred_element_type=jnp.float32
            )
            kept = sums[:row_total] * even_ref[j, :, start:] + sums[row_total:] * odd_ref[j, :, start:]
            out_ref[j, :, start:] = kept
            if start:
                out_ref[j, :, :start] = jnp.zeros((row_total, start), out_ref.dtype)

    for group in range(len(least)):
        pl.when(step == group)(functools.partial(run, group))

    @pl.when(step == len(least))
    def _():
        out_ref[...] = jnp.zeros(out_ref.shape, out_ref.dtype)


def analyze(folded, even, odd, legendre, row_total, least, chunk):
    slots, degrees, _ = legendre.shape
    block = 4
    near = len(least) - 1
    at, tiles = chunk
    mask_spec = pl.BlockSpec((block, 1, degrees), lambda i: (i, 0, 0))
    return pl.pallas_call(
        functools.partial(analysis_kernel, least),
        grid=(len(least) + 1,),
        in_specs=[
            pl.BlockSpec((block,) + folded.shape[1:], lambda i: (jnp.minimum(i, near), 0, 0)),
            mask_spec,
            mask_spec,
        ]
        + [
            pl.BlockSpec((block, degrees, LANES), lambda i, t=at + t: (jnp.minimum(i, near), 0, t))
            for t in range(tiles)
        ],
        out_specs=pl.BlockSpec((block, row_total, degrees), lambda i: (i, 0, 0)),
        out_shape=jax.ShapeDtypeStruct((slots, row_total, degrees), jnp.float32),
        compiler_params=pltpu.CompilerParams(vmem_limit_bytes=VMEM_BYTES),
        cost_estimate=pl.CostEstimate(
            flops=4 * slots * row_total * degrees * tiles * LANES,
            bytes_accessed=2 * slots * (degrees * tiles * LANES + 2 * row_total * (tiles * LANES + degrees)),
            transcendentals=0,
        ),
        name="analysis",
    )(folded, even, odd, *[legendre] * tiles)


def closing_kernel(
    levels, fields, least, chunk, hemi_ref, arrived_ref, table_ref, base_ref, even_ref, odd_ref, own_ref, other_ref, out_ref, *refs
):
    got_ref, north_ref, south_ref, far_ref, sems = refs[:5]
    held = refs[5:]
    at, tiles = chunk
    groups = len(least)
    _, row_total, degrees = base_ref.shape
    block = 4
    slots = block * groups
    each = 2 * slots
    stride = padded(slots)
    half = levels * each
    arriving = [
        pltpu.make_async_copy(
            arrived_ref.at[:, pl.ds(field * tiles * LANES, tiles * LANES)], got_ref.at[field], sems.at[3 * groups + field]
        )
        for field in range(fields)
    ]
    tables, sums, results = [], [], []
    for group, start in enumerate(least):
        mine = pl.ds(group * block, block)
        left = pl.ds(start, degrees - start)
        lanes = pl.ds(at * LANES, tiles * LANES)
        held_table, held_sums = held[2 * group], held[2 * group + 1]
        tables.append(pltpu.make_async_copy(table_ref.at[mine, left, lanes], held_table, sems.at[3 * group]))
        sums.append(pltpu.make_async_copy(base_ref.at[mine, :, left], held_sums, sems.at[3 * group + 1]))
        results.append(pltpu.make_async_copy(held_sums, out_ref.at[mine, :, left], sems.at[3 * group + 2]))
    for copy in arriving:
        copy.start()
    for group in range(groups):
        tables[group].start()
        sums[group].start()
    for local in range(4):
        rows = pl.ds(min(local, 2) * row_total, row_total)
        own, other = own_ref[rows, :], other_ref[rows, :].astype(jnp.float32)
        both, change = own + other, jnp.where(hemi_ref[0] == 0, own - other, other - own)
        if local == 2:
            both, change = pltpu.roll(both, LANES // 2, 1), pltpu.roll(change, LANES // 2, 1)
        even = even_ref[slots + local, :, degrees - LANES :]
        odd = odd_ref[slots + local, :, degrees - LANES :]
        far_ref[local] = both * even + change * odd
    finished = pltpu.make_async_copy(
        far_ref, out_ref.at[pl.ds(slots, 4), :, pl.ds(degrees - LANES, LANES)], sems.at[3 * groups + fields]
    )
    finished.start()
    for field in range(fields):
        arriving[field].wait()
        for tile in range(tiles):
            lanes = pl.ds(tile * LANES, LANES)
            north = got_ref[field, :half, lanes].astype(jnp.float32)
            south = got_ref[field, half:, lanes].astype(jnp.float32)
            plus, minus = north + south, north - south
            for level in range(levels):
                rows = pl.ds(stride * level, each)
                north_ref[field, tile, rows, :] = plus[each * level : each * (level + 1)]
                south_ref[field, tile, rows, :] = minus[each * level : each * (level + 1)]
    for group, start in enumerate(least):
        tables[group].wait()
        sums[group].wait()
        held_table, held_sums = held[2 * group], held[2 * group + 1]
        for j in range(block):
            slot = group * block + j
            folded = jnp.concatenate(
                [
                    jnp.concatenate(
                        [
                            ref[field, tile, pl.ds(2 * slot + part, levels, stride=stride), :].astype(jnp.bfloat16)
                            for ref in (north_ref, south_ref)
                            for part in range(2)
                            for field in range(fields)
                        ],
                        axis=0,
                    )
                    for tile in range(tiles)
                ],
                axis=1,
            )
            more = lax.dot_general(
                folded, held_table[j], (((1,), (1,)), ((), ())), preferred_element_type=jnp.float32
            )
            even, odd = even_ref[slot, :, start:], odd_ref[slot, :, start:]
            held_sums[j] = held_sums[j] + more[:row_total] * even + more[row_total:] * odd
        results[group].start()
    for copy in results:
        copy.wait()
    finished.wait()


def close(hemi, own, other, arrived, base, even, odd, legendre, fields, levels, least, chunk):
    slots, row_total, degrees = base.shape
    block = 4
    rows, width = arrived.shape
    tiles = chunk[1]
    half = pltpu.VMEM((fields, tiles, levels * padded(block * len(least)), LANES), jnp.float32)
    held = []
    for start in least:
        held.append(pltpu.VMEM((block, degrees - start, tiles * LANES), jnp.bfloat16))
        held.append(pltpu.VMEM((block, row_total, degrees - start), jnp.float32))
    anywhere = pl.BlockSpec(memory_space=pl.ANY)
    return pl.pallas_call(
        functools.partial(closing_kernel, levels, fields, least, chunk),
        in_specs=[pl.BlockSpec(memory_space=pltpu.SMEM), anywhere, anywhere, anywhere]
        + [pl.BlockSpec(even.shape, lambda: (0, 0, 0))] * 2
        + [pl.BlockSpec(own.shape, lambda: (0, 0))] * 2,
        out_specs=anywhere,
        out_shape=jax.ShapeDtypeStruct(base.shape, jnp.float32),
        input_output_aliases={3: 0},
        scratch_shapes=[
            pltpu.VMEM((fields, rows, tiles * LANES), jnp.bfloat16),
            half,
            half,
            pltpu.VMEM((4, row_total, LANES), jnp.float32),
            pltpu.SemaphoreType.DMA((3 * len(least) + fields + 1,)),
            *held,
        ],
        compiler_params=pltpu.CompilerParams(vmem_limit_bytes=VMEM_BYTES),
        cost_estimate=pl.CostEstimate(
            flops=4 * slots * row_total * degrees * tiles * LANES,
            bytes_accessed=8 * slots * row_total * degrees + 2 * rows * width,
            transcendentals=0,
        ),
        name="closing",
    )(hemi, arrived, legendre, base, even, odd, own, other)


def across_halves(value):
    planes = lax.axis_size("grp")
    return lax.ppermute(value, "grp", [(p, (p + planes // 2) % planes) for p in range(planes)])


def within_half(parts):
    bands, planes = lax.axis_size("band"), lax.axis_size("grp")
    half = planes // 2
    moved = [parts[0]]
    for x in range(1, len(parts)):
        pairs = []
        for band in range(bands):
            for plane in range(planes):
                level = (plane % half * bands + band) ^ x
                target = level % bands * planes + plane // half * half + level // bands
                pairs.append((band * planes + plane, target))
        moved.append(lax.ppermute(parts[x], AXES, pairs))
    return moved


def after(value, *others):
    return lax.optimization_barrier((value, others))[0]


def trig_kernel(small_ref, cos_turn_ref, sin_turn_ref, by_wave_ref, by_lon_ref):
    shape = cos_turn_ref.shape
    cos_start, sin_start, cos_step, sin_step = [
        jnp.broadcast_to(small_ref[:, column : column + 1], shape) for column in range(4)
    ]
    cos_turn, sin_turn = cos_turn_ref[...], sin_turn_ref[...]
    cosine = cos_start * cos_turn - sin_start * sin_turn
    sine = sin_start * cos_turn + cos_start * sin_turn
    flipped = [x.T for x in (cosine, sine, cos_step, sin_step)]
    blocks = by_wave_ref.shape[1] // LANES
    for position, (c, s, dc, ds) in enumerate(((cosine, sine, cos_step, sin_step), flipped)):
        for block in range(blocks):
            part = pl.ds(block * LANES, LANES)
            if position == 0:
                by_wave_ref[:, part] = c.astype(by_wave_ref.dtype)
            else:
                by_lon_ref[part, :] = c.astype(by_lon_ref.dtype)
            c, s = c * dc - s * ds, s * dc + c * ds


def trig_tables(owner_table, lon_count, *others):
    waves = jnp.repeat(owner_table, 2).astype(jnp.float32)[:, None]
    quarter = jnp.tile(jnp.array([0, lon_count // 4], jnp.float32), owner_table.shape[0])[:, None]
    unit = 2.0 * math.pi / lon_count

    def angles(phase):
        return (phase - lon_count * jnp.floor(phase * (1.0 / lon_count))) * unit

    start = angles(quarter)
    step = angles(waves * LANES)
    turn = angles(waves * jnp.arange(LANES, dtype=jnp.float32)[None, :])
    small = jnp.concatenate([jnp.cos(start), jnp.sin(start), jnp.cos(step), jnp.sin(step)], axis=1)
    parts = after((small, jnp.cos(turn), jnp.sin(turn)), *others)
    depth = waves.shape[0]
    rows = 256
    wide = pl.BlockSpec((rows, LANES), lambda i: (i, 0))
    return pl.pallas_call(
        trig_kernel,
        grid=(depth // rows,),
        in_specs=[pl.BlockSpec((rows, 4), lambda i: (i, 0)), wide, wide],
        out_specs=[
            pl.BlockSpec((rows, lon_count), lambda i: (i, 0)),
            pl.BlockSpec((lon_count, rows), lambda i: (0, i)),
        ],
        out_shape=[
            jax.ShapeDtypeStruct((depth, lon_count), jnp.bfloat16),
            jax.ShapeDtypeStruct((lon_count, depth), jnp.bfloat16),
        ],
        compiler_params=pltpu.CompilerParams(vmem_limit_bytes=VMEM_BYTES),
        cost_estimate=pl.CostEstimate(
            flops=12 * depth * lon_count, bytes_accessed=4 * depth * lon_count, transcendentals=0
        ),
        name="trig",
    )(*parts)


def exchange(rows):
    return lax.all_to_all(rows, AXES[::-1], split_axis=0, concat_axis=0, tiled=True)


def by_hemisphere_and_level(spectral, legendre, owner_table):
    slots, _, fields, levels, degrees = spectral.shape
    half_lat = legendre.shape[2]
    lon_count = 4 * half_lat
    row_total = 2 * fields * levels
    tiles = half_lat // LANES
    first = lax.axis_index(AXES).astype(jnp.int32) * slots
    spec_rows = spectral.reshape(slots, row_total, degrees)
    devices = 2 * levels
    least = tuple(4 * g * devices for g in range(slots // 4 - 1))
    near = slots - 4
    far_least = near * devices
    cut = tiles - tiles // 2
    chunks = [(0, cut), (cut, tiles - cut)]

    def send(spec, chunk):
        return synthesize(first.reshape(1), owner_table, spec, legendre, chunk, fields, levels, least)

    own_pack = pack(spec_rows, legendre, near)
    partner_pack = across_halves(own_pack)
    large = send(after(spec_rows, own_pack), chunks[0])

    bands, planes = lax.axis_size("band"), lax.axis_size("grp")
    by_device = jnp.swapaxes(owner_table.reshape(bands, planes, slots), 0, 1).reshape(2, levels, slots)
    plane = lax.axis_index("grp").astype(jnp.int32)
    hemi = plane // (planes // 2)
    level = plane % (planes // 2) * bands + lax.axis_index("band").astype(jnp.int32)
    place = jnp.stack([hemi, level])
    far = by_device[:, :, near:]
    both_halves = jnp.concatenate([far[0], far[1]], axis=1)
    swapped = jnp.concatenate([far[1], far[0]], axis=1)
    far_waves = jnp.where(hemi == 0, both_halves, swapped)
    far_waves = jnp.take(far_waves, jnp.arange(levels, dtype=jnp.int32) ^ level, axis=0)
    waves = jnp.concatenate([by_device[:, :, :near].reshape(-1), far_waves.reshape(-1)])

    small = send(after(spec_rows, large), chunks[1])
    by_wave, by_lon = trig_tables(after(waves, own_pack), lon_count, large)
    arrived = [exchange(after(large, small, by_wave, partner_pack))]
    far_rows = far_synthesize(
        place, far_waves[0] - far_least, own_pack, partner_pack, levels, fields, 1.0 / math.sqrt(degrees)
    )
    far_rows = jnp.concatenate(within_half(far_rows))
    arrived.append(exchange(after(small, far_rows, *arrived)))
    zonal = [
        longitudes(rows, far_rows, by_lon, by_wave, fields, chunk) for rows, chunk in zip(arrived, chunks)
    ]
    returned = [exchange(zonal[0][0])]
    far_zonal = jnp.concatenate([zonal[0][1], zonal[1][1]], axis=1)
    far_zonal = within_half([far_zonal[16 * x : 16 * x + 16] for x in range(levels)])
    returned.append(exchange(after(zonal[1][0], *far_zonal[: levels - 4], *returned)))
    own_sums, partner_sums = far_analyze(place, own_pack, partner_pack, far_zonal, levels, fields, chunks)
    other_sums = across_halves(partner_sums)
    wavenumber = lax.dynamic_slice_in_dim(after(owner_table, by_wave), first, slots)
    distance = jnp.arange(degrees, dtype=jnp.int32)[None, :] - wavenumber[:, None]
    scale = 1.0 / math.sqrt(2 * half_lat)
    even = jnp.where((distance >= 0) & (distance % 2 == 0), scale, 0.0).astype(jnp.float32)[:, None, :]
    odd = jnp.where((distance >= 0) & (distance % 2 != 0), scale, 0.0).astype(jnp.float32)[:, None, :]

    folded = fold(returned[0], near, levels, fields)
    base = analyze(folded, even, odd, legendre, row_total, least, chunks[0])
    last = after(returned[1], base)
    out = close(hemi.reshape(1), own_sums, other_sums, last, base, even, odd, legendre, fields, levels, least, chunks[1])
    return out.reshape(slots, 2, fields, levels, degrees)


def make_trig(wavenumber, lon_count):
    lon_index = jnp.arange(lon_count, dtype=jnp.int32)
    phases = wavenumber[:, None] * lon_index[None, :] % lon_count
    angles = phases.astype(jnp.float32) * (2.0 * math.pi / lon_count)
    return jnp.stack([jnp.cos(angles), -jnp.sin(angles)], axis=1).astype(jnp.bfloat16)


def by_level_and_latitude(spectral, legendre, owner_table):
    slot_count, _, fields, levels, degrees = spectral.shape
    half_lat = legendre.shape[2]
    lat_count = 2 * half_lat
    lon_count = 2 * lat_count
    wave_count = owner_table.shape[0]
    band_count = lax.axis_size("band")
    group_count = lax.axis_size("grp")
    device_count = band_count * group_count
    level_block = levels // band_count
    lat_block = lat_count // group_count
    row_total = 2 * fields * levels
    row_width = fields * level_block * lat_block
    slot_start = lax.axis_index(("band", "grp")) * slot_count
    wavenumber = lax.dynamic_slice_in_dim(owner_table, slot_start, slot_count)
    degree_index = jnp.arange(degrees, dtype=jnp.int32)
    keep_mask = (degree_index[None, :] >= wavenumber[:, None]).astype(jnp.bfloat16)
    odd_part = (degree_index[None, :] - wavenumber[:, None]) % 2
    flip_sign = (1 - 2 * odd_part).astype(jnp.bfloat16)
    spec_rows = spectral.reshape(slot_count, row_total, degrees) * keep_mask[:, None, :]
    both_rows = jnp.concatenate([spec_rows, spec_rows * flip_sign[:, None, :]], axis=1)
    halves = jnp.einsum("srn,snt->srt", both_rows, legendre, preferred_element_type=jnp.float32)
    northern = halves[:, :row_total]
    mirrored = halves[:, row_total:]
    fourier = jnp.concatenate([northern, jnp.flip(mirrored, axis=2)], axis=2)
    fourier = fourier.reshape(
        slot_count, 2, fields, band_count, level_block, group_count, lat_block
    )
    fourier = jnp.transpose(fourier, (0, 1, 2, 3, 5, 4, 6))
    fourier_low = (fourier * (1.0 / math.sqrt(degrees))).astype(jnp.bfloat16)
    packed = fourier_low.reshape(1, slot_count, 2, fields, device_count, level_block, lat_block)
    arrived = lax.all_to_all(packed, ("band", "grp"), split_axis=4, concat_axis=0, tiled=True)
    arrived = arrived.reshape(-1, 2, row_width)
    trig_rows = make_trig(owner_table, lon_count)
    grid_values = jnp.einsum("scw,scl->wl", arrived, trig_rows, preferred_element_type=jnp.float32)
    grid_values = (grid_values * (1.0 / math.sqrt(wave_count))).reshape(
        fields, level_block * lat_block, lon_count
    )
    product = (grid_values * jnp.roll(grid_values, -1, axis=0)).astype(jnp.bfloat16)
    zonal_coeffs = jnp.einsum(
        "wl,scl->scw",
        product.reshape(row_width, lon_count),
        trig_rows,
        preferred_element_type=jnp.float32,
    )
    zonal_coeffs = (zonal_coeffs * (2.0 / math.sqrt(lon_count))).astype(jnp.bfloat16)
    sendback = zonal_coeffs.reshape(device_count, slot_count, 2, fields, 1, level_block, lat_block)
    returned = lax.all_to_all(sendback, ("band", "grp"), split_axis=0, concat_axis=4, tiled=True)
    returned = returned.reshape(
        slot_count, 2, fields, band_count, group_count, level_block, lat_block
    )
    returned = jnp.transpose(returned, (0, 1, 2, 3, 5, 4, 6)).reshape(slot_count, row_total, lat_count)
    northern_part = returned[:, :, :half_lat].astype(jnp.float32)
    mirror_part = jnp.flip(returned[:, :, half_lat:], axis=2).astype(jnp.float32)
    plus_part = (northern_part + mirror_part).astype(jnp.bfloat16)
    minus_part = (northern_part - mirror_part).astype(jnp.bfloat16)
    stacked = jnp.concatenate([plus_part, minus_part], axis=1)
    projected = jnp.einsum("srt,snt->srn", stacked, legendre, preferred_element_type=jnp.float32)
    even_rows = flip_sign[:, None, :] > 0
    chosen = jnp.where(even_rows, projected[:, :row_total], projected[:, row_total:])
    chosen = chosen * keep_mask.astype(jnp.float32)[:, None, :] * (1.0 / math.sqrt(lat_count))
    return chosen.reshape(slot_count, 2, fields, levels, degrees)


def on_device(spectral, legendre, owner_table):
    slots, _, _, levels, _ = spectral.shape
    whole_hemispheres = lax.axis_size("band") * lax.axis_size("grp") == 2 * levels
    halves = lax.axis_size("grp") % 2 == 0 and levels & (levels - 1) == 0
    few_left = legendre.shape[1] - (slots - 4) * 2 * levels == LANES
    if whole_hemispheres and halves and few_left and legendre.shape[2] % LANES == 0 and legendre.shape[2] > LANES and slots % 4 == 0 and levels % 16 == 0:
        return by_hemisphere_and_level(spectral, legendre, owner_table)
    return by_level_and_latitude(spectral, legendre, owner_table)


def solution(mesh):
    placed = (P(("band", "grp"), None, None, None, None), P(("band", "grp"), None, None), P())
    return jax.shard_map(
        on_device,
        mesh=mesh,
        in_specs=placed,
        out_specs=P(("band", "grp"), None, None, None, None),
        check_vma=False,
    )
```

```python
import functools
import math

import jax
import jax.numpy as jnp
from jax import lax
from jax.experimental import pallas as pl
from jax.experimental.pallas import tpu as pltpu
from jax.sharding import PartitionSpec as P

LANES = 128
AXES = ("band", "grp")
VMEM_BYTES = 62 * 1024 * 1024


def padded(slots):
    return 2 * slots + 8


def synthesis_kernel(
    slots, levels, fields, least, chunk, scale, first_ref, owner_ref, spec_ref, table_ref, out_ref, rows_ref, sems, *held
):
    at, tiles = chunk
    groups = len(least)
    block = 4
    row_total, degrees = spec_ref.shape[1:]
    stride = padded(slots)
    copies = []
    for group, start in enumerate(least):
        mine = pl.ds(group * block, block)
        left = pl.ds(start, degrees - start)
        lanes = pl.ds(at * LANES, tiles * LANES)
        copies.append(
            (
                pltpu.make_async_copy(spec_ref.at[mine, :, left], held[2 * group], sems.at[2 * group]),
                pltpu.make_async_copy(table_ref.at[mine, left, lanes], held[2 * group + 1], sems.at[2 * group + 1]),
            )
        )
    order = range(groups - 1, -1, -1)
    for group in order:
        for copy in copies[group]:
            copy.start()
    for group in order:
        for copy in copies[group]:
            copy.wait()
        for j in range(block):
            spec = held[2 * group][j]
            wave = owner_ref[first_ref[0] + group * block + j]
            distance = lax.broadcasted_iota(jnp.int32, (1, spec.shape[1]), 1) + (least[group] - wave)
            keep = jnp.where(distance >= 0, 1.0, 0.0)
            flip = jnp.where(distance % 2 == 0, keep, -keep)
            both = jnp.concatenate([spec * keep.astype(spec.dtype), spec * flip.astype(spec.dtype)], axis=0)
            halves = jnp.dot(both, held[2 * group + 1][j], preferred_element_type=jnp.float32) * scale
            first = 2 * (group * block + j)
            for hemi in range(2):
                for part in range(2):
                    for field in range(fields):
                        row = hemi * row_total + (part * fields + field) * levels
                        target = pl.ds(hemi * levels * stride + first + part, levels, stride=stride)
                        for tile in range(tiles):
                            lanes = slice(tile * LANES, (tile + 1) * LANES)
                            rows_ref[field, tile, target, :] = halves[row : row + levels, lanes]
    for field in range(fields):
        for tile in range(tiles):
            lanes = pl.ds((field * tiles + tile) * LANES, LANES)
            rows = rows_ref[field, tile].reshape(2 * levels, stride, LANES)[:, : 2 * slots]
            out_ref[:, lanes] = rows.reshape(out_ref.shape[0], LANES).astype(out_ref.dtype)


def synthesize(first, owner_table, spec_rows, legendre, chunk, fields, levels, least):
    _, row_total, degrees = spec_rows.shape
    block = 4
    slots = block * len(least)
    rows = 2 * levels * 2 * slots
    tiles = chunk[1]
    shape = (rows, fields * tiles * LANES)
    held = []
    for start in least:
        held.append(pltpu.VMEM((block, row_total, degrees - start), jnp.bfloat16))
        held.append(pltpu.VMEM((block, degrees - start, tiles * LANES), jnp.bfloat16))
    return pl.pallas_call(
        functools.partial(synthesis_kernel, slots, levels, fields, least, chunk, 1.0 / math.sqrt(degrees)),
        in_specs=[pl.BlockSpec(memory_space=pltpu.SMEM)] * 2 + [pl.BlockSpec(memory_space=pl.ANY)] * 2,
        out_specs=pl.BlockSpec(shape, lambda: (0, 0)),
        out_shape=jax.ShapeDtypeStruct(shape, jnp.bfloat16),
        scratch_shapes=[
            pltpu.VMEM((fields, tiles, 2 * levels * padded(slots), LANES), jnp.float32),
            pltpu.SemaphoreType.DMA((2 * len(least),)),
            *held,
        ],
        compiler_params=pltpu.CompilerParams(vmem_limit_bytes=VMEM_BYTES),
        cost_estimate=pl.CostEstimate(
            flops=4 * slots * row_total * degrees * tiles * LANES,
            bytes_accessed=2 * slots * degrees * (row_total + tiles * LANES) + 2 * rows * shape[1],
            transcendentals=0,
        ),
        name="synthesis",
    )(first, owner_table, spec_rows, legendre)


def longitude_kernel(
    fields, chunk, grid_scale, zonal_scale, rows_ref, far_ref, by_lon_ref, by_wave_ref, out_ref, far_out_ref, sum_ref
):
    step = pl.program_id(0)
    near = rows_ref.shape[0]
    values = jnp.dot(by_lon_ref[:, :near], rows_ref[...], preferred_element_type=jnp.float32)
    one = values.shape[1] // fields
    each = far_ref.shape[1] // fields
    starts = [field * each + chunk[0] * LANES for field in range(fields)]
    far = jnp.concatenate([far_ref[:, start : start + one] for start in starts], axis=1)
    values = values + jnp.dot(by_lon_ref[:, near:], far, preferred_element_type=jnp.float32)
    values = values * grid_scale
    following = jnp.concatenate([values[:, one:], values[:, :one]], axis=1)
    product = (values * following).astype(jnp.bfloat16)
    share = jnp.dot(by_wave_ref[...], product, preferred_element_type=jnp.float32)

    @pl.when(step == 0)
    def _():
        sum_ref[...] = share

    @pl.when(step > 0)
    def _():
        sum_ref[...] += share

    @pl.when(step == pl.num_programs(0) - 1)
    def _():
        out_ref[...] = (sum_ref[:near, :] * zonal_scale).astype(out_ref.dtype)
        far_out_ref[...] = (sum_ref[near:, :] * zonal_scale).astype(far_out_ref.dtype)


def longitudes(rows, far, by_lon, by_wave, fields, chunk):
    depth, width = rows.shape[0] + far.shape[0], rows.shape[1]
    lon_count = by_lon.shape[0]
    lon_block = lon_count // 5
    near_spec = pl.BlockSpec(rows.shape, lambda i: (0, 0))
    far_out = jax.ShapeDtypeStruct((far.shape[0], width), jnp.bfloat16)
    return pl.pallas_call(
        functools.partial(longitude_kernel, fields, chunk, 1.0 / math.sqrt(depth // 2), 2.0 / math.sqrt(lon_count)),
        grid=(lon_count // lon_block,),
        in_specs=[
            near_spec,
            pl.BlockSpec(far.shape, lambda i: (0, 0)),
            pl.BlockSpec((lon_block, depth), lambda i: (i, 0)),
            pl.BlockSpec((depth, lon_block), lambda i: (0, i)),
        ],
        out_specs=[near_spec, pl.BlockSpec(far_out.shape, lambda i: (0, 0))],
        out_shape=[jax.ShapeDtypeStruct(rows.shape, jnp.bfloat16), far_out],
        scratch_shapes=[pltpu.VMEM((depth, width), jnp.float32)],
        compiler_params=pltpu.CompilerParams(vmem_limit_bytes=VMEM_BYTES),
        cost_estimate=pl.CostEstimate(
            flops=4 * depth * width * lon_count,
            bytes_accessed=4 * depth * (width + lon_count),
            transcendentals=0,
        ),
        name="longitudes",
    )(rows, far, by_lon, by_wave)


def pack_kernel(near, spec_ref, table_ref, out_ref, tail_ref, sems):
    degrees, half_lat = table_ref.shape[1:]
    half = LANES // 2
    copies = []

    def fetch(source, target):
        copies.append(pltpu.make_async_copy(source, target, sems.at[len(copies)]))
        copies[-1].start()

    lanes, sides = pl.ds(0, half_lat), pl.ds(half_lat, LANES)
    for slot in range(2):
        rows = pl.ds(slot * LANES, LANES)
        fetch(table_ref.at[near + slot, pl.ds(degrees - LANES, LANES), :], out_ref.at[rows, lanes])
        fetch(spec_ref.at[near + slot, :, pl.ds(degrees - LANES, LANES)], out_ref.at[rows, sides])
    for slot in range(2):
        rows = pl.ds(2 * LANES + slot * half, half)
        fetch(table_ref.at[near + 2 + slot, pl.ds(degrees - half, half), :], out_ref.at[rows, lanes])
        fetch(spec_ref.at[near + 2 + slot, :, pl.ds(degrees - LANES, LANES)], tail_ref.at[slot])
    for copy in copies:
        copy.wait()
    third = pltpu.roll(tail_ref[0].astype(jnp.float32), half, 1)
    lower = lax.broadcasted_iota(jnp.int32, third.shape, 1) < half
    both = jnp.where(lower, third, tail_ref[1].astype(jnp.float32))
    out_ref[pl.ds(2 * LANES, LANES), sides] = both.astype(out_ref.dtype)


def pack(spec_rows, legendre, near):
    shape = (3 * LANES, legendre.shape[2] + LANES)
    return pl.pallas_call(
        functools.partial(pack_kernel, near),
        in_specs=[pl.BlockSpec(memory_space=pl.ANY)] * 2,
        out_specs=pl.BlockSpec(shape, lambda: (0, 0)),
        out_shape=jax.ShapeDtypeStruct(shape, jnp.bfloat16),
        scratch_shapes=[
            pltpu.VMEM((2, spec_rows.shape[1], LANES), jnp.bfloat16),
            pltpu.SemaphoreType.DMA((8,)),
        ],
        compiler_params=pltpu.CompilerParams(vmem_limit_bytes=VMEM_BYTES),
        cost_estimate=pl.CostEstimate(flops=0, bytes_accessed=4 * shape[0] * shape[1], transcendentals=0),
        name="pack",
    )(spec_rows, legendre)


def far_synthesis_kernel(levels, fields, scale, place_ref, waves_ref, own_ref, partner_ref, *refs):
    out_refs, rows_ref = refs[:-1], refs[-1]
    tiles = rows_ref.shape[1]
    half_lat = tiles * LANES
    stride = rows_ref.shape[2] // levels
    degree = lax.broadcasted_iota(jnp.int32, (1, LANES), 1)
    for slot in range(8):
        pack_ref, local = (own_ref, slot) if slot < 4 else (partner_ref, slot - 4)
        rows = pl.ds(min(local, 2) * LANES, LANES)
        distance = degree - waves_ref[slot] + (LANES // 2 if local == 2 else 0)
        keep = jnp.where(distance >= 0, 1.0, 0.0)
        if local >= 2:
            keep = jnp.where((degree < LANES // 2) if local == 2 else (degree >= LANES // 2), keep, 0.0)
        turned = jnp.where(distance % 2 == 0, keep, -keep)
        sign = jnp.where(place_ref[0] == 0, keep, turned)
        spec = pack_ref[rows, half_lat:]
        table = pack_ref[rows, :half_lat]
        sums = jnp.dot(spec * sign.astype(spec.dtype), table, preferred_element_type=jnp.float32) * scale
        for part in range(2):
            for field in range(fields):
                row = (part * fields + field) * levels
                for tile in range(tiles):
                    target = pl.ds(2 * slot + part, levels, stride=stride)
                    rows_ref[field, tile, target, :] = sums[row : row + levels, tile * LANES : (tile + 1) * LANES]
    for apart, out_ref in enumerate(out_refs):
        rows = pl.ds(pl.multiple_of((place_ref[1] ^ apart) * stride, stride), stride)
        for field in range(fields):
            for tile in range(tiles):
                lanes = pl.ds((field * tiles + tile) * LANES, LANES)
                out_ref[:, lanes] = rows_ref[field, tile, rows, :].astype(out_ref.dtype)


def far_synthesize(place, waves, own, partner, levels, fields, scale):
    tiles = own.shape[1] // LANES - 1
    shape = (16, fields * tiles * LANES)
    whole = pl.BlockSpec(own.shape, lambda: (0, 0))
    return pl.pallas_call(
        functools.partial(far_synthesis_kernel, levels, fields, scale),
        in_specs=[pl.BlockSpec(memory_space=pltpu.SMEM)] * 2 + [whole, whole],
        out_specs=[pl.BlockSpec(shape, lambda: (0, 0))] * levels,
        out_shape=[jax.ShapeDtypeStruct(shape, jnp.bfloat16)] * levels,
        scratch_shapes=[pltpu.VMEM((fields, tiles, 16 * levels, LANES), jnp.float32)],
        compiler_params=pltpu.CompilerParams(vmem_limit_bytes=VMEM_BYTES),
        cost_estimate=pl.CostEstimate(
            flops=16 * 2 * fields * levels * LANES * tiles * LANES, bytes_accessed=4 * own.size, transcendentals=0
        ),
        name="far_synthesis",
    )(place, waves, own, partner)


def far_analysis_kernel(levels, fields, chunks, place_ref, own_ref, partner_ref, *refs):
    zonal_refs, own_out_ref, partner_out_ref, rows_ref = refs[:levels], refs[-3], refs[-2], refs[-1]
    tiles = rows_ref.shape[1]
    stride = rows_ref.shape[2] // levels
    for apart, zonal_ref in enumerate(zonal_refs):
        rows = pl.ds(pl.multiple_of((place_ref[1] ^ apart) * stride, stride), stride)
        offset = 0
        for at, count in chunks:
            for field in range(fields):
                for tile in range(at, at + count):
                    rows_ref[field, tile, rows, :] = zonal_ref[:, pl.ds(offset, LANES)].astype(jnp.float32)
                    offset += LANES
    lower = lax.broadcasted_iota(jnp.int32, (1, LANES), 1) < LANES // 2
    for pack_ref, out_ref, base in ((own_ref, own_out_ref, 0), (partner_ref, partner_out_ref, 4)):
        sums = []
        for local in range(4):
            rows = pl.ds(min(local, 2) * LANES, LANES)
            zonal = jnp.concatenate(
                [
                    jnp.concatenate(
                        [
                            rows_ref[field, tile, pl.ds(2 * (base + local) + part, levels, stride=stride), :]
                            for part in range(2)
                            for field in range(fields)
                        ],
                        axis=0,
                    ).astype(jnp.bfloat16)
                    for tile in range(tiles)
                ],
                axis=1,
            )
            table = pack_ref[rows, : tiles * LANES]
            sums.append(
                lax.dot_general(zonal, table, (((1,), (1,)), ((), ())), preferred_element_type=jnp.float32)
            )
        sums[2] = jnp.where(lower, sums[2], sums[3])
        size = sums[0].shape[0]
        for block in range(3):
            out_ref[pl.ds(block * size, size), :] = sums[block].astype(out_ref.dtype)


def far_analyze(place, own, partner, zonal, levels, fields, chunks):
    tiles = own.shape[1] // LANES - 1
    shape = (3 * 2 * fields * levels, LANES)
    whole = pl.BlockSpec(own.shape, lambda: (0, 0))
    out_spec = pl.BlockSpec(shape, lambda: (0, 0))
    return pl.pallas_call(
        functools.partial(far_analysis_kernel, levels, fields, chunks),
        in_specs=[pl.BlockSpec(memory_space=pltpu.SMEM), whole, whole]
        + [pl.BlockSpec(x.shape, lambda: (0, 0)) for x in zonal],
        out_specs=[out_spec, out_spec],
        out_shape=[jax.ShapeDtypeStruct(shape, jnp.float32), jax.ShapeDtypeStruct(shape, jnp.bfloat16)],
        scratch_shapes=[pltpu.VMEM((fields, tiles, 16 * levels, LANES), jnp.float32)],
        compiler_params=pltpu.CompilerParams(vmem_limit_bytes=VMEM_BYTES),
        cost_estimate=pl.CostEstimate(
            flops=16 * 2 * fields * levels * LANES * tiles * LANES, bytes_accessed=4 * own.size, transcendentals=0
        ),
        name="far_analysis",
    )(place, own, partner, *zonal)


def fold_kernel(slots, levels, fields, arrived_ref, out_ref, rows_ref):
    tiles = rows_ref.shape[1]
    stride = padded(slots)
    half = levels * stride
    for field in range(fields):
        for tile in range(tiles):
            lanes = pl.ds((field * tiles + tile) * LANES, LANES)
            rows = arrived_ref[:, lanes].astype(jnp.float32)
            for source in range(2 * levels):
                mine = rows[2 * slots * source : 2 * slots * (source + 1)]
                rows_ref[field, tile, pl.ds(stride * source, 2 * slots), :] = mine
    for slot in range(slots):
        for part in range(2):
            for field in range(fields):
                for tile in range(tiles):
                    first = 2 * slot + part
                    north = rows_ref[field, tile, pl.ds(first, levels, stride=stride), :]
                    south = rows_ref[field, tile, pl.ds(half + first, levels, stride=stride), :]
                    lanes = pl.ds(tile * LANES, LANES)
                    at = (part * fields + field) * levels
                    out_ref[slot, at : at + levels, lanes] = (north + south).astype(out_ref.dtype)
                    at += 2 * fields * levels
                    out_ref[slot, at : at + levels, lanes] = (north - south).astype(out_ref.dtype)


def fold(arrived, slots, levels, fields):
    row_total = 2 * fields * levels
    rows, width = arrived.shape
    tiles = width // (fields * LANES)
    shape = (slots, 2 * row_total, tiles * LANES)
    return pl.pallas_call(
        functools.partial(fold_kernel, slots, levels, fields),
        in_specs=[pl.BlockSpec((rows, width), lambda: (0, 0))],
        out_specs=pl.BlockSpec(shape, lambda: (0, 0, 0)),
        out_shape=jax.ShapeDtypeStruct(shape, jnp.bfloat16),
        scratch_shapes=[pltpu.VMEM((fields, tiles, 2 * levels * padded(slots), LANES), jnp.float32)],
        compiler_params=pltpu.CompilerParams(vmem_limit_bytes=VMEM_BYTES),
        cost_estimate=pl.CostEstimate(flops=2 * rows * width, bytes_accessed=4 * rows * width, transcendentals=0),
        name="fold",
    )(arrived)


def analysis_kernel(least, folded_ref, even_ref, odd_ref, *refs):
    table_refs, out_ref = refs[:-1], refs[-1]
    row_total, degrees = out_ref.shape[1:]
    step = pl.program_id(0)

    def run(group):
        start = least[group]
        for j in range(out_ref.shape[0]):
            table = jnp.concatenate([ref[j, start:, :] for ref in table_refs], axis=1)
            sums = lax.dot_general(
                folded_ref[j], table, (((1,), (1,)), ((), ())), preferred_element_type=jnp.float32
            )
            kept = sums[:row_total] * even_ref[j, :, start:] + sums[row_total:] * odd_ref[j, :, start:]
            out_ref[j, :, start:] = kept
            if start:
                out_ref[j, :, :start] = jnp.zeros((row_total, start), out_ref.dtype)

    for group in range(len(least)):
        pl.when(step == group)(functools.partial(run, group))

    @pl.when(step == len(least))
    def _():
        out_ref[...] = jnp.zeros(out_ref.shape, out_ref.dtype)


def analyze(folded, even, odd, legendre, row_total, least, chunk):
    slots, degrees, _ = legendre.shape
    block = 4
    near = len(least) - 1
    at, tiles = chunk
    mask_spec = pl.BlockSpec((block, 1, degrees), lambda i: (i, 0, 0))
    return pl.pallas_call(
        functools.partial(analysis_kernel, least),
        grid=(len(least) + 1,),
        in_specs=[
            pl.BlockSpec((block,) + folded.shape[1:], lambda i: (jnp.minimum(i, near), 0, 0)),
            mask_spec,
            mask_spec,
        ]
        + [
            pl.BlockSpec((block, degrees, LANES), lambda i, t=at + t: (jnp.minimum(i, near), 0, t))
            for t in range(tiles)
        ],
        out_specs=pl.BlockSpec((block, row_total, degrees), lambda i: (i, 0, 0)),
        out_shape=jax.ShapeDtypeStruct((slots, row_total, degrees), jnp.float32),
        compiler_params=pltpu.CompilerParams(vmem_limit_bytes=VMEM_BYTES),
        cost_estimate=pl.CostEstimate(
            flops=4 * slots * row_total * degrees * tiles * LANES,
            bytes_accessed=2 * slots * (degrees * tiles * LANES + 2 * row_total * (tiles * LANES + degrees)),
            transcendentals=0,
        ),
        name="analysis",
    )(folded, even, odd, *[legendre] * tiles)


def closing_kernel(
    levels, fields, least, chunk, hemi_ref, arrived_ref, table_ref, base_ref, even_ref, odd_ref, own_ref, other_ref, out_ref, *refs
):
    got_ref, north_ref, south_ref, far_ref, sems = refs[:5]
    held = refs[5:]
    at, tiles = chunk
    groups = len(least)
    _, row_total, degrees = base_ref.shape
    block = 4
    slots = block * groups
    each = 2 * slots
    stride = padded(slots)
    half = levels * each
    arriving = [
        pltpu.make_async_copy(
            arrived_ref.at[:, pl.ds(field * tiles * LANES, tiles * LANES)], got_ref.at[field], sems.at[3 * groups + field]
        )
        for field in range(fields)
    ]
    tables, sums, results = [], [], []
    for group, start in enumerate(least):
        mine = pl.ds(group * block, block)
        left = pl.ds(start, degrees - start)
        lanes = pl.ds(at * LANES, tiles * LANES)
        held_table, held_sums = held[2 * group], held[2 * group + 1]
        tables.append(pltpu.make_async_copy(table_ref.at[mine, left, lanes], held_table, sems.at[3 * group]))
        sums.append(pltpu.make_async_copy(base_ref.at[mine, :, left], held_sums, sems.at[3 * group + 1]))
        results.append(pltpu.make_async_copy(held_sums, out_ref.at[mine, :, left], sems.at[3 * group + 2]))
    for copy in arriving:
        copy.start()
    for group in range(groups):
        tables[group].start()
        sums[group].start()
    for local in range(4):
        rows = pl.ds(min(local, 2) * row_total, row_total)
        own, other = own_ref[rows, :], other_ref[rows, :].astype(jnp.float32)
        both, change = own + other, jnp.where(hemi_ref[0] == 0, own - other, other - own)
        if local == 2:
            both, change = pltpu.roll(both, LANES // 2, 1), pltpu.roll(change, LANES // 2, 1)
        even = even_ref[slots + local, :, degrees - LANES :]
        odd = odd_ref[slots + local, :, degrees - LANES :]
        far_ref[local] = both * even + change * odd
    finished = pltpu.make_async_copy(
        far_ref, out_ref.at[pl.ds(slots, 4), :, pl.ds(degrees - LANES, LANES)], sems.at[3 * groups + fields]
    )
    finished.start()
    for field in range(fields):
        arriving[field].wait()
        for tile in range(tiles):
            lanes = pl.ds(tile * LANES, LANES)
            north = got_ref[field, :half, lanes].astype(jnp.float32)
            south = got_ref[field, half:, lanes].astype(jnp.float32)
            plus, minus = north + south, north - south
            for level in range(levels):
                rows = pl.ds(stride * level, each)
                north_ref[field, tile, rows, :] = plus[each * level : each * (level + 1)]
                south_ref[field, tile, rows, :] = minus[each * level : each * (level + 1)]
    for group, start in enumerate(least):
        tables[group].wait()
        sums[group].wait()
        held_table, held_sums = held[2 * group], held[2 * group + 1]
        for j in range(block):
            slot = group * block + j
            folded = jnp.concatenate(
                [
                    jnp.concatenate(
                        [
                            ref[field, tile, pl.ds(2 * slot + part, levels, stride=stride), :].astype(jnp.bfloat16)
                            for ref in (north_ref, south_ref)
                            for part in range(2)
                            for field in range(fields)
                        ],
                        axis=0,
                    )
                    for tile in range(tiles)
                ],
                axis=1,
            )
            more = lax.dot_general(
                folded, held_table[j], (((1,), (1,)), ((), ())), preferred_element_type=jnp.float32
            )
            even, odd = even_ref[slot, :, start:], odd_ref[slot, :, start:]
            held_sums[j] = held_sums[j] + more[:row_total] * even + more[row_total:] * odd
        results[group].start()
    for copy in results:
        copy.wait()
    finished.wait()


def close(hemi, own, other, arrived, base, even, odd, legendre, fields, levels, least, chunk):
    slots, row_total, degrees = base.shape
    block = 4
    rows, width = arrived.shape
    tiles = chunk[1]
    half = pltpu.VMEM((fields, tiles, levels * padded(block * len(least)), LANES), jnp.float32)
    held = []
    for start in least:
        held.append(pltpu.VMEM((block, degrees - start, tiles * LANES), jnp.bfloat16))
        held.append(pltpu.VMEM((block, row_total, degrees - start), jnp.float32))
    anywhere = pl.BlockSpec(memory_space=pl.ANY)
    return pl.pallas_call(
        functools.partial(closing_kernel, levels, fields, least, chunk),
        in_specs=[pl.BlockSpec(memory_space=pltpu.SMEM), anywhere, anywhere, anywhere]
        + [pl.BlockSpec(even.shape, lambda: (0, 0, 0))] * 2
        + [pl.BlockSpec(own.shape, lambda: (0, 0))] * 2,
        out_specs=anywhere,
        out_shape=jax.ShapeDtypeStruct(base.shape, jnp.float32),
        input_output_aliases={3: 0},
        scratch_shapes=[
            pltpu.VMEM((fields, rows, tiles * LANES), jnp.bfloat16),
            half,
            half,
            pltpu.VMEM((4, row_total, LANES), jnp.float32),
            pltpu.SemaphoreType.DMA((3 * len(least) + fields + 1,)),
            *held,
        ],
        compiler_params=pltpu.CompilerParams(vmem_limit_bytes=VMEM_BYTES),
        cost_estimate=pl.CostEstimate(
            flops=4 * slots * row_total * degrees * tiles * LANES,
            bytes_accessed=8 * slots * row_total * degrees + 2 * rows * width,
            transcendentals=0,
        ),
        name="closing",
    )(hemi, arrived, legendre, base, even, odd, own, other)


def across_halves(value):
    planes = lax.axis_size("grp")
    return lax.ppermute(value, "grp", [(p, (p + planes // 2) % planes) for p in range(planes)])


def within_half(parts):
    bands, planes = lax.axis_size("band"), lax.axis_size("grp")
    half = planes // 2
    moved = [parts[0]]
    for x in range(1, len(parts)):
        pairs = []
        for band in range(bands):
            for plane in range(planes):
                level = (plane % half * bands + band) ^ x
                target = level % bands * planes + plane // half * half + level // bands
                pairs.append((band * planes + plane, target))
        moved.append(lax.ppermute(parts[x], AXES, pairs))
    return moved


def after(value, *others):
    return lax.optimization_barrier((value, others))[0]


def trig_kernel(small_ref, cos_turn_ref, sin_turn_ref, by_wave_ref, by_lon_ref):
    shape = cos_turn_ref.shape
    cos_start, sin_start, cos_step, sin_step = [
        jnp.broadcast_to(small_ref[:, column : column + 1], shape) for column in range(4)
    ]
    cos_turn, sin_turn = cos_turn_ref[...], sin_turn_ref[...]
    cosine = cos_start * cos_turn - sin_start * sin_turn
    sine = sin_start * cos_turn + cos_start * sin_turn
    flipped = [x.T for x in (cosine, sine, cos_step, sin_step)]
    blocks = by_wave_ref.shape[1] // LANES
    for position, (c, s, dc, ds) in enumerate(((cosine, sine, cos_step, sin_step), flipped)):
        for block in range(blocks):
            part = pl.ds(block * LANES, LANES)
            if position == 0:
                by_wave_ref[:, part] = c.astype(by_wave_ref.dtype)
            else:
                by_lon_ref[part, :] = c.astype(by_lon_ref.dtype)
            c, s = c * dc - s * ds, s * dc + c * ds


def trig_tables(owner_table, lon_count, *others):
    waves = jnp.repeat(owner_table, 2).astype(jnp.float32)[:, None]
    quarter = jnp.tile(jnp.array([0, lon_count // 4], jnp.float32), owner_table.shape[0])[:, None]
    unit = 2.0 * math.pi / lon_count

    def angles(phase):
        return (phase - lon_count * jnp.floor(phase * (1.0 / lon_count))) * unit

    start = angles(quarter)
    step = angles(waves * LANES)
    turn = angles(waves * jnp.arange(LANES, dtype=jnp.float32)[None, :])
    small = jnp.concatenate([jnp.cos(start), jnp.sin(start), jnp.cos(step), jnp.sin(step)], axis=1)
    parts = after((small, jnp.cos(turn), jnp.sin(turn)), *others)
    depth = waves.shape[0]
    rows = 256
    wide = pl.BlockSpec((rows, LANES), lambda i: (i, 0))
    return pl.pallas_call(
        trig_kernel,
        grid=(depth // rows,),
        in_specs=[pl.BlockSpec((rows, 4), lambda i: (i, 0)), wide, wide],
        out_specs=[
            pl.BlockSpec((rows, lon_count), lambda i: (i, 0)),
            pl.BlockSpec((lon_count, rows), lambda i: (0, i)),
        ],
        out_shape=[
            jax.ShapeDtypeStruct((depth, lon_count), jnp.bfloat16),
            jax.ShapeDtypeStruct((lon_count, depth), jnp.bfloat16),
        ],
        compiler_params=pltpu.CompilerParams(vmem_limit_bytes=VMEM_BYTES),
        cost_estimate=pl.CostEstimate(
            flops=12 * depth * lon_count, bytes_accessed=4 * depth * lon_count, transcendentals=0
        ),
        name="trig",
    )(*parts)


def exchange(rows):
    return lax.all_to_all(rows, AXES[::-1], split_axis=0, concat_axis=0, tiled=True)


def by_hemisphere_and_level(spectral, legendre, owner_table):
    slots, _, fields, levels, degrees = spectral.shape
    half_lat = legendre.shape[2]
    lon_count = 4 * half_lat
    row_total = 2 * fields * levels
    tiles = half_lat // LANES
    first = lax.axis_index(AXES).astype(jnp.int32) * slots
    spec_rows = spectral.reshape(slots, row_total, degrees)
    devices = 2 * levels
    least = tuple(4 * g * devices for g in range(slots // 4 - 1))
    near = slots - 4
    far_least = near * devices
    cut = tiles - tiles // 2
    chunks = [(0, cut), (cut, tiles - cut)]

    def send(spec, chunk):
        return synthesize(first.reshape(1), owner_table, spec, legendre, chunk, fields, levels, least)

    own_pack = pack(spec_rows, legendre, near)
    partner_pack = across_halves(own_pack)
    large = send(after(spec_rows, own_pack), chunks[0])

    bands, planes = lax.axis_size("band"), lax.axis_size("grp")
    by_device = jnp.swapaxes(owner_table.reshape(bands, planes, slots), 0, 1).reshape(2, levels, slots)
    plane = lax.axis_index("grp").astype(jnp.int32)
    hemi = plane // (planes // 2)
    level = plane % (planes // 2) * bands + lax.axis_index("band").astype(jnp.int32)
    place = jnp.stack([hemi, level])
    far = by_device[:, :, near:]
    both_halves = jnp.concatenate([far[0], far[1]], axis=1)
    swapped = jnp.concatenate([far[1], far[0]], axis=1)
    far_waves = jnp.where(hemi == 0, both_halves, swapped)
    far_waves = jnp.take(far_waves, jnp.arange(levels, dtype=jnp.int32) ^ level, axis=0)
    waves = jnp.concatenate([by_device[:, :, :near].reshape(-1), far_waves.reshape(-1)])

    small = send(after(spec_rows, large), chunks[1])
    by_wave, by_lon = trig_tables(after(waves, large), lon_count, small)
    arrived = [exchange(after(large, small, partner_pack))]
    far_rows = far_synthesize(
        place, far_waves[0] - far_least, own_pack, partner_pack, levels, fields, 1.0 / math.sqrt(degrees)
    )
    far_rows = jnp.concatenate(within_half(far_rows))
    arrived.append(exchange(after(small, far_rows, *arrived)))
    zonal = [
        longitudes(rows, far_rows, by_lon, by_wave, fields, chunk) for rows, chunk in zip(arrived, chunks)
    ]
    returned = [exchange(zonal[0][0])]
    far_zonal = jnp.concatenate([zonal[0][1], zonal[1][1]], axis=1)
    far_zonal = within_half([far_zonal[16 * x : 16 * x + 16] for x in range(levels)])
    returned.append(exchange(after(zonal[1][0], *far_zonal, *returned)))
    own_sums, partner_sums = far_analyze(place, own_pack, partner_pack, far_zonal, levels, fields, chunks)
    other_sums = across_halves(partner_sums)
    wavenumber = lax.dynamic_slice_in_dim(after(owner_table, by_wave), first, slots)
    distance = jnp.arange(degrees, dtype=jnp.int32)[None, :] - wavenumber[:, None]
    scale = 1.0 / math.sqrt(2 * half_lat)
    even = jnp.where((distance >= 0) & (distance % 2 == 0), scale, 0.0).astype(jnp.float32)[:, None, :]
    odd = jnp.where((distance >= 0) & (distance % 2 != 0), scale, 0.0).astype(jnp.float32)[:, None, :]

    folded = fold(returned[0], near, levels, fields)
    base = analyze(folded, even, odd, legendre, row_total, least, chunks[0])
    last = after(returned[1], base)
    out = close(hemi.reshape(1), own_sums, other_sums, last, base, even, odd, legendre, fields, levels, least, chunks[1])
    return out.reshape(slots, 2, fields, levels, degrees)


def make_trig(wavenumber, lon_count):
    lon_index = jnp.arange(lon_count, dtype=jnp.int32)
    phases = wavenumber[:, None] * lon_index[None, :] % lon_count
    angles = phases.astype(jnp.float32) * (2.0 * math.pi / lon_count)
    return jnp.stack([jnp.cos(angles), -jnp.sin(angles)], axis=1).astype(jnp.bfloat16)


def by_level_and_latitude(spectral, legendre, owner_table):
    slot_count, _, fields, levels, degrees = spectral.shape
    half_lat = legendre.shape[2]
    lat_count = 2 * half_lat
    lon_count = 2 * lat_count
    wave_count = owner_table.shape[0]
    band_count = lax.axis_size("band")
    group_count = lax.axis_size("grp")
    device_count = band_count * group_count
    level_block = levels // band_count
    lat_block = lat_count // group_count
    row_total = 2 * fields * levels
    row_width = fields * level_block * lat_block
    slot_start = lax.axis_index(("band", "grp")) * slot_count
    wavenumber = lax.dynamic_slice_in_dim(owner_table, slot_start, slot_count)
    degree_index = jnp.arange(degrees, dtype=jnp.int32)
    keep_mask = (degree_index[None, :] >= wavenumber[:, None]).astype(jnp.bfloat16)
    odd_part = (degree_index[None, :] - wavenumber[:, None]) % 2
    flip_sign = (1 - 2 * odd_part).astype(jnp.bfloat16)
    spec_rows = spectral.reshape(slot_count, row_total, degrees) * keep_mask[:, None, :]
    both_rows = jnp.concatenate([spec_rows, spec_rows * flip_sign[:, None, :]], axis=1)
    halves = jnp.einsum("srn,snt->srt", both_rows, legendre, preferred_element_type=jnp.float32)
    northern = halves[:, :row_total]
    mirrored = halves[:, row_total:]
    fourier = jnp.concatenate([northern, jnp.flip(mirrored, axis=2)], axis=2)
    fourier = fourier.reshape(
        slot_count, 2, fields, band_count, level_block, group_count, lat_block
    )
    fourier = jnp.transpose(fourier, (0, 1, 2, 3, 5, 4, 6))
    fourier_low = (fourier * (1.0 / math.sqrt(degrees))).astype(jnp.bfloat16)
    packed = fourier_low.reshape(1, slot_count, 2, fields, device_count, level_block, lat_block)
    arrived = lax.all_to_all(packed, ("band", "grp"), split_axis=4, concat_axis=0, tiled=True)
    arrived = arrived.reshape(-1, 2, row_width)
    trig_rows = make_trig(owner_table, lon_count)
    grid_values = jnp.einsum("scw,scl->wl", arrived, trig_rows, preferred_element_type=jnp.float32)
    grid_values = (grid_values * (1.0 / math.sqrt(wave_count))).reshape(
        fields, level_block * lat_block, lon_count
    )
    product = (grid_values * jnp.roll(grid_values, -1, axis=0)).astype(jnp.bfloat16)
    zonal_coeffs = jnp.einsum(
        "wl,scl->scw",
        product.reshape(row_width, lon_count),
        trig_rows,
        preferred_element_type=jnp.float32,
    )
    zonal_coeffs = (zonal_coeffs * (2.0 / math.sqrt(lon_count))).astype(jnp.bfloat16)
    sendback = zonal_coeffs.reshape(device_count, slot_count, 2, fields, 1, level_block, lat_block)
    returned = lax.all_to_all(sendback, ("band", "grp"), split_axis=0, concat_axis=4, tiled=True)
    returned = returned.reshape(
        slot_count, 2, fields, band_count, group_count, level_block, lat_block
    )
    returned = jnp.transpose(returned, (0, 1, 2, 3, 5, 4, 6)).reshape(slot_count, row_total, lat_count)
    northern_part = returned[:, :, :half_lat].astype(jnp.float32)
    mirror_part = jnp.flip(returned[:, :, half_lat:], axis=2).astype(jnp.float32)
    plus_part = (northern_part + mirror_part).astype(jnp.bfloat16)
    minus_part = (northern_part - mirror_part).astype(jnp.bfloat16)
    stacked = jnp.concatenate([plus_part, minus_part], axis=1)
    projected = jnp.einsum("srt,snt->srn", stacked, legendre, preferred_element_type=jnp.float32)
    even_rows = flip_sign[:, None, :] > 0
    chosen = jnp.where(even_rows, projected[:, :row_total], projected[:, row_total:])
    chosen = chosen * keep_mask.astype(jnp.float32)[:, None, :] * (1.0 / math.sqrt(lat_count))
    return chosen.reshape(slot_count, 2, fields, levels, degrees)


def on_device(spectral, legendre, owner_table):
    slots, _, _, levels, _ = spectral.shape
    whole_hemispheres = lax.axis_size("band") * lax.axis_size("grp") == 2 * levels
    halves = lax.axis_size("grp") % 2 == 0 and levels & (levels - 1) == 0
    few_left = legendre.shape[1] - (slots - 4) * 2 * levels == LANES
    if whole_hemispheres and halves and few_left and legendre.shape[2] % LANES == 0 and legendre.shape[2] > LANES and slots % 4 == 0 and levels % 16 == 0:
        return by_hemisphere_and_level(spectral, legendre, owner_table)
    return by_level_and_latitude(spectral, legendre, owner_table)


def solution(mesh):
    placed = (P(("band", "grp"), None, None, None, None), P(("band", "grp"), None, None), P())
    return jax.shard_map(
        on_device,
        mesh=mesh,
        in_specs=placed,
        out_specs=P(("band", "grp"), None, None, None, None),
        check_vma=False,
    )
```

```python
import functools
import math

import jax
import jax.numpy as jnp
from jax import lax
from jax.experimental import pallas as pl
from jax.experimental.pallas import tpu as pltpu
from jax.sharding import PartitionSpec as P

LANES = 128
AXES = ("band", "grp")
VMEM_BYTES = 62 * 1024 * 1024


def padded(slots):
    return 2 * slots + 8


def synthesis_kernel(
    slots, levels, fields, least, chunk, scale, first_ref, owner_ref, spec_ref, table_ref, out_ref, rows_ref, sems, *held
):
    at, tiles = chunk
    groups = len(least)
    block = 4
    row_total, degrees = spec_ref.shape[1:]
    stride = padded(slots)
    copies = []
    for group, start in enumerate(least):
        mine = pl.ds(group * block, block)
        left = pl.ds(start, degrees - start)
        lanes = pl.ds(at * LANES, tiles * LANES)
        copies.append(
            (
                pltpu.make_async_copy(spec_ref.at[mine, :, left], held[2 * group], sems.at[2 * group]),
                pltpu.make_async_copy(table_ref.at[mine, left, lanes], held[2 * group + 1], sems.at[2 * group + 1]),
            )
        )
    order = range(groups - 1, -1, -1)
    for group in order:
        for copy in copies[group]:
            copy.start()
    for group in order:
        for copy in copies[group]:
            copy.wait()
        for j in range(block):
            spec = held[2 * group][j]
            wave = owner_ref[first_ref[0] + group * block + j]
            distance = lax.broadcasted_iota(jnp.int32, (1, spec.shape[1]), 1) + (least[group] - wave)
            keep = jnp.where(distance >= 0, 1.0, 0.0)
            flip = jnp.where(distance % 2 == 0, keep, -keep)
            both = jnp.concatenate([spec * keep.astype(spec.dtype), spec * flip.astype(spec.dtype)], axis=0)
            halves = jnp.dot(both, held[2 * group + 1][j], preferred_element_type=jnp.float32) * scale
            first = 2 * (group * block + j)
            for hemi in range(2):
                for part in range(2):
                    for field in range(fields):
                        row = hemi * row_total + (part * fields + field) * levels
                        target = pl.ds(hemi * levels * stride + first + part, levels, stride=stride)
                        for tile in range(tiles):
                            lanes = slice(tile * LANES, (tile + 1) * LANES)
                            rows_ref[field, tile, target, :] = halves[row : row + levels, lanes]
    for field in range(fields):
        for tile in range(tiles):
            lanes = pl.ds((field * tiles + tile) * LANES, LANES)
            rows = rows_ref[field, tile].reshape(2 * levels, stride, LANES)[:, : 2 * slots]
            out_ref[:, lanes] = rows.reshape(out_ref.shape[0], LANES).astype(out_ref.dtype)


def synthesize(first, owner_table, spec_rows, legendre, chunk, fields, levels, least):
    _, row_total, degrees = spec_rows.shape
    block = 4
    slots = block * len(least)
    rows = 2 * levels * 2 * slots
    tiles = chunk[1]
    shape = (rows, fields * tiles * LANES)
    held = []
    for start in least:
        held.append(pltpu.VMEM((block, row_total, degrees - start), jnp.bfloat16))
        held.append(pltpu.VMEM((block, degrees - start, tiles * LANES), jnp.bfloat16))
    return pl.pallas_call(
        functools.partial(synthesis_kernel, slots, levels, fields, least, chunk, 1.0 / math.sqrt(degrees)),
        in_specs=[pl.BlockSpec(memory_space=pltpu.SMEM)] * 2 + [pl.BlockSpec(memory_space=pl.ANY)] * 2,
        out_specs=pl.BlockSpec(shape, lambda: (0, 0)),
        out_shape=jax.ShapeDtypeStruct(shape, jnp.bfloat16),
        scratch_shapes=[
            pltpu.VMEM((fields, tiles, 2 * levels * padded(slots), LANES), jnp.float32),
            pltpu.SemaphoreType.DMA((2 * len(least),)),
            *held,
        ],
        compiler_params=pltpu.CompilerParams(vmem_limit_bytes=VMEM_BYTES),
        cost_estimate=pl.CostEstimate(
            flops=4 * slots * row_total * degrees * tiles * LANES,
            bytes_accessed=2 * slots * degrees * (row_total + tiles * LANES) + 2 * rows * shape[1],
            transcendentals=0,
        ),
        name="synthesis",
    )(first, owner_table, spec_rows, legendre)


def longitude_kernel(
    fields, chunk, grid_scale, zonal_scale, rows_ref, far_ref, by_lon_ref, by_wave_ref, out_ref, far_out_ref, sum_ref
):
    step = pl.program_id(0)
    near = rows_ref.shape[0]
    values = jnp.dot(by_lon_ref[:, :near], rows_ref[...], preferred_element_type=jnp.float32)
    one = values.shape[1] // fields
    each = far_ref.shape[1] // fields
    starts = [field * each + chunk[0] * LANES for field in range(fields)]
    far = jnp.concatenate([far_ref[:, start : start + one] for start in starts], axis=1)
    values = values + jnp.dot(by_lon_ref[:, near:], far, preferred_element_type=jnp.float32)
    values = values * grid_scale
    following = jnp.concatenate([values[:, one:], values[:, :one]], axis=1)
    product = (values * following).astype(jnp.bfloat16)
    share = jnp.dot(by_wave_ref[...], product, preferred_element_type=jnp.float32)

    @pl.when(step == 0)
    def _():
        sum_ref[...] = share

    @pl.when(step > 0)
    def _():
        sum_ref[...] += share

    @pl.when(step == pl.num_programs(0) - 1)
    def _():
        out_ref[...] = (sum_ref[:near, :] * zonal_scale).astype(out_ref.dtype)
        far_out_ref[...] = (sum_ref[near:, :] * zonal_scale).astype(far_out_ref.dtype)


def longitudes(rows, far, by_lon, by_wave, fields, chunk):
    depth, width = rows.shape[0] + far.shape[0], rows.shape[1]
    lon_count = by_lon.shape[0]
    lon_block = lon_count // 5
    near_spec = pl.BlockSpec(rows.shape, lambda i: (0, 0))
    far_out = jax.ShapeDtypeStruct((far.shape[0], width), jnp.bfloat16)
    return pl.pallas_call(
        functools.partial(longitude_kernel, fields, chunk, 1.0 / math.sqrt(depth // 2), 2.0 / math.sqrt(lon_count)),
        grid=(lon_count // lon_block,),
        in_specs=[
            near_spec,
            pl.BlockSpec(far.shape, lambda i: (0, 0)),
            pl.BlockSpec((lon_block, depth), lambda i: (i, 0)),
            pl.BlockSpec((depth, lon_block), lambda i: (0, i)),
        ],
        out_specs=[near_spec, pl.BlockSpec(far_out.shape, lambda i: (0, 0))],
        out_shape=[jax.ShapeDtypeStruct(rows.shape, jnp.bfloat16), far_out],
        scratch_shapes=[pltpu.VMEM((depth, width), jnp.float32)],
        compiler_params=pltpu.CompilerParams(vmem_limit_bytes=VMEM_BYTES),
        cost_estimate=pl.CostEstimate(
            flops=4 * depth * width * lon_count,
            bytes_accessed=4 * depth * (width + lon_count),
            transcendentals=0,
        ),
        name="longitudes",
    )(rows, far, by_lon, by_wave)


def pack_kernel(near, spec_ref, table_ref, out_ref, last_ref, tail_ref, sems):
    degrees, half_lat = table_ref.shape[1:]
    half = LANES // 2
    copies = []

    def fetch(source, target):
        copies.append(pltpu.make_async_copy(source, target, sems.at[len(copies)]))
        copies[-1].start()

    lanes, sides = pl.ds(0, half_lat), pl.ds(half_lat, LANES)
    for slot in range(2):
        rows = pl.ds(slot * LANES, LANES)
        fetch(table_ref.at[near + slot, pl.ds(degrees - LANES, LANES), :], out_ref.at[rows, lanes])
        fetch(spec_ref.at[near + slot, :, pl.ds(degrees - LANES, LANES)], out_ref.at[rows, sides])
    for slot in range(2):
        rows = pl.ds(slot * half, half)
        fetch(table_ref.at[near + 2 + slot, pl.ds(degrees - half, half), :], last_ref.at[rows, lanes])
        fetch(spec_ref.at[near + 2 + slot, :, pl.ds(degrees - LANES, LANES)], tail_ref.at[slot])
    for copy in copies:
        copy.wait()
    third = pltpu.roll(tail_ref[0].astype(jnp.float32), half, 1)
    lower = lax.broadcasted_iota(jnp.int32, third.shape, 1) < half
    both = jnp.where(lower, third, tail_ref[1].astype(jnp.float32))
    last_ref[:, sides] = both.astype(last_ref.dtype)


def pack(spec_rows, legendre, near):
    shapes = [(rows * LANES, legendre.shape[2] + LANES) for rows in (2, 1)]
    return pl.pallas_call(
        functools.partial(pack_kernel, near),
        in_specs=[pl.BlockSpec(memory_space=pl.ANY)] * 2,
        out_specs=[pl.BlockSpec(shape, lambda: (0, 0)) for shape in shapes],
        out_shape=[jax.ShapeDtypeStruct(shape, jnp.bfloat16) for shape in shapes],
        scratch_shapes=[
            pltpu.VMEM((2, spec_rows.shape[1], LANES), jnp.bfloat16),
            pltpu.SemaphoreType.DMA((8,)),
        ],
        compiler_params=pltpu.CompilerParams(vmem_limit_bytes=VMEM_BYTES),
        cost_estimate=pl.CostEstimate(flops=0, bytes_accessed=12 * LANES * shapes[0][1], transcendentals=0),
        name="pack",
    )(spec_rows, legendre)


def far_synthesis_kernel(levels, fields, scale, place_ref, waves_ref, *refs):
    pack_refs, out_refs, rows_ref = refs[:4], refs[4:-1], refs[-1]
    tiles = rows_ref.shape[1]
    half_lat = tiles * LANES
    stride = rows_ref.shape[2] // levels
    degree = lax.broadcasted_iota(jnp.int32, (1, LANES), 1)
    for slot in range(8):
        local = slot % 4
        pack_ref = pack_refs[slot // 4 * 2 + local // 2]
        rows = pl.ds(local % 2 * LANES if local < 2 else 0, LANES)
        distance = degree - waves_ref[slot] + (LANES // 2 if local == 2 else 0)
        keep = jnp.where(distance >= 0, 1.0, 0.0)
        if local >= 2:
            keep = jnp.where((degree < LANES // 2) if local == 2 else (degree >= LANES // 2), keep, 0.0)
        turned = jnp.where(distance % 2 == 0, keep, -keep)
        sign = jnp.where(place_ref[0] == 0, keep, turned)
        spec = pack_ref[rows, half_lat:]
        table = pack_ref[rows, :half_lat]
        sums = jnp.dot(spec * sign.astype(spec.dtype), table, preferred_element_type=jnp.float32) * scale
        for part in range(2):
            for field in range(fields):
                row = (part * fields + field) * levels
                for tile in range(tiles):
                    target = pl.ds(2 * slot + part, levels, stride=stride)
                    rows_ref[field, tile, target, :] = sums[row : row + levels, tile * LANES : (tile + 1) * LANES]
    for apart, out_ref in enumerate(out_refs):
        rows = pl.ds(pl.multiple_of((place_ref[1] ^ apart) * stride, stride), stride)
        for field in range(fields):
            for tile in range(tiles):
                lanes = pl.ds((field * tiles + tile) * LANES, LANES)
                out_ref[:, lanes] = rows_ref[field, tile, rows, :].astype(out_ref.dtype)


def far_synthesize(place, waves, packs, levels, fields, scale):
    tiles = packs[0].shape[1] // LANES - 1
    shape = (16, fields * tiles * LANES)
    return pl.pallas_call(
        functools.partial(far_synthesis_kernel, levels, fields, scale),
        in_specs=[pl.BlockSpec(memory_space=pltpu.SMEM)] * 2 + [pl.BlockSpec(x.shape, lambda: (0, 0)) for x in packs],
        out_specs=[pl.BlockSpec(shape, lambda: (0, 0))] * levels,
        out_shape=[jax.ShapeDtypeStruct(shape, jnp.bfloat16)] * levels,
        scratch_shapes=[pltpu.VMEM((fields, tiles, 16 * levels, LANES), jnp.float32)],
        compiler_params=pltpu.CompilerParams(vmem_limit_bytes=VMEM_BYTES),
        cost_estimate=pl.CostEstimate(
            flops=16 * 2 * fields * levels * LANES * tiles * LANES, bytes_accessed=12 * packs[0].size, transcendentals=0
        ),
        name="far_synthesis",
    )(place, waves, *packs)


def far_analysis_kernel(levels, fields, chunks, place_ref, *refs):
    pack_refs, zonal_refs = refs[:4], refs[4:-3]
    own_out_ref, partner_out_ref, rows_ref = refs[-3:]
    tiles = rows_ref.shape[1]
    stride = rows_ref.shape[2] // levels
    for apart, zonal_ref in enumerate(zonal_refs):
        rows = pl.ds(pl.multiple_of((place_ref[1] ^ apart) * stride, stride), stride)
        offset = 0
        for at, count in chunks:
            for field in range(fields):
                for tile in range(at, at + count):
                    rows_ref[field, tile, rows, :] = zonal_ref[:, pl.ds(offset, LANES)].astype(jnp.float32)
                    offset += LANES
    lower = lax.broadcasted_iota(jnp.int32, (1, LANES), 1) < LANES // 2
    for out_ref, base in ((own_out_ref, 0), (partner_out_ref, 4)):
        sums = []
        for local in range(4):
            pack_ref = pack_refs[base // 2 + local // 2]
            rows = pl.ds(local % 2 * LANES if local < 2 else 0, LANES)
            zonal = jnp.concatenate(
                [
                    jnp.concatenate(
                        [
                            rows_ref[field, tile, pl.ds(2 * (base + local) + part, levels, stride=stride), :]
                            for part in range(2)
                            for field in range(fields)
                        ],
                        axis=0,
                    ).astype(jnp.bfloat16)
                    for tile in range(tiles)
                ],
                axis=1,
            )
            table = pack_ref[rows, : tiles * LANES]
            sums.append(
                lax.dot_general(zonal, table, (((1,), (1,)), ((), ())), preferred_element_type=jnp.float32)
            )
        sums[2] = jnp.where(lower, sums[2], sums[3])
        size = sums[0].shape[0]
        for block in range(3):
            out_ref[pl.ds(block * size, size), :] = sums[block].astype(out_ref.dtype)


def far_analyze(place, packs, zonal, levels, fields, chunks):
    tiles = packs[0].shape[1] // LANES - 1
    shape = (3 * 2 * fields * levels, LANES)
    out_spec = pl.BlockSpec(shape, lambda: (0, 0))
    return pl.pallas_call(
        functools.partial(far_analysis_kernel, levels, fields, chunks),
        in_specs=[pl.BlockSpec(memory_space=pltpu.SMEM)]
        + [pl.BlockSpec(x.shape, lambda: (0, 0)) for x in (*packs, *zonal)],
        out_specs=[out_spec, out_spec],
        out_shape=[jax.ShapeDtypeStruct(shape, jnp.float32), jax.ShapeDtypeStruct(shape, jnp.bfloat16)],
        scratch_shapes=[pltpu.VMEM((fields, tiles, 16 * levels, LANES), jnp.float32)],
        compiler_params=pltpu.CompilerParams(vmem_limit_bytes=VMEM_BYTES),
        cost_estimate=pl.CostEstimate(
            flops=16 * 2 * fields * levels * LANES * tiles * LANES, bytes_accessed=12 * packs[0].size, transcendentals=0
        ),
        name="far_analysis",
    )(place, *packs, *zonal)


def fold_kernel(slots, levels, fields, arrived_ref, out_ref, rows_ref):
    tiles = rows_ref.shape[1]
    stride = padded(slots)
    half = levels * stride
    for field in range(fields):
        for tile in range(tiles):
            lanes = pl.ds((field * tiles + tile) * LANES, LANES)
            rows = arrived_ref[:, lanes].astype(jnp.float32)
            for source in range(2 * levels):
                mine = rows[2 * slots * source : 2 * slots * (source + 1)]
                rows_ref[field, tile, pl.ds(stride * source, 2 * slots), :] = mine
    for slot in range(slots):
        for part in range(2):
            for field in range(fields):
                for tile in range(tiles):
                    first = 2 * slot + part
                    north = rows_ref[field, tile, pl.ds(first, levels, stride=stride), :]
                    south = rows_ref[field, tile, pl.ds(half + first, levels, stride=stride), :]
                    lanes = pl.ds(tile * LANES, LANES)
                    at = (part * fields + field) * levels
                    out_ref[slot, at : at + levels, lanes] = (north + south).astype(out_ref.dtype)
                    at += 2 * fields * levels
                    out_ref[slot, at : at + levels, lanes] = (north - south).astype(out_ref.dtype)


def fold(arrived, slots, levels, fields):
    row_total = 2 * fields * levels
    rows, width = arrived.shape
    tiles = width // (fields * LANES)
    shape = (slots, 2 * row_total, tiles * LANES)
    return pl.pallas_call(
        functools.partial(fold_kernel, slots, levels, fields),
        in_specs=[pl.BlockSpec((rows, width), lambda: (0, 0))],
        out_specs=pl.BlockSpec(shape, lambda: (0, 0, 0)),
        out_shape=jax.ShapeDtypeStruct(shape, jnp.bfloat16),
        scratch_shapes=[pltpu.VMEM((fields, tiles, 2 * levels * padded(slots), LANES), jnp.float32)],
        compiler_params=pltpu.CompilerParams(vmem_limit_bytes=VMEM_BYTES),
        cost_estimate=pl.CostEstimate(flops=2 * rows * width, bytes_accessed=4 * rows * width, transcendentals=0),
        name="fold",
    )(arrived)


def analysis_kernel(least, folded_ref, even_ref, odd_ref, *refs):
    table_refs, out_ref = refs[:-1], refs[-1]
    row_total, degrees = out_ref.shape[1:]
    step = pl.program_id(0)

    def run(group):
        start = least[group]
        for j in range(out_ref.shape[0]):
            table = jnp.concatenate([ref[j, start:, :] for ref in table_refs], axis=1)
            sums = lax.dot_general(
                folded_ref[j], table, (((1,), (1,)), ((), ())), preferred_element_type=jnp.float32
            )
            kept = sums[:row_total] * even_ref[j, :, start:] + sums[row_total:] * odd_ref[j, :, start:]
            out_ref[j, :, start:] = kept
            if start:
                out_ref[j, :, :start] = jnp.zeros((row_total, start), out_ref.dtype)

    for group in range(len(least)):
        pl.when(step == group)(functools.partial(run, group))

    @pl.when(step == len(least))
    def _():
        out_ref[...] = jnp.zeros(out_ref.shape, out_ref.dtype)


def analyze(folded, even, odd, legendre, row_total, least, chunk):
    slots, degrees, _ = legendre.shape
    block = 4
    near = len(least) - 1
    at, tiles = chunk
    mask_spec = pl.BlockSpec((block, 1, degrees), lambda i: (i, 0, 0))
    return pl.pallas_call(
        functools.partial(analysis_kernel, least),
        grid=(len(least) + 1,),
        in_specs=[
            pl.BlockSpec((block,) + folded.shape[1:], lambda i: (jnp.minimum(i, near), 0, 0)),
            mask_spec,
            mask_spec,
        ]
        + [
            pl.BlockSpec((block, degrees, LANES), lambda i, t=at + t: (jnp.minimum(i, near), 0, t))
            for t in range(tiles)
        ],
        out_specs=pl.BlockSpec((block, row_total, degrees), lambda i: (i, 0, 0)),
        out_shape=jax.ShapeDtypeStruct((slots, row_total, degrees), jnp.float32),
        compiler_params=pltpu.CompilerParams(vmem_limit_bytes=VMEM_BYTES),
        cost_estimate=pl.CostEstimate(
            flops=4 * slots * row_total * degrees * tiles * LANES,
            bytes_accessed=2 * slots * (degrees * tiles * LANES + 2 * row_total * (tiles * LANES + degrees)),
            transcendentals=0,
        ),
        name="analysis",
    )(folded, even, odd, *[legendre] * tiles)


def closing_kernel(
    levels, fields, least, chunk, hemi_ref, arrived_ref, table_ref, base_ref, even_ref, odd_ref, own_ref, other_ref, out_ref, *refs
):
    got_ref, north_ref, south_ref, far_ref, sems = refs[:5]
    held = refs[5:]
    at, tiles = chunk
    groups = len(least)
    _, row_total, degrees = base_ref.shape
    block = 4
    slots = block * groups
    each = 2 * slots
    stride = padded(slots)
    half = levels * each
    arriving = [
        pltpu.make_async_copy(
            arrived_ref.at[:, pl.ds(field * tiles * LANES, tiles * LANES)], got_ref.at[field], sems.at[3 * groups + field]
        )
        for field in range(fields)
    ]
    tables, sums, results = [], [], []
    for group, start in enumerate(least):
        mine = pl.ds(group * block, block)
        left = pl.ds(start, degrees - start)
        lanes = pl.ds(at * LANES, tiles * LANES)
        held_table, held_sums = held[2 * group], held[2 * group + 1]
        tables.append(pltpu.make_async_copy(table_ref.at[mine, left, lanes], held_table, sems.at[3 * group]))
        sums.append(pltpu.make_async_copy(base_ref.at[mine, :, left], held_sums, sems.at[3 * group + 1]))
        results.append(pltpu.make_async_copy(held_sums, out_ref.at[mine, :, left], sems.at[3 * group + 2]))
    for copy in arriving:
        copy.start()
    for group in range(groups):
        tables[group].start()
        sums[group].start()
    for local in range(4):
        rows = pl.ds(min(local, 2) * row_total, row_total)
        own, other = own_ref[rows, :], other_ref[rows, :].astype(jnp.float32)
        both, change = own + other, jnp.where(hemi_ref[0] == 0, own - other, other - own)
        if local == 2:
            both, change = pltpu.roll(both, LANES // 2, 1), pltpu.roll(change, LANES // 2, 1)
        even = even_ref[slots + local, :, degrees - LANES :]
        odd = odd_ref[slots + local, :, degrees - LANES :]
        far_ref[local] = both * even + change * odd
    finished = pltpu.make_async_copy(
        far_ref, out_ref.at[pl.ds(slots, 4), :, pl.ds(degrees - LANES, LANES)], sems.at[3 * groups + fields]
    )
    finished.start()
    for field in range(fields):
        arriving[field].wait()
        for tile in range(tiles):
            lanes = pl.ds(tile * LANES, LANES)
            north = got_ref[field, :half, lanes].astype(jnp.float32)
            south = got_ref[field, half:, lanes].astype(jnp.float32)
            plus, minus = north + south, north - south
            for level in range(levels):
                rows = pl.ds(stride * level, each)
                north_ref[field, tile, rows, :] = plus[each * level : each * (level + 1)]
                south_ref[field, tile, rows, :] = minus[each * level : each * (level + 1)]
    for group, start in enumerate(least):
        tables[group].wait()
        sums[group].wait()
        held_table, held_sums = held[2 * group], held[2 * group + 1]
        for j in range(block):
            slot = group * block + j
            folded = jnp.concatenate(
                [
                    jnp.concatenate(
                        [
                            ref[field, tile, pl.ds(2 * slot + part, levels, stride=stride), :].astype(jnp.bfloat16)
                            for ref in (north_ref, south_ref)
                            for part in range(2)
                            for field in range(fields)
                        ],
                        axis=0,
                    )
                    for tile in range(tiles)
                ],
                axis=1,
            )
            more = lax.dot_general(
                folded, held_table[j], (((1,), (1,)), ((), ())), preferred_element_type=jnp.float32
            )
            even, odd = even_ref[slot, :, start:], odd_ref[slot, :, start:]
            held_sums[j] = held_sums[j] + more[:row_total] * even + more[row_total:] * odd
        results[group].start()
    for copy in results:
        copy.wait()
    finished.wait()


def close(hemi, own, other, arrived, base, even, odd, legendre, fields, levels, least, chunk):
    slots, row_total, degrees = base.shape
    block = 4
    rows, width = arrived.shape
    tiles = chunk[1]
    half = pltpu.VMEM((fields, tiles, levels * padded(block * len(least)), LANES), jnp.float32)
    held = []
    for start in least:
        held.append(pltpu.VMEM((block, degrees - start, tiles * LANES), jnp.bfloat16))
        held.append(pltpu.VMEM((block, row_total, degrees - start), jnp.float32))
    anywhere = pl.BlockSpec(memory_space=pl.ANY)
    return pl.pallas_call(
        functools.partial(closing_kernel, levels, fields, least, chunk),
        in_specs=[pl.BlockSpec(memory_space=pltpu.SMEM), anywhere, anywhere, anywhere]
        + [pl.BlockSpec(even.shape, lambda: (0, 0, 0))] * 2
        + [pl.BlockSpec(own.shape, lambda: (0, 0))] * 2,
        out_specs=anywhere,
        out_shape=jax.ShapeDtypeStruct(base.shape, jnp.float32),
        input_output_aliases={3: 0},
        scratch_shapes=[
            pltpu.VMEM((fields, rows, tiles * LANES), jnp.bfloat16),
            half,
            half,
            pltpu.VMEM((4, row_total, LANES), jnp.float32),
            pltpu.SemaphoreType.DMA((3 * len(least) + fields + 1,)),
            *held,
        ],
        compiler_params=pltpu.CompilerParams(vmem_limit_bytes=VMEM_BYTES),
        cost_estimate=pl.CostEstimate(
            flops=4 * slots * row_total * degrees * tiles * LANES,
            bytes_accessed=8 * slots * row_total * degrees + 2 * rows * width,
            transcendentals=0,
        ),
        name="closing",
    )(hemi, arrived, legendre, base, even, odd, own, other)


def across_halves(value):
    planes = lax.axis_size("grp")
    return lax.ppermute(value, "grp", [(p, (p + planes // 2) % planes) for p in range(planes)])


def within_half(parts):
    bands, planes = lax.axis_size("band"), lax.axis_size("grp")
    half = planes // 2
    moved = [parts[0]]
    for x in range(1, len(parts)):
        pairs = []
        for band in range(bands):
            for plane in range(planes):
                level = (plane % half * bands + band) ^ x
                target = level % bands * planes + plane // half * half + level // bands
                pairs.append((band * planes + plane, target))
        moved.append(lax.ppermute(parts[x], AXES, pairs))
    return moved


def after(value, *others):
    return lax.optimization_barrier((value, others))[0]


def trig_kernel(small_ref, cos_turn_ref, sin_turn_ref, by_wave_ref, by_lon_ref):
    shape = cos_turn_ref.shape
    cos_start, sin_start, cos_step, sin_step = [
        jnp.broadcast_to(small_ref[:, column : column + 1], shape) for column in range(4)
    ]
    cos_turn, sin_turn = cos_turn_ref[...], sin_turn_ref[...]
    cosine = cos_start * cos_turn - sin_start * sin_turn
    sine = sin_start * cos_turn + cos_start * sin_turn
    flipped = [x.T for x in (cosine, sine, cos_step, sin_step)]
    blocks = by_wave_ref.shape[1] // LANES
    for position, (c, s, dc, ds) in enumerate(((cosine, sine, cos_step, sin_step), flipped)):
        for block in range(blocks):
            part = pl.ds(block * LANES, LANES)
            if position == 0:
                by_wave_ref[:, part] = c.astype(by_wave_ref.dtype)
            else:
                by_lon_ref[part, :] = c.astype(by_lon_ref.dtype)
            c, s = c * dc - s * ds, s * dc + c * ds


def trig_tables(owner_table, lon_count, *others):
    waves = jnp.repeat(owner_table, 2).astype(jnp.float32)[:, None]
    quarter = jnp.tile(jnp.array([0, lon_count // 4], jnp.float32), owner_table.shape[0])[:, None]
    unit = 2.0 * math.pi / lon_count

    def angles(phase):
        return (phase - lon_count * jnp.floor(phase * (1.0 / lon_count))) * unit

    start = angles(quarter)
    step = angles(waves * LANES)
    turn = angles(waves * jnp.arange(LANES, dtype=jnp.float32)[None, :])
    small = jnp.concatenate([jnp.cos(start), jnp.sin(start), jnp.cos(step), jnp.sin(step)], axis=1)
    parts = after((small, jnp.cos(turn), jnp.sin(turn)), *others)
    depth = waves.shape[0]
    rows = 256
    wide = pl.BlockSpec((rows, LANES), lambda i: (i, 0))
    return pl.pallas_call(
        trig_kernel,
        grid=(depth // rows,),
        in_specs=[pl.BlockSpec((rows, 4), lambda i: (i, 0)), wide, wide],
        out_specs=[
            pl.BlockSpec((rows, lon_count), lambda i: (i, 0)),
            pl.BlockSpec((lon_count, rows), lambda i: (0, i)),
        ],
        out_shape=[
            jax.ShapeDtypeStruct((depth, lon_count), jnp.bfloat16),
            jax.ShapeDtypeStruct((lon_count, depth), jnp.bfloat16),
        ],
        compiler_params=pltpu.CompilerParams(vmem_limit_bytes=VMEM_BYTES),
        cost_estimate=pl.CostEstimate(
            flops=12 * depth * lon_count, bytes_accessed=4 * depth * lon_count, transcendentals=0
        ),
        name="trig",
    )(*parts)


def exchange(rows):
    return lax.all_to_all(rows, AXES[::-1], split_axis=0, concat_axis=0, tiled=True)


def by_hemisphere_and_level(spectral, legendre, owner_table):
    slots, _, fields, levels, degrees = spectral.shape
    half_lat = legendre.shape[2]
    lon_count = 4 * half_lat
    row_total = 2 * fields * levels
    tiles = half_lat // LANES
    first = lax.axis_index(AXES).astype(jnp.int32) * slots
    spec_rows = spectral.reshape(slots, row_total, degrees)
    devices = 2 * levels
    least = tuple(4 * g * devices for g in range(slots // 4 - 1))
    near = slots - 4
    far_least = near * devices
    cut = tiles - tiles // 2
    chunks = [(0, cut), (cut, tiles - cut)]

    def send(spec, chunk):
        return synthesize(first.reshape(1), owner_table, spec, legendre, chunk, fields, levels, least)

    packs = list(pack(spec_rows, legendre, near))
    packs += [across_halves(packs[0]), across_halves(packs[1])]
    large = send(after(spec_rows, packs[0]), chunks[0])

    bands, planes = lax.axis_size("band"), lax.axis_size("grp")
    by_device = jnp.swapaxes(owner_table.reshape(bands, planes, slots), 0, 1).reshape(2, levels, slots)
    plane = lax.axis_index("grp").astype(jnp.int32)
    hemi = plane // (planes // 2)
    level = plane % (planes // 2) * bands + lax.axis_index("band").astype(jnp.int32)
    place = jnp.stack([hemi, level])
    far = by_device[:, :, near:]
    both_halves = jnp.concatenate([far[0], far[1]], axis=1)
    swapped = jnp.concatenate([far[1], far[0]], axis=1)
    far_waves = jnp.where(hemi == 0, both_halves, swapped)
    far_waves = jnp.take(far_waves, jnp.arange(levels, dtype=jnp.int32) ^ level, axis=0)
    waves = jnp.concatenate([by_device[:, :, :near].reshape(-1), far_waves.reshape(-1)])

    small = send(after(spec_rows, large), chunks[1])
    by_wave, by_lon = trig_tables(after(waves, large), lon_count, small)
    arrived = [exchange(after(large, small, packs[2]))]
    far_rows = far_synthesize(
        place, far_waves[0] - far_least, packs, levels, fields, 1.0 / math.sqrt(degrees)
    )
    far_rows = jnp.concatenate(within_half(far_rows))
    arrived.append(exchange(after(small, far_rows, *arrived)))
    zonal = [
        longitudes(rows, far_rows, by_lon, by_wave, fields, chunk) for rows, chunk in zip(arrived, chunks)
    ]
    returned = [exchange(zonal[0][0])]
    far_zonal = jnp.concatenate([zonal[0][1], zonal[1][1]], axis=1)
    far_zonal = within_half([far_zonal[16 * x : 16 * x + 16] for x in range(levels)])
    returned.append(exchange(after(zonal[1][0], *far_zonal, *returned)))
    own_sums, partner_sums = far_analyze(place, packs, far_zonal, levels, fields, chunks)
    other_sums = across_halves(partner_sums)
    wavenumber = lax.dynamic_slice_in_dim(after(owner_table, by_wave), first, slots)
    distance = jnp.arange(degrees, dtype=jnp.int32)[None, :] - wavenumber[:, None]
    scale = 1.0 / math.sqrt(2 * half_lat)
    even = jnp.where((distance >= 0) & (distance % 2 == 0), scale, 0.0).astype(jnp.float32)[:, None, :]
    odd = jnp.where((distance >= 0) & (distance % 2 != 0), scale, 0.0).astype(jnp.float32)[:, None, :]

    folded = fold(returned[0], near, levels, fields)
    base = analyze(folded, even, odd, legendre, row_total, least, chunks[0])
    last = after(returned[1], base)
    out = close(hemi.reshape(1), own_sums, other_sums, last, base, even, odd, legendre, fields, levels, least, chunks[1])
    return out.reshape(slots, 2, fields, levels, degrees)


def make_trig(wavenumber, lon_count):
    lon_index = jnp.arange(lon_count, dtype=jnp.int32)
    phases = wavenumber[:, None] * lon_index[None, :] % lon_count
    angles = phases.astype(jnp.float32) * (2.0 * math.pi / lon_count)
    return jnp.stack([jnp.cos(angles), -jnp.sin(angles)], axis=1).astype(jnp.bfloat16)


def by_level_and_latitude(spectral, legendre, owner_table):
    slot_count, _, fields, levels, degrees = spectral.shape
    half_lat = legendre.shape[2]
    lat_count = 2 * half_lat
    lon_count = 2 * lat_count
    wave_count = owner_table.shape[0]
    band_count = lax.axis_size("band")
    group_count = lax.axis_size("grp")
    device_count = band_count * group_count
    level_block = levels // band_count
    lat_block = lat_count // group_count
    row_total = 2 * fields * levels
    row_width = fields * level_block * lat_block
    slot_start = lax.axis_index(("band", "grp")) * slot_count
    wavenumber = lax.dynamic_slice_in_dim(owner_table, slot_start, slot_count)
    degree_index = jnp.arange(degrees, dtype=jnp.int32)
    keep_mask = (degree_index[None, :] >= wavenumber[:, None]).astype(jnp.bfloat16)
    odd_part = (degree_index[None, :] - wavenumber[:, None]) % 2
    flip_sign = (1 - 2 * odd_part).astype(jnp.bfloat16)
    spec_rows = spectral.reshape(slot_count, row_total, degrees) * keep_mask[:, None, :]
    both_rows = jnp.concatenate([spec_rows, spec_rows * flip_sign[:, None, :]], axis=1)
    halves = jnp.einsum("srn,snt->srt", both_rows, legendre, preferred_element_type=jnp.float32)
    northern = halves[:, :row_total]
    mirrored = halves[:, row_total:]
    fourier = jnp.concatenate([northern, jnp.flip(mirrored, axis=2)], axis=2)
    fourier = fourier.reshape(
        slot_count, 2, fields, band_count, level_block, group_count, lat_block
    )
    fourier = jnp.transpose(fourier, (0, 1, 2, 3, 5, 4, 6))
    fourier_low = (fourier * (1.0 / math.sqrt(degrees))).astype(jnp.bfloat16)
    packed = fourier_low.reshape(1, slot_count, 2, fields, device_count, level_block, lat_block)
    arrived = lax.all_to_all(packed, ("band", "grp"), split_axis=4, concat_axis=0, tiled=True)
    arrived = arrived.reshape(-1, 2, row_width)
    trig_rows = make_trig(owner_table, lon_count)
    grid_values = jnp.einsum("scw,scl->wl", arrived, trig_rows, preferred_element_type=jnp.float32)
    grid_values = (grid_values * (1.0 / math.sqrt(wave_count))).reshape(
        fields, level_block * lat_block, lon_count
    )
    product = (grid_values * jnp.roll(grid_values, -1, axis=0)).astype(jnp.bfloat16)
    zonal_coeffs = jnp.einsum(
        "wl,scl->scw",
        product.reshape(row_width, lon_count),
        trig_rows,
        preferred_element_type=jnp.float32,
    )
    zonal_coeffs = (zonal_coeffs * (2.0 / math.sqrt(lon_count))).astype(jnp.bfloat16)
    sendback = zonal_coeffs.reshape(device_count, slot_count, 2, fields, 1, level_block, lat_block)
    returned = lax.all_to_all(sendback, ("band", "grp"), split_axis=0, concat_axis=4, tiled=True)
    returned = returned.reshape(
        slot_count, 2, fields, band_count, group_count, level_block, lat_block
    )
    returned = jnp.transpose(returned, (0, 1, 2, 3, 5, 4, 6)).reshape(slot_count, row_total, lat_count)
    northern_part = returned[:, :, :half_lat].astype(jnp.float32)
    mirror_part = jnp.flip(returned[:, :, half_lat:], axis=2).astype(jnp.float32)
    plus_part = (northern_part + mirror_part).astype(jnp.bfloat16)
    minus_part = (northern_part - mirror_part).astype(jnp.bfloat16)
    stacked = jnp.concatenate([plus_part, minus_part], axis=1)
    projected = jnp.einsum("srt,snt->srn", stacked, legendre, preferred_element_type=jnp.float32)
    even_rows = flip_sign[:, None, :] > 0
    chosen = jnp.where(even_rows, projected[:, :row_total], projected[:, row_total:])
    chosen = chosen * keep_mask.astype(jnp.float32)[:, None, :] * (1.0 / math.sqrt(lat_count))
    return chosen.reshape(slot_count, 2, fields, levels, degrees)


def on_device(spectral, legendre, owner_table):
    slots, _, _, levels, _ = spectral.shape
    whole_hemispheres = lax.axis_size("band") * lax.axis_size("grp") == 2 * levels
    halves = lax.axis_size("grp") % 2 == 0 and levels & (levels - 1) == 0
    few_left = legendre.shape[1] - (slots - 4) * 2 * levels == LANES
    if whole_hemispheres and halves and few_left and legendre.shape[2] % LANES == 0 and legendre.shape[2] > LANES and slots % 4 == 0 and levels % 16 == 0:
        return by_hemisphere_and_level(spectral, legendre, owner_table)
    return by_level_and_latitude(spectral, legendre, owner_table)


def solution(mesh):
    placed = (P(("band", "grp"), None, None, None, None), P(("band", "grp"), None, None), P())
    return jax.shard_map(
        on_device,
        mesh=mesh,
        in_specs=placed,
        out_specs=P(("band", "grp"), None, None, None, None),
        check_vma=False,
    )
```

```python
import functools
import math

import jax
import jax.numpy as jnp
from jax import lax
from jax.experimental import pallas as pl
from jax.experimental.pallas import tpu as pltpu
from jax.sharding import PartitionSpec as P

LANES = 128
AXES = ("band", "grp")
VMEM_BYTES = 62 * 1024 * 1024


def padded(slots):
    return 2 * slots + 8


def synthesis_kernel(
    slots, levels, fields, least, chunk, scale, first_ref, owner_ref, spec_ref, table_ref, out_ref, rows_ref, sems, *held
):
    at, tiles = chunk
    groups = len(least)
    block = 4
    row_total, degrees = spec_ref.shape[1:]
    stride = padded(slots)
    copies = []
    for group, start in enumerate(least):
        mine = pl.ds(group * block, block)
        left = pl.ds(start, degrees - start)
        lanes = pl.ds(at * LANES, tiles * LANES)
        copies.append(
            (
                pltpu.make_async_copy(spec_ref.at[mine, :, left], held[2 * group], sems.at[2 * group]),
                pltpu.make_async_copy(table_ref.at[mine, left, lanes], held[2 * group + 1], sems.at[2 * group + 1]),
            )
        )
    order = range(groups - 1, -1, -1)
    for group in order:
        for copy in copies[group]:
            copy.start()
    for group in order:
        for copy in copies[group]:
            copy.wait()
        for j in range(block):
            spec = held[2 * group][j]
            wave = owner_ref[first_ref[0] + group * block + j]
            distance = lax.broadcasted_iota(jnp.int32, (1, spec.shape[1]), 1) + (least[group] - wave)
            keep = jnp.where(distance >= 0, 1.0, 0.0)
            flip = jnp.where(distance % 2 == 0, keep, -keep)
            both = jnp.concatenate([spec * keep.astype(spec.dtype), spec * flip.astype(spec.dtype)], axis=0)
            halves = jnp.dot(both, held[2 * group + 1][j], preferred_element_type=jnp.float32) * scale
            first = 2 * (group * block + j)
            for hemi in range(2):
                for part in range(2):
                    for field in range(fields):
                        row = hemi * row_total + (part * fields + field) * levels
                        target = pl.ds(hemi * levels * stride + first + part, levels, stride=stride)
                        for tile in range(tiles):
                            lanes = slice(tile * LANES, (tile + 1) * LANES)
                            rows_ref[field, tile, target, :] = halves[row : row + levels, lanes]
    for field in range(fields):
        for tile in range(tiles):
            lanes = pl.ds((field * tiles + tile) * LANES, LANES)
            rows = rows_ref[field, tile].reshape(2 * levels, stride, LANES)[:, : 2 * slots]
            out_ref[:, lanes] = rows.reshape(out_ref.shape[0], LANES).astype(out_ref.dtype)


def synthesize(first, owner_table, spec_rows, legendre, chunk, fields, levels, least):
    _, row_total, degrees = spec_rows.shape
    block = 4
    slots = block * len(least)
    rows = 2 * levels * 2 * slots
    tiles = chunk[1]
    shape = (rows, fields * tiles * LANES)
    held = []
    for start in least:
        held.append(pltpu.VMEM((block, row_total, degrees - start), jnp.bfloat16))
        held.append(pltpu.VMEM((block, degrees - start, tiles * LANES), jnp.bfloat16))
    return pl.pallas_call(
        functools.partial(synthesis_kernel, slots, levels, fields, least, chunk, 1.0 / math.sqrt(degrees)),
        in_specs=[pl.BlockSpec(memory_space=pltpu.SMEM)] * 2 + [pl.BlockSpec(memory_space=pl.ANY)] * 2,
        out_specs=pl.BlockSpec(shape, lambda: (0, 0)),
        out_shape=jax.ShapeDtypeStruct(shape, jnp.bfloat16),
        scratch_shapes=[
            pltpu.VMEM((fields, tiles, 2 * levels * padded(slots), LANES), jnp.float32),
            pltpu.SemaphoreType.DMA((2 * len(least),)),
            *held,
        ],
        compiler_params=pltpu.CompilerParams(vmem_limit_bytes=VMEM_BYTES),
        cost_estimate=pl.CostEstimate(
            flops=4 * slots * row_total * degrees * tiles * LANES,
            bytes_accessed=2 * slots * degrees * (row_total + tiles * LANES) + 2 * rows * shape[1],
            transcendentals=0,
        ),
        name="synthesis",
    )(first, owner_table, spec_rows, legendre)


def longitude_kernel(
    fields, chunk, grid_scale, zonal_scale, rows_ref, far_ref, by_lon_ref, by_wave_ref, out_ref, far_out_ref, sum_ref
):
    step = pl.program_id(0)
    near = rows_ref.shape[0]
    values = jnp.dot(by_lon_ref[:, :near], rows_ref[...], preferred_element_type=jnp.float32)
    one = values.shape[1] // fields
    each = far_ref.shape[1] // fields
    starts = [field * each + chunk[0] * LANES for field in range(fields)]
    far = jnp.concatenate([far_ref[:, start : start + one] for start in starts], axis=1)
    values = values + jnp.dot(by_lon_ref[:, near:], far, preferred_element_type=jnp.float32)
    values = values * grid_scale
    following = jnp.concatenate([values[:, one:], values[:, :one]], axis=1)
    product = (values * following).astype(jnp.bfloat16)
    share = jnp.dot(by_wave_ref[...], product, preferred_element_type=jnp.float32)

    @pl.when(step == 0)
    def _():
        sum_ref[...] = share

    @pl.when(step > 0)
    def _():
        sum_ref[...] += share

    @pl.when(step == pl.num_programs(0) - 1)
    def _():
        out_ref[...] = (sum_ref[:near, :] * zonal_scale).astype(out_ref.dtype)
        far_out_ref[...] = (sum_ref[near:, :] * zonal_scale).astype(far_out_ref.dtype)


def longitudes(rows, far, by_lon, by_wave, fields, chunk):
    depth, width = rows.shape[0] + far.shape[0], rows.shape[1]
    lon_count = by_lon.shape[0]
    lon_block = lon_count // 5
    near_spec = pl.BlockSpec(rows.shape, lambda i: (0, 0))
    far_out = jax.ShapeDtypeStruct((far.shape[0], width), jnp.bfloat16)
    return pl.pallas_call(
        functools.partial(longitude_kernel, fields, chunk, 1.0 / math.sqrt(depth // 2), 2.0 / math.sqrt(lon_count)),
        grid=(lon_count // lon_block,),
        in_specs=[
            near_spec,
            pl.BlockSpec(far.shape, lambda i: (0, 0)),
            pl.BlockSpec((lon_block, depth), lambda i: (i, 0)),
            pl.BlockSpec((depth, lon_block), lambda i: (0, i)),
        ],
        out_specs=[near_spec, pl.BlockSpec(far_out.shape, lambda i: (0, 0))],
        out_shape=[jax.ShapeDtypeStruct(rows.shape, jnp.bfloat16), far_out],
        scratch_shapes=[pltpu.VMEM((depth, width), jnp.float32)],
        compiler_params=pltpu.CompilerParams(vmem_limit_bytes=VMEM_BYTES),
        cost_estimate=pl.CostEstimate(
            flops=4 * depth * width * lon_count,
            bytes_accessed=4 * depth * (width + lon_count),
            transcendentals=0,
        ),
        name="longitudes",
    )(rows, far, by_lon, by_wave)


def pack_kernel(near, spec_ref, table_ref, out_ref, last_ref, tail_ref, sems):
    degrees, half_lat = table_ref.shape[1:]
    half = LANES // 2
    copies = []

    def fetch(source, target):
        copies.append(pltpu.make_async_copy(source, target, sems.at[len(copies)]))
        copies[-1].start()

    lanes, sides = pl.ds(0, half_lat), pl.ds(half_lat, LANES)
    for slot in range(2):
        rows = pl.ds(slot * LANES, LANES)
        fetch(table_ref.at[near + slot, pl.ds(degrees - LANES, LANES), :], out_ref.at[rows, lanes])
        fetch(spec_ref.at[near + slot, :, pl.ds(degrees - LANES, LANES)], out_ref.at[rows, sides])
    for slot in range(2):
        rows = pl.ds(slot * half, half)
        fetch(table_ref.at[near + 2 + slot, pl.ds(degrees - half, half), :], last_ref.at[rows, lanes])
        fetch(spec_ref.at[near + 2 + slot, :, pl.ds(degrees - LANES, LANES)], tail_ref.at[slot])
    for copy in copies:
        copy.wait()
    third = pltpu.roll(tail_ref[0].astype(jnp.float32), half, 1)
    lower = lax.broadcasted_iota(jnp.int32, third.shape, 1) < half
    both = jnp.where(lower, third, tail_ref[1].astype(jnp.float32))
    last_ref[:, sides] = both.astype(last_ref.dtype)


def pack(spec_rows, legendre, near):
    shapes = [(rows * LANES, legendre.shape[2] + LANES) for rows in (2, 1)]
    return pl.pallas_call(
        functools.partial(pack_kernel, near),
        in_specs=[pl.BlockSpec(memory_space=pl.ANY)] * 2,
        out_specs=[pl.BlockSpec(shape, lambda: (0, 0)) for shape in shapes],
        out_shape=[jax.ShapeDtypeStruct(shape, jnp.bfloat16) for shape in shapes],
        scratch_shapes=[
            pltpu.VMEM((2, spec_rows.shape[1], LANES), jnp.bfloat16),
            pltpu.SemaphoreType.DMA((8,)),
        ],
        compiler_params=pltpu.CompilerParams(vmem_limit_bytes=VMEM_BYTES),
        cost_estimate=pl.CostEstimate(flops=0, bytes_accessed=12 * LANES * shapes[0][1], transcendentals=0),
        name="pack",
    )(spec_rows, legendre)


def far_synthesis_kernel(levels, fields, scale, place_ref, waves_ref, *refs):
    pack_refs, out_refs, rows_ref = refs[:4], refs[4:-1], refs[-1]
    tiles = rows_ref.shape[1]
    half_lat = tiles * LANES
    stride = rows_ref.shape[2] // levels
    degree = lax.broadcasted_iota(jnp.int32, (1, LANES), 1)
    for slot in range(8):
        local = slot % 4
        pack_ref = pack_refs[slot // 4 * 2 + local // 2]
        rows = pl.ds(local % 2 * LANES if local < 2 else 0, LANES)
        distance = degree - waves_ref[slot] + (LANES // 2 if local == 2 else 0)
        keep = jnp.where(distance >= 0, 1.0, 0.0)
        if local >= 2:
            keep = jnp.where((degree < LANES // 2) if local == 2 else (degree >= LANES // 2), keep, 0.0)
        turned = jnp.where(distance % 2 == 0, keep, -keep)
        sign = jnp.where(place_ref[0] == 0, keep, turned)
        spec = pack_ref[rows, half_lat:]
        table = pack_ref[rows, :half_lat]
        sums = jnp.dot(spec * sign.astype(spec.dtype), table, preferred_element_type=jnp.float32) * scale
        for part in range(2):
            for field in range(fields):
                row = (part * fields + field) * levels
                for tile in range(tiles):
                    target = pl.ds(2 * slot + part, levels, stride=stride)
                    rows_ref[field, tile, target, :] = sums[row : row + levels, tile * LANES : (tile + 1) * LANES]
    for apart, out_ref in enumerate(out_refs):
        rows = pl.ds(pl.multiple_of((place_ref[1] ^ apart) * stride, stride), stride)
        for field in range(fields):
            for tile in range(tiles):
                lanes = pl.ds((field * tiles + tile) * LANES, LANES)
                out_ref[:, lanes] = rows_ref[field, tile, rows, :].astype(out_ref.dtype)


def far_synthesize(place, waves, packs, levels, fields, scale):
    tiles = packs[0].shape[1] // LANES - 1
    shape = (16, fields * tiles * LANES)
    return pl.pallas_call(
        functools.partial(far_synthesis_kernel, levels, fields, scale),
        in_specs=[pl.BlockSpec(memory_space=pltpu.SMEM)] * 2 + [pl.BlockSpec(x.shape, lambda: (0, 0)) for x in packs],
        out_specs=[pl.BlockSpec(shape, lambda: (0, 0))] * levels,
        out_shape=[jax.ShapeDtypeStruct(shape, jnp.bfloat16)] * levels,
        scratch_shapes=[pltpu.VMEM((fields, tiles, 16 * levels, LANES), jnp.float32)],
        compiler_params=pltpu.CompilerParams(vmem_limit_bytes=VMEM_BYTES),
        cost_estimate=pl.CostEstimate(
            flops=16 * 2 * fields * levels * LANES * tiles * LANES, bytes_accessed=12 * packs[0].size, transcendentals=0
        ),
        name="far_synthesis",
    )(place, waves, *packs)


def far_analysis_kernel(levels, fields, chunks, place_ref, *refs):
    pack_refs, zonal_refs = refs[:4], refs[4:-3]
    own_out_ref, partner_out_ref, rows_ref = refs[-3:]
    tiles = rows_ref.shape[1]
    stride = rows_ref.shape[2] // levels
    for apart, zonal_ref in enumerate(zonal_refs):
        rows = pl.ds(pl.multiple_of((place_ref[1] ^ apart) * stride, stride), stride)
        offset = 0
        for at, count in chunks:
            for field in range(fields):
                for tile in range(at, at + count):
                    rows_ref[field, tile, rows, :] = zonal_ref[:, pl.ds(offset, LANES)].astype(jnp.float32)
                    offset += LANES
    lower = lax.broadcasted_iota(jnp.int32, (1, LANES), 1) < LANES // 2
    for out_ref, base in ((own_out_ref, 0), (partner_out_ref, 4)):
        sums = []
        for local in range(4):
            pack_ref = pack_refs[base // 2 + local // 2]
            rows = pl.ds(local % 2 * LANES if local < 2 else 0, LANES)
            zonal = jnp.concatenate(
                [
                    jnp.concatenate(
                        [
                            rows_ref[field, tile, pl.ds(2 * (base + local) + part, levels, stride=stride), :]
                            for part in range(2)
                            for field in range(fields)
                        ],
                        axis=0,
                    ).astype(jnp.bfloat16)
                    for tile in range(tiles)
                ],
                axis=1,
            )
            table = pack_ref[rows, : tiles * LANES]
            sums.append(
                lax.dot_general(zonal, table, (((1,), (1,)), ((), ())), preferred_element_type=jnp.float32)
            )
        sums[2] = jnp.where(lower, sums[2], sums[3])
        size = sums[0].shape[0]
        for block in range(3):
            out_ref[pl.ds(block * size, size), :] = sums[block].astype(out_ref.dtype)


def far_analyze(place, packs, zonal, levels, fields, chunks):
    tiles = packs[0].shape[1] // LANES - 1
    shape = (3 * 2 * fields * levels, LANES)
    out_spec = pl.BlockSpec(shape, lambda: (0, 0))
    return pl.pallas_call(
        functools.partial(far_analysis_kernel, levels, fields, chunks),
        in_specs=[pl.BlockSpec(memory_space=pltpu.SMEM)]
        + [pl.BlockSpec(x.shape, lambda: (0, 0)) for x in (*packs, *zonal)],
        out_specs=[out_spec, out_spec],
        out_shape=[jax.ShapeDtypeStruct(shape, jnp.float32), jax.ShapeDtypeStruct(shape, jnp.bfloat16)],
        scratch_shapes=[pltpu.VMEM((fields, tiles, 16 * levels, LANES), jnp.float32)],
        compiler_params=pltpu.CompilerParams(vmem_limit_bytes=VMEM_BYTES),
        cost_estimate=pl.CostEstimate(
            flops=16 * 2 * fields * levels * LANES * tiles * LANES, bytes_accessed=12 * packs[0].size, transcendentals=0
        ),
        name="far_analysis",
    )(place, *packs, *zonal)


def fold_kernel(slots, levels, fields, arrived_ref, out_ref, rows_ref):
    tiles = rows_ref.shape[1]
    stride = padded(slots)
    half = levels * stride
    for field in range(fields):
        for tile in range(tiles):
            lanes = pl.ds((field * tiles + tile) * LANES, LANES)
            rows = arrived_ref[:, lanes].astype(jnp.float32)
            for source in range(2 * levels):
                mine = rows[2 * slots * source : 2 * slots * (source + 1)]
                rows_ref[field, tile, pl.ds(stride * source, 2 * slots), :] = mine
    for slot in range(slots):
        for part in range(2):
            for field in range(fields):
                for tile in range(tiles):
                    first = 2 * slot + part
                    north = rows_ref[field, tile, pl.ds(first, levels, stride=stride), :]
                    south = rows_ref[field, tile, pl.ds(half + first, levels, stride=stride), :]
                    lanes = pl.ds(tile * LANES, LANES)
                    at = (part * fields + field) * levels
                    out_ref[slot, at : at + levels, lanes] = (north + south).astype(out_ref.dtype)
                    at += 2 * fields * levels
                    out_ref[slot, at : at + levels, lanes] = (north - south).astype(out_ref.dtype)


def fold(arrived, slots, levels, fields):
    row_total = 2 * fields * levels
    rows, width = arrived.shape
    tiles = width // (fields * LANES)
    shape = (slots, 2 * row_total, tiles * LANES)
    return pl.pallas_call(
        functools.partial(fold_kernel, slots, levels, fields),
        in_specs=[pl.BlockSpec((rows, width), lambda: (0, 0))],
        out_specs=pl.BlockSpec(shape, lambda: (0, 0, 0)),
        out_shape=jax.ShapeDtypeStruct(shape, jnp.bfloat16),
        scratch_shapes=[pltpu.VMEM((fields, tiles, 2 * levels * padded(slots), LANES), jnp.float32)],
        compiler_params=pltpu.CompilerParams(vmem_limit_bytes=VMEM_BYTES),
        cost_estimate=pl.CostEstimate(flops=2 * rows * width, bytes_accessed=4 * rows * width, transcendentals=0),
        name="fold",
    )(arrived)


def analysis_kernel(least, folded_ref, even_ref, odd_ref, *refs):
    table_refs, out_ref = refs[:-1], refs[-1]
    row_total, degrees = out_ref.shape[1:]
    step = pl.program_id(0)

    def run(group):
        start = least[group]
        for j in range(out_ref.shape[0]):
            table = jnp.concatenate([ref[j, start:, :] for ref in table_refs], axis=1)
            sums = lax.dot_general(
                folded_ref[j], table, (((1,), (1,)), ((), ())), preferred_element_type=jnp.float32
            )
            kept = sums[:row_total] * even_ref[j, :, start:] + sums[row_total:] * odd_ref[j, :, start:]
            out_ref[j, :, start:] = kept
            if start:
                out_ref[j, :, :start] = jnp.zeros((row_total, start), out_ref.dtype)

    for group in range(len(least)):
        pl.when(step == group)(functools.partial(run, group))

    @pl.when(step == len(least))
    def _():
        out_ref[...] = jnp.zeros(out_ref.shape, out_ref.dtype)


def analyze(folded, even, odd, legendre, row_total, least, chunk):
    slots, degrees, _ = legendre.shape
    block = 4
    near = len(least) - 1
    at, tiles = chunk
    mask_spec = pl.BlockSpec((block, 1, degrees), lambda i: (i, 0, 0))
    return pl.pallas_call(
        functools.partial(analysis_kernel, least),
        grid=(len(least) + 1,),
        in_specs=[
            pl.BlockSpec((block,) + folded.shape[1:], lambda i: (jnp.minimum(i, near), 0, 0)),
            mask_spec,
            mask_spec,
        ]
        + [
            pl.BlockSpec((block, degrees, LANES), lambda i, t=at + t: (jnp.minimum(i, near), 0, t))
            for t in range(tiles)
        ],
        out_specs=pl.BlockSpec((block, row_total, degrees), lambda i: (i, 0, 0)),
        out_shape=jax.ShapeDtypeStruct((slots, row_total, degrees), jnp.float32),
        compiler_params=pltpu.CompilerParams(vmem_limit_bytes=VMEM_BYTES),
        cost_estimate=pl.CostEstimate(
            flops=4 * slots * row_total * degrees * tiles * LANES,
            bytes_accessed=2 * slots * (degrees * tiles * LANES + 2 * row_total * (tiles * LANES + degrees)),
            transcendentals=0,
        ),
        name="analysis",
    )(folded, even, odd, *[legendre] * tiles)


def closing_kernel(
    levels, fields, least, chunk, hemi_ref, arrived_ref, table_ref, base_ref, even_ref, odd_ref, own_ref, other_ref, out_ref, *refs
):
    got_ref, north_ref, south_ref, far_ref, sems = refs[:5]
    held = refs[5:]
    at, tiles = chunk
    groups = len(least)
    _, row_total, degrees = base_ref.shape
    block = 4
    slots = block * groups
    each = 2 * slots
    stride = padded(slots)
    half = levels * each
    arriving = [
        pltpu.make_async_copy(
            arrived_ref.at[:, pl.ds(field * tiles * LANES, tiles * LANES)], got_ref.at[field], sems.at[3 * groups + field]
        )
        for field in range(fields)
    ]
    tables, sums, results = [], [], []
    for group, start in enumerate(least):
        mine = pl.ds(group * block, block)
        left = pl.ds(start, degrees - start)
        lanes = pl.ds(at * LANES, tiles * LANES)
        held_table, held_sums = held[2 * group], held[2 * group + 1]
        tables.append(pltpu.make_async_copy(table_ref.at[mine, left, lanes], held_table, sems.at[3 * group]))
        sums.append(pltpu.make_async_copy(base_ref.at[mine, :, left], held_sums, sems.at[3 * group + 1]))
        results.append(pltpu.make_async_copy(held_sums, out_ref.at[mine, :, left], sems.at[3 * group + 2]))
    for copy in arriving:
        copy.start()
    for group in range(groups):
        tables[group].start()
        sums[group].start()
    for local in range(4):
        rows = pl.ds(min(local, 2) * row_total, row_total)
        own, other = own_ref[rows, :], other_ref[rows, :].astype(jnp.float32)
        both, change = own + other, jnp.where(hemi_ref[0] == 0, own - other, other - own)
        if local == 2:
            both, change = pltpu.roll(both, LANES // 2, 1), pltpu.roll(change, LANES // 2, 1)
        even = even_ref[slots + local, :, degrees - LANES :]
        odd = odd_ref[slots + local, :, degrees - LANES :]
        far_ref[local] = both * even + change * odd
    finished = pltpu.make_async_copy(
        far_ref, out_ref.at[pl.ds(slots, 4), :, pl.ds(degrees - LANES, LANES)], sems.at[3 * groups + fields]
    )
    finished.start()
    for field in range(fields):
        arriving[field].wait()
        for tile in range(tiles):
            lanes = pl.ds(tile * LANES, LANES)
            north = got_ref[field, :half, lanes].astype(jnp.float32)
            south = got_ref[field, half:, lanes].astype(jnp.float32)
            plus, minus = north + south, north - south
            for level in range(levels):
                rows = pl.ds(stride * level, each)
                north_ref[field, tile, rows, :] = plus[each * level : each * (level + 1)]
                south_ref[field, tile, rows, :] = minus[each * level : each * (level + 1)]
    for group, start in enumerate(least):
        tables[group].wait()
        sums[group].wait()
        held_table, held_sums = held[2 * group], held[2 * group + 1]
        for j in range(block):
            slot = group * block + j
            folded = jnp.concatenate(
                [
                    jnp.concatenate(
                        [
                            ref[field, tile, pl.ds(2 * slot + part, levels, stride=stride), :].astype(jnp.bfloat16)
                            for ref in (north_ref, south_ref)
                            for part in range(2)
                            for field in range(fields)
                        ],
                        axis=0,
                    )
                    for tile in range(tiles)
                ],
                axis=1,
            )
            more = lax.dot_general(
                folded, held_table[j], (((1,), (1,)), ((), ())), preferred_element_type=jnp.float32
            )
            even, odd = even_ref[slot, :, start:], odd_ref[slot, :, start:]
            held_sums[j] = held_sums[j] + more[:row_total] * even + more[row_total:] * odd
        results[group].start()
    for copy in results:
        copy.wait()
    finished.wait()


def close(hemi, own, other, arrived, base, even, odd, legendre, fields, levels, least, chunk):
    slots, row_total, degrees = base.shape
    block = 4
    rows, width = arrived.shape
    tiles = chunk[1]
    half = pltpu.VMEM((fields, tiles, levels * padded(block * len(least)), LANES), jnp.float32)
    held = []
    for start in least:
        held.append(pltpu.VMEM((block, degrees - start, tiles * LANES), jnp.bfloat16))
        held.append(pltpu.VMEM((block, row_total, degrees - start), jnp.float32))
    anywhere = pl.BlockSpec(memory_space=pl.ANY)
    return pl.pallas_call(
        functools.partial(closing_kernel, levels, fields, least, chunk),
        in_specs=[pl.BlockSpec(memory_space=pltpu.SMEM), anywhere, anywhere, anywhere]
        + [pl.BlockSpec(even.shape, lambda: (0, 0, 0))] * 2
        + [pl.BlockSpec(own.shape, lambda: (0, 0))] * 2,
        out_specs=anywhere,
        out_shape=jax.ShapeDtypeStruct(base.shape, jnp.float32),
        input_output_aliases={3: 0},
        scratch_shapes=[
            pltpu.VMEM((fields, rows, tiles * LANES), jnp.bfloat16),
            half,
            half,
            pltpu.VMEM((4, row_total, LANES), jnp.float32),
            pltpu.SemaphoreType.DMA((3 * len(least) + fields + 1,)),
            *held,
        ],
        compiler_params=pltpu.CompilerParams(vmem_limit_bytes=VMEM_BYTES),
        cost_estimate=pl.CostEstimate(
            flops=4 * slots * row_total * degrees * tiles * LANES,
            bytes_accessed=8 * slots * row_total * degrees + 2 * rows * width,
            transcendentals=0,
        ),
        name="closing",
    )(hemi, arrived, legendre, base, even, odd, own, other)


def across_halves(value):
    planes = lax.axis_size("grp")
    return lax.ppermute(value, "grp", [(p, (p + planes // 2) % planes) for p in range(planes)])


def within_half(parts):
    bands, planes = lax.axis_size("band"), lax.axis_size("grp")
    half = planes // 2
    moved = [parts[0]]
    for x in range(1, len(parts)):
        pairs = []
        for band in range(bands):
            for plane in range(planes):
                level = (plane % half * bands + band) ^ x
                target = level % bands * planes + plane // half * half + level // bands
                pairs.append((band * planes + plane, target))
        moved.append(lax.ppermute(parts[x], AXES, pairs))
    return moved


def after(value, *others):
    return lax.optimization_barrier((value, others))[0]


def trig_kernel(small_ref, cos_turn_ref, sin_turn_ref, by_wave_ref, by_lon_ref):
    shape = cos_turn_ref.shape
    cos_start, sin_start, cos_step, sin_step = [
        jnp.broadcast_to(small_ref[:, column : column + 1], shape) for column in range(4)
    ]
    cos_turn, sin_turn = cos_turn_ref[...], sin_turn_ref[...]
    cosine = cos_start * cos_turn - sin_start * sin_turn
    sine = sin_start * cos_turn + cos_start * sin_turn
    flipped = [x.T for x in (cosine, sine, cos_step, sin_step)]
    blocks = by_wave_ref.shape[1] // LANES
    for position, (c, s, dc, ds) in enumerate(((cosine, sine, cos_step, sin_step), flipped)):
        for block in range(blocks):
            part = pl.ds(block * LANES, LANES)
            if position == 0:
                by_wave_ref[:, part] = c.astype(by_wave_ref.dtype)
            else:
                by_lon_ref[part, :] = c.astype(by_lon_ref.dtype)
            c, s = c * dc - s * ds, s * dc + c * ds


def trig_tables(owner_table, lon_count, *others):
    waves = jnp.repeat(owner_table, 2).astype(jnp.float32)[:, None]
    quarter = jnp.tile(jnp.array([0, lon_count // 4], jnp.float32), owner_table.shape[0])[:, None]
    unit = 2.0 * math.pi / lon_count

    def angles(phase):
        return (phase - lon_count * jnp.floor(phase * (1.0 / lon_count))) * unit

    start = angles(quarter)
    step = angles(waves * LANES)
    turn = angles(waves * jnp.arange(LANES, dtype=jnp.float32)[None, :])
    small = jnp.concatenate([jnp.cos(start), jnp.sin(start), jnp.cos(step), jnp.sin(step)], axis=1)
    parts = after((small, jnp.cos(turn), jnp.sin(turn)), *others)
    depth = waves.shape[0]
    rows = 256
    wide = pl.BlockSpec((rows, LANES), lambda i: (i, 0))
    return pl.pallas_call(
        trig_kernel,
        grid=(depth // rows,),
        in_specs=[pl.BlockSpec((rows, 4), lambda i: (i, 0)), wide, wide],
        out_specs=[
            pl.BlockSpec((rows, lon_count), lambda i: (i, 0)),
            pl.BlockSpec((lon_count, rows), lambda i: (0, i)),
        ],
        out_shape=[
            jax.ShapeDtypeStruct((depth, lon_count), jnp.bfloat16),
            jax.ShapeDtypeStruct((lon_count, depth), jnp.bfloat16),
        ],
        compiler_params=pltpu.CompilerParams(vmem_limit_bytes=VMEM_BYTES),
        cost_estimate=pl.CostEstimate(
            flops=12 * depth * lon_count, bytes_accessed=4 * depth * lon_count, transcendentals=0
        ),
        name="trig",
    )(*parts)


def exchange(rows):
    return lax.all_to_all(rows, AXES[::-1], split_axis=0, concat_axis=0, tiled=True)


def by_hemisphere_and_level(spectral, legendre, owner_table):
    slots, _, fields, levels, degrees = spectral.shape
    half_lat = legendre.shape[2]
    lon_count = 4 * half_lat
    row_total = 2 * fields * levels
    tiles = half_lat // LANES
    first = lax.axis_index(AXES).astype(jnp.int32) * slots
    spec_rows = spectral.reshape(slots, row_total, degrees)
    devices = 2 * levels
    least = tuple(4 * g * devices for g in range(slots // 4 - 1))
    near = slots - 4
    far_least = near * devices
    cut = tiles - tiles // 2
    chunks = [(0, cut), (cut, tiles - cut)]

    def send(spec, chunk):
        return synthesize(first.reshape(1), owner_table, spec, legendre, chunk, fields, levels, least)

    packs = list(pack(spec_rows, legendre, near))
    packs.append(across_halves(packs[0]))
    large = send(after(spec_rows, packs[0]), chunks[0])
    packs.append(across_halves(after(packs[1], large)))

    bands, planes = lax.axis_size("band"), lax.axis_size("grp")
    by_device = jnp.swapaxes(owner_table.reshape(bands, planes, slots), 0, 1).reshape(2, levels, slots)
    plane = lax.axis_index("grp").astype(jnp.int32)
    hemi = plane // (planes // 2)
    level = plane % (planes // 2) * bands + lax.axis_index("band").astype(jnp.int32)
    place = jnp.stack([hemi, level])
    far = by_device[:, :, near:]
    both_halves = jnp.concatenate([far[0], far[1]], axis=1)
    swapped = jnp.concatenate([far[1], far[0]], axis=1)
    far_waves = jnp.where(hemi == 0, both_halves, swapped)
    far_waves = jnp.take(far_waves, jnp.arange(levels, dtype=jnp.int32) ^ level, axis=0)
    waves = jnp.concatenate([by_device[:, :, :near].reshape(-1), far_waves.reshape(-1)])

    small = send(after(spec_rows, large), chunks[1])
    by_wave, by_lon = trig_tables(after(waves, large), lon_count, small)
    arrived = [exchange(after(large, small, packs[2]))]
    far_rows = far_synthesize(
        place, far_waves[0] - far_least, packs, levels, fields, 1.0 / math.sqrt(degrees)
    )
    far_rows = jnp.concatenate(within_half(far_rows))
    arrived.append(exchange(after(small, far_rows, *arrived)))
    zonal = [
        longitudes(rows, far_rows, by_lon, by_wave, fields, chunk) for rows, chunk in zip(arrived, chunks)
    ]
    returned = [exchange(zonal[0][0])]
    far_zonal = jnp.concatenate([zonal[0][1], zonal[1][1]], axis=1)
    far_zonal = within_half([far_zonal[16 * x : 16 * x + 16] for x in range(levels)])
    returned.append(exchange(after(zonal[1][0], *far_zonal, *returned)))
    own_sums, partner_sums = far_analyze(place, packs, far_zonal, levels, fields, chunks)
    other_sums = across_halves(partner_sums)
    wavenumber = lax.dynamic_slice_in_dim(after(owner_table, by_wave), first, slots)
    distance = jnp.arange(degrees, dtype=jnp.int32)[None, :] - wavenumber[:, None]
    scale = 1.0 / math.sqrt(2 * half_lat)
    even = jnp.where((distance >= 0) & (distance % 2 == 0), scale, 0.0).astype(jnp.float32)[:, None, :]
    odd = jnp.where((distance >= 0) & (distance % 2 != 0), scale, 0.0).astype(jnp.float32)[:, None, :]

    folded = fold(returned[0], near, levels, fields)
    base = analyze(folded, even, odd, legendre, row_total, least, chunks[0])
    last = after(returned[1], base)
    out = close(hemi.reshape(1), own_sums, other_sums, last, base, even, odd, legendre, fields, levels, least, chunks[1])
    return out.reshape(slots, 2, fields, levels, degrees)


def make_trig(wavenumber, lon_count):
    lon_index = jnp.arange(lon_count, dtype=jnp.int32)
    phases = wavenumber[:, None] * lon_index[None, :] % lon_count
    angles = phases.astype(jnp.float32) * (2.0 * math.pi / lon_count)
    return jnp.stack([jnp.cos(angles), -jnp.sin(angles)], axis=1).astype(jnp.bfloat16)


def by_level_and_latitude(spectral, legendre, owner_table):
    slot_count, _, fields, levels, degrees = spectral.shape
    half_lat = legendre.shape[2]
    lat_count = 2 * half_lat
    lon_count = 2 * lat_count
    wave_count = owner_table.shape[0]
    band_count = lax.axis_size("band")
    group_count = lax.axis_size("grp")
    device_count = band_count * group_count
    level_block = levels // band_count
    lat_block = lat_count // group_count
    row_total = 2 * fields * levels
    row_width = fields * level_block * lat_block
    slot_start = lax.axis_index(("band", "grp")) * slot_count
    wavenumber = lax.dynamic_slice_in_dim(owner_table, slot_start, slot_count)
    degree_index = jnp.arange(degrees, dtype=jnp.int32)
    keep_mask = (degree_index[None, :] >= wavenumber[:, None]).astype(jnp.bfloat16)
    odd_part = (degree_index[None, :] - wavenumber[:, None]) % 2
    flip_sign = (1 - 2 * odd_part).astype(jnp.bfloat16)
    spec_rows = spectral.reshape(slot_count, row_total, degrees) * keep_mask[:, None, :]
    both_rows = jnp.concatenate([spec_rows, spec_rows * flip_sign[:, None, :]], axis=1)
    halves = jnp.einsum("srn,snt->srt", both_rows, legendre, preferred_element_type=jnp.float32)
    northern = halves[:, :row_total]
    mirrored = halves[:, row_total:]
    fourier = jnp.concatenate([northern, jnp.flip(mirrored, axis=2)], axis=2)
    fourier = fourier.reshape(
        slot_count, 2, fields, band_count, level_block, group_count, lat_block
    )
    fourier = jnp.transpose(fourier, (0, 1, 2, 3, 5, 4, 6))
    fourier_low = (fourier * (1.0 / math.sqrt(degrees))).astype(jnp.bfloat16)
    packed = fourier_low.reshape(1, slot_count, 2, fields, device_count, level_block, lat_block)
    arrived = lax.all_to_all(packed, ("band", "grp"), split_axis=4, concat_axis=0, tiled=True)
    arrived = arrived.reshape(-1, 2, row_width)
    trig_rows = make_trig(owner_table, lon_count)
    grid_values = jnp.einsum("scw,scl->wl", arrived, trig_rows, preferred_element_type=jnp.float32)
    grid_values = (grid_values * (1.0 / math.sqrt(wave_count))).reshape(
        fields, level_block * lat_block, lon_count
    )
    product = (grid_values * jnp.roll(grid_values, -1, axis=0)).astype(jnp.bfloat16)
    zonal_coeffs = jnp.einsum(
        "wl,scl->scw",
        product.reshape(row_width, lon_count),
        trig_rows,
        preferred_element_type=jnp.float32,
    )
    zonal_coeffs = (zonal_coeffs * (2.0 / math.sqrt(lon_count))).astype(jnp.bfloat16)
    sendback = zonal_coeffs.reshape(device_count, slot_count, 2, fields, 1, level_block, lat_block)
    returned = lax.all_to_all(sendback, ("band", "grp"), split_axis=0, concat_axis=4, tiled=True)
    returned = returned.reshape(
        slot_count, 2, fields, band_count, group_count, level_block, lat_block
    )
    returned = jnp.transpose(returned, (0, 1, 2, 3, 5, 4, 6)).reshape(slot_count, row_total, lat_count)
    northern_part = returned[:, :, :half_lat].astype(jnp.float32)
    mirror_part = jnp.flip(returned[:, :, half_lat:], axis=2).astype(jnp.float32)
    plus_part = (northern_part + mirror_part).astype(jnp.bfloat16)
    minus_part = (northern_part - mirror_part).astype(jnp.bfloat16)
    stacked = jnp.concatenate([plus_part, minus_part], axis=1)
    projected = jnp.einsum("srt,snt->srn", stacked, legendre, preferred_element_type=jnp.float32)
    even_rows = flip_sign[:, None, :] > 0
    chosen = jnp.where(even_rows, projected[:, :row_total], projected[:, row_total:])
    chosen = chosen * keep_mask.astype(jnp.float32)[:, None, :] * (1.0 / math.sqrt(lat_count))
    return chosen.reshape(slot_count, 2, fields, levels, degrees)


def on_device(spectral, legendre, owner_table):
    slots, _, _, levels, _ = spectral.shape
    whole_hemispheres = lax.axis_size("band") * lax.axis_size("grp") == 2 * levels
    halves = lax.axis_size("grp") % 2 == 0 and levels & (levels - 1) == 0
    few_left = legendre.shape[1] - (slots - 4) * 2 * levels == LANES
    if whole_hemispheres and halves and few_left and legendre.shape[2] % LANES == 0 and legendre.shape[2] > LANES and slots % 4 == 0 and levels % 16 == 0:
        return by_hemisphere_and_level(spectral, legendre, owner_table)
    return by_level_and_latitude(spectral, legendre, owner_table)


def solution(mesh):
    placed = (P(("band", "grp"), None, None, None, None), P(("band", "grp"), None, None), P())
    return jax.shard_map(
        on_device,
        mesh=mesh,
        in_specs=placed,
        out_specs=P(("band", "grp"), None, None, None, None),
        check_vma=False,
    )
```

```python
import functools
import math

import jax
import jax.numpy as jnp
from jax import lax
from jax.experimental import pallas as pl
from jax.experimental.pallas import tpu as pltpu
from jax.sharding import PartitionSpec as P

LANES = 128
AXES = ("band", "grp")
VMEM_BYTES = 62 * 1024 * 1024


def padded(slots):
    return 2 * slots + 8


def synthesis_kernel(
    slots, levels, fields, least, chunk, scale, first_ref, owner_ref, spec_ref, table_ref, out_ref, rows_ref, sems, *held
):
    at, tiles = chunk
    groups = len(least)
    block = 4
    row_total, degrees = spec_ref.shape[1:]
    stride = padded(slots)
    copies = []
    for group, start in enumerate(least):
        mine = pl.ds(group * block, block)
        left = pl.ds(start, degrees - start)
        lanes = pl.ds(at * LANES, tiles * LANES)
        copies.append(
            (
                pltpu.make_async_copy(spec_ref.at[mine, :, left], held[2 * group], sems.at[2 * group]),
                pltpu.make_async_copy(table_ref.at[mine, left, lanes], held[2 * group + 1], sems.at[2 * group + 1]),
            )
        )
    order = range(groups - 1, -1, -1)
    for group in order:
        for copy in copies[group]:
            copy.start()
    for group in order:
        for copy in copies[group]:
            copy.wait()
        for j in range(block):
            spec = held[2 * group][j]
            wave = owner_ref[first_ref[0] + group * block + j]
            distance = lax.broadcasted_iota(jnp.int32, (1, spec.shape[1]), 1) + (least[group] - wave)
            keep = jnp.where(distance >= 0, 1.0, 0.0)
            flip = jnp.where(distance % 2 == 0, keep, -keep)
            both = jnp.concatenate([spec * keep.astype(spec.dtype), spec * flip.astype(spec.dtype)], axis=0)
            halves = jnp.dot(both, held[2 * group + 1][j], preferred_element_type=jnp.float32) * scale
            first = 2 * (group * block + j)
            for hemi in range(2):
                for part in range(2):
                    for field in range(fields):
                        row = hemi * row_total + (part * fields + field) * levels
                        target = pl.ds(hemi * levels * stride + first + part, levels, stride=stride)
                        for tile in range(tiles):
                            lanes = slice(tile * LANES, (tile + 1) * LANES)
                            rows_ref[field, tile, target, :] = halves[row : row + levels, lanes]
    for field in range(fields):
        for tile in range(tiles):
            lanes = pl.ds((field * tiles + tile) * LANES, LANES)
            rows = rows_ref[field, tile, : 2 * levels * stride].reshape(2 * levels, stride, LANES)[:, : 2 * slots]
            out_ref[:, lanes] = rows.reshape(out_ref.shape[0], LANES).astype(out_ref.dtype)


def synthesize(first, owner_table, spec_rows, legendre, chunk, fields, levels, least):
    _, row_total, degrees = spec_rows.shape
    block = 4
    slots = block * len(least)
    rows = 2 * levels * 2 * slots
    tiles = chunk[1]
    shape = (rows, fields * tiles * LANES)
    held = []
    for start in least:
        held.append(pltpu.VMEM((block, row_total, degrees - start), jnp.bfloat16))
        held.append(pltpu.VMEM((block, degrees - start, tiles * LANES), jnp.bfloat16))
    return pl.pallas_call(
        functools.partial(synthesis_kernel, slots, levels, fields, least, chunk, 1.0 / math.sqrt(degrees)),
        in_specs=[pl.BlockSpec(memory_space=pltpu.SMEM)] * 2 + [pl.BlockSpec(memory_space=pl.ANY)] * 2,
        out_specs=pl.BlockSpec(shape, lambda: (0, 0)),
        out_shape=jax.ShapeDtypeStruct(shape, jnp.bfloat16),
        scratch_shapes=[
            pltpu.VMEM((fields, tiles, (2 * levels + 1) * padded(slots), LANES), jnp.float32),
            pltpu.SemaphoreType.DMA((2 * len(least),)),
            *held,
        ],
        compiler_params=pltpu.CompilerParams(vmem_limit_bytes=VMEM_BYTES),
        cost_estimate=pl.CostEstimate(
            flops=4 * slots * row_total * degrees * tiles * LANES,
            bytes_accessed=2 * slots * degrees * (row_total + tiles * LANES) + 2 * rows * shape[1],
            transcendentals=0,
        ),
        name="synthesis",
    )(first, owner_table, spec_rows, legendre)


def longitude_kernel(
    fields, chunk, grid_scale, zonal_scale, rows_ref, far_ref, by_lon_ref, by_wave_ref, out_ref, far_out_ref, sum_ref
):
    step = pl.program_id(0)
    near = rows_ref.shape[0]
    values = jnp.dot(by_lon_ref[:, :near], rows_ref[...], preferred_element_type=jnp.float32)
    one = values.shape[1] // fields
    each = far_ref.shape[1] // fields
    starts = [field * each + chunk[0] * LANES for field in range(fields)]
    far = jnp.concatenate([far_ref[:, start : start + one] for start in starts], axis=1)
    values = values + jnp.dot(by_lon_ref[:, near:], far, preferred_element_type=jnp.float32)
    values = values * grid_scale
    following = jnp.concatenate([values[:, one:], values[:, :one]], axis=1)
    product = (values * following).astype(jnp.bfloat16)
    share = jnp.dot(by_wave_ref[...], product, preferred_element_type=jnp.float32)

    @pl.when(step == 0)
    def _():
        sum_ref[...] = share

    @pl.when(step > 0)
    def _():
        sum_ref[...] += share

    @pl.when(step == pl.num_programs(0) - 1)
    def _():
        out_ref[...] = (sum_ref[:near, :] * zonal_scale).astype(out_ref.dtype)
        far_out_ref[...] = (sum_ref[near:, :] * zonal_scale).astype(far_out_ref.dtype)


def longitudes(rows, far, by_lon, by_wave, fields, chunk):
    depth, width = rows.shape[0] + far.shape[0], rows.shape[1]
    lon_count = by_lon.shape[0]
    lon_block = lon_count // 5
    near_spec = pl.BlockSpec(rows.shape, lambda i: (0, 0))
    far_out = jax.ShapeDtypeStruct((far.shape[0], width), jnp.bfloat16)
    return pl.pallas_call(
        functools.partial(longitude_kernel, fields, chunk, 1.0 / math.sqrt(depth // 2), 2.0 / math.sqrt(lon_count)),
        grid=(lon_count // lon_block,),
        in_specs=[
            near_spec,
            pl.BlockSpec(far.shape, lambda i: (0, 0)),
            pl.BlockSpec((lon_block, depth), lambda i: (i, 0)),
            pl.BlockSpec((depth, lon_block), lambda i: (0, i)),
        ],
        out_specs=[near_spec, pl.BlockSpec(far_out.shape, lambda i: (0, 0))],
        out_shape=[jax.ShapeDtypeStruct(rows.shape, jnp.bfloat16), far_out],
        scratch_shapes=[pltpu.VMEM((depth, width), jnp.float32)],
        compiler_params=pltpu.CompilerParams(vmem_limit_bytes=VMEM_BYTES),
        cost_estimate=pl.CostEstimate(
            flops=4 * depth * width * lon_count,
            bytes_accessed=4 * depth * (width + lon_count),
            transcendentals=0,
        ),
        name="longitudes",
    )(rows, far, by_lon, by_wave)


def pack_kernel(near, spec_ref, table_ref, out_ref, last_ref, tail_ref, sems):
    degrees, half_lat = table_ref.shape[1:]
    half = LANES // 2
    copies = []

    def fetch(source, target):
        copies.append(pltpu.make_async_copy(source, target, sems.at[len(copies)]))
        copies[-1].start()

    lanes, sides = pl.ds(0, half_lat), pl.ds(half_lat, LANES)
    for slot in range(2):
        rows = pl.ds(slot * LANES, LANES)
        fetch(table_ref.at[near + slot, pl.ds(degrees - LANES, LANES), :], out_ref.at[rows, lanes])
        fetch(spec_ref.at[near + slot, :, pl.ds(degrees - LANES, LANES)], out_ref.at[rows, sides])
    for slot in range(2):
        rows = pl.ds(slot * half, half)
        fetch(table_ref.at[near + 2 + slot, pl.ds(degrees - half, half), :], last_ref.at[rows, lanes])
        fetch(spec_ref.at[near + 2 + slot, :, pl.ds(degrees - LANES, LANES)], tail_ref.at[slot])
    for copy in copies:
        copy.wait()
    third = pltpu.roll(tail_ref[0].astype(jnp.float32), half, 1)
    lower = lax.broadcasted_iota(jnp.int32, third.shape, 1) < half
    both = jnp.where(lower, third, tail_ref[1].astype(jnp.float32))
    last_ref[:, sides] = both.astype(last_ref.dtype)


def pack(spec_rows, legendre, near):
    shapes = [(rows * LANES, legendre.shape[2] + LANES) for rows in (2, 1)]
    return pl.pallas_call(
        functools.partial(pack_kernel, near),
        in_specs=[pl.BlockSpec(memory_space=pl.ANY)] * 2,
        out_specs=[pl.BlockSpec(shape, lambda: (0, 0)) for shape in shapes],
        out_shape=[jax.ShapeDtypeStruct(shape, jnp.bfloat16) for shape in shapes],
        scratch_shapes=[
            pltpu.VMEM((2, spec_rows.shape[1], LANES), jnp.bfloat16),
            pltpu.SemaphoreType.DMA((8,)),
        ],
        compiler_params=pltpu.CompilerParams(vmem_limit_bytes=VMEM_BYTES),
        cost_estimate=pl.CostEstimate(flops=0, bytes_accessed=12 * LANES * shapes[0][1], transcendentals=0),
        name="pack",
    )(spec_rows, legendre)


def far_synthesis_kernel(levels, fields, scale, place_ref, waves_ref, *refs):
    pack_refs, out_refs, rows_ref = refs[:4], refs[4:-1], refs[-1]
    tiles = rows_ref.shape[1]
    half_lat = tiles * LANES
    stride = out_refs[0].shape[0]
    degree = lax.broadcasted_iota(jnp.int32, (1, LANES), 1)
    for slot in range(8):
        local = slot % 4
        pack_ref = pack_refs[slot // 4 * 2 + local // 2]
        rows = pl.ds(local % 2 * LANES if local < 2 else 0, LANES)
        distance = degree - waves_ref[slot] + (LANES // 2 if local == 2 else 0)
        keep = jnp.where(distance >= 0, 1.0, 0.0)
        if local >= 2:
            keep = jnp.where((degree < LANES // 2) if local == 2 else (degree >= LANES // 2), keep, 0.0)
        turned = jnp.where(distance % 2 == 0, keep, -keep)
        sign = jnp.where(place_ref[0] == 0, keep, turned)
        spec = pack_ref[rows, half_lat:]
        table = pack_ref[rows, :half_lat]
        sums = jnp.dot(spec * sign.astype(spec.dtype), table, preferred_element_type=jnp.float32) * scale
        for part in range(2):
            for field in range(fields):
                row = (part * fields + field) * levels
                for tile in range(tiles):
                    target = pl.ds(2 * slot + part, levels, stride=stride)
                    rows_ref[field, tile, target, :] = sums[row : row + levels, tile * LANES : (tile + 1) * LANES]
    for apart, out_ref in enumerate(out_refs):
        rows = pl.ds(pl.multiple_of((place_ref[1] ^ apart) * stride, stride), stride)
        for field in range(fields):
            for tile in range(tiles):
                lanes = pl.ds((field * tiles + tile) * LANES, LANES)
                out_ref[:, lanes] = rows_ref[field, tile, rows, :].astype(out_ref.dtype)


def far_synthesize(place, waves, packs, levels, fields, scale):
    tiles = packs[0].shape[1] // LANES - 1
    shape = (16, fields * tiles * LANES)
    return pl.pallas_call(
        functools.partial(far_synthesis_kernel, levels, fields, scale),
        in_specs=[pl.BlockSpec(memory_space=pltpu.SMEM)] * 2 + [pl.BlockSpec(x.shape, lambda: (0, 0)) for x in packs],
        out_specs=[pl.BlockSpec(shape, lambda: (0, 0))] * levels,
        out_shape=[jax.ShapeDtypeStruct(shape, jnp.bfloat16)] * levels,
        scratch_shapes=[pltpu.VMEM((fields, tiles, 16 * (levels + 1), LANES), jnp.float32)],
        compiler_params=pltpu.CompilerParams(vmem_limit_bytes=VMEM_BYTES),
        cost_estimate=pl.CostEstimate(
            flops=16 * 2 * fields * levels * LANES * tiles * LANES, bytes_accessed=12 * packs[0].size, transcendentals=0
        ),
        name="far_synthesis",
    )(place, waves, *packs)


def far_analysis_kernel(levels, fields, chunks, place_ref, *refs):
    pack_refs, zonal_refs = refs[:4], refs[4:-3]
    own_out_ref, partner_out_ref, rows_ref = refs[-3:]
    tiles = rows_ref.shape[1]
    stride = zonal_refs[0].shape[0]
    for apart, zonal_ref in enumerate(zonal_refs):
        rows = pl.ds(pl.multiple_of((place_ref[1] ^ apart) * stride, stride), stride)
        offset = 0
        for at, count in chunks:
            for field in range(fields):
                for tile in range(at, at + count):
                    rows_ref[field, tile, rows, :] = zonal_ref[:, pl.ds(offset, LANES)].astype(jnp.float32)
                    offset += LANES
    lower = lax.broadcasted_iota(jnp.int32, (1, LANES), 1) < LANES // 2
    for out_ref, base in ((own_out_ref, 0), (partner_out_ref, 4)):
        sums = []
        for local in range(4):
            pack_ref = pack_refs[base // 2 + local // 2]
            rows = pl.ds(local % 2 * LANES if local < 2 else 0, LANES)
            zonal = jnp.concatenate(
                [
                    jnp.concatenate(
                        [
                            rows_ref[field, tile, pl.ds(2 * (base + local) + part, levels, stride=stride), :]
                            for part in range(2)
                            for field in range(fields)
                        ],
                        axis=0,
                    ).astype(jnp.bfloat16)
                    for tile in range(tiles)
                ],
                axis=1,
            )
            table = pack_ref[rows, : tiles * LANES]
            sums.append(
                lax.dot_general(zonal, table, (((1,), (1,)), ((), ())), preferred_element_type=jnp.float32)
            )
        sums[2] = jnp.where(lower, sums[2], sums[3])
        size = sums[0].shape[0]
        for block in range(3):
            out_ref[pl.ds(block * size, size), :] = sums[block].astype(out_ref.dtype)


def far_analyze(place, packs, zonal, levels, fields, chunks):
    tiles = packs[0].shape[1] // LANES - 1
    shape = (3 * 2 * fields * levels, LANES)
    out_spec = pl.BlockSpec(shape, lambda: (0, 0))
    return pl.pallas_call(
        functools.partial(far_analysis_kernel, levels, fields, chunks),
        in_specs=[pl.BlockSpec(memory_space=pltpu.SMEM)]
        + [pl.BlockSpec(x.shape, lambda: (0, 0)) for x in (*packs, *zonal)],
        out_specs=[out_spec, out_spec],
        out_shape=[jax.ShapeDtypeStruct(shape, jnp.float32), jax.ShapeDtypeStruct(shape, jnp.bfloat16)],
        scratch_shapes=[pltpu.VMEM((fields, tiles, 16 * (levels + 1), LANES), jnp.float32)],
        compiler_params=pltpu.CompilerParams(vmem_limit_bytes=VMEM_BYTES),
        cost_estimate=pl.CostEstimate(
            flops=16 * 2 * fields * levels * LANES * tiles * LANES, bytes_accessed=12 * packs[0].size, transcendentals=0
        ),
        name="far_analysis",
    )(place, *packs, *zonal)


def fold_kernel(slots, levels, fields, arrived_ref, out_ref, rows_ref):
    tiles = rows_ref.shape[1]
    stride = padded(slots)
    half = levels * stride
    for field in range(fields):
        for tile in range(tiles):
            lanes = pl.ds((field * tiles + tile) * LANES, LANES)
            rows = arrived_ref[:, lanes].astype(jnp.float32)
            for source in range(2 * levels):
                mine = rows[2 * slots * source : 2 * slots * (source + 1)]
                rows_ref[field, tile, pl.ds(stride * source, 2 * slots), :] = mine
    for slot in range(slots):
        for part in range(2):
            for field in range(fields):
                for tile in range(tiles):
                    first = 2 * slot + part
                    north = rows_ref[field, tile, pl.ds(first, levels, stride=stride), :]
                    south = rows_ref[field, tile, pl.ds(half + first, levels, stride=stride), :]
                    lanes = pl.ds(tile * LANES, LANES)
                    at = (part * fields + field) * levels
                    out_ref[slot, at : at + levels, lanes] = (north + south).astype(out_ref.dtype)
                    at += 2 * fields * levels
                    out_ref[slot, at : at + levels, lanes] = (north - south).astype(out_ref.dtype)


def fold(arrived, slots, levels, fields):
    row_total = 2 * fields * levels
    rows, width = arrived.shape
    tiles = width // (fields * LANES)
    shape = (slots, 2 * row_total, tiles * LANES)
    return pl.pallas_call(
        functools.partial(fold_kernel, slots, levels, fields),
        in_specs=[pl.BlockSpec((rows, width), lambda: (0, 0))],
        out_specs=pl.BlockSpec(shape, lambda: (0, 0, 0)),
        out_shape=jax.ShapeDtypeStruct(shape, jnp.bfloat16),
        scratch_shapes=[pltpu.VMEM((fields, tiles, (2 * levels + 1) * padded(slots), LANES), jnp.float32)],
        compiler_params=pltpu.CompilerParams(vmem_limit_bytes=VMEM_BYTES),
        cost_estimate=pl.CostEstimate(flops=2 * rows * width, bytes_accessed=4 * rows * width, transcendentals=0),
        name="fold",
    )(arrived)


def analysis_kernel(least, folded_ref, even_ref, odd_ref, *refs):
    table_refs, out_ref = refs[:-1], refs[-1]
    row_total, degrees = out_ref.shape[1:]
    step = pl.program_id(0)

    def run(group):
        start = least[group]
        for j in range(out_ref.shape[0]):
            table = jnp.concatenate([ref[j, start:, :] for ref in table_refs], axis=1)
            sums = lax.dot_general(
                folded_ref[j], table, (((1,), (1,)), ((), ())), preferred_element_type=jnp.float32
            )
            kept = sums[:row_total] * even_ref[j, :, start:] + sums[row_total:] * odd_ref[j, :, start:]
            out_ref[j, :, start:] = kept
            if start:
                out_ref[j, :, :start] = jnp.zeros((row_total, start), out_ref.dtype)

    for group in range(len(least)):
        pl.when(step == group)(functools.partial(run, group))

    @pl.when(step == len(least))
    def _():
        out_ref[...] = jnp.zeros(out_ref.shape, out_ref.dtype)


def analyze(folded, even, odd, legendre, row_total, least, chunk):
    slots, degrees, _ = legendre.shape
    block = 4
    near = len(least) - 1
    at, tiles = chunk
    mask_spec = pl.BlockSpec((block, 1, degrees), lambda i: (i, 0, 0))
    return pl.pallas_call(
        functools.partial(analysis_kernel, least),
        grid=(len(least) + 1,),
        in_specs=[
            pl.BlockSpec((block,) + folded.shape[1:], lambda i: (jnp.minimum(i, near), 0, 0)),
            mask_spec,
            mask_spec,
        ]
        + [
            pl.BlockSpec((block, degrees, LANES), lambda i, t=at + t: (jnp.minimum(i, near), 0, t))
            for t in range(tiles)
        ],
        out_specs=pl.BlockSpec((block, row_total, degrees), lambda i: (i, 0, 0)),
        out_shape=jax.ShapeDtypeStruct((slots, row_total, degrees), jnp.float32),
        compiler_params=pltpu.CompilerParams(vmem_limit_bytes=VMEM_BYTES),
        cost_estimate=pl.CostEstimate(
            flops=4 * slots * row_total * degrees * tiles * LANES,
            bytes_accessed=2 * slots * (degrees * tiles * LANES + 2 * row_total * (tiles * LANES + degrees)),
            transcendentals=0,
        ),
        name="analysis",
    )(folded, even, odd, *[legendre] * tiles)


def closing_kernel(
    levels, fields, least, chunk, hemi_ref, arrived_ref, table_ref, base_ref, even_ref, odd_ref, own_ref, other_ref, out_ref, *refs
):
    got_ref, north_ref, south_ref, far_ref, sems = refs[:5]
    held = refs[5:]
    at, tiles = chunk
    groups = len(least)
    _, row_total, degrees = base_ref.shape
    block = 4
    slots = block * groups
    each = 2 * slots
    stride = padded(slots)
    half = levels * each
    arriving = [
        pltpu.make_async_copy(
            arrived_ref.at[:, pl.ds(field * tiles * LANES, tiles * LANES)], got_ref.at[field], sems.at[3 * groups + field]
        )
        for field in range(fields)
    ]
    tables, sums, results = [], [], []
    for group, start in enumerate(least):
        mine = pl.ds(group * block, block)
        left = pl.ds(start, degrees - start)
        lanes = pl.ds(at * LANES, tiles * LANES)
        held_table, held_sums = held[2 * group], held[2 * group + 1]
        tables.append(pltpu.make_async_copy(table_ref.at[mine, left, lanes], held_table, sems.at[3 * group]))
        sums.append(pltpu.make_async_copy(base_ref.at[mine, :, left], held_sums, sems.at[3 * group + 1]))
        results.append(pltpu.make_async_copy(held_sums, out_ref.at[mine, :, left], sems.at[3 * group + 2]))
    for copy in arriving:
        copy.start()
    for group in range(groups):
        tables[group].start()
        sums[group].start()
    for local in range(4):
        rows = pl.ds(min(local, 2) * row_total, row_total)
        own, other = own_ref[rows, :], other_ref[rows, :].astype(jnp.float32)
        both, change = own + other, jnp.where(hemi_ref[0] == 0, own - other, other - own)
        if local == 2:
            both, change = pltpu.roll(both, LANES // 2, 1), pltpu.roll(change, LANES // 2, 1)
        even = even_ref[slots + local, :, degrees - LANES :]
        odd = odd_ref[slots + local, :, degrees - LANES :]
        far_ref[local] = both * even + change * odd
    finished = pltpu.make_async_copy(
        far_ref, out_ref.at[pl.ds(slots, 4), :, pl.ds(degrees - LANES, LANES)], sems.at[3 * groups + fields]
    )
    finished.start()
    for field in range(fields):
        arriving[field].wait()
        for tile in range(tiles):
            lanes = pl.ds(tile * LANES, LANES)
            north = got_ref[field, :half, lanes].astype(jnp.float32)
            south = got_ref[field, half:, lanes].astype(jnp.float32)
            plus, minus = north + south, north - south
            for level in range(levels):
                rows = pl.ds(stride * level, each)
                north_ref[field, tile, rows, :] = plus[each * level : each * (level + 1)]
                south_ref[field, tile, rows, :] = minus[each * level : each * (level + 1)]
    for group, start in enumerate(least):
        tables[group].wait()
        sums[group].wait()
        held_table, held_sums = held[2 * group], held[2 * group + 1]
        for j in range(block):
            slot = group * block + j
            folded = jnp.concatenate(
                [
                    jnp.concatenate(
                        [
                            ref[field, tile, pl.ds(2 * slot + part, levels, stride=stride), :].astype(jnp.bfloat16)
                            for ref in (north_ref, south_ref)
                            for part in range(2)
                            for field in range(fields)
                        ],
                        axis=0,
                    )
                    for tile in range(tiles)
                ],
                axis=1,
            )
            more = lax.dot_general(
                folded, held_table[j], (((1,), (1,)), ((), ())), preferred_element_type=jnp.float32
            )
            even, odd = even_ref[slot, :, start:], odd_ref[slot, :, start:]
            held_sums[j] = held_sums[j] + more[:row_total] * even + more[row_total:] * odd
        results[group].start()
    for copy in results:
        copy.wait()
    finished.wait()


def close(hemi, own, other, arrived, base, even, odd, legendre, fields, levels, least, chunk):
    slots, row_total, degrees = base.shape
    block = 4
    rows, width = arrived.shape
    tiles = chunk[1]
    half = pltpu.VMEM((fields, tiles, (levels + 1) * padded(block * len(least)), LANES), jnp.float32)
    held = []
    for start in least:
        held.append(pltpu.VMEM((block, degrees - start, tiles * LANES), jnp.bfloat16))
        held.append(pltpu.VMEM((block, row_total, degrees - start), jnp.float32))
    anywhere = pl.BlockSpec(memory_space=pl.ANY)
    return pl.pallas_call(
        functools.partial(closing_kernel, levels, fields, least, chunk),
        in_specs=[pl.BlockSpec(memory_space=pltpu.SMEM), anywhere, anywhere, anywhere]
        + [pl.BlockSpec(even.shape, lambda: (0, 0, 0))] * 2
        + [pl.BlockSpec(own.shape, lambda: (0, 0))] * 2,
        out_specs=anywhere,
        out_shape=jax.ShapeDtypeStruct(base.shape, jnp.float32),
        input_output_aliases={3: 0},
        scratch_shapes=[
            pltpu.VMEM((fields, rows, tiles * LANES), jnp.bfloat16),
            half,
            half,
            pltpu.VMEM((4, row_total, LANES), jnp.float32),
            pltpu.SemaphoreType.DMA((3 * len(least) + fields + 1,)),
            *held,
        ],
        compiler_params=pltpu.CompilerParams(vmem_limit_bytes=VMEM_BYTES),
        cost_estimate=pl.CostEstimate(
            flops=4 * slots * row_total * degrees * tiles * LANES,
            bytes_accessed=8 * slots * row_total * degrees + 2 * rows * width,
            transcendentals=0,
        ),
        name="closing",
    )(hemi, arrived, legendre, base, even, odd, own, other)


def across_halves(value):
    planes = lax.axis_size("grp")
    return lax.ppermute(value, "grp", [(p, (p + planes // 2) % planes) for p in range(planes)])


def within_half(parts):
    bands, planes = lax.axis_size("band"), lax.axis_size("grp")
    half = planes // 2
    moved = [parts[0]]
    for x in range(1, len(parts)):
        pairs = []
        for band in range(bands):
            for plane in range(planes):
                level = (plane % half * bands + band) ^ x
                target = level % bands * planes + plane // half * half + level // bands
                pairs.append((band * planes + plane, target))
        moved.append(lax.ppermute(parts[x], AXES, pairs))
    return moved


def after(value, *others):
    return lax.optimization_barrier((value, others))[0]


def trig_kernel(small_ref, cos_turn_ref, sin_turn_ref, by_wave_ref, by_lon_ref):
    shape = cos_turn_ref.shape
    cos_start, sin_start, cos_step, sin_step = [
        jnp.broadcast_to(small_ref[:, column : column + 1], shape) for column in range(4)
    ]
    cos_turn, sin_turn = cos_turn_ref[...], sin_turn_ref[...]
    cosine = cos_start * cos_turn - sin_start * sin_turn
    sine = sin_start * cos_turn + cos_start * sin_turn
    flipped = [x.T for x in (cosine, sine, cos_step, sin_step)]
    blocks = by_wave_ref.shape[1] // LANES
    for position, (c, s, dc, ds) in enumerate(((cosine, sine, cos_step, sin_step), flipped)):
        for block in range(blocks):
            part = pl.ds(block * LANES, LANES)
            if position == 0:
                by_wave_ref[:, part] = c.astype(by_wave_ref.dtype)
            else:
                by_lon_ref[part, :] = c.astype(by_lon_ref.dtype)
            c, s = c * dc - s * ds, s * dc + c * ds


def trig_tables(owner_table, lon_count, *others):
    waves = jnp.repeat(owner_table, 2).astype(jnp.float32)[:, None]
    quarter = jnp.tile(jnp.array([0, lon_count // 4], jnp.float32), owner_table.shape[0])[:, None]
    unit = 2.0 * math.pi / lon_count

    def angles(phase):
        return (phase - lon_count * jnp.floor(phase * (1.0 / lon_count))) * unit

    start = angles(quarter)
    step = angles(waves * LANES)
    turn = angles(waves * jnp.arange(LANES, dtype=jnp.float32)[None, :])
    small = jnp.concatenate([jnp.cos(start), jnp.sin(start), jnp.cos(step), jnp.sin(step)], axis=1)
    parts = after((small, jnp.cos(turn), jnp.sin(turn)), *others)
    depth = waves.shape[0]
    rows = 256
    wide = pl.BlockSpec((rows, LANES), lambda i: (i, 0))
    return pl.pallas_call(
        trig_kernel,
        grid=(depth // rows,),
        in_specs=[pl.BlockSpec((rows, 4), lambda i: (i, 0)), wide, wide],
        out_specs=[
            pl.BlockSpec((rows, lon_count), lambda i: (i, 0)),
            pl.BlockSpec((lon_count, rows), lambda i: (0, i)),
        ],
        out_shape=[
            jax.ShapeDtypeStruct((depth, lon_count), jnp.bfloat16),
            jax.ShapeDtypeStruct((lon_count, depth), jnp.bfloat16),
        ],
        compiler_params=pltpu.CompilerParams(vmem_limit_bytes=VMEM_BYTES),
        cost_estimate=pl.CostEstimate(
            flops=12 * depth * lon_count, bytes_accessed=4 * depth * lon_count, transcendentals=0
        ),
        name="trig",
    )(*parts)


def exchange(rows):
    return lax.all_to_all(rows, AXES[::-1], split_axis=0, concat_axis=0, tiled=True)


def by_hemisphere_and_level(spectral, legendre, owner_table):
    slots, _, fields, levels, degrees = spectral.shape
    half_lat = legendre.shape[2]
    lon_count = 4 * half_lat
    row_total = 2 * fields * levels
    tiles = half_lat // LANES
    first = lax.axis_index(AXES).astype(jnp.int32) * slots
    spec_rows = spectral.reshape(slots, row_total, degrees)
    devices = 2 * levels
    least = tuple(4 * g * devices for g in range(slots // 4 - 1))
    near = slots - 4
    far_least = near * devices
    cut = tiles - tiles // 2
    chunks = [(0, cut), (cut, tiles - cut)]

    def send(spec, chunk):
        return synthesize(first.reshape(1), owner_table, spec, legendre, chunk, fields, levels, least)

    packs = list(pack(spec_rows, legendre, near))
    packs += [across_halves(packs[0]), across_halves(packs[1])]
    large = send(after(spec_rows, packs[0]), chunks[0])

    bands, planes = lax.axis_size("band"), lax.axis_size("grp")
    by_device = jnp.swapaxes(owner_table.reshape(bands, planes, slots), 0, 1).reshape(2, levels, slots)
    plane = lax.axis_index("grp").astype(jnp.int32)
    hemi = plane // (planes // 2)
    level = plane % (planes // 2) * bands + lax.axis_index("band").astype(jnp.int32)
    place = jnp.stack([hemi, level])
    far = by_device[:, :, near:]
    both_halves = jnp.concatenate([far[0], far[1]], axis=1)
    swapped = jnp.concatenate([far[1], far[0]], axis=1)
    far_waves = jnp.where(hemi == 0, both_halves, swapped)
    far_waves = jnp.take(far_waves, jnp.arange(levels, dtype=jnp.int32) ^ level, axis=0)
    waves = jnp.concatenate([by_device[:, :, :near].reshape(-1), far_waves.reshape(-1)])

    small = send(after(spec_rows, large), chunks[1])
    by_wave, by_lon = trig_tables(after(waves, large), lon_count, small)
    arrived = [exchange(after(large, small, packs[2]))]
    far_rows = far_synthesize(
        place, far_waves[0] - far_least, packs, levels, fields, 1.0 / math.sqrt(degrees)
    )
    far_rows = jnp.concatenate(within_half(far_rows))
    arrived.append(exchange(after(small, far_rows, *arrived)))
    zonal = [
        longitudes(rows, far_rows, by_lon, by_wave, fields, chunk) for rows, chunk in zip(arrived, chunks)
    ]
    returned = [exchange(zonal[0][0])]
    far_zonal = jnp.concatenate([zonal[0][1], zonal[1][1]], axis=1)
    far_zonal = within_half([far_zonal[16 * x : 16 * x + 16] for x in range(levels)])
    returned.append(exchange(after(zonal[1][0], *far_zonal, *returned)))
    own_sums, partner_sums = far_analyze(place, packs, far_zonal, levels, fields, chunks)
    other_sums = across_halves(partner_sums)
    wavenumber = lax.dynamic_slice_in_dim(after(owner_table, by_wave), first, slots)
    distance = jnp.arange(degrees, dtype=jnp.int32)[None, :] - wavenumber[:, None]
    scale = 1.0 / math.sqrt(2 * half_lat)
    even = jnp.where((distance >= 0) & (distance % 2 == 0), scale, 0.0).astype(jnp.float32)[:, None, :]
    odd = jnp.where((distance >= 0) & (distance % 2 != 0), scale, 0.0).astype(jnp.float32)[:, None, :]

    folded = fold(returned[0], near, levels, fields)
    base = analyze(folded, even, odd, legendre, row_total, least, chunks[0])
    last = after(returned[1], base)
    out = close(hemi.reshape(1), own_sums, other_sums, last, base, even, odd, legendre, fields, levels, least, chunks[1])
    return out.reshape(slots, 2, fields, levels, degrees)


def make_trig(wavenumber, lon_count):
    lon_index = jnp.arange(lon_count, dtype=jnp.int32)
    phases = wavenumber[:, None] * lon_index[None, :] % lon_count
    angles = phases.astype(jnp.float32) * (2.0 * math.pi / lon_count)
    return jnp.stack([jnp.cos(angles), -jnp.sin(angles)], axis=1).astype(jnp.bfloat16)


def by_level_and_latitude(spectral, legendre, owner_table):
    slot_count, _, fields, levels, degrees = spectral.shape
    half_lat = legendre.shape[2]
    lat_count = 2 * half_lat
    lon_count = 2 * lat_count
    wave_count = owner_table.shape[0]
    band_count = lax.axis_size("band")
    group_count = lax.axis_size("grp")
    device_count = band_count * group_count
    level_block = levels // band_count
    lat_block = lat_count // group_count
    row_total = 2 * fields * levels
    row_width = fields * level_block * lat_block
    slot_start = lax.axis_index(("band", "grp")) * slot_count
    wavenumber = lax.dynamic_slice_in_dim(owner_table, slot_start, slot_count)
    degree_index = jnp.arange(degrees, dtype=jnp.int32)
    keep_mask = (degree_index[None, :] >= wavenumber[:, None]).astype(jnp.bfloat16)
    odd_part = (degree_index[None, :] - wavenumber[:, None]) % 2
    flip_sign = (1 - 2 * odd_part).astype(jnp.bfloat16)
    spec_rows = spectral.reshape(slot_count, row_total, degrees) * keep_mask[:, None, :]
    both_rows = jnp.concatenate([spec_rows, spec_rows * flip_sign[:, None, :]], axis=1)
    halves = jnp.einsum("srn,snt->srt", both_rows, legendre, preferred_element_type=jnp.float32)
    northern = halves[:, :row_total]
    mirrored = halves[:, row_total:]
    fourier = jnp.concatenate([northern, jnp.flip(mirrored, axis=2)], axis=2)
    fourier = fourier.reshape(
        slot_count, 2, fields, band_count, level_block, group_count, lat_block
    )
    fourier = jnp.transpose(fourier, (0, 1, 2, 3, 5, 4, 6))
    fourier_low = (fourier * (1.0 / math.sqrt(degrees))).astype(jnp.bfloat16)
    packed = fourier_low.reshape(1, slot_count, 2, fields, device_count, level_block, lat_block)
    arrived = lax.all_to_all(packed, ("band", "grp"), split_axis=4, concat_axis=0, tiled=True)
    arrived = arrived.reshape(-1, 2, row_width)
    trig_rows = make_trig(owner_table, lon_count)
    grid_values = jnp.einsum("scw,scl->wl", arrived, trig_rows, preferred_element_type=jnp.float32)
    grid_values = (grid_values * (1.0 / math.sqrt(wave_count))).reshape(
        fields, level_block * lat_block, lon_count
    )
    product = (grid_values * jnp.roll(grid_values, -1, axis=0)).astype(jnp.bfloat16)
    zonal_coeffs = jnp.einsum(
        "wl,scl->scw",
        product.reshape(row_width, lon_count),
        trig_rows,
        preferred_element_type=jnp.float32,
    )
    zonal_coeffs = (zonal_coeffs * (2.0 / math.sqrt(lon_count))).astype(jnp.bfloat16)
    sendback = zonal_coeffs.reshape(device_count, slot_count, 2, fields, 1, level_block, lat_block)
    returned = lax.all_to_all(sendback, ("band", "grp"), split_axis=0, concat_axis=4, tiled=True)
    returned = returned.reshape(
        slot_count, 2, fields, band_count, group_count, level_block, lat_block
    )
    returned = jnp.transpose(returned, (0, 1, 2, 3, 5, 4, 6)).reshape(slot_count, row_total, lat_count)
    northern_part = returned[:, :, :half_lat].astype(jnp.float32)
    mirror_part = jnp.flip(returned[:, :, half_lat:], axis=2).astype(jnp.float32)
    plus_part = (northern_part + mirror_part).astype(jnp.bfloat16)
    minus_part = (northern_part - mirror_part).astype(jnp.bfloat16)
    stacked = jnp.concatenate([plus_part, minus_part], axis=1)
    projected = jnp.einsum("srt,snt->srn", stacked, legendre, preferred_element_type=jnp.float32)
    even_rows = flip_sign[:, None, :] > 0
    chosen = jnp.where(even_rows, projected[:, :row_total], projected[:, row_total:])
    chosen = chosen * keep_mask.astype(jnp.float32)[:, None, :] * (1.0 / math.sqrt(lat_count))
    return chosen.reshape(slot_count, 2, fields, levels, degrees)


def on_device(spectral, legendre, owner_table):
    slots, _, _, levels, _ = spectral.shape
    whole_hemispheres = lax.axis_size("band") * lax.axis_size("grp") == 2 * levels
    halves = lax.axis_size("grp") % 2 == 0 and levels & (levels - 1) == 0
    few_left = legendre.shape[1] - (slots - 4) * 2 * levels == LANES
    if whole_hemispheres and halves and few_left and legendre.shape[2] % LANES == 0 and legendre.shape[2] > LANES and slots % 4 == 0 and levels % 16 == 0:
        return by_hemisphere_and_level(spectral, legendre, owner_table)
    return by_level_and_latitude(spectral, legendre, owner_table)


def solution(mesh):
    placed = (P(("band", "grp"), None, None, None, None), P(("band", "grp"), None, None), P())
    return jax.shard_map(
        on_device,
        mesh=mesh,
        in_specs=placed,
        out_specs=P(("band", "grp"), None, None, None, None),
        check_vma=False,
    )
```

```python
import functools
import math

import jax
import jax.numpy as jnp
from jax import lax
from jax.experimental import pallas as pl
from jax.experimental.pallas import tpu as pltpu
from jax.sharding import PartitionSpec as P

LANES = 128
AXES = ("band", "grp")
VMEM_BYTES = 62 * 1024 * 1024


def padded(slots):
    return 2 * slots + 8


def synthesis_kernel(
    slots, levels, fields, least, chunk, scale, first_ref, owner_ref, spec_ref, table_ref, out_ref, rows_ref, sems, *held
):
    at, tiles = chunk
    groups = len(least)
    block = 4
    row_total, degrees = spec_ref.shape[1:]
    stride = padded(slots)
    copies = []
    for group, start in enumerate(least):
        mine = pl.ds(group * block, block)
        left = pl.ds(start, degrees - start)
        lanes = pl.ds(at * LANES, tiles * LANES)
        copies.append(
            (
                pltpu.make_async_copy(spec_ref.at[mine, :, left], held[2 * group], sems.at[2 * group]),
                pltpu.make_async_copy(table_ref.at[mine, left, lanes], held[2 * group + 1], sems.at[2 * group + 1]),
            )
        )
    order = range(groups - 1, -1, -1)
    for group in order:
        for copy in copies[group]:
            copy.start()
    for group in order:
        for copy in copies[group]:
            copy.wait()
        for j in range(block):
            spec = held[2 * group][j]
            wave = owner_ref[first_ref[0] + group * block + j]
            distance = lax.broadcasted_iota(jnp.int32, (1, spec.shape[1]), 1) + (least[group] - wave)
            keep = jnp.where(distance >= 0, 1.0, 0.0)
            flip = jnp.where(distance % 2 == 0, keep, -keep)
            both = jnp.concatenate([spec * keep.astype(spec.dtype), spec * flip.astype(spec.dtype)], axis=0)
            halves = jnp.dot(both, held[2 * group + 1][j], preferred_element_type=jnp.float32) * scale
            first = 2 * (group * block + j)
            for hemi in range(2):
                for part in range(2):
                    for field in range(fields):
                        row = hemi * row_total + (part * fields + field) * levels
                        target = pl.ds(hemi * levels * stride + first + part, levels, stride=stride)
                        for tile in range(tiles):
                            lanes = slice(tile * LANES, (tile + 1) * LANES)
                            rows_ref[field, tile, target, :] = halves[row : row + levels, lanes]
    for field in range(fields):
        for tile in range(tiles):
            lanes = pl.ds((field * tiles + tile) * LANES, LANES)
            rows = rows_ref[field, tile, : 2 * levels * stride].reshape(2 * levels, stride, LANES)[:, : 2 * slots]
            out_ref[:, lanes] = rows.reshape(out_ref.shape[0], LANES).astype(out_ref.dtype)


def synthesize(first, owner_table, spec_rows, legendre, chunk, fields, levels, least):
    _, row_total, degrees = spec_rows.shape
    block = 4
    slots = block * len(least)
    rows = 2 * levels * 2 * slots
    tiles = chunk[1]
    shape = (rows, fields * tiles * LANES)
    held = []
    for start in least:
        held.append(pltpu.VMEM((block, row_total, degrees - start), jnp.bfloat16))
        held.append(pltpu.VMEM((block, degrees - start, tiles * LANES), jnp.bfloat16))
    return pl.pallas_call(
        functools.partial(synthesis_kernel, slots, levels, fields, least, chunk, 1.0 / math.sqrt(degrees)),
        in_specs=[pl.BlockSpec(memory_space=pltpu.SMEM)] * 2 + [pl.BlockSpec(memory_space=pl.ANY)] * 2,
        out_specs=pl.BlockSpec(shape, lambda: (0, 0)),
        out_shape=jax.ShapeDtypeStruct(shape, jnp.bfloat16),
        scratch_shapes=[
            pltpu.VMEM((fields, tiles, (2 * levels + 1) * padded(slots), LANES), jnp.float32),
            pltpu.SemaphoreType.DMA((2 * len(least),)),
            *held,
        ],
        compiler_params=pltpu.CompilerParams(vmem_limit_bytes=VMEM_BYTES),
        cost_estimate=pl.CostEstimate(
            flops=4 * slots * row_total * degrees * tiles * LANES,
            bytes_accessed=2 * slots * degrees * (row_total + tiles * LANES) + 2 * rows * shape[1],
            transcendentals=0,
        ),
        name="synthesis",
    )(first, owner_table, spec_rows, legendre)


def longitude_kernel(
    fields, chunk, grid_scale, zonal_scale, rows_ref, far_ref, by_lon_ref, by_wave_ref, out_ref, far_out_ref, sum_ref
):
    step = pl.program_id(0)
    near = rows_ref.shape[0]
    values = jnp.dot(by_lon_ref[:, :near], rows_ref[...], preferred_element_type=jnp.float32)
    one = values.shape[1] // fields
    each = far_ref.shape[1] // fields
    starts = [field * each + chunk[0] * LANES for field in range(fields)]
    far = jnp.concatenate([far_ref[:, start : start + one] for start in starts], axis=1)
    values = values + jnp.dot(by_lon_ref[:, near:], far, preferred_element_type=jnp.float32)
    values = values * grid_scale
    following = jnp.concatenate([values[:, one:], values[:, :one]], axis=1)
    product = (values * following).astype(jnp.bfloat16)
    share = jnp.dot(by_wave_ref[...], product, preferred_element_type=jnp.float32)

    @pl.when(step == 0)
    def _():
        sum_ref[...] = share

    @pl.when(step > 0)
    def _():
        sum_ref[...] += share

    @pl.when(step == pl.num_programs(0) - 1)
    def _():
        out_ref[...] = (sum_ref[:near, :] * zonal_scale).astype(out_ref.dtype)
        far_out_ref[...] = (sum_ref[near:, :] * zonal_scale).astype(far_out_ref.dtype)


def longitudes(rows, far, by_lon, by_wave, fields, chunk):
    depth, width = rows.shape[0] + far.shape[0], rows.shape[1]
    lon_count = by_lon.shape[0]
    lon_block = lon_count // 5
    near_spec = pl.BlockSpec(rows.shape, lambda i: (0, 0))
    far_out = jax.ShapeDtypeStruct((far.shape[0], width), jnp.bfloat16)
    return pl.pallas_call(
        functools.partial(longitude_kernel, fields, chunk, 1.0 / math.sqrt(depth // 2), 2.0 / math.sqrt(lon_count)),
        grid=(lon_count // lon_block,),
        in_specs=[
            near_spec,
            pl.BlockSpec(far.shape, lambda i: (0, 0)),
            pl.BlockSpec((lon_block, depth), lambda i: (i, 0)),
            pl.BlockSpec((depth, lon_block), lambda i: (0, i)),
        ],
        out_specs=[near_spec, pl.BlockSpec(far_out.shape, lambda i: (0, 0))],
        out_shape=[jax.ShapeDtypeStruct(rows.shape, jnp.bfloat16), far_out],
        scratch_shapes=[pltpu.VMEM((depth, width), jnp.float32)],
        compiler_params=pltpu.CompilerParams(vmem_limit_bytes=VMEM_BYTES),
        cost_estimate=pl.CostEstimate(
            flops=4 * depth * width * lon_count,
            bytes_accessed=4 * depth * (width + lon_count),
            transcendentals=0,
        ),
        name="longitudes",
    )(rows, far, by_lon, by_wave)


def pack_kernel(near, spec_ref, table_ref, out_ref, last_ref, tail_ref, sems):
    degrees, half_lat = table_ref.shape[1:]
    half = LANES // 2
    copies = []

    def fetch(source, target):
        copies.append(pltpu.make_async_copy(source, target, sems.at[len(copies)]))
        copies[-1].start()

    lanes, sides = pl.ds(0, half_lat), pl.ds(half_lat, LANES)
    for slot in range(2):
        rows = pl.ds(slot * LANES, LANES)
        fetch(table_ref.at[near + slot, pl.ds(degrees - LANES, LANES), :], out_ref.at[rows, lanes])
        fetch(spec_ref.at[near + slot, :, pl.ds(degrees - LANES, LANES)], out_ref.at[rows, sides])
    for slot in range(2):
        rows = pl.ds(slot * half, half)
        fetch(table_ref.at[near + 2 + slot, pl.ds(degrees - half, half), :], last_ref.at[rows, lanes])
        fetch(spec_ref.at[near + 2 + slot, :, pl.ds(degrees - LANES, LANES)], tail_ref.at[slot])
    for copy in copies:
        copy.wait()
    third = pltpu.roll(tail_ref[0].astype(jnp.float32), half, 1)
    lower = lax.broadcasted_iota(jnp.int32, third.shape, 1) < half
    both = jnp.where(lower, third, tail_ref[1].astype(jnp.float32))
    last_ref[:, sides] = both.astype(last_ref.dtype)


def pack(spec_rows, legendre, near):
    shapes = [(rows * LANES, legendre.shape[2] + LANES) for rows in (2, 1)]
    return pl.pallas_call(
        functools.partial(pack_kernel, near),
        in_specs=[pl.BlockSpec(memory_space=pl.ANY)] * 2,
        out_specs=[pl.BlockSpec(shape, lambda: (0, 0)) for shape in shapes],
        out_shape=[jax.ShapeDtypeStruct(shape, jnp.bfloat16) for shape in shapes],
        scratch_shapes=[
            pltpu.VMEM((2, spec_rows.shape[1], LANES), jnp.bfloat16),
            pltpu.SemaphoreType.DMA((8,)),
        ],
        compiler_params=pltpu.CompilerParams(vmem_limit_bytes=VMEM_BYTES),
        cost_estimate=pl.CostEstimate(flops=0, bytes_accessed=12 * LANES * shapes[0][1], transcendentals=0),
        name="pack",
    )(spec_rows, legendre)


def far_synthesis_kernel(levels, fields, scale, place_ref, waves_ref, *refs):
    pack_refs, out_refs, rows_ref = refs[:4], refs[4:-1], refs[-1]
    tiles = rows_ref.shape[1]
    half_lat = tiles * LANES
    stride = out_refs[0].shape[0]
    degree = lax.broadcasted_iota(jnp.int32, (1, LANES), 1)
    for slot in range(8):
        local = slot % 4
        pack_ref = pack_refs[slot // 4 * 2 + local // 2]
        rows = pl.ds(local % 2 * LANES if local < 2 else 0, LANES)
        distance = degree - waves_ref[slot] + (LANES // 2 if local == 2 else 0)
        keep = jnp.where(distance >= 0, 1.0, 0.0)
        if local >= 2:
            keep = jnp.where((degree < LANES // 2) if local == 2 else (degree >= LANES // 2), keep, 0.0)
        turned = jnp.where(distance % 2 == 0, keep, -keep)
        sign = jnp.where(place_ref[0] == 0, keep, turned)
        spec = pack_ref[rows, half_lat:]
        table = pack_ref[rows, :half_lat]
        sums = jnp.dot(spec * sign.astype(spec.dtype), table, preferred_element_type=jnp.float32) * scale
        for part in range(2):
            for field in range(fields):
                row = (part * fields + field) * levels
                for tile in range(tiles):
                    target = pl.ds(2 * slot + part, levels, stride=stride)
                    rows_ref[field, tile, target, :] = sums[row : row + levels, tile * LANES : (tile + 1) * LANES]
    for apart, out_ref in enumerate(out_refs):
        rows = pl.ds(pl.multiple_of((place_ref[1] ^ apart) * stride, stride), stride)
        for field in range(fields):
            for tile in range(tiles):
                lanes = pl.ds((field * tiles + tile) * LANES, LANES)
                out_ref[:, lanes] = rows_ref[field, tile, rows, :].astype(out_ref.dtype)


def far_synthesize(place, waves, packs, levels, fields, scale):
    tiles = packs[0].shape[1] // LANES - 1
    shape = (16, fields * tiles * LANES)
    return pl.pallas_call(
        functools.partial(far_synthesis_kernel, levels, fields, scale),
        in_specs=[pl.BlockSpec(memory_space=pltpu.SMEM)] * 2 + [pl.BlockSpec(x.shape, lambda: (0, 0)) for x in packs],
        out_specs=[pl.BlockSpec(shape, lambda: (0, 0))] * levels,
        out_shape=[jax.ShapeDtypeStruct(shape, jnp.bfloat16)] * levels,
        scratch_shapes=[pltpu.VMEM((fields, tiles, 16 * (levels + 1), LANES), jnp.float32)],
        compiler_params=pltpu.CompilerParams(vmem_limit_bytes=VMEM_BYTES),
        cost_estimate=pl.CostEstimate(
            flops=16 * 2 * fields * levels * LANES * tiles * LANES, bytes_accessed=12 * packs[0].size, transcendentals=0
        ),
        name="far_synthesis",
    )(place, waves, *packs)


def far_analysis_kernel(levels, fields, chunks, place_ref, *refs):
    pack_refs, zonal_refs = refs[:4], refs[4:-3]
    own_out_ref, partner_out_ref, rows_ref = refs[-3:]
    tiles = rows_ref.shape[1]
    stride = zonal_refs[0].shape[0]
    for apart, zonal_ref in enumerate(zonal_refs):
        rows = pl.ds(pl.multiple_of((place_ref[1] ^ apart) * stride, stride), stride)
        offset = 0
        for at, count in chunks:
            for field in range(fields):
                for tile in range(at, at + count):
                    rows_ref[field, tile, rows, :] = zonal_ref[:, pl.ds(offset, LANES)].astype(jnp.float32)
                    offset += LANES
    lower = lax.broadcasted_iota(jnp.int32, (1, LANES), 1) < LANES // 2
    for out_ref, base in ((own_out_ref, 0), (partner_out_ref, 4)):
        sums = []
        for local in range(4):
            pack_ref = pack_refs[base // 2 + local // 2]
            rows = pl.ds(local % 2 * LANES if local < 2 else 0, LANES)
            zonal = jnp.concatenate(
                [
                    jnp.concatenate(
                        [
                            rows_ref[field, tile, pl.ds(2 * (base + local) + part, levels, stride=stride), :]
                            for part in range(2)
                            for field in range(fields)
                        ],
                        axis=0,
                    ).astype(jnp.bfloat16)
                    for tile in range(tiles)
                ],
                axis=1,
            )
            table = pack_ref[rows, : tiles * LANES]
            sums.append(
                lax.dot_general(zonal, table, (((1,), (1,)), ((), ())), preferred_element_type=jnp.float32)
            )
        sums[2] = jnp.where(lower, sums[2], sums[3])
        size = sums[0].shape[0]
        for block in range(3):
            out_ref[pl.ds(block * size, size), :] = sums[block].astype(out_ref.dtype)


def far_analyze(place, packs, zonal, levels, fields, chunks):
    tiles = packs[0].shape[1] // LANES - 1
    shape = (3 * 2 * fields * levels, LANES)
    out_spec = pl.BlockSpec(shape, lambda: (0, 0))
    return pl.pallas_call(
        functools.partial(far_analysis_kernel, levels, fields, chunks),
        in_specs=[pl.BlockSpec(memory_space=pltpu.SMEM)]
        + [pl.BlockSpec(x.shape, lambda: (0, 0)) for x in (*packs, *zonal)],
        out_specs=[out_spec, out_spec],
        out_shape=[jax.ShapeDtypeStruct(shape, jnp.float32), jax.ShapeDtypeStruct(shape, jnp.bfloat16)],
        scratch_shapes=[pltpu.VMEM((fields, tiles, 16 * (levels + 1), LANES), jnp.float32)],
        compiler_params=pltpu.CompilerParams(vmem_limit_bytes=VMEM_BYTES),
        cost_estimate=pl.CostEstimate(
            flops=16 * 2 * fields * levels * LANES * tiles * LANES, bytes_accessed=12 * packs[0].size, transcendentals=0
        ),
        name="far_analysis",
    )(place, *packs, *zonal)


def fold_kernel(slots, levels, fields, arrived_ref, out_ref, rows_ref):
    tiles = rows_ref.shape[1]
    stride = padded(slots)
    half = levels * stride
    for field in range(fields):
        for tile in range(tiles):
            lanes = pl.ds((field * tiles + tile) * LANES, LANES)
            rows = arrived_ref[:, lanes].astype(jnp.float32)
            for source in range(2 * levels):
                mine = rows[2 * slots * source : 2 * slots * (source + 1)]
                rows_ref[field, tile, pl.ds(stride * source, 2 * slots), :] = mine
    for slot in range(slots):
        for part in range(2):
            for field in range(fields):
                for tile in range(tiles):
                    first = 2 * slot + part
                    north = rows_ref[field, tile, pl.ds(first, levels, stride=stride), :]
                    south = rows_ref[field, tile, pl.ds(half + first, levels, stride=stride), :]
                    lanes = pl.ds(tile * LANES, LANES)
                    at = (part * fields + field) * levels
                    out_ref[slot, at : at + levels, lanes] = (north + south).astype(out_ref.dtype)
                    at += 2 * fields * levels
                    out_ref[slot, at : at + levels, lanes] = (north - south).astype(out_ref.dtype)


def fold(arrived, slots, levels, fields):
    row_total = 2 * fields * levels
    rows, width = arrived.shape
    tiles = width // (fields * LANES)
    shape = (slots, 2 * row_total, tiles * LANES)
    return pl.pallas_call(
        functools.partial(fold_kernel, slots, levels, fields),
        in_specs=[pl.BlockSpec((rows, width), lambda: (0, 0))],
        out_specs=pl.BlockSpec(shape, lambda: (0, 0, 0)),
        out_shape=jax.ShapeDtypeStruct(shape, jnp.bfloat16),
        scratch_shapes=[pltpu.VMEM((fields, tiles, (2 * levels + 1) * padded(slots), LANES), jnp.float32)],
        compiler_params=pltpu.CompilerParams(vmem_limit_bytes=VMEM_BYTES),
        cost_estimate=pl.CostEstimate(flops=2 * rows * width, bytes_accessed=4 * rows * width, transcendentals=0),
        name="fold",
    )(arrived)


def analysis_kernel(least, folded_ref, even_ref, odd_ref, *refs):
    table_refs, out_ref = refs[:-1], refs[-1]
    row_total, degrees = out_ref.shape[1:]
    step = pl.program_id(0)

    def run(group):
        start = least[group]
        for j in range(out_ref.shape[0]):
            table = jnp.concatenate([ref[j, start:, :] for ref in table_refs], axis=1)
            sums = lax.dot_general(
                folded_ref[j], table, (((1,), (1,)), ((), ())), preferred_element_type=jnp.float32
            )
            kept = sums[:row_total] * even_ref[j, :, start:] + sums[row_total:] * odd_ref[j, :, start:]
            out_ref[j, :, start:] = kept
            if start:
                out_ref[j, :, :start] = jnp.zeros((row_total, start), out_ref.dtype)

    for group in range(len(least)):
        pl.when(step == group)(functools.partial(run, group))

    @pl.when(step == len(least))
    def _():
        out_ref[...] = jnp.zeros(out_ref.shape, out_ref.dtype)


def analyze(folded, even, odd, legendre, row_total, least, chunk):
    slots, degrees, _ = legendre.shape
    block = 4
    near = len(least) - 1
    at, tiles = chunk
    mask_spec = pl.BlockSpec((block, 1, degrees), lambda i: (i, 0, 0))
    return pl.pallas_call(
        functools.partial(analysis_kernel, least),
        grid=(len(least) + 1,),
        in_specs=[
            pl.BlockSpec((block,) + folded.shape[1:], lambda i: (jnp.minimum(i, near), 0, 0)),
            mask_spec,
            mask_spec,
        ]
        + [
            pl.BlockSpec((block, degrees, LANES), lambda i, t=at + t: (jnp.minimum(i, near), 0, t))
            for t in range(tiles)
        ],
        out_specs=pl.BlockSpec((block, row_total, degrees), lambda i: (i, 0, 0)),
        out_shape=jax.ShapeDtypeStruct((slots, row_total, degrees), jnp.float32),
        compiler_params=pltpu.CompilerParams(vmem_limit_bytes=VMEM_BYTES),
        cost_estimate=pl.CostEstimate(
            flops=4 * slots * row_total * degrees * tiles * LANES,
            bytes_accessed=2 * slots * (degrees * tiles * LANES + 2 * row_total * (tiles * LANES + degrees)),
            transcendentals=0,
        ),
        name="analysis",
    )(folded, even, odd, *[legendre] * tiles)


def closing_kernel(
    levels, fields, least, chunk, hemi_ref, arrived_ref, table_ref, base_ref, even_ref, odd_ref, own_ref, other_ref, out_ref, *refs
):
    got_ref, north_ref, south_ref, far_ref, sems = refs[:5]
    held = refs[5:]
    at, tiles = chunk
    groups = len(least)
    _, row_total, degrees = base_ref.shape
    block = 4
    slots = block * groups
    each = 2 * slots
    stride = padded(slots)
    half = levels * each
    arriving = [
        pltpu.make_async_copy(
            arrived_ref.at[:, pl.ds(field * tiles * LANES, tiles * LANES)], got_ref.at[field], sems.at[3 * groups + field]
        )
        for field in range(fields)
    ]
    tables, sums, results = [], [], []
    for group, start in enumerate(least):
        mine = pl.ds(group * block, block)
        left = pl.ds(start, degrees - start)
        lanes = pl.ds(at * LANES, tiles * LANES)
        held_table, held_sums = held[2 * group], held[2 * group + 1]
        tables.append(pltpu.make_async_copy(table_ref.at[mine, left, lanes], held_table, sems.at[3 * group]))
        sums.append(pltpu.make_async_copy(base_ref.at[mine, :, left], held_sums, sems.at[3 * group + 1]))
        results.append(pltpu.make_async_copy(held_sums, out_ref.at[mine, :, left], sems.at[3 * group + 2]))
    for copy in arriving:
        copy.start()
    for group in range(groups):
        tables[group].start()
        sums[group].start()
    for local in range(4):
        rows = pl.ds(min(local, 2) * row_total, row_total)
        own, other = own_ref[rows, :], other_ref[rows, :].astype(jnp.float32)
        both, change = own + other, jnp.where(hemi_ref[0] == 0, own - other, other - own)
        if local == 2:
            both, change = pltpu.roll(both, LANES // 2, 1), pltpu.roll(change, LANES // 2, 1)
        even = even_ref[slots + local, :, degrees - LANES :]
        odd = odd_ref[slots + local, :, degrees - LANES :]
        far_ref[local] = both * even + change * odd
    finished = pltpu.make_async_copy(
        far_ref, out_ref.at[pl.ds(slots, 4), :, pl.ds(degrees - LANES, LANES)], sems.at[3 * groups + fields]
    )
    finished.start()
    for field in range(fields):
        arriving[field].wait()
        for tile in range(tiles):
            lanes = pl.ds(tile * LANES, LANES)
            north = got_ref[field, :half, lanes].astype(jnp.float32)
            south = got_ref[field, half:, lanes].astype(jnp.float32)
            plus, minus = north + south, north - south
            for level in range(levels):
                rows = pl.ds(stride * level, each)
                north_ref[field, tile, rows, :] = plus[each * level : each * (level + 1)]
                south_ref[field, tile, rows, :] = minus[each * level : each * (level + 1)]
    for group, start in enumerate(least):
        tables[group].wait()
        sums[group].wait()
        held_table, held_sums = held[2 * group], held[2 * group + 1]
        for j in range(block):
            slot = group * block + j
            folded = jnp.concatenate(
                [
                    jnp.concatenate(
                        [
                            ref[field, tile, pl.ds(2 * slot + part, levels, stride=stride), :].astype(jnp.bfloat16)
                            for ref in (north_ref, south_ref)
                            for part in range(2)
                            for field in range(fields)
                        ],
                        axis=0,
                    )
                    for tile in range(tiles)
                ],
                axis=1,
            )
            more = lax.dot_general(
                folded, held_table[j], (((1,), (1,)), ((), ())), preferred_element_type=jnp.float32
            )
            even, odd = even_ref[slot, :, start:], odd_ref[slot, :, start:]
            held_sums[j] = held_sums[j] + more[:row_total] * even + more[row_total:] * odd
        results[group].start()
    for copy in results:
        copy.wait()
    finished.wait()


def close(hemi, own, other, arrived, base, even, odd, legendre, fields, levels, least, chunk):
    slots, row_total, degrees = base.shape
    block = 4
    rows, width = arrived.shape
    tiles = chunk[1]
    half = pltpu.VMEM((fields, tiles, (levels + 1) * padded(block * len(least)), LANES), jnp.float32)
    held = []
    for start in least:
        held.append(pltpu.VMEM((block, degrees - start, tiles * LANES), jnp.bfloat16))
        held.append(pltpu.VMEM((block, row_total, degrees - start), jnp.float32))
    anywhere = pl.BlockSpec(memory_space=pl.ANY)
    return pl.pallas_call(
        functools.partial(closing_kernel, levels, fields, least, chunk),
        in_specs=[pl.BlockSpec(memory_space=pltpu.SMEM), anywhere, anywhere, anywhere]
        + [pl.BlockSpec(even.shape, lambda: (0, 0, 0))] * 2
        + [pl.BlockSpec(own.shape, lambda: (0, 0))] * 2,
        out_specs=anywhere,
        out_shape=jax.ShapeDtypeStruct(base.shape, jnp.float32),
        input_output_aliases={3: 0},
        scratch_shapes=[
            pltpu.VMEM((fields, rows, tiles * LANES), jnp.bfloat16),
            half,
            half,
            pltpu.VMEM((4, row_total, LANES), jnp.float32),
            pltpu.SemaphoreType.DMA((3 * len(least) + fields + 1,)),
            *held,
        ],
        compiler_params=pltpu.CompilerParams(vmem_limit_bytes=VMEM_BYTES),
        cost_estimate=pl.CostEstimate(
            flops=4 * slots * row_total * degrees * tiles * LANES,
            bytes_accessed=8 * slots * row_total * degrees + 2 * rows * width,
            transcendentals=0,
        ),
        name="closing",
    )(hemi, arrived, legendre, base, even, odd, own, other)


def across_halves(value):
    planes = lax.axis_size("grp")
    return lax.ppermute(value, "grp", [(p, (p + planes // 2) % planes) for p in range(planes)])


def within_half(parts):
    bands, planes = lax.axis_size("band"), lax.axis_size("grp")
    half = planes // 2
    moved = [parts[0]]
    for x in range(1, len(parts)):
        pairs = []
        for band in range(bands):
            for plane in range(planes):
                level = (plane % half * bands + band) ^ x
                target = level % bands * planes + plane // half * half + level // bands
                pairs.append((band * planes + plane, target))
        moved.append(lax.ppermute(parts[x], AXES, pairs))
    return moved


def after(value, *others):
    return lax.optimization_barrier((value, others))[0]


def trig_kernel(small_ref, cos_turn_ref, sin_turn_ref, by_wave_ref, by_lon_ref):
    shape = cos_turn_ref.shape
    cos_start, sin_start, cos_step, sin_step = [
        jnp.broadcast_to(small_ref[:, column : column + 1], shape) for column in range(4)
    ]
    cos_turn, sin_turn = cos_turn_ref[...], sin_turn_ref[...]
    cosine = cos_start * cos_turn - sin_start * sin_turn
    sine = sin_start * cos_turn + cos_start * sin_turn
    flipped = [x.T for x in (cosine, sine, cos_step, sin_step)]
    blocks = by_wave_ref.shape[1] // LANES
    for position, (c, s, dc, ds) in enumerate(((cosine, sine, cos_step, sin_step), flipped)):
        for block in range(blocks):
            part = pl.ds(block * LANES, LANES)
            if position == 0:
                by_wave_ref[:, part] = c.astype(by_wave_ref.dtype)
            else:
                by_lon_ref[part, :] = c.astype(by_lon_ref.dtype)
            c, s = c * dc - s * ds, s * dc + c * ds


def trig_tables(owner_table, lon_count, *others):
    waves = jnp.repeat(owner_table, 2).astype(jnp.float32)[:, None]
    quarter = jnp.tile(jnp.array([0, lon_count // 4], jnp.float32), owner_table.shape[0])[:, None]
    unit = 2.0 * math.pi / lon_count

    def angles(phase):
        return (phase - lon_count * jnp.floor(phase * (1.0 / lon_count))) * unit

    start = angles(quarter)
    step = angles(waves * LANES)
    turn = angles(waves * jnp.arange(LANES, dtype=jnp.float32)[None, :])
    small = jnp.concatenate([jnp.cos(start), jnp.sin(start), jnp.cos(step), jnp.sin(step)], axis=1)
    parts = after((small, jnp.cos(turn), jnp.sin(turn)), *others)
    depth = waves.shape[0]
    rows = 256
    wide = pl.BlockSpec((rows, LANES), lambda i: (i, 0))
    return pl.pallas_call(
        trig_kernel,
        grid=(depth // rows,),
        in_specs=[pl.BlockSpec((rows, 4), lambda i: (i, 0)), wide, wide],
        out_specs=[
            pl.BlockSpec((rows, lon_count), lambda i: (i, 0)),
            pl.BlockSpec((lon_count, rows), lambda i: (0, i)),
        ],
        out_shape=[
            jax.ShapeDtypeStruct((depth, lon_count), jnp.bfloat16),
            jax.ShapeDtypeStruct((lon_count, depth), jnp.bfloat16),
        ],
        compiler_params=pltpu.CompilerParams(vmem_limit_bytes=VMEM_BYTES),
        cost_estimate=pl.CostEstimate(
            flops=12 * depth * lon_count, bytes_accessed=4 * depth * lon_count, transcendentals=0
        ),
        name="trig",
    )(*parts)


def exchange(rows):
    return lax.all_to_all(rows, AXES[::-1], split_axis=0, concat_axis=0, tiled=True)


def by_hemisphere_and_level(spectral, legendre, owner_table):
    slots, _, fields, levels, degrees = spectral.shape
    half_lat = legendre.shape[2]
    lon_count = 4 * half_lat
    row_total = 2 * fields * levels
    tiles = half_lat // LANES
    first = lax.axis_index(AXES).astype(jnp.int32) * slots
    spec_rows = spectral.reshape(slots, row_total, degrees)
    devices = 2 * levels
    least = tuple(4 * g * devices for g in range(slots // 4 - 1))
    near = slots - 4
    far_least = near * devices
    cut = tiles - tiles // 2
    chunks = [(0, cut), (cut, tiles - cut)]

    def send(spec, chunk):
        return synthesize(first.reshape(1), owner_table, spec, legendre, chunk, fields, levels, least)

    packs = list(pack(spec_rows, legendre, near))
    packs += [across_halves(packs[0]), across_halves(packs[1])]
    large = send(after(spec_rows, packs[0]), chunks[0])

    bands, planes = lax.axis_size("band"), lax.axis_size("grp")
    by_device = jnp.swapaxes(owner_table.reshape(bands, planes, slots), 0, 1).reshape(2, levels, slots)
    plane = lax.axis_index("grp").astype(jnp.int32)
    hemi = plane // (planes // 2)
    level = plane % (planes // 2) * bands + lax.axis_index("band").astype(jnp.int32)
    place = jnp.stack([hemi, level])
    far = by_device[:, :, near:]
    both_halves = jnp.concatenate([far[0], far[1]], axis=1)
    swapped = jnp.concatenate([far[1], far[0]], axis=1)
    far_waves = jnp.where(hemi == 0, both_halves, swapped)
    far_waves = jnp.take(far_waves, jnp.arange(levels, dtype=jnp.int32) ^ level, axis=0)
    waves = jnp.concatenate([by_device[:, :, :near].reshape(-1), far_waves.reshape(-1)])

    small = send(after(spec_rows, large), chunks[1])
    by_wave, by_lon = trig_tables(after(waves, large), lon_count, small)
    arrived = [exchange(after(large, small))]
    far_rows = far_synthesize(
        place, far_waves[0] - far_least, packs, levels, fields, 1.0 / math.sqrt(degrees)
    )
    far_rows = jnp.concatenate(within_half(far_rows))
    arrived.append(exchange(after(small, far_rows, *arrived)))
    zonal = [
        longitudes(rows, far_rows, by_lon, by_wave, fields, chunk) for rows, chunk in zip(arrived, chunks)
    ]
    returned = [exchange(zonal[0][0])]
    far_zonal = jnp.concatenate([zonal[0][1], zonal[1][1]], axis=1)
    far_zonal = within_half([far_zonal[16 * x : 16 * x + 16] for x in range(levels)])
    returned.append(exchange(after(zonal[1][0], *far_zonal, *returned)))
    own_sums, partner_sums = far_analyze(place, packs, far_zonal, levels, fields, chunks)
    other_sums = across_halves(partner_sums)
    wavenumber = lax.dynamic_slice_in_dim(after(owner_table, by_wave), first, slots)
    distance = jnp.arange(degrees, dtype=jnp.int32)[None, :] - wavenumber[:, None]
    scale = 1.0 / math.sqrt(2 * half_lat)
    even = jnp.where((distance >= 0) & (distance % 2 == 0), scale, 0.0).astype(jnp.float32)[:, None, :]
    odd = jnp.where((distance >= 0) & (distance % 2 != 0), scale, 0.0).astype(jnp.float32)[:, None, :]

    folded = fold(returned[0], near, levels, fields)
    base = analyze(folded, even, odd, legendre, row_total, least, chunks[0])
    last = after(returned[1], base)
    out = close(hemi.reshape(1), own_sums, other_sums, last, base, even, odd, legendre, fields, levels, least, chunks[1])
    return out.reshape(slots, 2, fields, levels, degrees)


def make_trig(wavenumber, lon_count):
    lon_index = jnp.arange(lon_count, dtype=jnp.int32)
    phases = wavenumber[:, None] * lon_index[None, :] % lon_count
    angles = phases.astype(jnp.float32) * (2.0 * math.pi / lon_count)
    return jnp.stack([jnp.cos(angles), -jnp.sin(angles)], axis=1).astype(jnp.bfloat16)


def by_level_and_latitude(spectral, legendre, owner_table):
    slot_count, _, fields, levels, degrees = spectral.shape
    half_lat = legendre.shape[2]
    lat_count = 2 * half_lat
    lon_count = 2 * lat_count
    wave_count = owner_table.shape[0]
    band_count = lax.axis_size("band")
    group_count = lax.axis_size("grp")
    device_count = band_count * group_count
    level_block = levels // band_count
    lat_block = lat_count // group_count
    row_total = 2 * fields * levels
    row_width = fields * level_block * lat_block
    slot_start = lax.axis_index(("band", "grp")) * slot_count
    wavenumber = lax.dynamic_slice_in_dim(owner_table, slot_start, slot_count)
    degree_index = jnp.arange(degrees, dtype=jnp.int32)
    keep_mask = (degree_index[None, :] >= wavenumber[:, None]).astype(jnp.bfloat16)
    odd_part = (degree_index[None, :] - wavenumber[:, None]) % 2
    flip_sign = (1 - 2 * odd_part).astype(jnp.bfloat16)
    spec_rows = spectral.reshape(slot_count, row_total, degrees) * keep_mask[:, None, :]
    both_rows = jnp.concatenate([spec_rows, spec_rows * flip_sign[:, None, :]], axis=1)
    halves = jnp.einsum("srn,snt->srt", both_rows, legendre, preferred_element_type=jnp.float32)
    northern = halves[:, :row_total]
    mirrored = halves[:, row_total:]
    fourier = jnp.concatenate([northern, jnp.flip(mirrored, axis=2)], axis=2)
    fourier = fourier.reshape(
        slot_count, 2, fields, band_count, level_block, group_count, lat_block
    )
    fourier = jnp.transpose(fourier, (0, 1, 2, 3, 5, 4, 6))
    fourier_low = (fourier * (1.0 / math.sqrt(degrees))).astype(jnp.bfloat16)
    packed = fourier_low.reshape(1, slot_count, 2, fields, device_count, level_block, lat_block)
    arrived = lax.all_to_all(packed, ("band", "grp"), split_axis=4, concat_axis=0, tiled=True)
    arrived = arrived.reshape(-1, 2, row_width)
    trig_rows = make_trig(owner_table, lon_count)
    grid_values = jnp.einsum("scw,scl->wl", arrived, trig_rows, preferred_element_type=jnp.float32)
    grid_values = (grid_values * (1.0 / math.sqrt(wave_count))).reshape(
        fields, level_block * lat_block, lon_count
    )
    product = (grid_values * jnp.roll(grid_values, -1, axis=0)).astype(jnp.bfloat16)
    zonal_coeffs = jnp.einsum(
        "wl,scl->scw",
        product.reshape(row_width, lon_count),
        trig_rows,
        preferred_element_type=jnp.float32,
    )
    zonal_coeffs = (zonal_coeffs * (2.0 / math.sqrt(lon_count))).astype(jnp.bfloat16)
    sendback = zonal_coeffs.reshape(device_count, slot_count, 2, fields, 1, level_block, lat_block)
    returned = lax.all_to_all(sendback, ("band", "grp"), split_axis=0, concat_axis=4, tiled=True)
    returned = returned.reshape(
        slot_count, 2, fields, band_count, group_count, level_block, lat_block
    )
    returned = jnp.transpose(returned, (0, 1, 2, 3, 5, 4, 6)).reshape(slot_count, row_total, lat_count)
    northern_part = returned[:, :, :half_lat].astype(jnp.float32)
    mirror_part = jnp.flip(returned[:, :, half_lat:], axis=2).astype(jnp.float32)
    plus_part = (northern_part + mirror_part).astype(jnp.bfloat16)
    minus_part = (northern_part - mirror_part).astype(jnp.bfloat16)
    stacked = jnp.concatenate([plus_part, minus_part], axis=1)
    projected = jnp.einsum("srt,snt->srn", stacked, legendre, preferred_element_type=jnp.float32)
    even_rows = flip_sign[:, None, :] > 0
    chosen = jnp.where(even_rows, projected[:, :row_total], projected[:, row_total:])
    chosen = chosen * keep_mask.astype(jnp.float32)[:, None, :] * (1.0 / math.sqrt(lat_count))
    return chosen.reshape(slot_count, 2, fields, levels, degrees)


def on_device(spectral, legendre, owner_table):
    slots, _, _, levels, _ = spectral.shape
    whole_hemispheres = lax.axis_size("band") * lax.axis_size("grp") == 2 * levels
    halves = lax.axis_size("grp") % 2 == 0 and levels & (levels - 1) == 0
    few_left = legendre.shape[1] - (slots - 4) * 2 * levels == LANES
    if whole_hemispheres and halves and few_left and legendre.shape[2] % LANES == 0 and legendre.shape[2] > LANES and slots % 4 == 0 and levels % 16 == 0:
        return by_hemisphere_and_level(spectral, legendre, owner_table)
    return by_level_and_latitude(spectral, legendre, owner_table)


def solution(mesh):
    placed = (P(("band", "grp"), None, None, None, None), P(("band", "grp"), None, None), P())
    return jax.shard_map(
        on_device,
        mesh=mesh,
        in_specs=placed,
        out_specs=P(("band", "grp"), None, None, None, None),
        check_vma=False,
    )
```
